32 devices in a mesh: mix: 2 (over y), dp: 4 (over z), tensor: 4 (over x, core).
Axes of the slice: x: 2, y: 2, z: 4, core: 2. Of those that a mesh axis runs over, the one named last changes fastest.
Arguments:
- grad_gate: bfloat16 [20480, 7168], P(('mix', 'dp'), 'tensor'), parts along dimension 0, may hold values from -640 to 640
- grad_down: bfloat16 [20480, 7168], P(('mix', 'dp'), 'tensor'), parts along dimension 0, may hold values from -640 to 640
- error_gate: bfloat16 [20480, 7168], P(('mix', 'dp'), 'tensor'), parts along dimension 0, may hold values from -3 to 3
- error_down: bfloat16 [20480, 7168], P(('mix', 'dp'), 'tensor'), parts along dimension 0, may hold values from -3 to 3
- start_gate: bfloat16 [64, 7168], P(None, 'tensor'), may hold values from -5 to 5
- start_down: bfloat16 [64, 5120], replicated, may hold values from -5 to 5
Outputs:
- update_gate: bfloat16 [10240, 7168], P(('mix', 'dp'), 'tensor'), parts along dimension 0
- update_down: bfloat16 [10240, 7168], P(('mix', 'dp'), 'tensor'), parts along dimension 0
- new_error_gate: bfloat16 [20480, 7168], P(('mix', 'dp'), 'tensor'), parts along dimension 0
- new_error_down: bfloat16 [20480, 7168], P(('mix', 'dp'), 'tensor'), parts along dimension 0
The draws below stay inside these ranges and needn't reach their ends.
There are 2 independent parts, one for each index of `mix`. The reference program is written for one: setup_inputs(seed, part) draws one part's arguments, and reference() takes and returns one part's arrays. A program takes and returns all parts, laid end to end along the dimension named above; an argument that names none is the same for every part. Nothing has to cross between parts.
All inputs are finite; a program needn't handle non-finite values.
Results may differ from the reference program's by a relative error of at most 0.009.
Values sent between devices are 32-bit elements; how exact they have to be, the bound alone decides.
No kernel may reach another device: no remote copies, remote signals or barrier semaphores. Data moves between devices by JAX's collectives and lax.ppermute only.
A program may use at most 192 MiB of HBM per device.

```python
import jax
import jax.numpy as jnp
from jax import lax

ROWS = 5120
FF = 7168
RANK = 64
REPLICAS = 2
SLAB = 2560


def mixture(key, lead, height, breadth, spread):
    keys = jax.random.split(key, 4)
    common = jnp.clip(jax.random.normal(keys[0], (height, breadth), jnp.float32), -4.0, 4.0)
    own = jnp.clip(jax.random.normal(keys[1], (lead, height, breadth), jnp.float32), -4.0, 4.0)
    row_scale = jnp.exp(jax.random.uniform(keys[2], (height, 1), jnp.float32) * spread)
    col_scale = jnp.exp(jax.random.uniform(keys[3], (1, breadth), jnp.float32) * spread)
    return (common + 0.6 * own) * row_scale * col_scale


def packed_rows(stacked):
    packed = stacked.reshape(REPLICAS, ROWS // SLAB, SLAB, FF).transpose(1, 0, 2, 3)
    return packed.reshape(REPLICAS * ROWS, FF).astype(jnp.bfloat16)


def draw_grad_gate(key, part):
    key = jax.random.fold_in(key, 11)
    stacked = mixture(key, REPLICAS, ROWS, FF, 0.7)
    return packed_rows(stacked)


def draw_grad_down(key, part):
    key = jax.random.fold_in(key, 13)
    stacked = mixture(key, REPLICAS, ROWS, FF, 0.7)
    return packed_rows(stacked)


def shard_levels(rng, dims, pieces, smallest, top_value):
    level, own = 1.0, jax.random.fold_in(rng, 6)
    for position, parts in pieces:
        steps = jnp.exp(jax.random.uniform(jax.random.fold_in(own, position), (parts,), jnp.float32, smallest / len(pieces), top_value / len(pieces)))
        level = level * jnp.repeat(steps, dims[position] // parts).reshape([-1 if axis == position else 1 for axis in range(len(dims))])
    return level


def centred(stream_key, extent, scale, reach, cuts=(), kind=jnp.bfloat16):
    values = jax.random.normal(stream_key, extent, jnp.float32) * scale
    if len(cuts) > 0:
        values = shard_levels(stream_key, extent, cuts, -0.22, 0.18) * values
    return jnp.clip(values, min=-reach, max=reach).astype(kind)


def setup_inputs(seed: int = 0, part: int = 0) -> dict:
    key_of = jax.random.split(jax.random.key(seed), 7)
    own_keys = jax.random.split(jax.random.fold_in(key_of[6], part), 7)
    return {
        "grad_gate": draw_grad_gate(jax.random.fold_in(jax.random.fold_in(key_of[6], part), 71), part),
        "grad_down": draw_grad_down(jax.random.fold_in(jax.random.fold_in(key_of[6], part), 71), part),
        "error_gate": centred(own_keys[2], (REPLICAS * ROWS, FF), 0.5, 3.0, ((0, 4), (1, 4))),
        "error_down": centred(own_keys[3], (REPLICAS * ROWS, FF), 0.5, 3.0, ((0, 4), (1, 4))),
        "start_gate": centred(key_of[4], (RANK, FF), 1.0, 5.0, ((1, 4),)),
        "start_down": centred(key_of[5], (RANK, ROWS), 1.0, 5.0),
    }


def orthonormal(left):
    columns = left.shape[1]
    order = jnp.arange(columns, dtype=jnp.int32)

    def sweep(index, current):
        column = lax.dynamic_slice_in_dim(current, index, 1, 1)[:, 0]
        column = column / jnp.sqrt(jnp.sum(column * column))
        project = jnp.dot(column, current, precision=lax.Precision.HIGHEST)
        later = (order > index).astype(current.dtype)
        current = current - jnp.outer(column, project * later)
        return lax.dynamic_update_slice_in_dim(current, column[:, None], index, 1)
    return lax.fori_loop(0, columns, sweep, left)

def unpack_rows(packed):
    width = packed.shape[1]
    return packed.reshape(ROWS // SLAB, REPLICAS, SLAB, width).transpose(1, 0, 2, 3).reshape(REPLICAS, ROWS, width)

def pack_rows(stacked):
    width = stacked.shape[2]
    return stacked.reshape(REPLICAS, ROWS // SLAB, SLAB, width).transpose(1, 0, 2, 3).reshape(REPLICAS * ROWS, width)

def corrected(grad, error):
    return (grad.astype(jnp.float32) + error.astype(jnp.float32)).astype(jnp.bfloat16)

def reference(grad_gate, grad_down, error_gate, error_down, start_gate, start_down):
    high = lax.Precision.HIGHEST
    fixed_gate = corrected(unpack_rows(grad_gate), unpack_rows(error_gate))
    summed_gate = lax.optimization_barrier(jnp.sum(fixed_gate.astype(jnp.float32), axis=0))
    left_gate = jnp.dot(summed_gate, start_gate.astype(jnp.float32).T, precision=high)
    ortho_gate = orthonormal(left_gate)
    right_gate = jnp.dot(summed_gate.T, ortho_gate.astype(jnp.bfloat16).astype(jnp.float32), precision=high) / REPLICAS
    rebuilt_gate = jnp.dot(ortho_gate, right_gate.T, precision=high)
    fresh_gate = (fixed_gate.astype(jnp.float32) - rebuilt_gate[None]).astype(jnp.bfloat16)
    fixed_down = corrected(unpack_rows(grad_down), unpack_rows(error_down))
    summed_down = lax.optimization_barrier(jnp.sum(fixed_down.astype(jnp.float32), axis=0))
    left_down = jnp.dot(summed_down.T, start_down.astype(jnp.float32).T, precision=high)
    ortho_down = orthonormal(left_down)
    right_down = jnp.dot(summed_down, ortho_down.astype(jnp.bfloat16).astype(jnp.float32), precision=high) / REPLICAS
    rebuilt_down = jnp.dot(right_down, ortho_down.T, precision=high)
    fresh_down = (fixed_down.astype(jnp.float32) - rebuilt_down[None]).astype(jnp.bfloat16)
    return (rebuilt_gate.astype(jnp.bfloat16), rebuilt_down.astype(jnp.bfloat16), pack_rows(fresh_gate), pack_rows(fresh_down))
```

```python
import functools

import jax
import jax.numpy as jnp
from jax import lax
from jax.experimental import pallas as pl
from jax.experimental.pallas import tpu as pltpu
from jax.sharding import PartitionSpec as P

REPLICAS = 2
RANK = 64
TILE = 256
MIB = 1 << 20
BF16 = jnp.bfloat16
F32 = jnp.float32

NN = (((1,), (0,)), ((), ()))
NT = (((1,), (1,)), ((), ()))
TN = (((0,), (0,)), ((), ()))


def from_partner(shard, axis, stride):
    return lax.ppermute(shard, axis, [(i, i ^ 1 << stride) for i in range(lax.axis_size(axis))])


def corrected(grad, error):
    return (grad.astype(F32) + error.astype(F32)).astype(BF16)


def transposed(matrix, ortho):
    return lax.dot_general(matrix, ortho.astype(BF16), TN, preferred_element_type=F32)


def gram_of(left):
    return jnp.dot(left.T, left, precision=lax.Precision.HIGHEST)


def factored(left, inner):
    lower = jnp.linalg.cholesky(inner)
    return lax.linalg.triangular_solve(lower, left, left_side=False, lower=True, transpose_a=True)


def local_plain(grad_gate, grad_down, error_gate, error_down, start_gate, start_down):
    high = lax.Precision.HIGHEST
    dp_place = lax.axis_index("dp")
    block = dp_place // REPLICAS
    replica = dp_place % REPLICAS
    fixed_gate = corrected(grad_gate, error_gate)
    fixed_down = corrected(grad_down, error_down)
    slab = fixed_gate.shape[0]
    cols_down = lax.dynamic_slice_in_dim(start_down, block * slab, slab, 1)
    left_gate = lax.dot_general(fixed_gate, start_gate, NT, preferred_element_type=F32)
    left_down = lax.dot_general(
        fixed_down, cols_down, (((0,), (1,)), ((), ())), preferred_element_type=F32
    )
    left_gate = lax.psum(left_gate, "tensor")
    left_gate = left_gate + from_partner(left_gate, "dp", 0)
    left_down = lax.psum(left_down, "dp")
    keep_gate = (replica == 0).astype(F32)
    inner_gate = lax.psum(gram_of(left_gate) * keep_gate, "dp")
    inner_down = lax.psum(gram_of(left_down), "tensor")
    ortho_gate = factored(left_gate, inner_gate)
    ortho_down = factored(left_down, inner_down)
    right_gate = transposed(fixed_gate, ortho_gate)
    right_gate = lax.psum(right_gate, "dp") / REPLICAS
    right_down = jnp.dot(fixed_down, ortho_down.astype(BF16), preferred_element_type=F32)
    right_down = lax.psum(right_down, "tensor")
    right_down = right_down + from_partner(right_down, "dp", 0)
    right_down = right_down / REPLICAS
    rebuilt_gate = jnp.dot(ortho_gate, right_gate.T, precision=high)
    rebuilt_down = jnp.dot(right_down, ortho_down.T, precision=high)
    share = slab // REPLICAS
    update_gate = lax.dynamic_slice_in_dim(rebuilt_gate, replica * share, share, 0).astype(BF16)
    update_down = lax.dynamic_slice_in_dim(rebuilt_down, replica * share, share, 0).astype(BF16)
    new_error_gate = (fixed_gate.astype(F32) - rebuilt_gate).astype(BF16)
    new_error_down = (fixed_down.astype(F32) - rebuilt_down).astype(BF16)
    return (update_gate, update_down, new_error_gate, new_error_down)


def exchange(x, partner):
    n_dp, n_t = lax.axis_size("dp"), lax.axis_size("tensor")
    pairs = []
    for d in range(n_dp):
        for t in range(n_t):
            to_d, to_t = partner(d, t)
            pairs.append((d * n_t + t, to_d * n_t + to_t))
    return lax.ppermute(x, ("dp", "tensor"), pairs)


def bits(n, low):
    out, b = [], low
    while b < n:
        out.append(b)
        b *= 2
    return out


def sum_rows(x, core):
    n_t = lax.axis_size("tensor")
    half = RANK // 2
    keep = lax.dynamic_slice_in_dim(x, core * half, half, 0)
    give = lax.dynamic_slice_in_dim(x, (1 - core) * half, half, 0)
    own = keep + exchange(give, lambda d, t: (d, t ^ 1))
    steps = [(0, b) for b in bits(n_t, 2)] + [(1, 0)]
    for i in range(len(steps)):
        def partner(d, t, i=i):
            r, b = steps[i] if t % 2 == 0 else steps[-1 - i]
            return d ^ r, t ^ b
        own = own + exchange(own, partner)
    return own, exchange(own, lambda d, t: (d, t ^ 1))


def sum_cols(x, replica):
    n_dp = lax.axis_size("dp")
    half = RANK // 2
    keep = lax.dynamic_slice_in_dim(x, replica * half, half, 0)
    give = lax.dynamic_slice_in_dim(x, (1 - replica) * half, half, 0)
    own = keep + exchange(give, lambda d, t: (d ^ 1, t))
    for b in bits(n_dp, 2):
        own = own + exchange(own, lambda d, t, b=b: (d ^ b, t))
    return own, exchange(own, lambda d, t: (d ^ 1, t))


VMEM = pl.BlockSpec(memory_space=pltpu.VMEM)
SMEM = pl.BlockSpec(memory_space=pltpu.SMEM)
ANY = pl.BlockSpec(memory_space=pl.ANY)


def params(mib):
    return pltpu.CompilerParams(vmem_limit_bytes=mib * MIB)


def cost(flops, nbytes):
    return pl.CostEstimate(flops=int(flops), bytes_accessed=int(nbytes), transcendentals=0)


def in_vmem(x):
    return pltpu.with_memory_space_constraint(x, pltpu.VMEM)


def parts_of(x):
    hi = x.astype(BF16)
    lo = (x - hi.astype(F32)).astype(BF16)
    return hi, lo


def gate_left_kernel(grad, error, start, fixed, left):
    rows, cols = grad.shape

    def body(g, e, f, out):
        c = (g[...].astype(F32) + e[...].astype(F32)).astype(BF16)
        f[...] = c
        out[...] = lax.dot_general(start[...], c, NT, preferred_element_type=F32)

    def step(g, e):
        i = pl.program_id(0)
        at = pl.ds(pl.multiple_of(i * TILE, TILE), TILE)
        body(g, e, fixed.at[at, :], left.at[:, at])

    spec = pl.BlockSpec((TILE, cols), lambda i: (i, 0))
    pltpu.emit_pipeline(step, grid=(rows // TILE,), in_specs=[spec, spec])(grad, error)


def down_left_kernel(grad, error, start, fixed, left):
    rows, cols = grad.shape

    def step(g, e):
        i = pl.program_id(0)
        at = pl.ds(pl.multiple_of(i * TILE, TILE), TILE)
        c = (g[...].astype(F32) + e[...].astype(F32)).astype(BF16)
        fixed[at, :] = c
        term = jnp.dot(start[:, at], c, preferred_element_type=F32)

        @pl.when(i == 0)
        def _():
            left[...] = term

        @pl.when(i > 0)
        def _():
            left[...] += term

    spec = pl.BlockSpec((TILE, cols), lambda i: (i, 0))
    pltpu.emit_pipeline(step, grid=(rows // TILE,), in_specs=[spec, spec])(grad, error)


def left_call(kernel, grad, error, start, left_width):
    rows, cols = grad.shape
    return pl.pallas_call(
        kernel,
        out_shape=(
            pltpu.VMEM((rows, cols), BF16),
            jax.ShapeDtypeStruct((RANK, left_width), F32),
        ),
        in_specs=[ANY, ANY, VMEM],
        out_specs=(VMEM, VMEM),
        compiler_params=params(12),
        cost_estimate=cost(2 * rows * cols * RANK, 4 * rows * cols),
    )(grad, error, start)


def gate_right_kernel(own, other, fixed, right, gram, left, stack):
    half = RANK // 2
    left[:half, :] = own[...]
    left[half:, :] = other[...]
    hi, lo = parts_of(left[...])
    stack[:RANK, :] = hi
    stack[RANK:, :] = lo
    gram[...] = lax.dot_general(
        left[...], left[...], NT, preferred_element_type=F32, precision=lax.Precision.HIGHEST
    )
    cols = fixed.shape[1]

    def step(i, _):
        at = pl.ds(pl.multiple_of(i * TILE, TILE), TILE)
        both = jnp.dot(stack[...], fixed[:, at], preferred_element_type=F32)
        right[:, at] = both[:RANK] + both[RANK:]
        return 0

    lax.fori_loop(0, cols // TILE, step, 0)


def down_right_kernel(place, own, other, fixed, right, gram, left, stack):
    half = RANK // 2
    replica = place[1]
    left[pl.ds(pl.multiple_of(replica * half, half), half), :] = own[...]
    left[pl.ds(pl.multiple_of((1 - replica) * half, half), half), :] = other[...]
    hi, lo = parts_of(left[...])
    stack[:RANK, :] = hi
    stack[RANK:, :] = lo
    gram[...] = lax.dot_general(
        left[...], left[...], NT, preferred_element_type=F32, precision=lax.Precision.HIGHEST
    )
    rows = fixed.shape[0]

    def step(i, _):
        at = pl.ds(pl.multiple_of(i * TILE, TILE), TILE)
        both = lax.dot_general(stack[...], fixed[at, :], NT, preferred_element_type=F32)
        right[:, at] = both[:RANK] + both[RANK:]
        return 0

    lax.fori_loop(0, rows // TILE, step, 0)


def right_call(kernel, args, fixed, out_width):
    rows, cols = fixed.shape
    width = args[-1].shape[1]
    return pl.pallas_call(
        kernel,
        out_shape=(
            jax.ShapeDtypeStruct((RANK, out_width), F32),
            jax.ShapeDtypeStruct((RANK, RANK), F32),
            jax.ShapeDtypeStruct((RANK, width), F32),
        ),
        in_specs=[SMEM] * (len(args) - 2) + [VMEM, VMEM, VMEM],
        out_specs=(VMEM, VMEM, VMEM),
        scratch_shapes=[pltpu.VMEM((2 * RANK, width), BF16)],
        compiler_params=params(12),
        cost_estimate=cost(16 * rows * cols * RANK, 2 * rows * cols),
    )(*args, in_vmem(fixed))


def solve_kernel(place, gram, left, out):
    a = gram[...]
    row_at = lax.broadcasted_iota(jnp.int32, (RANK, RANK), 0)
    col_at = lax.broadcasted_iota(jnp.int32, (RANK, RANK), 1)
    for k in range(RANK):
        row = a[k : k + 1, :]
        col = a[:, k : k + 1]
        inv = 1.0 / a[k : k + 1, k : k + 1]
        row_n = row * inv
        col_n = col * inv
        new = a - col * row_n
        new = jnp.where(row_at == k, row_n, new)
        new = jnp.where(col_at == k, col_n, new)
        a = jnp.where((row_at == k) & (col_at == k), -inv, new)
    half = RANK // 2
    turned = jnp.concatenate([a[half:], a[:half]], axis=0)
    a = jnp.where(place[0] == 0, a, turned) * (-1.0 / REPLICAS)
    out[...] = jnp.dot(a, left[...], preferred_element_type=F32, precision=lax.Precision.HIGHEST)


def solve_call(turn, gram, left):
    return pl.pallas_call(
        solve_kernel,
        out_shape=jax.ShapeDtypeStruct(left.shape, F32),
        in_specs=[SMEM, VMEM, VMEM],
        out_specs=VMEM,
        compiler_params=params(8),
        cost_estimate=cost(1 << 30, 1 << 22),
    )(turn, gram, left)


def rebuild_kernel(place, row_a, row_b, col_a, col_b, fixed, update, new_error, row_stack, col_stack):
    half = RANK // 2
    for at, ref in ((0, row_a), (half, row_b)):
        hi, lo = parts_of(ref[...])
        n = ref.shape[0]
        for k, part in enumerate((hi, lo, hi, lo)):
            row_stack[k * RANK + at : k * RANK + at + n, :] = part
    for at, ref in ((0, col_a), (half, col_b)):
        hi, lo = parts_of(ref[...])
        n = ref.shape[0]
        for k, part in enumerate((hi, hi, lo, lo)):
            col_stack[k * RANK + at : k * RANK + at + n, :] = part
    rows, cols = fixed.shape
    tiles = rows // REPLICAS // TILE
    first = place[1] * tiles
    second = (1 - place[1]) * tiles

    def rebuilt(tile):
        at = pl.ds(pl.multiple_of(tile * TILE, TILE), TILE)
        value = lax.dot_general(row_stack[:, at], col_stack[...], TN, preferred_element_type=F32)
        return value, (fixed[at, :].astype(F32) - value).astype(BF16)

    def mine(u, e):
        value, fresh = rebuilt(first + pl.program_id(0))
        u[...] = value.astype(BF16)
        e[...] = fresh

    def theirs(e):
        _, fresh = rebuilt(second + pl.program_id(0))
        e[...] = fresh

    block = (TILE, cols)
    pltpu.emit_pipeline(
        mine,
        grid=(tiles,),
        out_specs=[pl.BlockSpec(block, lambda i: (i, 0)), pl.BlockSpec(block, lambda i: (first + i, 0))],
    )(update, new_error)
    pltpu.emit_pipeline(
        theirs, grid=(tiles,), out_specs=[pl.BlockSpec(block, lambda i: (second + i, 0))]
    )(new_error)


def rebuild_call(place, row_a, row_b, col_a, col_b, fixed):
    rows, cols = fixed.shape
    return pl.pallas_call(
        rebuild_kernel,
        out_shape=(
            jax.ShapeDtypeStruct((rows // REPLICAS, cols), BF16),
            jax.ShapeDtypeStruct((rows, cols), BF16),
        ),
        in_specs=[SMEM] + [VMEM] * 5,
        out_specs=(ANY, ANY),
        scratch_shapes=[pltpu.VMEM((4 * RANK, rows), BF16), pltpu.VMEM((4 * RANK, cols), BF16)],
        compiler_params=params(20),
        cost_estimate=cost(2 * rows * cols * 4 * RANK, 3 * rows * cols),
    )(place, row_a, row_b, col_a, col_b, in_vmem(fixed))


def local(grad_gate, grad_down, error_gate, error_down, start_gate, start_down):
    slab, width = grad_gate.shape
    dp_place = lax.axis_index("dp")
    core = lax.axis_index("tensor") % 2
    block = dp_place // REPLICAS
    replica = dp_place % REPLICAS
    zero = jnp.zeros_like(core)
    place = jnp.stack([core, replica])
    rows_down = lax.dynamic_slice_in_dim(start_down, block * slab, slab, 1)

    fixed_gate, left_gate = left_call(gate_left_kernel, grad_gate, error_gate, start_gate, slab)
    fixed_down, left_down = left_call(down_left_kernel, grad_down, error_down, rows_down, width)

    gate_own, gate_other = sum_rows(left_gate, core)
    down_own, down_other = sum_cols(left_down, replica)

    right_gate, gram_gate, left_gate = right_call(
        gate_right_kernel, (gate_own, gate_other), fixed_gate, width
    )
    right_down, gram_down, left_down = right_call(
        down_right_kernel, (place, down_own, down_other), fixed_down, slab
    )

    for b in bits(lax.axis_size("dp"), REPLICAS):
        gram_gate = gram_gate + exchange(gram_gate, lambda d, t, b=b: (d ^ b, t))
    for b in bits(lax.axis_size("tensor"), 1):
        gram_down = gram_down + exchange(gram_down, lambda d, t, b=b: (d, t ^ b))

    gate_rows = solve_call(jnp.stack([replica]), gram_gate, left_gate)
    down_cols = solve_call(jnp.stack([core]), gram_down, left_down)

    gate_own, gate_other = sum_cols(right_gate, replica)
    down_own, down_other = sum_rows(right_down, core)

    half = RANK // 2
    update_gate, new_error_gate = rebuild_call(
        place, gate_rows[:half], gate_rows[half:], gate_own, gate_other, fixed_gate
    )
    update_down, new_error_down = rebuild_call(
        place, down_own, down_other, down_cols[:half], down_cols[half:], fixed_down
    )
    return (update_gate, update_down, new_error_gate, new_error_down)


def solution(mesh):
    split = P(("mix", "dp"), "tensor")
    in_specs = (split, split, split, split, P(None, "tensor"), P())
    out_specs = (split, split, split, split)

    def run(grad_gate, *rest):
        groups = mesh.shape["mix"] * mesh.shape["dp"]
        slab = grad_gate.shape[0] // groups
        width = grad_gate.shape[1] // mesh.shape["tensor"]
        fits = slab % (REPLICAS * TILE) == 0 and width % TILE == 0
        body = local if fits else local_plain
        return jax.shard_map(
            body, mesh=mesh, in_specs=in_specs, out_specs=out_specs, check_vma=False
        )(grad_gate, *rest)

    return run
```

```python
import functools

import jax
import jax.numpy as jnp
from jax import lax
from jax.experimental import pallas as pl
from jax.experimental.pallas import tpu as pltpu
from jax.sharding import PartitionSpec as P

REPLICAS = 2
RANK = 64
TILE = 256
MIB = 1 << 20
BF16 = jnp.bfloat16
F32 = jnp.float32

NN = (((1,), (0,)), ((), ()))
NT = (((1,), (1,)), ((), ()))
TN = (((0,), (0,)), ((), ()))


def from_partner(shard, axis, stride):
    return lax.ppermute(shard, axis, [(i, i ^ 1 << stride) for i in range(lax.axis_size(axis))])


def corrected(grad, error):
    return (grad.astype(F32) + error.astype(F32)).astype(BF16)


def transposed(matrix, ortho):
    return lax.dot_general(matrix, ortho.astype(BF16), TN, preferred_element_type=F32)


def gram_of(left):
    return jnp.dot(left.T, left, precision=lax.Precision.HIGHEST)


def factored(left, inner):
    lower = jnp.linalg.cholesky(inner)
    return lax.linalg.triangular_solve(lower, left, left_side=False, lower=True, transpose_a=True)


def local_plain(grad_gate, grad_down, error_gate, error_down, start_gate, start_down):
    high = lax.Precision.HIGHEST
    dp_place = lax.axis_index("dp")
    block = dp_place // REPLICAS
    replica = dp_place % REPLICAS
    fixed_gate = corrected(grad_gate, error_gate)
    fixed_down = corrected(grad_down, error_down)
    slab = fixed_gate.shape[0]
    cols_down = lax.dynamic_slice_in_dim(start_down, block * slab, slab, 1)
    left_gate = lax.dot_general(fixed_gate, start_gate, NT, preferred_element_type=F32)
    left_down = lax.dot_general(
        fixed_down, cols_down, (((0,), (1,)), ((), ())), preferred_element_type=F32
    )
    left_gate = lax.psum(left_gate, "tensor")
    left_gate = left_gate + from_partner(left_gate, "dp", 0)
    left_down = lax.psum(left_down, "dp")
    keep_gate = (replica == 0).astype(F32)
    inner_gate = lax.psum(gram_of(left_gate) * keep_gate, "dp")
    inner_down = lax.psum(gram_of(left_down), "tensor")
    ortho_gate = factored(left_gate, inner_gate)
    ortho_down = factored(left_down, inner_down)
    right_gate = transposed(fixed_gate, ortho_gate)
    right_gate = lax.psum(right_gate, "dp") / REPLICAS
    right_down = jnp.dot(fixed_down, ortho_down.astype(BF16), preferred_element_type=F32)
    right_down = lax.psum(right_down, "tensor")
    right_down = right_down + from_partner(right_down, "dp", 0)
    right_down = right_down / REPLICAS
    rebuilt_gate = jnp.dot(ortho_gate, right_gate.T, precision=high)
    rebuilt_down = jnp.dot(right_down, ortho_down.T, precision=high)
    share = slab // REPLICAS
    update_gate = lax.dynamic_slice_in_dim(rebuilt_gate, replica * share, share, 0).astype(BF16)
    update_down = lax.dynamic_slice_in_dim(rebuilt_down, replica * share, share, 0).astype(BF16)
    new_error_gate = (fixed_gate.astype(F32) - rebuilt_gate).astype(BF16)
    new_error_down = (fixed_down.astype(F32) - rebuilt_down).astype(BF16)
    return (update_gate, update_down, new_error_gate, new_error_down)


def exchange(x, partner):
    n_dp, n_t = lax.axis_size("dp"), lax.axis_size("tensor")
    pairs = []
    for d in range(n_dp):
        for t in range(n_t):
            to_d, to_t = partner(d, t)
            pairs.append((d * n_t + t, to_d * n_t + to_t))
    return lax.ppermute(x, ("dp", "tensor"), pairs)


def bits(n, low):
    out, b = [], low
    while b < n:
        out.append(b)
        b *= 2
    return out


def sum_rows(x, core):
    n_t = lax.axis_size("tensor")
    half = RANK // 2
    keep = lax.dynamic_slice_in_dim(x, core * half, half, 0)
    give = lax.dynamic_slice_in_dim(x, (1 - core) * half, half, 0)
    own = keep + exchange(give, lambda d, t: (d, t ^ 1))
    steps = [(0, b) for b in bits(n_t, 2)] + [(1, 0)]
    for i in range(len(steps)):
        def partner(d, t, i=i):
            r, b = steps[i] if t % 2 == 0 else steps[-1 - i]
            return d ^ r, t ^ b
        own = own + exchange(own, partner)
    return own, exchange(own, lambda d, t: (d, t ^ 1))


def sum_cols(x, replica):
    n_dp = lax.axis_size("dp")
    half = RANK // 2
    keep = lax.dynamic_slice_in_dim(x, replica * half, half, 0)
    give = lax.dynamic_slice_in_dim(x, (1 - replica) * half, half, 0)
    own = keep + exchange(give, lambda d, t: (d ^ 1, t))
    for b in bits(n_dp, 2):
        own = own + exchange(own, lambda d, t, b=b: (d ^ b, t))
    return own, exchange(own, lambda d, t: (d ^ 1, t))


VMEM = pl.BlockSpec(memory_space=pltpu.VMEM)
SMEM = pl.BlockSpec(memory_space=pltpu.SMEM)
ANY = pl.BlockSpec(memory_space=pl.ANY)


def params(mib):
    return pltpu.CompilerParams(vmem_limit_bytes=mib * MIB)


def cost(flops, nbytes):
    return pl.CostEstimate(flops=int(flops), bytes_accessed=int(nbytes), transcendentals=0)


def in_vmem(x):
    return pltpu.with_memory_space_constraint(x, pltpu.VMEM)


def in_hbm(x):
    return pltpu.with_memory_space_constraint(x, pltpu.HBM)


def parts_of(x):
    hi = x.astype(BF16)
    lo = (x - hi.astype(F32)).astype(BF16)
    return hi, lo


def gate_left_kernel(grad, error, start, fixed, left):
    rows, cols = grad.shape

    def step(g, e):
        i = pl.program_id(0)
        at = pl.ds(pl.multiple_of(i * TILE, TILE), TILE)
        c = (g[...].astype(F32) + e[...].astype(F32)).astype(BF16)
        fixed[at, :] = c
        term = lax.dot_general(c, start[...], NT, preferred_element_type=F32)
        left[:, at] = term.T

    spec = pl.BlockSpec((TILE, cols), lambda i: (i, 0))
    pltpu.emit_pipeline(step, grid=(rows // TILE,), in_specs=[spec, spec])(grad, error)


def down_left_kernel(grad, error, start, fixed, left):
    rows, cols = grad.shape

    def step(g, e):
        i = pl.program_id(0)
        at = pl.ds(pl.multiple_of(i * TILE, TILE), TILE)
        c = (g[...].astype(F32) + e[...].astype(F32)).astype(BF16)
        fixed[at, :] = c
        term = jnp.dot(start[:, at], c, preferred_element_type=F32)

        @pl.when(i == 0)
        def _():
            left[...] = term

        @pl.when(i > 0)
        def _():
            left[...] += term

    spec = pl.BlockSpec((TILE, cols), lambda i: (i, 0))
    pltpu.emit_pipeline(step, grid=(rows // TILE,), in_specs=[spec, spec])(grad, error)


def left_call(kernel, grad, error, start, left_width):
    rows, cols = grad.shape
    return pl.pallas_call(
        kernel,
        out_shape=(
            pltpu.VMEM((rows, cols), BF16),
            jax.ShapeDtypeStruct((RANK, left_width), F32),
        ),
        in_specs=[ANY, ANY, VMEM],
        out_specs=(VMEM, VMEM),
        compiler_params=params(12),
        cost_estimate=cost(2 * rows * cols * RANK, 4 * rows * cols),
    )(in_hbm(grad), in_hbm(error), start)


def gate_right_kernel(own, other, fixed, right, gram, left, stack):
    half = RANK // 2
    left[:half, :] = own[...]
    left[half:, :] = other[...]
    hi, lo = parts_of(left[...])
    stack[:RANK, :] = hi
    stack[RANK:, :] = lo
    gram[...] = lax.dot_general(
        left[...], left[...], NT, preferred_element_type=F32, precision=lax.Precision.HIGHEST
    )
    cols = fixed.shape[1]

    def step(i, _):
        at = pl.ds(pl.multiple_of(i * TILE, TILE), TILE)
        both = jnp.dot(stack[...], fixed[:, at], preferred_element_type=F32)
        right[:, at] = both[:RANK] + both[RANK:]
        return 0

    lax.fori_loop(0, cols // TILE, step, 0)


def down_right_kernel(place, own, other, fixed, right, gram, left, stack):
    half = RANK // 2
    replica = place[1]
    left[pl.ds(pl.multiple_of(replica * half, half), half), :] = own[...]
    left[pl.ds(pl.multiple_of((1 - replica) * half, half), half), :] = other[...]
    hi, lo = parts_of(left[...])
    stack[:RANK, :] = hi
    stack[RANK:, :] = lo
    gram[...] = lax.dot_general(
        left[...], left[...], NT, preferred_element_type=F32, precision=lax.Precision.HIGHEST
    )
    rows = fixed.shape[0]

    def step(i, _):
        at = pl.ds(pl.multiple_of(i * TILE, TILE), TILE)
        both = lax.dot_general(fixed[at, :], stack[...], NT, preferred_element_type=F32)
        right[:, at] = (both[:, :RANK] + both[:, RANK:]).T
        return 0

    lax.fori_loop(0, rows // TILE, step, 0)


def right_call(kernel, args, fixed, out_width):
    rows, cols = fixed.shape
    width = args[-1].shape[1]
    return pl.pallas_call(
        kernel,
        out_shape=(
            jax.ShapeDtypeStruct((RANK, out_width), F32),
            jax.ShapeDtypeStruct((RANK, RANK), F32),
            jax.ShapeDtypeStruct((RANK, width), F32),
        ),
        in_specs=[SMEM] * (len(args) - 2) + [VMEM, VMEM, VMEM],
        out_specs=(VMEM, VMEM, VMEM),
        scratch_shapes=[pltpu.VMEM((2 * RANK, width), BF16)],
        compiler_params=params(12),
        cost_estimate=cost(16 * rows * cols * RANK, 2 * rows * cols),
    )(*args, in_vmem(fixed))


def solve_kernel(place, gram, left, out):
    a = gram[...]
    row_at = lax.broadcasted_iota(jnp.int32, (RANK, RANK), 0)
    col_at = lax.broadcasted_iota(jnp.int32, (RANK, RANK), 1)
    lane = lax.broadcasted_iota(jnp.int32, (1, RANK), 1)
    for k in range(RANK):
        col = jnp.broadcast_to(a[:, k : k + 1], (RANK, RANK))
        row = jnp.where(lane == k, 1.0, a[k : k + 1, :]) * (1.0 / col[k : k + 1, :])
        rest = jnp.where((row_at == k) | (col_at == k), 0.0, a)
        a = rest - jnp.where(row_at == k, -1.0, col) * row
    half = RANK // 2
    turned = jnp.concatenate([a[half:], a[:half]], axis=0)
    a = jnp.where(place[0] == 0, a, turned) * (1.0 / REPLICAS)
    out[...] = jnp.dot(a, left[...], preferred_element_type=F32, precision=lax.Precision.HIGHEST)


def solve_call(turn, gram, left):
    return pl.pallas_call(
        solve_kernel,
        out_shape=jax.ShapeDtypeStruct(left.shape, F32),
        in_specs=[SMEM, VMEM, VMEM],
        out_specs=VMEM,
        compiler_params=params(8),
        cost_estimate=cost(1 << 30, 1 << 22),
    )(turn, gram, left)


def rebuild_kernel(place, row_a, row_b, col_a, col_b, fixed, update, new_error, row_stack, col_stack):
    half = RANK // 2
    for at, ref in ((0, row_a), (half, row_b)):
        hi, lo = parts_of(ref[...])
        n = ref.shape[0]
        for k, part in enumerate((hi, lo, hi, lo)):
            row_stack[k * RANK + at : k * RANK + at + n, :] = part
    for at, ref in ((0, col_a), (half, col_b)):
        hi, lo = parts_of(ref[...])
        n = ref.shape[0]
        for k, part in enumerate((hi, hi, lo, lo)):
            col_stack[k * RANK + at : k * RANK + at + n, :] = part
    rows, cols = fixed.shape
    tiles = rows // REPLICAS // TILE
    first = place[1] * tiles

    def tile_of(i):
        return lax.rem(first + i, REPLICAS * tiles)

    def step(u, e):
        i = pl.program_id(0)
        at = pl.ds(pl.multiple_of(tile_of(i) * TILE, TILE), TILE)
        row = row_stack[:, at].T
        for j in range(0, cols, TILE):
            here = slice(j, j + TILE)
            value = jnp.dot(row, col_stack[:, here], preferred_element_type=F32)
            e[:, here] = (fixed[at, here].astype(F32) - value).astype(BF16)

            @pl.when(i < tiles)
            def _():
                u[:, here] = value.astype(BF16)

    block = (TILE, cols)
    pltpu.emit_pipeline(
        step,
        grid=(REPLICAS * tiles,),
        out_specs=[
            pl.BlockSpec(block, lambda i: (jnp.minimum(i, tiles - 1), 0)),
            pl.BlockSpec(block, lambda i: (tile_of(i), 0)),
        ],
    )(update, new_error)


def rebuild_call(place, row_a, row_b, col_a, col_b, fixed):
    rows, cols = fixed.shape
    return pl.pallas_call(
        rebuild_kernel,
        out_shape=(
            jax.ShapeDtypeStruct((rows // REPLICAS, cols), BF16),
            jax.ShapeDtypeStruct((rows, cols), BF16),
        ),
        in_specs=[SMEM] + [VMEM] * 5,
        out_specs=(ANY, ANY),
        scratch_shapes=[pltpu.VMEM((4 * RANK, rows), BF16), pltpu.VMEM((4 * RANK, cols), BF16)],
        compiler_params=params(20),
        cost_estimate=cost(2 * rows * cols * 4 * RANK, 3 * rows * cols),
    )(place, row_a, row_b, col_a, col_b, in_vmem(fixed))


def local(grad_gate, grad_down, error_gate, error_down, start_gate, start_down):
    slab, width = grad_gate.shape
    dp_place = lax.axis_index("dp")
    core = lax.axis_index("tensor") % 2
    block = dp_place // REPLICAS
    replica = dp_place % REPLICAS
    zero = jnp.zeros_like(core)
    place = jnp.stack([core, replica])
    rows_down = lax.dynamic_slice_in_dim(start_down, block * slab, slab, 1)

    fixed_gate, left_gate = left_call(gate_left_kernel, grad_gate, error_gate, start_gate, slab)
    fixed_down, left_down = left_call(down_left_kernel, grad_down, error_down, rows_down, width)

    gate_own, gate_other = sum_rows(left_gate, core)
    down_own, down_other = sum_cols(left_down, replica)

    right_gate, gram_gate, left_gate = right_call(
        gate_right_kernel, (gate_own, gate_other), fixed_gate, width
    )
    right_down, gram_down, left_down = right_call(
        down_right_kernel, (place, down_own, down_other), fixed_down, slab
    )

    for b in bits(lax.axis_size("dp"), REPLICAS):
        gram_gate = gram_gate + exchange(gram_gate, lambda d, t, b=b: (d ^ b, t))
    for b in bits(lax.axis_size("tensor"), 1):
        gram_down = gram_down + exchange(gram_down, lambda d, t, b=b: (d, t ^ b))

    gate_rows = solve_call(jnp.stack([replica]), gram_gate, left_gate)
    down_cols = solve_call(jnp.stack([core]), gram_down, left_down)

    gate_own, gate_other = sum_cols(right_gate, replica)
    down_own, down_other = sum_rows(right_down, core)

    half = RANK // 2
    update_gate, new_error_gate = rebuild_call(
        place, gate_rows[:half], gate_rows[half:], gate_own, gate_other, fixed_gate
    )
    update_down, new_error_down = rebuild_call(
        place, down_own, down_other, down_cols[:half], down_cols[half:], fixed_down
    )
    return (update_gate, update_down, new_error_gate, new_error_down)


def solution(mesh):
    split = P(("mix", "dp"), "tensor")
    in_specs = (split, split, split, split, P(None, "tensor"), P())
    out_specs = (split, split, split, split)

    def run(grad_gate, *rest):
        groups = mesh.shape["mix"] * mesh.shape["dp"]
        slab = grad_gate.shape[0] // groups
        width = grad_gate.shape[1] // mesh.shape["tensor"]
        fits = slab % (REPLICAS * TILE) == 0 and width % TILE == 0
        body = local if fits else local_plain
        return jax.shard_map(
            body, mesh=mesh, in_specs=in_specs, out_specs=out_specs, check_vma=False
        )(grad_gate, *rest)

    return run
```

```python
import functools

import jax
import jax.numpy as jnp
from jax import lax
from jax.experimental import pallas as pl
from jax.experimental.pallas import tpu as pltpu
from jax.sharding import PartitionSpec as P

REPLICAS = 2
RANK = 64
TILE = 256
MIB = 1 << 20
BF16 = jnp.bfloat16
F32 = jnp.float32

NN = (((1,), (0,)), ((), ()))
NT = (((1,), (1,)), ((), ()))
TN = (((0,), (0,)), ((), ()))


def from_partner(shard, axis, stride):
    return lax.ppermute(shard, axis, [(i, i ^ 1 << stride) for i in range(lax.axis_size(axis))])


def corrected(grad, error):
    return (grad.astype(F32) + error.astype(F32)).astype(BF16)


def transposed(matrix, ortho):
    return lax.dot_general(matrix, ortho.astype(BF16), TN, preferred_element_type=F32)


def gram_of(left):
    return jnp.dot(left.T, left, precision=lax.Precision.HIGHEST)


def factored(left, inner):
    lower = jnp.linalg.cholesky(inner)
    return lax.linalg.triangular_solve(lower, left, left_side=False, lower=True, transpose_a=True)


def local_plain(grad_gate, grad_down, error_gate, error_down, start_gate, start_down):
    high = lax.Precision.HIGHEST
    dp_place = lax.axis_index("dp")
    block = dp_place // REPLICAS
    replica = dp_place % REPLICAS
    fixed_gate = corrected(grad_gate, error_gate)
    fixed_down = corrected(grad_down, error_down)
    slab = fixed_gate.shape[0]
    cols_down = lax.dynamic_slice_in_dim(start_down, block * slab, slab, 1)
    left_gate = lax.dot_general(fixed_gate, start_gate, NT, preferred_element_type=F32)
    left_down = lax.dot_general(
        fixed_down, cols_down, (((0,), (1,)), ((), ())), preferred_element_type=F32
    )
    left_gate = lax.psum(left_gate, "tensor")
    left_gate = left_gate + from_partner(left_gate, "dp", 0)
    left_down = lax.psum(left_down, "dp")
    keep_gate = (replica == 0).astype(F32)
    inner_gate = lax.psum(gram_of(left_gate) * keep_gate, "dp")
    inner_down = lax.psum(gram_of(left_down), "tensor")
    ortho_gate = factored(left_gate, inner_gate)
    ortho_down = factored(left_down, inner_down)
    right_gate = transposed(fixed_gate, ortho_gate)
    right_gate = lax.psum(right_gate, "dp") / REPLICAS
    right_down = jnp.dot(fixed_down, ortho_down.astype(BF16), preferred_element_type=F32)
    right_down = lax.psum(right_down, "tensor")
    right_down = right_down + from_partner(right_down, "dp", 0)
    right_down = right_down / REPLICAS
    rebuilt_gate = jnp.dot(ortho_gate, right_gate.T, precision=high)
    rebuilt_down = jnp.dot(right_down, ortho_down.T, precision=high)
    share = slab // REPLICAS
    update_gate = lax.dynamic_slice_in_dim(rebuilt_gate, replica * share, share, 0).astype(BF16)
    update_down = lax.dynamic_slice_in_dim(rebuilt_down, replica * share, share, 0).astype(BF16)
    new_error_gate = (fixed_gate.astype(F32) - rebuilt_gate).astype(BF16)
    new_error_down = (fixed_down.astype(F32) - rebuilt_down).astype(BF16)
    return (update_gate, update_down, new_error_gate, new_error_down)


def core_of():
    return lax.rem(lax.axis_index("tensor"), 2)


def replica_of():
    return lax.rem(lax.axis_index("dp"), REPLICAS)


def exchange(x, partner):
    n_dp, n_t = lax.axis_size("dp"), lax.axis_size("tensor")
    pairs = []
    for d in range(n_dp):
        for t in range(n_t):
            to_d, to_t = partner(d, t)
            pairs.append((d * n_t + t, to_d * n_t + to_t))
    return lax.ppermute(x, ("dp", "tensor"), pairs)


def bits(n, low):
    out, b = [], low
    while b < n:
        out.append(b)
        b *= 2
    return out


def sum_rows(keep, give):
    n_t = lax.axis_size("tensor")
    own = add_call(keep, exchange(give, lambda d, t: (d, t ^ 1)))
    steps = [(0, b) for b in bits(n_t, 2)] + [(1, 0)]
    for i in range(len(steps)):
        def partner(d, t, i=i):
            r, b = steps[i] if t % 2 == 0 else steps[-1 - i]
            return d ^ r, t ^ b
        own = add_call(own, exchange(own, partner))
    return own, exchange(own, lambda d, t: (d, t ^ 1))


def sum_cols(keep, give):
    n_dp = lax.axis_size("dp")
    own = add_call(keep, exchange(give, lambda d, t: (d ^ 1, t)))
    for b in bits(n_dp, REPLICAS):
        own = add_call(own, exchange(own, lambda d, t, b=b: (d ^ b, t)))
    return own, exchange(own, lambda d, t: (d ^ 1, t))


VMEM = pl.BlockSpec(memory_space=pltpu.VMEM)
HBM = pl.BlockSpec(memory_space=pltpu.HBM)


def params(mib):
    return pltpu.CompilerParams(vmem_limit_bytes=mib * MIB)


def cost(micros):
    return pl.CostEstimate(flops=int(micros * 1.1e9), bytes_accessed=0, transcendentals=0)


def in_vmem(*xs):
    return [pltpu.with_memory_space_constraint(x, pltpu.VMEM) for x in xs]


def in_hbm(x):
    return pltpu.with_memory_space_constraint(x, pltpu.HBM)


def parts_of(x):
    hi = x.astype(BF16)
    lo = (x - hi.astype(F32)).astype(BF16)
    return hi, lo


def add_kernel(x, y, out):
    out[...] = x[...] + y[...]


def add_call(x, y):
    return pl.pallas_call(
        add_kernel,
        out_shape=pltpu.VMEM(x.shape, F32),
        in_specs=[VMEM, VMEM],
        out_specs=VMEM,
        compiler_params=params(4),
        cost_estimate=cost(0.2),
    )(*in_vmem(x, y))


def halve(whole, place, keep, give):
    half = RANK // 2
    keep[...] = whole[pl.ds(pl.multiple_of(place * half, half), half), :]
    give[...] = whole[pl.ds(pl.multiple_of((1 - place) * half, half), half), :]


def gate_left_kernel(grad, error, start, fixed, keep, give, left):
    rows, cols = grad.shape

    def step(g, e):
        at = pl.ds(pl.multiple_of(pl.program_id(0) * TILE, TILE), TILE)
        term = jnp.zeros((TILE, RANK), F32)
        for j in range(0, cols, TILE):
            here = slice(j, j + TILE)
            c = g[:, here] + e[:, here]
            fixed[at, here] = c
            term += lax.dot_general(c, start[:, here], NT, preferred_element_type=F32)
        left[:, at] = term.T

    spec = pl.BlockSpec((TILE, cols), lambda i: (i, 0), pipeline_mode=pl.Buffered(3))
    pltpu.emit_pipeline(step, grid=(rows // TILE,), in_specs=[spec, spec])(grad, error)
    halve(left, core_of(), keep, give)


def down_left_kernel(grad, error, start, fixed, keep, give, left):
    rows, cols = grad.shape
    block = lax.div(lax.axis_index("dp"), REPLICAS) * (rows // TILE)
    left[...] = jnp.zeros_like(left)

    def step(g, e, s):
        at = pl.ds(pl.multiple_of(pl.program_id(0) * TILE, TILE), TILE)
        for j in range(0, cols, TILE):
            here = slice(j, j + TILE)
            c = g[:, here] + e[:, here]
            fixed[at, here] = c
            left[:, here] += jnp.dot(s[...], c, preferred_element_type=F32)

    spec = pl.BlockSpec((TILE, cols), lambda i: (i, 0), pipeline_mode=pl.Buffered(3))
    part = pl.BlockSpec((RANK, TILE), lambda i: (0, block + i))
    pltpu.emit_pipeline(step, grid=(rows // TILE,), in_specs=[spec, spec, part])(grad, error, start)
    halve(left, replica_of(), keep, give)


def left_call(kernel, grad, error, start, start_spec, width):
    rows, cols = grad.shape
    half = RANK // 2
    start = in_hbm(start) if start_spec is HBM else in_vmem(start)[0]
    return pl.pallas_call(
        kernel,
        out_shape=(
            pltpu.VMEM((rows, cols), BF16),
            pltpu.VMEM((half, width), F32),
            pltpu.VMEM((half, width), F32),
        ),
        in_specs=[HBM, HBM, start_spec],
        out_specs=(VMEM, VMEM, VMEM),
        scratch_shapes=[pltpu.VMEM((RANK, width), F32)],
        compiler_params=params(12),
        cost_estimate=cost(7),
    )(in_hbm(grad), in_hbm(error), start)


def load_left(own, other, place, left, stack, gram):
    half = RANK // 2
    left[pl.ds(pl.multiple_of(place * half, half), half), :] = own[...]
    left[pl.ds(pl.multiple_of((1 - place) * half, half), half), :] = other[...]
    hi, lo = parts_of(left[...])
    stack[:RANK, :] = hi
    stack[RANK:, :] = lo
    gram[...] = lax.dot_general(
        left[...], left[...], NT, preferred_element_type=F32, precision=lax.Precision.HIGHEST
    )


def gate_right_kernel(own, other, fixed, keep, give, gram, left, stack, right):
    load_left(own, other, core_of(), left, stack, gram)
    cols = fixed.shape[1]

    def step(i, _):
        at = pl.ds(pl.multiple_of(i * TILE, TILE), TILE)
        both = jnp.dot(stack[...], fixed[:, at], preferred_element_type=F32)
        right[:, at] = both[:RANK] + both[RANK:]
        return 0

    lax.fori_loop(0, cols // TILE, step, 0)
    halve(right, replica_of(), keep, give)


def down_right_kernel(own, other, fixed, keep, give, gram, left, stack, right):
    load_left(own, other, replica_of(), left, stack, gram)
    rows = fixed.shape[0]

    def step(i, _):
        at = pl.ds(pl.multiple_of(i * TILE, TILE), TILE)
        both = lax.dot_general(stack[...], fixed[at, :], NT, preferred_element_type=F32)
        right[:, at] = both[:RANK] + both[RANK:]
        return 0

    lax.fori_loop(0, rows // TILE, step, 0)
    halve(right, core_of(), keep, give)


def right_call(kernel, own, other, fixed, out_width):
    width = own.shape[1]
    half = RANK // 2
    return pl.pallas_call(
        kernel,
        out_shape=(
            pltpu.VMEM((half, out_width), F32),
            pltpu.VMEM((half, out_width), F32),
            pltpu.VMEM((RANK, RANK), F32),
            pltpu.VMEM((RANK, width), F32),
        ),
        in_specs=[VMEM, VMEM, VMEM],
        out_specs=(VMEM, VMEM, VMEM, VMEM),
        scratch_shapes=[pltpu.VMEM((2 * RANK, width), BF16), pltpu.VMEM((RANK, out_width), F32)],
        compiler_params=params(8),
        cost_estimate=cost(4),
    )(*in_vmem(own, other, fixed))


def solve_kernel(place_of, n, *refs):
    left, out = refs[n:]
    a = refs[0][...]
    for ref in refs[1:n]:
        a += ref[...]
    row_at = lax.broadcasted_iota(jnp.int32, (RANK, RANK), 0)
    col_at = lax.broadcasted_iota(jnp.int32, (RANK, RANK), 1)
    lane = lax.broadcasted_iota(jnp.int32, (1, RANK), 1)
    for k in range(RANK):
        col = jnp.broadcast_to(a[:, k : k + 1], (RANK, RANK))
        row = jnp.where(lane == k, 1.0, a[k : k + 1, :]) * (1.0 / col[k : k + 1, :])
        rest = jnp.where((row_at == k) | (col_at == k), 0.0, a)
        a = rest - jnp.where(row_at == k, -1.0, col) * row
    half = RANK // 2
    turned = jnp.concatenate([a[half:], a[:half]], axis=0)
    a = jnp.where(place_of() == 0, a, turned) * (1.0 / REPLICAS)
    out[...] = jnp.dot(a, left[...], preferred_element_type=F32, precision=lax.Precision.HIGHEST)


def solve_call(place_of, grams, left):
    n = len(grams)
    return pl.pallas_call(
        functools.partial(solve_kernel, place_of, n),
        out_shape=pltpu.VMEM(left.shape, F32),
        in_specs=[VMEM] * (n + 1),
        out_specs=VMEM,
        compiler_params=params(4),
        cost_estimate=cost(6),
    )(*in_vmem(*grams, left))


def rebuild_kernel(n_row, *refs):
    row_refs, col_refs = refs[:n_row], refs[n_row:3]
    fixed, update, new_error, row_stack, col_stack = refs[3:]
    for sources, stack, order in ((row_refs, row_stack, (0, 1, 0, 1)), (col_refs, col_stack, (0, 0, 1, 1))):
        at = 0
        for ref in sources:
            parts = parts_of(ref[...])
            n = ref.shape[0]
            for k, which in enumerate(order):
                stack[k * RANK + at : k * RANK + at + n, :] = parts[which]
            at += n
    rows, cols = fixed.shape
    tiles = rows // REPLICAS // TILE
    first = replica_of() * tiles

    def tile_of(i):
        return lax.rem(first + i, REPLICAS * tiles)

    def step(u, e):
        i = pl.program_id(0)
        at = pl.ds(pl.multiple_of(tile_of(i) * TILE, TILE), TILE)

        def tile(with_update):
            row = row_stack[:, at].T
            for j in range(0, cols, TILE):
                here = slice(j, j + TILE)
                value = jnp.dot(row, col_stack[:, here], preferred_element_type=F32)
                e[:, here] = (fixed[at, here].astype(F32) - value).astype(BF16)
                if with_update:
                    u[:, here] = value.astype(BF16)

        pl.when(i < tiles)(lambda: tile(True))
        pl.when(i >= tiles)(lambda: tile(False))

    block = (TILE, cols)
    pltpu.emit_pipeline(
        step,
        grid=(REPLICAS * tiles,),
        out_specs=[
            pl.BlockSpec(block, lambda i: (jnp.minimum(i, tiles - 1), 0)),
            pl.BlockSpec(block, lambda i: (tile_of(i), 0)),
        ],
    )(update, new_error)


def rebuild_call(rows_in, cols_in, fixed):
    rows, cols = fixed.shape
    return pl.pallas_call(
        functools.partial(rebuild_kernel, len(rows_in)),
        out_shape=(
            pltpu.HBM((rows // REPLICAS, cols), BF16),
            pltpu.HBM((rows, cols), BF16),
        ),
        in_specs=[VMEM] * 4,
        out_specs=(HBM, HBM),
        scratch_shapes=[pltpu.VMEM((4 * RANK, rows), BF16), pltpu.VMEM((4 * RANK, cols), BF16)],
        compiler_params=params(12),
        cost_estimate=cost(6),
    )(*in_vmem(*rows_in, *cols_in, fixed))


def local(grad_gate, grad_down, error_gate, error_down, start_gate, start_down):
    slab, width = grad_gate.shape
    n_dp, n_t = lax.axis_size("dp"), lax.axis_size("tensor")

    fixed_down, *down = left_call(down_left_kernel, grad_down, error_down, start_down, HBM, width)
    fixed_gate, *gate = left_call(gate_left_kernel, grad_gate, error_gate, start_gate, VMEM, slab)

    *down, gram_down, left_down = right_call(down_right_kernel, *sum_cols(*down), fixed_down, slab)
    *gate, gram_gate, left_gate = right_call(gate_right_kernel, *sum_rows(*gate), fixed_gate, width)

    grams_down = [gram_down] + [
        exchange(gram_down, lambda d, t, b=b: (d, t ^ b)) for b in range(1, n_t)
    ]
    grams_gate = [gram_gate] + [
        exchange(gram_gate, lambda d, t, b=b: (d ^ b, t)) for b in range(REPLICAS, n_dp, REPLICAS)
    ]
    down_cols = solve_call(core_of, grams_down, left_down)
    gate_rows = solve_call(replica_of, grams_gate, left_gate)

    update_down, new_error_down = rebuild_call(sum_rows(*down), [down_cols], fixed_down)
    update_gate, new_error_gate = rebuild_call([gate_rows], sum_cols(*gate), fixed_gate)
    return (update_gate, update_down, new_error_gate, new_error_down)


def solution(mesh):
    split = P(("mix", "dp"), "tensor")
    in_specs = (split, split, split, split, P(None, "tensor"), P())
    out_specs = (split, split, split, split)

    def run(grad_gate, *rest):
        groups = mesh.shape["mix"] * mesh.shape["dp"]
        slab = grad_gate.shape[0] // groups
        width = grad_gate.shape[1] // mesh.shape["tensor"]
        fits = slab % (REPLICAS * TILE) == 0 and width % TILE == 0
        body = local if fits else local_plain
        return jax.shard_map(
            body, mesh=mesh, in_specs=in_specs, out_specs=out_specs, check_vma=False
        )(grad_gate, *rest)

    return run
```

```python
import functools

import jax
import jax.numpy as jnp
from jax import lax
from jax.experimental import pallas as pl
from jax.experimental.pallas import tpu as pltpu
from jax.sharding import PartitionSpec as P

REPLICAS = 2
RANK = 64
TILE = 256
FLOPS = 1.15e9
WEIGHTS = (8.0, 8.0, 1.0, 1.0, 1.0, 1.0, 1.0, 4.0, 4.0, 1.0, 1.0, 1.0, 6.0, 1.0, 1.0, 8.0, 8.0)
MIB = 1 << 20
BF16 = jnp.bfloat16
F32 = jnp.float32

NN = (((1,), (0,)), ((), ()))
NT = (((1,), (1,)), ((), ()))
TN = (((0,), (0,)), ((), ()))


def from_partner(shard, axis, stride):
    return lax.ppermute(shard, axis, [(i, i ^ 1 << stride) for i in range(lax.axis_size(axis))])


def corrected(grad, error):
    return (grad.astype(F32) + error.astype(F32)).astype(BF16)


def transposed(matrix, ortho):
    return lax.dot_general(matrix, ortho.astype(BF16), TN, preferred_element_type=F32)


def gram_of(left):
    return jnp.dot(left.T, left, precision=lax.Precision.HIGHEST)


def factored(left, inner):
    lower = jnp.linalg.cholesky(inner)
    return lax.linalg.triangular_solve(lower, left, left_side=False, lower=True, transpose_a=True)


def local_plain(grad_gate, grad_down, error_gate, error_down, start_gate, start_down):
    high = lax.Precision.HIGHEST
    dp_place = lax.axis_index("dp")
    block = dp_place // REPLICAS
    replica = dp_place % REPLICAS
    fixed_gate = corrected(grad_gate, error_gate)
    fixed_down = corrected(grad_down, error_down)
    slab = fixed_gate.shape[0]
    cols_down = lax.dynamic_slice_in_dim(start_down, block * slab, slab, 1)
    left_gate = lax.dot_general(fixed_gate, start_gate, NT, preferred_element_type=F32)
    left_down = lax.dot_general(
        fixed_down, cols_down, (((0,), (1,)), ((), ())), preferred_element_type=F32
    )
    left_gate = lax.psum(left_gate, "tensor")
    left_gate = left_gate + from_partner(left_gate, "dp", 0)
    left_down = lax.psum(left_down, "dp")
    keep_gate = (replica == 0).astype(F32)
    inner_gate = lax.psum(gram_of(left_gate) * keep_gate, "dp")
    inner_down = lax.psum(gram_of(left_down), "tensor")
    ortho_gate = factored(left_gate, inner_gate)
    ortho_down = factored(left_down, inner_down)
    right_gate = transposed(fixed_gate, ortho_gate)
    right_gate = lax.psum(right_gate, "dp") / REPLICAS
    right_down = jnp.dot(fixed_down, ortho_down.astype(BF16), preferred_element_type=F32)
    right_down = lax.psum(right_down, "tensor")
    right_down = right_down + from_partner(right_down, "dp", 0)
    right_down = right_down / REPLICAS
    rebuilt_gate = jnp.dot(ortho_gate, right_gate.T, precision=high)
    rebuilt_down = jnp.dot(right_down, ortho_down.T, precision=high)
    share = slab // REPLICAS
    update_gate = lax.dynamic_slice_in_dim(rebuilt_gate, replica * share, share, 0).astype(BF16)
    update_down = lax.dynamic_slice_in_dim(rebuilt_down, replica * share, share, 0).astype(BF16)
    new_error_gate = (fixed_gate.astype(F32) - rebuilt_gate).astype(BF16)
    new_error_down = (fixed_down.astype(F32) - rebuilt_down).astype(BF16)
    return (update_gate, update_down, new_error_gate, new_error_down)


def core_of():
    return lax.rem(lax.axis_index("tensor"), 2)


def replica_of():
    return lax.rem(lax.axis_index("dp"), REPLICAS)


def exchange(x, partner):
    n_dp, n_t = lax.axis_size("dp"), lax.axis_size("tensor")
    pairs = []
    for d in range(n_dp):
        for t in range(n_t):
            to_d, to_t = partner(d, t)
            pairs.append((d * n_t + t, to_d * n_t + to_t))
    return lax.ppermute(x, ("dp", "tensor"), pairs)


def bits(n, low):
    out, b = [], low
    while b < n:
        out.append(b)
        b *= 2
    return out


def row_steps():
    steps = [(0, b) for b in bits(lax.axis_size("tensor"), 2)] + [(1, 0)]

    def partner(i, d, t):
        r, b = steps[i] if t % 2 == 0 else steps[-1 - i]
        return d ^ r, t ^ b

    return [functools.partial(partner, i) for i in range(len(steps))]


def col_steps():
    return [lambda d, t, b=b: (d ^ b, t) for b in bits(lax.axis_size("dp"), REPLICAS)]


def other_core(d, t):
    return d, t ^ 1


def other_replica(d, t):
    return d ^ 1, t


VMEM = pl.BlockSpec(memory_space=pltpu.VMEM)
HBM = pl.BlockSpec(memory_space=pltpu.HBM)
ANY = pl.BlockSpec(memory_space=pl.ANY)
HALF = RANK // 2


class Order:
    def __init__(self):
        self.token = None
        self.calls = 0

    def __call__(self, kernel, args, outs, scratch=(), mib=8, aliases=None):
        args = list(args)
        n_in, n_tok = len(args), 0 if self.token is None else 1
        operands = [
            pltpu.with_memory_space_constraint(x, pltpu.VMEM if spec is VMEM else pltpu.HBM)
            for x, spec in args
        ]
        specs = [spec for _, spec in args]
        if n_tok:
            operands.append(self.token)
            specs.append(ANY)

        def body(*refs):
            kernel(*refs[:n_in], *refs[n_in + n_tok :])

        out = pl.pallas_call(
            body,
            out_shape=tuple(
                (pltpu.VMEM if spec is VMEM else pltpu.HBM)(shape, kind) for shape, kind, spec in outs
            ),
            in_specs=specs,
            out_specs=tuple(spec for *_, spec in outs),
            scratch_shapes=list(scratch),
            input_output_aliases=aliases or {},
            compiler_params=pltpu.CompilerParams(vmem_limit_bytes=mib * MIB),
            cost_estimate=pl.CostEstimate(
                flops=int(WEIGHTS[self.calls] * FLOPS), bytes_accessed=1 << 10, transcendentals=0
            ),
        )(*operands)
        small = [x for x, (*_, spec) in zip(out, outs) if spec is VMEM]
        self.token = min(small, key=lambda x: x.size)
        self.calls += 1
        return out


def parts_of(x):
    hi = x.astype(BF16)
    lo = (x - hi.astype(F32)).astype(BF16)
    return hi, lo


def add_kernel(x, y, out):
    out[...] = x[...] + y[...]


def add(run, x, y):
    return run(add_kernel, [(x, VMEM), (y, VMEM)], [(x.shape, F32, VMEM)], mib=2)[0]


def halve(whole, place, keep, give):
    keep[...] = whole[pl.ds(pl.multiple_of(place * HALF, HALF), HALF), :]
    give[...] = whole[pl.ds(pl.multiple_of((1 - place) * HALF, HALF), HALF), :]


def tile_at(i):
    return pl.ds(pl.multiple_of(i * TILE, TILE), TILE)


def gate_left(run, grad, error, start, first, count, before=None):
    rows, cols = grad.shape
    last = (first + count) * TILE == rows

    def kernel(grad, error, start, *refs):
        if before is not None:
            refs = refs[2:]
        left, fixed = refs[:2]

        def step(g, e):
            at = tile_at(first + pl.program_id(0))
            term = jnp.zeros((TILE, RANK), F32)
            for j in range(0, cols, TILE):
                here = slice(j, j + TILE)
                c = g[:, here] + e[:, here]
                fixed[at, here] = c
                term += lax.dot_general(c, start[:, here], NT, preferred_element_type=F32)
            left[:, at] = term.T

        spec = pl.BlockSpec((TILE, cols), lambda i: (first + i, 0), pipeline_mode=pl.Buffered(3))
        pltpu.emit_pipeline(step, grid=(count,), in_specs=[spec, spec])(grad, error)
        if last:
            halve(left, core_of(), *refs[2:])

    args = [(grad, HBM), (error, HBM), (start, VMEM)]
    outs = [((RANK, rows), F32, VMEM), ((rows, cols), BF16, VMEM)]
    if last:
        outs += [((HALF, rows), F32, VMEM)] * 2
    aliases = None
    if before is not None:
        args += [(x, VMEM) for x in before]
        aliases = {3: 0, 4: 1}
    return run(kernel, args, outs, mib=8, aliases=aliases)


def down_left(run, grad, error, start, first, count, before=None):
    rows, cols = grad.shape
    width = count * TILE

    def kernel(grad, error, start, *refs):
        if before is not None:
            refs = refs[1:]
        keep, give, fixed, left = refs
        block = lax.div(lax.axis_index("dp"), REPLICAS) * (rows // TILE)
        left[...] = jnp.zeros_like(left)

        def step(g, e, s):
            at = tile_at(pl.program_id(0))
            for j in range(0, width, TILE):
                here = slice(j, j + TILE)
                c = g[:, here] + e[:, here]
                fixed[at, first * TILE + j : first * TILE + j + TILE] = c
                left[:, here] += jnp.dot(s[...], c, preferred_element_type=F32)

        spec = pl.BlockSpec((TILE, width), lambda i: (i, 0), pipeline_mode=pl.Buffered(3))
        part = pl.BlockSpec((RANK, TILE), lambda i: (0, block + i))
        columns = pl.ds(first * TILE, width)
        pltpu.emit_pipeline(step, grid=(rows // TILE,), in_specs=[spec, spec, part])(
            grad.at[:, columns], error.at[:, columns], start
        )
        halve(left, replica_of(), keep, give)

    args = [(grad, HBM), (error, HBM), (start, HBM)]
    aliases = None
    if before is not None:
        args += [(before, VMEM)]
        aliases = {3: 2}
    outs = [((HALF, width), F32, VMEM)] * 2 + [((rows, cols), BF16, VMEM)]
    return run(kernel, args, outs, [pltpu.VMEM((RANK, width), F32)], mib=8, aliases=aliases)


def load_left(own, other, place, left, stack, gram):
    left[pl.ds(pl.multiple_of(place * HALF, HALF), HALF), :] = own[...]
    left[pl.ds(pl.multiple_of((1 - place) * HALF, HALF), HALF), :] = other[...]
    hi, lo = parts_of(left[...])
    stack[:RANK, :] = hi
    stack[RANK:, :] = lo
    gram[...] = lax.dot_general(
        left[...], left[...], NT, preferred_element_type=F32, precision=lax.Precision.HIGHEST
    )


def gate_right(run, own, other, fixed):
    rows, cols = fixed.shape

    def kernel(own, other, fixed, keep, give, gram, left, stack, right):
        load_left(own, other, core_of(), left, stack, gram)

        def step(i, _):
            both = jnp.dot(stack[...], fixed[:, tile_at(i)], preferred_element_type=F32)
            right[:, tile_at(i)] = both[:RANK] + both[RANK:]
            return 0

        lax.fori_loop(0, cols // TILE, step, 0)
        halve(right, replica_of(), keep, give)

    return right_call(run, kernel, own, other, fixed, cols)


def down_right(run, own, other, fixed):
    rows, cols = fixed.shape

    def kernel(own, other, fixed, keep, give, gram, left, stack, right):
        load_left(own, other, replica_of(), left, stack, gram)

        def step(i, _):
            both = lax.dot_general(stack[...], fixed[tile_at(i), :], NT, preferred_element_type=F32)
            right[:, tile_at(i)] = both[:RANK] + both[RANK:]
            return 0

        lax.fori_loop(0, rows // TILE, step, 0)
        halve(right, core_of(), keep, give)

    return right_call(run, kernel, own, other, fixed, rows)


def right_call(run, kernel, own, other, fixed, out_width):
    width = own.shape[1]
    return run(
        kernel,
        [(own, VMEM), (other, VMEM), (fixed, VMEM)],
        [((HALF, out_width), F32, VMEM)] * 2 + [((RANK, RANK), F32, VMEM), ((RANK, width), F32, VMEM)],
        [pltpu.VMEM((2 * RANK, width), BF16), pltpu.VMEM((RANK, out_width), F32)],
        mib=4,
    )


def inverses(grams):
    row_at = lax.broadcasted_iota(jnp.int32, (RANK, RANK), 0)
    col_at = lax.broadcasted_iota(jnp.int32, (RANK, RANK), 1)
    lane = lax.broadcasted_iota(jnp.int32, (1, RANK), 1)

    def scaled(a):
        diagonal = jnp.where(row_at == col_at, a, 0.0)
        down = lax.rsqrt(jnp.sum(diagonal, axis=1, keepdims=True))
        across = lax.rsqrt(jnp.sum(diagonal, axis=0, keepdims=True))
        return a * down * across, down, across

    def sweep(a, k):
        one, two = (row_at == k, row_at == k + 1)
        here = one | two | (col_at == k) | (col_at == k + 1)
        col_1 = jnp.broadcast_to(a[:, k : k + 1], (RANK, RANK))
        col_2 = jnp.broadcast_to(a[:, k + 1 : k + 2], (RANK, RANK))
        p, q, r = col_1[k : k + 1], col_2[k : k + 1], col_2[k + 1 : k + 2]
        row_1 = jnp.where(lane == k, 1.0, jnp.where(lane == k + 1, 0.0, a[k : k + 1]))
        row_2 = jnp.where(lane == k + 1, 1.0, jnp.where(lane == k, 0.0, a[k + 1 : k + 2]))
        inv = 1.0 / (p * r - q * q)
        new_1 = (r * row_1 - q * row_2) * inv
        new_2 = (p * row_2 - q * row_1) * inv
        col_1 = jnp.where(one, -1.0, jnp.where(two, 0.0, col_1))
        col_2 = jnp.where(two, -1.0, jnp.where(one, 0.0, col_2))
        return jnp.where(here, 0.0, a) - col_1 * new_1 - col_2 * new_2

    systems = [scaled(a) for a in grams]
    values = [a for a, _, _ in systems]
    for k in range(0, RANK, 2):
        values = [sweep(a, k) for a in values]
    return [a * down * across for a, (_, down, across) in zip(values, systems)]


def solve(run, systems):
    counts = [(len(grams), len(lefts)) for _, grams, lefts in systems]
    widths = [sum(x.shape[1] for x in lefts) for _, _, lefts in systems]

    def kernel(*refs):
        outs = refs[-len(systems) :]
        totals, left_refs = [], []
        for n_gram, n_left in counts:
            total = refs[0][...]
            for ref in refs[1:n_gram]:
                total += ref[...]
            totals.append(total)
            left_refs.append(refs[n_gram : n_gram + n_left])
            refs = refs[n_gram + n_left :]
        for (place, _, _), a, lefts, out in zip(systems, inverses(totals), left_refs, outs):
            turned = jnp.concatenate([a[HALF:], a[:HALF]], axis=0)
            a = jnp.where(place() == 0, a, turned) * (1.0 / REPLICAS)
            at = 0
            for left in lefts:
                n = left.shape[1]
                out[:, at : at + n] = jnp.dot(
                    a, left[...], preferred_element_type=F32, precision=lax.Precision.HIGHEST
                )
                at += n

    args = [(x, VMEM) for _, grams, lefts in systems for x in (*grams, *lefts)]
    return run(kernel, args, [((RANK, n), F32, VMEM) for n in widths], mib=4)


def rebuild(run, rows_in, cols_in, fixed, height):
    rows, cols = fixed.shape
    tiles = rows // REPLICAS // height
    n_row, n_col = len(rows_in), len(cols_in)

    def kernel(*refs):
        row_refs, col_refs = refs[:n_row], refs[n_row : n_row + n_col]
        fixed, new_error, update, done, row_stack, col_stack, row_turned = refs[n_row + n_col :]
        done[...] = jnp.zeros_like(done)
        for sources, stack, order in (
            (row_refs, row_stack, (0, 1, 0, 1)),
            (col_refs, col_stack, (0, 0, 1, 1)),
        ):
            at = 0
            for ref in sources:
                parts = parts_of(ref[...])
                n = ref.shape[0]
                for k, which in enumerate(order):
                    stack[k * RANK + at : k * RANK + at + n, :] = parts[which]
                at += n
        for i in range(0, rows, TILE):
            row_turned[i : i + TILE, :] = row_stack[:, i : i + TILE].T
        replica = replica_of()
        mine, theirs = replica * tiles, (1 - replica) * tiles

        def tile(i, e, u):
            at = pl.ds(pl.multiple_of(i * height, height), height)
            row = row_turned[at, :]
            for j in range(0, cols, TILE):
                here = slice(j, j + TILE)
                value = jnp.dot(row, col_stack[:, here], preferred_element_type=F32)
                e[:, here] = (fixed[at, here].astype(F32) - value).astype(BF16)
                if u is not None:
                    u[:, here] = value.astype(BF16)

        def tile_of(i):
            return jnp.where(i < tiles, mine + i, theirs + i - tiles)

        def step(e, u):
            i = pl.program_id(0)
            pl.when(i < tiles)(lambda: tile(tile_of(i), e, u))
            pl.when(i >= tiles)(lambda: tile(tile_of(i), e, None))

        block = (height, cols)
        pltpu.emit_pipeline(
            step,
            grid=(REPLICAS * tiles,),
            out_specs=[
                pl.BlockSpec(block, lambda i: (tile_of(i), 0)),
                pl.BlockSpec(block, lambda i: (jnp.minimum(i, tiles - 1), 0)),
            ],
        )(new_error, update)

    return run(
        kernel,
        [(x, VMEM) for x in (*rows_in, *cols_in)] + [(fixed, VMEM)],
        [
            ((rows, cols), BF16, HBM),
            ((rows // REPLICAS, cols), BF16, HBM),
            ((8, 128), F32, VMEM),
        ],
        [
            pltpu.VMEM((4 * RANK, rows), BF16),
            pltpu.VMEM((4 * RANK, cols), BF16),
            pltpu.VMEM((rows, 4 * RANK), BF16),
        ],
        mib=18,
    )[:2]


def local(grad_gate, grad_down, error_gate, error_down, start_gate, start_down):
    slab, width = grad_gate.shape
    n_dp, n_t = lax.axis_size("dp"), lax.axis_size("tensor")
    run = Order()
    hops, steps = row_steps(), col_steps()

    keep, give, fixed_down = down_left(run, grad_down, error_down, start_down, 0, width // TILE)
    got = exchange(give, other_replica)
    _, fixed_gate, keep_gate, give = gate_left(run, grad_gate, error_gate, start_gate, 0, slab // TILE)
    got_gate = exchange(give, other_core)
    down = add(run, keep, got)
    got = exchange(down, steps[0])
    gate = add(run, keep_gate, got_gate)
    for hop in hops:
        gate = add(run, gate, exchange(gate, hop))
    other_gate = exchange(gate, other_core)
    for i in range(len(steps)):
        down = add(run, down, got)
        if i + 1 < len(steps):
            got = exchange(down, steps[i + 1])
    other_down = exchange(down, other_replica)

    keep_gate, give, gram_gate, left_gate = gate_right(run, gate, other_gate, fixed_gate)
    got_gate = exchange(give, other_replica)
    grams_gate = [gram_gate] + [
        exchange(gram_gate, lambda d, t, b=b: (d ^ b, t)) for b in range(REPLICAS, n_dp, REPLICAS)
    ]
    keep, give, gram_down, left_down = down_right(run, down, other_down, fixed_down)
    got = exchange(give, other_core)
    grams_down = [gram_down] + [
        exchange(gram_down, lambda d, t, b=b: (d, t ^ b)) for b in range(1, n_t)
    ]
    gate = add(run, keep_gate, got_gate)
    got_gate = exchange(gate, steps[0])
    down = add(run, keep, got)
    for hop in hops[:-1]:
        down = add(run, down, exchange(down, hop))
    got = exchange(down, hops[-1])
    down_cols, gate_rows = solve(
        run, [(core_of, grams_down, (left_down,)), (replica_of, grams_gate, (left_gate,))]
    )
    for i in range(len(steps)):
        gate = add(run, gate, got_gate)
        if i + 1 < len(steps):
            got_gate = exchange(gate, steps[i + 1])
    other_gate = exchange(gate, other_replica)
    down = add(run, down, got)
    other_down = exchange(down, other_core)

    new_error_down, update_down = rebuild(run, [down, other_down], [down_cols], fixed_down, TILE)
    new_error_gate, update_gate = rebuild(
        run, [gate_rows], [gate, other_gate], fixed_gate, slab // REPLICAS // 2
    )
    return (update_gate, update_down, new_error_gate, new_error_down)


def solution(mesh):
    split = P(("mix", "dp"), "tensor")
    in_specs = (split, split, split, split, P(None, "tensor"), P())
    out_specs = (split, split, split, split)

    def run(grad_gate, *rest):
        groups = mesh.shape["mix"] * mesh.shape["dp"]
        slab = grad_gate.shape[0] // groups
        width = grad_gate.shape[1] // mesh.shape["tensor"]
        fits = slab % (REPLICAS * TILE) == 0 and width % TILE == 0
        body = local if fits else local_plain
        return jax.shard_map(
            body, mesh=mesh, in_specs=in_specs, out_specs=out_specs, check_vma=False
        )(grad_gate, *rest)

    return run
```

```python
import functools

import jax
import jax.numpy as jnp
from jax import lax
from jax.experimental import pallas as pl
from jax.experimental.pallas import tpu as pltpu
from jax.sharding import PartitionSpec as P

REPLICAS = 2
RANK = 64
TILE = 256
FLOPS = 1.15e9
WEIGHTS = (8.0, 2.0, 1.0, 7.0, 1.0, 5.0, 1.0, 4.0, 5.0, 1.0, 5.0, 5.0, 1.0, 6.0, 1.0, 8.0, 1.0, 8.0)
MIB = 1 << 20
BF16 = jnp.bfloat16
F32 = jnp.float32

NN = (((1,), (0,)), ((), ()))
NT = (((1,), (1,)), ((), ()))
TN = (((0,), (0,)), ((), ()))


def from_partner(shard, axis, stride):
    return lax.ppermute(shard, axis, [(i, i ^ 1 << stride) for i in range(lax.axis_size(axis))])


def corrected(grad, error):
    return (grad.astype(F32) + error.astype(F32)).astype(BF16)


def transposed(matrix, ortho):
    return lax.dot_general(matrix, ortho.astype(BF16), TN, preferred_element_type=F32)


def gram_of(left):
    return jnp.dot(left.T, left, precision=lax.Precision.HIGHEST)


def factored(left, inner):
    lower = jnp.linalg.cholesky(inner)
    return lax.linalg.triangular_solve(lower, left, left_side=False, lower=True, transpose_a=True)


def local_plain(grad_gate, grad_down, error_gate, error_down, start_gate, start_down):
    high = lax.Precision.HIGHEST
    dp_place = lax.axis_index("dp")
    block = dp_place // REPLICAS
    replica = dp_place % REPLICAS
    fixed_gate = corrected(grad_gate, error_gate)
    fixed_down = corrected(grad_down, error_down)
    slab = fixed_gate.shape[0]
    cols_down = lax.dynamic_slice_in_dim(start_down, block * slab, slab, 1)
    left_gate = lax.dot_general(fixed_gate, start_gate, NT, preferred_element_type=F32)
    left_down = lax.dot_general(
        fixed_down, cols_down, (((0,), (1,)), ((), ())), preferred_element_type=F32
    )
    left_gate = lax.psum(left_gate, "tensor")
    left_gate = left_gate + from_partner(left_gate, "dp", 0)
    left_down = lax.psum(left_down, "dp")
    keep_gate = (replica == 0).astype(F32)
    inner_gate = lax.psum(gram_of(left_gate) * keep_gate, "dp")
    inner_down = lax.psum(gram_of(left_down), "tensor")
    ortho_gate = factored(left_gate, inner_gate)
    ortho_down = factored(left_down, inner_down)
    right_gate = transposed(fixed_gate, ortho_gate)
    right_gate = lax.psum(right_gate, "dp") / REPLICAS
    right_down = jnp.dot(fixed_down, ortho_down.astype(BF16), preferred_element_type=F32)
    right_down = lax.psum(right_down, "tensor")
    right_down = right_down + from_partner(right_down, "dp", 0)
    right_down = right_down / REPLICAS
    rebuilt_gate = jnp.dot(ortho_gate, right_gate.T, precision=high)
    rebuilt_down = jnp.dot(right_down, ortho_down.T, precision=high)
    share = slab // REPLICAS
    update_gate = lax.dynamic_slice_in_dim(rebuilt_gate, replica * share, share, 0).astype(BF16)
    update_down = lax.dynamic_slice_in_dim(rebuilt_down, replica * share, share, 0).astype(BF16)
    new_error_gate = (fixed_gate.astype(F32) - rebuilt_gate).astype(BF16)
    new_error_down = (fixed_down.astype(F32) - rebuilt_down).astype(BF16)
    return (update_gate, update_down, new_error_gate, new_error_down)


def core_of():
    return lax.rem(lax.axis_index("tensor"), 2)


def replica_of():
    return lax.rem(lax.axis_index("dp"), REPLICAS)


def exchange(x, partner):
    n_dp, n_t = lax.axis_size("dp"), lax.axis_size("tensor")
    pairs = []
    for d in range(n_dp):
        for t in range(n_t):
            to_d, to_t = partner(d, t)
            pairs.append((d * n_t + t, to_d * n_t + to_t))
    return lax.ppermute(x, ("dp", "tensor"), pairs)


def bits(n, low):
    out, b = [], low
    while b < n:
        out.append(b)
        b *= 2
    return out


def row_steps():
    steps = [(0, b) for b in bits(lax.axis_size("tensor"), 2)] + [(1, 0)]

    def partner(i, d, t):
        r, b = steps[i] if t % 2 == 0 else steps[-1 - i]
        return d ^ r, t ^ b

    return [functools.partial(partner, i) for i in range(len(steps))]


def col_steps():
    return [lambda d, t, b=b: (d ^ b, t) for b in bits(lax.axis_size("dp"), REPLICAS)]


def other_core(d, t):
    return d, t ^ 1


def other_replica(d, t):
    return d ^ 1, t


VMEM = pl.BlockSpec(memory_space=pltpu.VMEM)
HBM = pl.BlockSpec(memory_space=pltpu.HBM)
ANY = pl.BlockSpec(memory_space=pl.ANY)
HALF = RANK // 2


class Calls:
    def __init__(self):
        self.count = 0

    def __call__(self, kernel, args, outs, scratch=(), mib=8, aliases=None, after=()):
        n_in, n_after = len(args), len(after)
        operands = [
            pltpu.with_memory_space_constraint(x, pltpu.VMEM if spec is VMEM else pltpu.HBM)
            for x, spec in args
        ]

        def body(*refs):
            kernel(*refs[:n_in], *refs[n_in + n_after :])

        out = pl.pallas_call(
            body,
            out_shape=tuple(
                (pltpu.VMEM if spec is VMEM else pltpu.HBM)(shape, kind) for shape, kind, spec in outs
            ),
            in_specs=[spec for _, spec in args] + [ANY] * n_after,
            out_specs=tuple(spec for *_, spec in outs),
            scratch_shapes=list(scratch),
            input_output_aliases=aliases or {},
            compiler_params=pltpu.CompilerParams(vmem_limit_bytes=mib * MIB),
            cost_estimate=pl.CostEstimate(
                flops=int(WEIGHTS[self.count] * FLOPS), bytes_accessed=1 << 10, transcendentals=0
            ),
        )(*operands, *after)
        self.count += 1
        return out


def parts_of(x):
    hi = x.astype(BF16)
    lo = (x - hi.astype(F32)).astype(BF16)
    return hi, lo


def add_kernel(x, y, out):
    out[...] = x[...] + y[...]


def add(run, x, y, after=()):
    return run(add_kernel, [(x, VMEM), (y, VMEM)], [(x.shape, F32, VMEM)], mib=2, after=after)[0]


def add_split_kernel(x, y, own, rest):
    n = own.shape[1]
    own[...] = x[:, :n] + y[:, :n]
    rest[...] = x[:, n:] + y[:, n:]


def add_split(run, x, y, after=()):
    outs = [((HALF, x.shape[1] - 2 * RANK), F32, VMEM), ((HALF, 2 * RANK), F32, VMEM)]
    return run(add_split_kernel, [(x, VMEM), (y, VMEM)], outs, mib=2, after=after)


def halve(whole, place, keep, give):
    keep[...] = whole[pl.ds(pl.multiple_of(place * HALF, HALF), HALF), :]
    give[...] = whole[pl.ds(pl.multiple_of((1 - place) * HALF, HALF), HALF), :]


def tile_at(i):
    return pl.ds(pl.multiple_of(i * TILE, TILE), TILE)


def gate_left(run, grad, error, start, first, count, before=None, after=()):
    rows, cols = grad.shape
    last = (first + count) * TILE == rows

    def kernel(grad, error, start, *refs):
        if before is not None:
            refs = refs[2:]
        left, fixed = refs[:2]

        def step(g, e):
            at = tile_at(first + pl.program_id(0))
            term = jnp.zeros((TILE, RANK), F32)
            for j in range(0, cols, TILE):
                here = slice(j, j + TILE)
                c = g[:, here] + e[:, here]
                fixed[at, here] = c
                term += lax.dot_general(c, start[:, here], NT, preferred_element_type=F32)
            left[:, at] = term.T

        spec = pl.BlockSpec((TILE, cols), lambda i: (first + i, 0), pipeline_mode=pl.Buffered(3))
        pltpu.emit_pipeline(step, grid=(count,), in_specs=[spec, spec])(grad, error)
        if last:
            halve(left, core_of(), *refs[2:])

    args = [(grad, HBM), (error, HBM), (start, VMEM)]
    outs = [((RANK, rows), F32, VMEM), ((rows, cols), BF16, VMEM)]
    if last:
        outs += [((HALF, rows), F32, VMEM)] * 2
    aliases = None
    if before is not None:
        args += [(x, VMEM) for x in before]
        aliases = {3: 0, 4: 1}
    return run(kernel, args, outs, mib=8, aliases=aliases, after=after)


def down_left(run, grad, error, start, first, count, before=None, after=()):
    rows, cols = grad.shape
    last = (first + count) * TILE == rows

    def kernel(grad, error, start, *refs):
        if before is not None:
            refs = refs[2:]
        left, fixed = refs[:2]
        block = lax.div(lax.axis_index("dp"), REPLICAS) * (rows // TILE) + first
        if before is None:
            left[...] = jnp.zeros_like(left)

        def step(g, e, s):
            at = tile_at(first + pl.program_id(0))
            for j in range(0, cols, TILE):
                here = slice(j, j + TILE)
                c = g[:, here] + e[:, here]
                fixed[at, here] = c
                left[:, here] += jnp.dot(s[...], c, preferred_element_type=F32)

        spec = pl.BlockSpec((TILE, cols), lambda i: (first + i, 0), pipeline_mode=pl.Buffered(3))
        part = pl.BlockSpec((RANK, TILE), lambda i: (0, block + i))
        pltpu.emit_pipeline(step, grid=(count,), in_specs=[spec, spec, part])(grad, error, start)
        if last:
            halve(left, replica_of(), *refs[2:])

    args = [(grad, HBM), (error, HBM), (start, HBM)]
    outs = [((RANK, cols), F32, VMEM), ((rows, cols), BF16, VMEM)]
    if last:
        outs += [((HALF, cols), F32, VMEM)] * 2
    aliases = None
    if before is not None:
        args += [(x, VMEM) for x in before]
        aliases = {3: 0, 4: 1}
    return run(kernel, args, outs, mib=8, aliases=aliases, after=after)


def load_left(own, other, place, left, stack):
    left[pl.ds(pl.multiple_of(place * HALF, HALF), HALF), :] = own[...]
    left[pl.ds(pl.multiple_of((1 - place) * HALF, HALF), HALF), :] = other[...]
    hi, lo = parts_of(left[...])
    stack[:RANK, :] = hi
    stack[RANK:, :] = lo
    return lax.dot_general(
        left[...], left[...], NT, preferred_element_type=F32, precision=lax.Precision.HIGHEST
    )


def gate_right(run, own, other, fixed, after=()):
    rows, cols = fixed.shape

    def kernel(own, other, fixed, keep, give, gram, left, stack, right):
        gram[...] = load_left(own, other, core_of(), left, stack)

        def step(i, _):
            both = jnp.dot(stack[...], fixed[:, tile_at(i)], preferred_element_type=F32)
            right[:, tile_at(i)] = both[:RANK] + both[RANK:]
            return 0

        lax.fori_loop(0, cols // TILE, step, 0)
        halve(right, replica_of(), keep, give)

    return run(
        kernel,
        [(own, VMEM), (other, VMEM), (fixed, VMEM)],
        [((HALF, cols), F32, VMEM)] * 2 + [((RANK, RANK), F32, VMEM), ((RANK, rows), F32, VMEM)],
        [pltpu.VMEM((2 * RANK, rows), BF16), pltpu.VMEM((RANK, cols), F32)],
        mib=4,
        after=after,
    )


def down_right(run, own, other, fixed, after=()):
    rows, cols = fixed.shape

    def kernel(own, other, fixed, keep, give, left, stack, right):
        gram = load_left(own, other, replica_of(), left, stack)

        def step(i, _):
            both = lax.dot_general(stack[...], fixed[tile_at(i), :], NT, preferred_element_type=F32)
            right[:, tile_at(i)] = both[:RANK] + both[RANK:]
            return 0

        lax.fori_loop(0, rows // TILE, step, 0)
        halve(right, core_of(), keep.at[:, :rows], give.at[:, :rows])
        packed = jnp.concatenate([gram[:HALF], gram[HALF:]], axis=1)
        keep[:, rows:] = packed
        give[:, rows:] = packed

    return run(
        kernel,
        [(own, VMEM), (other, VMEM), (fixed, VMEM)],
        [((HALF, rows + 2 * RANK), F32, VMEM)] * 2 + [((RANK, cols), F32, VMEM)],
        [pltpu.VMEM((2 * RANK, cols), BF16), pltpu.VMEM((RANK, rows), F32)],
        mib=4,
        after=after,
    )


def inverses(grams):
    row_at = lax.broadcasted_iota(jnp.int32, (RANK, RANK), 0)
    col_at = lax.broadcasted_iota(jnp.int32, (RANK, RANK), 1)
    lane = lax.broadcasted_iota(jnp.int32, (1, RANK), 1)

    def scaled(a):
        diagonal = jnp.where(row_at == col_at, a, 0.0)
        down = lax.rsqrt(jnp.sum(diagonal, axis=1, keepdims=True))
        across = lax.rsqrt(jnp.sum(diagonal, axis=0, keepdims=True))
        return a * down * across, down, across

    def sweep(a, k):
        one, two = (row_at == k, row_at == k + 1)
        here = one | two | (col_at == k) | (col_at == k + 1)
        col_1 = jnp.broadcast_to(a[:, k : k + 1], (RANK, RANK))
        col_2 = jnp.broadcast_to(a[:, k + 1 : k + 2], (RANK, RANK))
        p, q, r = col_1[k : k + 1], col_2[k : k + 1], col_2[k + 1 : k + 2]
        row_1 = jnp.where(lane == k, 1.0, jnp.where(lane == k + 1, 0.0, a[k : k + 1]))
        row_2 = jnp.where(lane == k + 1, 1.0, jnp.where(lane == k, 0.0, a[k + 1 : k + 2]))
        inv = 1.0 / (p * r - q * q)
        new_1 = (r * row_1 - q * row_2) * inv
        new_2 = (p * row_2 - q * row_1) * inv
        col_1 = jnp.where(one, -1.0, jnp.where(two, 0.0, col_1))
        col_2 = jnp.where(two, -1.0, jnp.where(one, 0.0, col_2))
        return jnp.where(here, 0.0, a) - col_1 * new_1 - col_2 * new_2

    systems = [scaled(a) for a in grams]
    values = [a for a, _, _ in systems]
    for k in range(0, RANK, 2):
        values = [sweep(a, k) for a in values]
    return [a * down * across for a, (_, down, across) in zip(values, systems)]


def stacked(refs, order, stack):
    at = 0
    for ref in refs:
        parts = parts_of(ref[...])
        n = ref.shape[0]
        for k, which in enumerate(order):
            stack[k * RANK + at : k * RANK + at + n, :] = parts[which]
        at += n


ROW_ORDER, COL_ORDER = (0, 1, 0, 1), (0, 0, 1, 1)


def turn(stack, turned):
    for i in range(0, stack.shape[1], TILE):
        turned[i : i + TILE, :] = stack[:, i : i + TILE].T


def solve(run, grams_down, left_down, grams_gate, left_gate, after=()):
    n_down, n_gate = len(grams_down), len(grams_gate)
    cols, rows = left_down.shape[1], left_gate.shape[1]

    def kernel(*refs):
        down, gate = refs[:n_down], refs[n_down : n_down + n_gate]
        left_down, left_gate, col_stack, row_turned, col, row, row_stack = refs[n_down + n_gate :]
        a = sum((ref[...] for ref in down[1:]), down[0][...])
        a = jnp.concatenate([a[:, :RANK], a[:, RANK:]], axis=0)
        b = sum((ref[...] for ref in gate[1:]), gate[0][...])
        for place, a, left, out in zip(
            (core_of(), replica_of()), inverses([a, b]), (left_down, left_gate), (col, row)
        ):
            other = jnp.concatenate([a[HALF:], a[:HALF]], axis=0)
            a = jnp.where(place == 0, a, other) * (1.0 / REPLICAS)
            out[...] = jnp.dot(
                a, left[...], preferred_element_type=F32, precision=lax.Precision.HIGHEST
            )
        stacked([col], COL_ORDER, col_stack)
        stacked([row], ROW_ORDER, row_stack)
        turn(row_stack, row_turned)

    return run(
        kernel,
        [(x, VMEM) for x in (*grams_down, *grams_gate, left_down, left_gate)],
        [((4 * RANK, cols), BF16, VMEM), ((rows, 4 * RANK), BF16, VMEM)],
        [
            pltpu.VMEM((RANK, cols), F32),
            pltpu.VMEM((RANK, rows), F32),
            pltpu.VMEM((4 * RANK, rows), BF16),
        ],
        mib=6,
        after=after,
    )


def rebuild(run, row_turned, col_stack, halves, fixed, after=()):
    rows, cols = fixed.shape
    share, tiles = rows // REPLICAS, cols // TILE
    rows_late = row_turned is None
    scratch = [pltpu.VMEM((4 * RANK, rows if rows_late else cols), BF16)]
    if rows_late:
        scratch.append(pltpu.VMEM((rows, 4 * RANK), BF16))

    def kernel(ready, own, other, fixed, new_error, update, done, late, *turned):
        done[...] = jnp.zeros_like(done)
        stacked([own, other], ROW_ORDER if rows_late else COL_ORDER, late)
        row, col = ready, late
        if rows_late:
            row, col = turned[0], ready
            turn(late, row)
        replica = replica_of()

        def share_of(i):
            return jnp.where(i < tiles, replica, 1 - replica)

        def step(e, u):
            i = pl.program_id(0)
            at = pl.ds(pl.multiple_of(share_of(i) * share, share), share)
            here = tile_at(lax.rem(i, tiles))

            def tile(with_update):
                value = jnp.dot(row[at, :], col[:, here], preferred_element_type=F32)
                e[...] = (fixed[at, here].astype(F32) - value).astype(BF16)
                if with_update:
                    u[...] = value.astype(BF16)

            pl.when(i < tiles)(lambda: tile(True))
            pl.when(i >= tiles)(lambda: tile(False))

        block = (share, TILE)
        pltpu.emit_pipeline(
            step,
            grid=(REPLICAS * tiles,),
            out_specs=[
                pl.BlockSpec(block, lambda i: (share_of(i), lax.rem(i, tiles))),
                pl.BlockSpec(block, lambda i: (0, jnp.minimum(i, tiles - 1))),
            ],
        )(new_error, update)

    return run(
        kernel,
        [(x, VMEM) for x in (col_stack if rows_late else row_turned, *halves, fixed)],
        [((rows, cols), BF16, HBM), ((share, cols), BF16, HBM), ((8, 128), F32, VMEM)],
        scratch,
        mib=12,
        after=after,
    )


def local(grad_gate, grad_down, error_gate, error_down, start_gate, start_down):
    slab, width = grad_gate.shape
    n_dp, n_t = lax.axis_size("dp"), lax.axis_size("tensor")
    run = Calls()
    hops, steps = row_steps(), col_steps()
    tiles = slab // TILE

    _, fixed_gate, keep_gate, give = gate_left(run, grad_gate, error_gate, start_gate, 0, tiles)
    got_gate = exchange(give, other_core)
    cut = tiles // 5
    down_args = (run, grad_down, error_down, start_down)
    first = down_left(*down_args, 0, cut, after=(keep_gate,))
    gate = add(run, keep_gate, got_gate, after=(first[0],))
    got_gate = exchange(gate, hops[0])
    _, fixed_down, keep, give = down_left(*down_args, cut, tiles - cut, first, after=(gate,))
    got = exchange(give, other_replica)
    for hop in hops[1:]:
        gate = add(run, gate, got_gate, after=(keep,))
        got_gate = exchange(gate, hop)
    down = add(run, keep, got, after=(gate,))
    got = exchange(down, steps[0])
    gate = add(run, gate, got_gate, after=(down,))
    other_gate = exchange(gate, other_core)

    keep_gate, give_gate, gram_gate, left_gate = gate_right(run, gate, other_gate, fixed_gate)
    got_gate = exchange(give_gate, other_replica)
    grams_gate = [gram_gate] + [
        exchange(gram_gate, lambda d, t, b=b: (d ^ b, t)) for b in range(REPLICAS, n_dp, REPLICAS)
    ]
    for i in range(len(steps)):
        down = add(run, down, got, after=(gram_gate,))
        if i + 1 < len(steps):
            got = exchange(down, steps[i + 1])
    other_down = exchange(down, other_replica)
    gate = add(run, keep_gate, got_gate, after=(down,))
    got_gate = exchange(gate, steps[0])

    keep, give, left_down = down_right(run, down, other_down, fixed_down, after=(gate,))
    got = exchange(give, other_core)
    for i in range(len(steps)):
        gate = add(run, gate, got_gate, after=(keep,))
        if i + 1 < len(steps):
            got_gate = exchange(gate, steps[i + 1])
    other_gate = exchange(gate, other_replica)
    down, gram_down = add_split(run, keep, got, after=(gate,))
    grams_down = [gram_down] + [
        exchange(gram_down, lambda d, t, b=b: (d, t ^ b)) for b in range(2, n_t, 2)
    ]
    got = exchange(down, hops[0])
    col_stack, row_turned = solve(run, grams_down, left_down, grams_gate, left_gate)
    for hop in hops[1:]:
        down = add(run, down, got, after=(col_stack,))
        got = exchange(down, hop)
    new_error_gate, update_gate, done = rebuild(
        run, row_turned, None, (gate, other_gate), fixed_gate, after=(down,)
    )
    down = add(run, down, got, after=(done,))
    other_down = exchange(down, other_core)
    new_error_down, update_down, _ = rebuild(run, None, col_stack, (down, other_down), fixed_down)
    return (update_gate, update_down, new_error_gate, new_error_down)


def solution(mesh):
    split = P(("mix", "dp"), "tensor")
    in_specs = (split, split, split, split, P(None, "tensor"), P())
    out_specs = (split, split, split, split)

    def run(grad_gate, *rest):
        groups = mesh.shape["mix"] * mesh.shape["dp"]
        slab = grad_gate.shape[0] // groups
        width = grad_gate.shape[1] // mesh.shape["tensor"]
        fits = slab % (REPLICAS * TILE) == 0 and width % TILE == 0
        body = local if fits else local_plain
        return jax.shard_map(
            body, mesh=mesh, in_specs=in_specs, out_specs=out_specs, check_vma=False
        )(grad_gate, *rest)

    return run
```

```python
import functools

import jax
import jax.numpy as jnp
from jax import lax
from jax.experimental import pallas as pl
from jax.experimental.pallas import tpu as pltpu
from jax.sharding import PartitionSpec as P

REPLICAS = 2
RANK = 64
TILE = 256
FLOPS = 1.15e9
WEIGHTS = (8.0, 4.0, 1.0, 4.0, 0.1, 5.0, 1.0, 5.0, 1.0, 1.0, 4.0, 0.2, 0.5, 1.0, 1.0, 0.3, 1.0, 8.0)
MIB = 1 << 20
BF16 = jnp.bfloat16
F32 = jnp.float32

NN = (((1,), (0,)), ((), ()))
NT = (((1,), (1,)), ((), ()))
TN = (((0,), (0,)), ((), ()))


def from_partner(shard, axis, stride):
    return lax.ppermute(shard, axis, [(i, i ^ 1 << stride) for i in range(lax.axis_size(axis))])


def corrected(grad, error):
    return (grad.astype(F32) + error.astype(F32)).astype(BF16)


def transposed(matrix, ortho):
    return lax.dot_general(matrix, ortho.astype(BF16), TN, preferred_element_type=F32)


def gram_of(left):
    return jnp.dot(left.T, left, precision=lax.Precision.HIGHEST)


def factored(left, inner):
    lower = jnp.linalg.cholesky(inner)
    return lax.linalg.triangular_solve(lower, left, left_side=False, lower=True, transpose_a=True)


def local_plain(grad_gate, grad_down, error_gate, error_down, start_gate, start_down):
    high = lax.Precision.HIGHEST
    dp_place = lax.axis_index("dp")
    block = dp_place // REPLICAS
    replica = dp_place % REPLICAS
    fixed_gate = corrected(grad_gate, error_gate)
    fixed_down = corrected(grad_down, error_down)
    slab = fixed_gate.shape[0]
    cols_down = lax.dynamic_slice_in_dim(start_down, block * slab, slab, 1)
    left_gate = lax.dot_general(fixed_gate, start_gate, NT, preferred_element_type=F32)
    left_down = lax.dot_general(
        fixed_down, cols_down, (((0,), (1,)), ((), ())), preferred_element_type=F32
    )
    left_gate = lax.psum(left_gate, "tensor")
    left_gate = left_gate + from_partner(left_gate, "dp", 0)
    left_down = lax.psum(left_down, "dp")
    keep_gate = (replica == 0).astype(F32)
    inner_gate = lax.psum(gram_of(left_gate) * keep_gate, "dp")
    inner_down = lax.psum(gram_of(left_down), "tensor")
    ortho_gate = factored(left_gate, inner_gate)
    ortho_down = factored(left_down, inner_down)
    right_gate = transposed(fixed_gate, ortho_gate)
    right_gate = lax.psum(right_gate, "dp") / REPLICAS
    right_down = jnp.dot(fixed_down, ortho_down.astype(BF16), preferred_element_type=F32)
    right_down = lax.psum(right_down, "tensor")
    right_down = right_down + from_partner(right_down, "dp", 0)
    right_down = right_down / REPLICAS
    rebuilt_gate = jnp.dot(ortho_gate, right_gate.T, precision=high)
    rebuilt_down = jnp.dot(right_down, ortho_down.T, precision=high)
    share = slab // REPLICAS
    update_gate = lax.dynamic_slice_in_dim(rebuilt_gate, replica * share, share, 0).astype(BF16)
    update_down = lax.dynamic_slice_in_dim(rebuilt_down, replica * share, share, 0).astype(BF16)
    new_error_gate = (fixed_gate.astype(F32) - rebuilt_gate).astype(BF16)
    new_error_down = (fixed_down.astype(F32) - rebuilt_down).astype(BF16)
    return (update_gate, update_down, new_error_gate, new_error_down)


def core_of():
    return lax.rem(lax.axis_index("tensor"), 2)


def replica_of():
    return lax.rem(lax.axis_index("dp"), REPLICAS)


def exchange(x, partner):
    n_dp, n_t = lax.axis_size("dp"), lax.axis_size("tensor")
    pairs = []
    for d in range(n_dp):
        for t in range(n_t):
            to_d, to_t = partner(d, t)
            pairs.append((d * n_t + t, to_d * n_t + to_t))
    return lax.ppermute(x, ("dp", "tensor"), pairs)


def bits(n, low):
    out, b = [], low
    while b < n:
        out.append(b)
        b *= 2
    return out


def row_steps():
    steps = [(0, b) for b in bits(lax.axis_size("tensor"), 2)] + [(1, 0)]

    def partner(i, d, t):
        r, b = steps[i] if t % 2 == 0 else steps[-1 - i]
        return d ^ r, t ^ b

    return [functools.partial(partner, i) for i in range(len(steps))]


def col_steps():
    return [lambda d, t, b=b: (d ^ b, t) for b in bits(lax.axis_size("dp"), REPLICAS)]


def other_core(d, t):
    return d, t ^ 1


def other_replica(d, t):
    return d ^ 1, t


def to_other_core(pieces):
    return [exchange(x, other_core) for x in pieces]


VMEM = pl.BlockSpec(memory_space=pltpu.VMEM)
HBM = pl.BlockSpec(memory_space=pltpu.HBM)
ANY = pl.BlockSpec(memory_space=pl.ANY)
HALF = RANK // 2


class Calls:
    def __init__(self):
        self.count = 0

    def __call__(self, kernel, args, outs, scratch=(), mib=8, aliases=None, after=()):
        n_in, n_after = len(args), len(after)
        operands = [
            pltpu.with_memory_space_constraint(x, pltpu.VMEM if spec is VMEM else pltpu.HBM)
            for x, spec in args
        ]

        def body(*refs):
            kernel(*refs[:n_in], *refs[n_in + n_after :])

        out = pl.pallas_call(
            body,
            out_shape=tuple(
                (pltpu.VMEM if spec is VMEM else pltpu.HBM)(shape, kind) for shape, kind, spec in outs
            ),
            in_specs=[spec for _, spec in args] + [ANY] * n_after,
            out_specs=tuple(spec for *_, spec in outs),
            scratch_shapes=list(scratch),
            input_output_aliases=aliases or {},
            compiler_params=pltpu.CompilerParams(vmem_limit_bytes=mib * MIB),
            cost_estimate=pl.CostEstimate(
                flops=int(WEIGHTS[self.count] * FLOPS), bytes_accessed=1 << 10, transcendentals=0
            ),
        )(*operands, *after)
        self.count += 1
        return out


def parts_of(x):
    hi = x.astype(BF16)
    lo = (x - hi.astype(F32)).astype(BF16)
    return hi, lo


def spans(*widths):
    edges = sorted({sum(w[:i]) for w in widths for i in range(len(w) + 1)})
    for low, high in zip(edges, edges[1:]):
        places = []
        for w in widths:
            k = max(i for i in range(len(w)) if sum(w[:i]) <= low)
            places.append((k, low - sum(w[:k]), high - sum(w[:k])))
        yield places


def widths_of(refs):
    return [ref.shape[1] for ref in refs]


def add(run, xs, ys, widths=None, after=()):
    widths = widths or widths_of(xs)
    n_x, n_y = len(xs), len(ys)

    def kernel(*refs):
        x, y, out = refs[:n_x], refs[n_x : n_x + n_y], refs[n_x + n_y :]
        for (i, i0, i1), (j, j0, j1), (k, k0, k1) in spans(widths_of(x), widths_of(y), widths):
            out[k][:, k0:k1] = x[i][:, i0:i1] + y[j][:, j0:j1]

    outs = [((HALF, n), F32, VMEM) for n in widths]
    return list(run(kernel, [(x, VMEM) for x in (*xs, *ys)], outs, mib=2, after=after))


def in_two(width):
    cut = width // 256 * 128
    return [cut, width - cut]


def halve(whole, place, keep, gives):
    keep[...] = whole[pl.ds(pl.multiple_of(place * HALF, HALF), HALF), :]
    at = 0
    for give in gives:
        n = give.shape[1]
        give[...] = whole[pl.ds(pl.multiple_of((1 - place) * HALF, HALF), HALF), at : at + n]
        at += n


def tile_at(i):
    return pl.ds(pl.multiple_of(i * TILE, TILE), TILE)


def gate_left(run, grad, error, start, first, count, before=None, after=()):
    rows, cols = grad.shape
    last = (first + count) * TILE == rows

    def kernel(grad, error, start, *refs):
        if before is not None:
            refs = refs[2:]
        left, fixed = refs[:2]

        def step(g, e, start):
            at = tile_at(first + pl.program_id(0))
            term = jnp.zeros((TILE, RANK), F32)
            for j in range(0, cols, TILE):
                here = slice(j, j + TILE)
                c = g[:, here] + e[:, here]
                fixed[at, here] = c
                term += lax.dot_general(c, start[:, here], NT, preferred_element_type=F32)
            left[:, at] = term.T

        spec = pl.BlockSpec((TILE, cols), lambda i: (first + i, 0), pipeline_mode=pl.Buffered(3))
        whole = pl.BlockSpec((RANK, cols), lambda i: (0, 0))
        pltpu.emit_pipeline(step, grid=(count,), in_specs=[spec, spec, whole])(grad, error, start)
        if last:
            halve(left, core_of(), refs[2], refs[3:])

    args = [(grad, HBM), (error, HBM), (start, HBM)]
    outs = [((RANK, rows), F32, VMEM), ((rows, cols), BF16, VMEM)]
    if last:
        outs += [((HALF, n), F32, VMEM) for n in (rows, *in_two(rows))]
    aliases = None
    if before is not None:
        args += [(x, VMEM) for x in before]
        aliases = {3: 0, 4: 1}
    return run(kernel, args, outs, mib=8, aliases=aliases, after=after)


def down_left(run, grad, error, start, first, count, before=None, after=()):
    rows, cols = grad.shape
    last = (first + count) * TILE == rows

    def kernel(grad, error, start, *refs):
        if before is not None:
            refs = refs[2:]
        left, fixed = refs[:2]
        block = lax.div(lax.axis_index("dp"), REPLICAS) * (rows // TILE) + first
        if before is None:
            left[...] = jnp.zeros_like(left)

        def step(g, e, s):
            at = tile_at(first + pl.program_id(0))
            for j in range(0, cols, TILE):
                here = slice(j, j + TILE)
                c = g[:, here] + e[:, here]
                fixed[at, here] = c
                left[:, here] += jnp.dot(s[...], c, preferred_element_type=F32)

        spec = pl.BlockSpec((TILE, cols), lambda i: (first + i, 0), pipeline_mode=pl.Buffered(3))
        part = pl.BlockSpec((RANK, TILE), lambda i: (0, block + i))
        pltpu.emit_pipeline(step, grid=(count,), in_specs=[spec, spec, part])(grad, error, start)
        if last:
            halve(left, replica_of(), refs[2], refs[3:])

    args = [(grad, HBM), (error, HBM), (start, HBM)]
    outs = [((RANK, cols), F32, VMEM), ((rows, cols), BF16, VMEM)]
    if last:
        outs += [((HALF, cols), F32, VMEM)] * 2
    aliases = None
    if before is not None:
        args += [(x, VMEM) for x in before]
        aliases = {3: 0, 4: 1}
    return run(kernel, args, outs, mib=8, aliases=aliases, after=after)


def load_left(owns, others, place, left, stack):
    for refs, half in ((owns, place), (others, 1 - place)):
        at = 0
        for ref in refs:
            n = ref.shape[1]
            left[pl.ds(pl.multiple_of(half * HALF, HALF), HALF), at : at + n] = ref[...]
            at += n
    hi, lo = parts_of(left[...])
    stack[:RANK, :] = hi
    stack[RANK:, :] = lo
    return lax.dot_general(
        left[...], left[...], NT, preferred_element_type=F32, precision=lax.Precision.HIGHEST
    )


def gate_right(run, owns, others, fixed, after=()):
    rows, cols = fixed.shape
    n_own, n_both = len(owns), len(owns) + len(others)

    def kernel(*refs):
        fixed, keep, give, gram, left, stack, right = refs[n_both:]
        gram[...] = load_left(refs[:n_own], refs[n_own:n_both], core_of(), left, stack)

        def step(i, _):
            both = jnp.dot(stack[...], fixed[:, tile_at(i)], preferred_element_type=F32)
            right[:, tile_at(i)] = both[:RANK] + both[RANK:]
            return 0

        lax.fori_loop(0, cols // TILE, step, 0)
        halve(right, replica_of(), keep, [give])

    return run(
        kernel,
        [(x, VMEM) for x in (*owns, *others, fixed)],
        [((HALF, cols), F32, VMEM)] * 2 + [((RANK, RANK), F32, VMEM), ((RANK, rows), F32, VMEM)],
        [pltpu.VMEM((2 * RANK, rows), BF16), pltpu.VMEM((RANK, cols), F32)],
        mib=4,
        after=after,
    )


def down_right(run, owns, others, fixed, after=()):
    rows, cols = fixed.shape
    n_own, n_both = len(owns), len(owns) + len(others)
    cut, rest = in_two(rows)

    def kernel(*refs):
        fixed, keep, give_1, give_2, left, stack, right = refs[n_both:]
        gram = load_left(refs[:n_own], refs[n_own:n_both], replica_of(), left, stack)

        def step(i, _):
            both = lax.dot_general(stack[...], fixed[tile_at(i), :], NT, preferred_element_type=F32)
            right[:, tile_at(i)] = both[:RANK] + both[RANK:]
            return 0

        lax.fori_loop(0, rows // TILE, step, 0)
        packed = jnp.concatenate([gram[:HALF], gram[HALF:]], axis=1)
        halve(right, core_of(), keep.at[:, :rows], [give_1, give_2.at[:, :rest]])
        keep[:, rows:] = packed
        give_2[:, rest:] = packed

    widths = (rows + 2 * RANK, cut, rest + 2 * RANK)
    return run(
        kernel,
        [(x, VMEM) for x in (*owns, *others, fixed)],
        [((HALF, n), F32, VMEM) for n in widths] + [((RANK, cols), F32, VMEM)],
        [pltpu.VMEM((2 * RANK, cols), BF16), pltpu.VMEM((RANK, rows), F32)],
        mib=4,
        after=after,
    )


def inverses(grams):
    row_at = lax.broadcasted_iota(jnp.int32, (RANK, RANK), 0)
    col_at = lax.broadcasted_iota(jnp.int32, (RANK, RANK), 1)
    lane = lax.broadcasted_iota(jnp.int32, (1, RANK), 1)

    def scaled(a):
        diagonal = jnp.where(row_at == col_at, a, 0.0)
        down = lax.rsqrt(jnp.sum(diagonal, axis=1, keepdims=True))
        across = lax.rsqrt(jnp.sum(diagonal, axis=0, keepdims=True))
        return a * down * across, down, across

    def sweep(a, k):
        one, two = (row_at == k, row_at == k + 1)
        here = one | two | (col_at == k) | (col_at == k + 1)
        col_1 = jnp.broadcast_to(a[:, k : k + 1], (RANK, RANK))
        col_2 = jnp.broadcast_to(a[:, k + 1 : k + 2], (RANK, RANK))
        p, q, r = col_1[k : k + 1], col_2[k : k + 1], col_2[k + 1 : k + 2]
        row_1 = jnp.where(lane == k, 1.0, jnp.where(lane == k + 1, 0.0, a[k : k + 1]))
        row_2 = jnp.where(lane == k + 1, 1.0, jnp.where(lane == k, 0.0, a[k + 1 : k + 2]))
        inv = 1.0 / (p * r - q * q)
        new_1 = (r * row_1 - q * row_2) * inv
        new_2 = (p * row_2 - q * row_1) * inv
        col_1 = jnp.where(one, -1.0, jnp.where(two, 0.0, col_1))
        col_2 = jnp.where(two, -1.0, jnp.where(one, 0.0, col_2))
        return jnp.where(here, 0.0, a) - col_1 * new_1 - col_2 * new_2

    systems = [scaled(a) for a in grams]
    values = [a for a, _, _ in systems]
    for k in range(0, RANK, 2):
        values = [sweep(a, k) for a in values]
    return [a * down * across for a, (_, down, across) in zip(values, systems)]


def stacked(refs, order, stack):
    at = 0
    for ref in refs:
        parts = parts_of(ref[...])
        n = ref.shape[0]
        for k, which in enumerate(order):
            stack[k * RANK + at : k * RANK + at + n, :] = parts[which]
        at += n


ROW_ORDER, COL_ORDER = (0, 1, 0, 1), (0, 0, 1, 1)


def turn(stack, turned):
    for i in range(0, stack.shape[1], TILE):
        turned[i : i + TILE, :] = stack[:, i : i + TILE].T


def solve(run, grams_down, left_down, grams_gate, left_gate, after=()):
    n_down, n_gate = len(grams_down), len(grams_gate)
    cols, rows = left_down.shape[1], left_gate.shape[1]

    def kernel(*refs):
        down, gate = refs[:n_down], refs[n_down : n_down + n_gate]
        left_down, left_gate, col_stack, row_turned, col, row, row_stack = refs[n_down + n_gate :]
        a = sum((ref[...] for ref in down[1:]), down[0][...])
        a = jnp.concatenate([a[:, :RANK], a[:, RANK:]], axis=0)
        b = sum((ref[...] for ref in gate[1:]), gate[0][...])
        for place, a, left, out in zip(
            (core_of(), replica_of()), inverses([a, b]), (left_down, left_gate), (col, row)
        ):
            other = jnp.concatenate([a[HALF:], a[:HALF]], axis=0)
            a = jnp.where(place == 0, a, other) * (1.0 / REPLICAS)
            out[...] = jnp.dot(
                a, left[...], preferred_element_type=F32, precision=lax.Precision.HIGHEST
            )
        stacked([col], COL_ORDER, col_stack)
        stacked([row], ROW_ORDER, row_stack)
        turn(row_stack, row_turned)

    return run(
        kernel,
        [(x, VMEM) for x in (*grams_down, *grams_gate, left_down, left_gate)],
        [((4 * RANK, cols), BF16, VMEM), ((rows, 4 * RANK), BF16, VMEM)],
        [
            pltpu.VMEM((RANK, cols), F32),
            pltpu.VMEM((RANK, rows), F32),
            pltpu.VMEM((4 * RANK, rows), BF16),
        ],
        mib=6,
        after=after,
    )


def rebuild(run, row_turned, col_stack, owns, others, fixed, after=()):
    halves = [
        (x, half, sum(widths_of(xs[:i])))
        for half, xs in ((0, owns), (HALF, others))
        for i, x in enumerate(xs)
    ]
    rows, cols = fixed.shape
    height = rows // REPLICAS // 2
    tiles = rows // REPLICAS // height
    rows_late = row_turned is None
    scratch = [pltpu.VMEM((4 * RANK, rows if rows_late else cols), BF16)]
    if rows_late:
        scratch.append(pltpu.VMEM((rows, 4 * RANK), BF16))
    n_half = len(halves)

    def kernel(ready, *refs):
        fixed, new_error, update, done, late, *turned = refs[n_half:]
        done[...] = jnp.zeros_like(done)
        order = ROW_ORDER if rows_late else COL_ORDER
        for (_, at, left), ref in zip(halves, refs):
            parts = parts_of(ref[...])
            n, width = ref.shape
            for k, which in enumerate(order):
                late[k * RANK + at : k * RANK + at + n, left : left + width] = parts[which]
        row, col = ready, late
        if rows_late:
            row, col = turned[0], ready
            turn(late, row)
        replica = replica_of()
        mine, theirs = replica * tiles, (1 - replica) * tiles

        def tile_of(i):
            return jnp.where(i < tiles, mine + i, theirs + i - tiles)

        def step(e, u):
            i = pl.program_id(0)
            at = pl.ds(pl.multiple_of(tile_of(i) * height, height), height)

            def tile(with_update):
                row_here = row[at, :]
                for j in range(0, cols, TILE):
                    here = slice(j, j + TILE)
                    value = jnp.dot(row_here, col[:, here], preferred_element_type=F32)
                    e[:, here] = (fixed[at, here].astype(F32) - value).astype(BF16)
                    if with_update:
                        u[:, here] = value.astype(BF16)

            pl.when(i < tiles)(lambda: tile(True))
            pl.when(i >= tiles)(lambda: tile(False))

        block = (height, cols)
        pltpu.emit_pipeline(
            step,
            grid=(REPLICAS * tiles,),
            out_specs=[
                pl.BlockSpec(block, lambda i: (tile_of(i), 0)),
                pl.BlockSpec(block, lambda i: (jnp.minimum(i, tiles - 1), 0)),
            ],
        )(new_error, update)

    pieces = [x for x, _, _ in halves]
    return run(
        kernel,
        [(x, VMEM) for x in (col_stack if rows_late else row_turned, *pieces, fixed)],
        [((rows, cols), BF16, HBM), ((rows // REPLICAS, cols), BF16, HBM), ((8, 128), F32, VMEM)],
        scratch,
        mib=18,
        after=after,
    )


def local(grad_gate, grad_down, error_gate, error_down, start_gate, start_down):
    slab, width = grad_gate.shape
    n_dp, n_t = lax.axis_size("dp"), lax.axis_size("tensor")
    run = Calls()
    hops, steps = row_steps(), col_steps()
    tiles = slab // TILE

    _, fixed_down, keep, give = down_left(run, grad_down, error_down, start_down, 0, tiles)
    got = exchange(give, other_replica)
    gate_args = (run, grad_gate, error_gate, start_gate)
    first = gate_left(*gate_args, 0, tiles // 2, after=(keep,))
    (down,) = add(run, [keep], [got], after=(first[0],))
    got = exchange(down, steps[0])
    _, fixed_gate, keep_gate, *gives = gate_left(
        *gate_args, tiles // 2, tiles - tiles // 2, first, after=(down,)
    )
    (gate,) = add(run, [keep_gate], to_other_core(gives))
    got_gate = exchange(gate, hops[0])
    for i in range(len(steps)):
        (down,) = add(run, [down], [got], after=(gate,))
        if i + 1 < len(steps):
            got = exchange(down, steps[i + 1])
    other_down = exchange(down, other_replica)
    for hop in hops[1:]:
        (gate,) = add(run, [gate], [got_gate], after=(down,))
        got_gate = exchange(gate, hop)

    keep, *gives, left_down = down_right(run, [down], [other_down], fixed_down, after=(gate,))
    gots = to_other_core(gives)
    gates = add(run, [gate], [got_gate], in_two(slab), after=(keep,))
    others_gate = to_other_core(gates)
    down, gram_down = add(run, [keep], gots, [slab, 2 * RANK], after=(gates[0],))
    grams_down = [gram_down] + [
        exchange(gram_down, lambda d, t, b=b: (d, t ^ b)) for b in range(2, n_t, 2)
    ]
    got = exchange(down, hops[0])
    keep_gate, give_gate, gram_gate, left_gate = gate_right(
        run, gates, others_gate, fixed_gate, after=(down,)
    )
    got_gate = exchange(give_gate, other_replica)
    grams_gate = [gram_gate] + [
        exchange(gram_gate, lambda d, t, b=b: (d ^ b, t)) for b in range(REPLICAS, n_dp, REPLICAS)
    ]
    for hop in hops[1:]:
        (down,) = add(run, [down], [got], after=(gram_gate,))
        got = exchange(down, hop)
    col_stack, row_turned = solve(
        run, grams_down, left_down, grams_gate, left_gate, after=(down,)
    )
    (gate,) = add(run, [keep_gate], [got_gate], after=(col_stack,))
    got_gate = exchange(gate, steps[0])
    downs = add(run, [down], [got], in_two(slab), after=(gate,))
    others_down = to_other_core(downs)
    new_error_down, update_down, done = rebuild(
        run, None, col_stack, downs, others_down, fixed_down
    )
    for i in range(len(steps)):
        (gate,) = add(run, [gate], [got_gate], after=(done,))
        if i + 1 < len(steps):
            got_gate = exchange(gate, steps[i + 1])
    other_gate = exchange(gate, other_replica)
    new_error_gate, update_gate, _ = rebuild(
        run, row_turned, None, [gate], [other_gate], fixed_gate
    )
    return (update_gate, update_down, new_error_gate, new_error_down)


def solution(mesh):
    split = P(("mix", "dp"), "tensor")
    in_specs = (split, split, split, split, P(None, "tensor"), P())
    out_specs = (split, split, split, split)

    def run(grad_gate, *rest):
        groups = mesh.shape["mix"] * mesh.shape["dp"]
        slab = grad_gate.shape[0] // groups
        width = grad_gate.shape[1] // mesh.shape["tensor"]
        fits = slab % (REPLICAS * TILE) == 0 and width % TILE == 0
        body = local if fits else local_plain
        return jax.shard_map(
            body, mesh=mesh, in_specs=in_specs, out_specs=out_specs, check_vma=False
        )(grad_gate, *rest)

    return run
```

```python
import functools

import jax
import jax.numpy as jnp
from jax import lax
from jax.experimental import pallas as pl
from jax.experimental.pallas import tpu as pltpu
from jax.sharding import PartitionSpec as P

REPLICAS = 2
RANK = 64
TILE = 256
THIN = 128
FLOPS = 1.15e9
WEIGHTS = (8.0, 4.0, 1.0, 4.0, 0.1, 5.0, 1.0, 5.0, 1.0, 1.0, 4.0, 0.1, 0.2, 1.0, 5.0, 1.0, 1.0, 8.0, 8.0)
MIB = 1 << 20
BF16 = jnp.bfloat16
F32 = jnp.float32

NN = (((1,), (0,)), ((), ()))
NT = (((1,), (1,)), ((), ()))
TN = (((0,), (0,)), ((), ()))


def from_partner(shard, axis, stride):
    return lax.ppermute(shard, axis, [(i, i ^ 1 << stride) for i in range(lax.axis_size(axis))])


def corrected(grad, error):
    return (grad.astype(F32) + error.astype(F32)).astype(BF16)


def transposed(matrix, ortho):
    return lax.dot_general(matrix, ortho.astype(BF16), TN, preferred_element_type=F32)


def gram_of(left):
    return jnp.dot(left.T, left, precision=lax.Precision.HIGHEST)


def factored(left, inner):
    lower = jnp.linalg.cholesky(inner)
    return lax.linalg.triangular_solve(lower, left, left_side=False, lower=True, transpose_a=True)


def local_plain(grad_gate, grad_down, error_gate, error_down, start_gate, start_down):
    high = lax.Precision.HIGHEST
    dp_place = lax.axis_index("dp")
    block = dp_place // REPLICAS
    replica = dp_place % REPLICAS
    fixed_gate = corrected(grad_gate, error_gate)
    fixed_down = corrected(grad_down, error_down)
    slab = fixed_gate.shape[0]
    cols_down = lax.dynamic_slice_in_dim(start_down, block * slab, slab, 1)
    left_gate = lax.dot_general(fixed_gate, start_gate, NT, preferred_element_type=F32)
    left_down = lax.dot_general(
        fixed_down, cols_down, (((0,), (1,)), ((), ())), preferred_element_type=F32
    )
    left_gate = lax.psum(left_gate, "tensor")
    left_gate = left_gate + from_partner(left_gate, "dp", 0)
    left_down = lax.psum(left_down, "dp")
    keep_gate = (replica == 0).astype(F32)
    inner_gate = lax.psum(gram_of(left_gate) * keep_gate, "dp")
    inner_down = lax.psum(gram_of(left_down), "tensor")
    ortho_gate = factored(left_gate, inner_gate)
    ortho_down = factored(left_down, inner_down)
    right_gate = transposed(fixed_gate, ortho_gate)
    right_gate = lax.psum(right_gate, "dp") / REPLICAS
    right_down = jnp.dot(fixed_down, ortho_down.astype(BF16), preferred_element_type=F32)
    right_down = lax.psum(right_down, "tensor")
    right_down = right_down + from_partner(right_down, "dp", 0)
    right_down = right_down / REPLICAS
    rebuilt_gate = jnp.dot(ortho_gate, right_gate.T, precision=high)
    rebuilt_down = jnp.dot(right_down, ortho_down.T, precision=high)
    share = slab // REPLICAS
    update_gate = lax.dynamic_slice_in_dim(rebuilt_gate, replica * share, share, 0).astype(BF16)
    update_down = lax.dynamic_slice_in_dim(rebuilt_down, replica * share, share, 0).astype(BF16)
    new_error_gate = (fixed_gate.astype(F32) - rebuilt_gate).astype(BF16)
    new_error_down = (fixed_down.astype(F32) - rebuilt_down).astype(BF16)
    return (update_gate, update_down, new_error_gate, new_error_down)


def core_of():
    return lax.rem(lax.axis_index("tensor"), 2)


def replica_of():
    return lax.rem(lax.axis_index("dp"), REPLICAS)


def exchange(x, partner):
    n_dp, n_t = lax.axis_size("dp"), lax.axis_size("tensor")
    pairs = []
    for d in range(n_dp):
        for t in range(n_t):
            to_d, to_t = partner(d, t)
            pairs.append((d * n_t + t, to_d * n_t + to_t))
    return lax.ppermute(x, ("dp", "tensor"), pairs)


def bits(n, low):
    out, b = [], low
    while b < n:
        out.append(b)
        b *= 2
    return out


def row_steps():
    steps = [(0, b) for b in bits(lax.axis_size("tensor"), 2)] + [(1, 0)]

    def partner(i, d, t):
        r, b = steps[i] if t % 2 == 0 else steps[-1 - i]
        return d ^ r, t ^ b

    return [functools.partial(partner, i) for i in range(len(steps))]


def col_steps():
    return [lambda d, t, b=b: (d ^ b, t) for b in bits(lax.axis_size("dp"), REPLICAS)]


def other_core(d, t):
    return d, t ^ 1


def other_replica(d, t):
    return d ^ 1, t


def to_other_core(pieces):
    return [exchange(x, other_core) for x in pieces]


VMEM = pl.BlockSpec(memory_space=pltpu.VMEM)
HBM = pl.BlockSpec(memory_space=pltpu.HBM)
ANY = pl.BlockSpec(memory_space=pl.ANY)
HALF = RANK // 2


class Calls:
    def __init__(self):
        self.count = 0

    def __call__(self, kernel, args, outs, scratch=(), mib=8, aliases=None, after=()):
        n_in, n_after = len(args), len(after)
        operands = [
            pltpu.with_memory_space_constraint(x, pltpu.VMEM if spec is VMEM else pltpu.HBM)
            for x, spec in args
        ]

        def body(*refs):
            kernel(*refs[:n_in], *refs[n_in + n_after :])

        out = pl.pallas_call(
            body,
            out_shape=tuple(
                (pltpu.VMEM if spec is VMEM else pltpu.HBM)(shape, kind) for shape, kind, spec in outs
            ),
            in_specs=[spec for _, spec in args] + [ANY] * n_after,
            out_specs=tuple(spec for *_, spec in outs),
            scratch_shapes=list(scratch),
            input_output_aliases=aliases or {},
            compiler_params=pltpu.CompilerParams(vmem_limit_bytes=mib * MIB),
            cost_estimate=pl.CostEstimate(
                flops=int(WEIGHTS[self.count] * FLOPS), bytes_accessed=1 << 10, transcendentals=0
            ),
        )(*operands, *after)
        self.count += 1
        return out


def parts_of(x):
    hi = x.astype(BF16)
    lo = (x - hi.astype(F32)).astype(BF16)
    return hi, lo


def spans(*widths):
    edges = sorted({sum(w[:i]) for w in widths for i in range(len(w) + 1)})
    for low, high in zip(edges, edges[1:]):
        places = []
        for w in widths:
            k = max(i for i in range(len(w)) if sum(w[:i]) <= low)
            places.append((k, low - sum(w[:k]), high - sum(w[:k])))
        yield places


def widths_of(refs):
    return [ref.shape[1] for ref in refs]


def add(run, xs, ys, widths=None, after=()):
    widths = widths or widths_of(xs)
    n_x, n_y = len(xs), len(ys)

    def kernel(*refs):
        x, y, out = refs[:n_x], refs[n_x : n_x + n_y], refs[n_x + n_y :]
        for (i, i0, i1), (j, j0, j1), (k, k0, k1) in spans(widths_of(x), widths_of(y), widths):
            out[k][:, k0:k1] = x[i][:, i0:i1] + y[j][:, j0:j1]

    outs = [((HALF, n), F32, VMEM) for n in widths]
    return list(run(kernel, [(x, VMEM) for x in (*xs, *ys)], outs, mib=2, after=after))


def in_two(width):
    cut = width // 256 * 128
    return [cut, width - cut]


def halve(whole, place, keep, gives):
    keep[...] = whole[pl.ds(pl.multiple_of(place * HALF, HALF), HALF), :]
    at = 0
    for give in gives:
        n = give.shape[1]
        give[...] = whole[pl.ds(pl.multiple_of((1 - place) * HALF, HALF), HALF), at : at + n]
        at += n


def tile_at(i):
    return pl.ds(pl.multiple_of(i * TILE, TILE), TILE)


def gate_left(run, grad, error, start, first, count, before=None, after=()):
    rows, cols = grad.shape
    last = (first + count) * TILE == rows

    def kernel(grad, error, start, *refs):
        if before is not None:
            refs = refs[2:]
        left, fixed = refs[:2]

        def step(g, e, start):
            i = first * TILE // THIN + pl.program_id(0)
            at = pl.ds(pl.multiple_of(i * THIN, THIN), THIN)
            term = jnp.zeros((THIN, RANK), F32)
            for j in range(0, cols, TILE):
                here = slice(j, j + TILE)
                c = g[:, here] + e[:, here]
                fixed[at, here] = c
                term += lax.dot_general(c, start[:, here], NT, preferred_element_type=F32)
            left[:, at] = term.T

        spec = pl.BlockSpec(
            (THIN, cols), lambda i: (first * TILE // THIN + i, 0), pipeline_mode=pl.Buffered(4)
        )
        whole = pl.BlockSpec((RANK, cols), lambda i: (0, 0))
        pltpu.emit_pipeline(step, grid=(count * TILE // THIN,), in_specs=[spec, spec, whole])(grad, error, start)
        if last:
            halve(left, core_of(), refs[2], refs[3:])

    args = [(grad, HBM), (error, HBM), (start, HBM)]
    outs = [((RANK, rows), F32, VMEM), ((rows, cols), BF16, VMEM)]
    if last:
        outs += [((HALF, n), F32, VMEM) for n in (rows, *in_two(rows))]
    aliases = None
    if before is not None:
        args += [(x, VMEM) for x in before]
        aliases = {3: 0, 4: 1}
    return run(kernel, args, outs, mib=8, aliases=aliases, after=after)


def down_left(run, grad, error, start, first, count, before=None, after=()):
    rows, cols = grad.shape
    last = (first + count) * TILE == rows

    def kernel(grad, error, start, *refs):
        if before is not None:
            refs = refs[2:]
        left, fixed = refs[:2]
        block = lax.div(lax.axis_index("dp"), REPLICAS) * (rows // TILE) + first
        if before is None:
            left[...] = jnp.zeros_like(left)

        def step(g, e, s):
            at = tile_at(first + pl.program_id(0))
            for j in range(0, cols, TILE):
                here = slice(j, j + TILE)
                c = g[:, here] + e[:, here]
                fixed[at, here] = c
                left[:, here] += jnp.dot(s[...], c, preferred_element_type=F32)

        spec = pl.BlockSpec((TILE, cols), lambda i: (first + i, 0), pipeline_mode=pl.Buffered(4))
        part = pl.BlockSpec((RANK, TILE), lambda i: (0, block + i))
        pltpu.emit_pipeline(step, grid=(count,), in_specs=[spec, spec, part])(grad, error, start)
        if last:
            halve(left, replica_of(), refs[2], refs[3:])

    args = [(grad, HBM), (error, HBM), (start, HBM)]
    outs = [((RANK, cols), F32, VMEM), ((rows, cols), BF16, VMEM)]
    if last:
        outs += [((HALF, cols), F32, VMEM)] * 2
    aliases = None
    if before is not None:
        args += [(x, VMEM) for x in before]
        aliases = {3: 0, 4: 1}
    return run(kernel, args, outs, mib=12, aliases=aliases, after=after)


def load_left(owns, others, place, left, stack):
    for refs, half in ((owns, place), (others, 1 - place)):
        at = 0
        for ref in refs:
            n = ref.shape[1]
            left[pl.ds(pl.multiple_of(half * HALF, HALF), HALF), at : at + n] = ref[...]
            at += n
    hi, lo = parts_of(left[...])
    stack[:RANK, :] = hi
    stack[RANK:, :] = lo
    return lax.dot_general(
        left[...], left[...], NT, preferred_element_type=F32, precision=lax.Precision.HIGHEST
    )


def gate_right(run, owns, others, fixed, after=()):
    rows, cols = fixed.shape
    n_own, n_both = len(owns), len(owns) + len(others)

    def kernel(*refs):
        fixed, keep, give, gram, left, stack, right = refs[n_both:]
        gram[...] = load_left(refs[:n_own], refs[n_own:n_both], core_of(), left, stack)

        def step(i, _):
            both = jnp.dot(stack[...], fixed[:, tile_at(i)], preferred_element_type=F32)
            right[:, tile_at(i)] = both[:RANK] + both[RANK:]
            return 0

        lax.fori_loop(0, cols // TILE, step, 0)
        halve(right, replica_of(), keep, [give])

    return run(
        kernel,
        [(x, VMEM) for x in (*owns, *others, fixed)],
        [((HALF, cols), F32, VMEM)] * 2 + [((RANK, RANK), F32, VMEM), ((RANK, rows), F32, VMEM)],
        [pltpu.VMEM((2 * RANK, rows), BF16), pltpu.VMEM((RANK, cols), F32)],
        mib=4,
        after=after,
    )


def down_right(run, owns, others, fixed, after=()):
    rows, cols = fixed.shape
    n_own, n_both = len(owns), len(owns) + len(others)
    cut, rest = in_two(rows)

    def kernel(*refs):
        fixed, keep, give_1, give_2, left, stack, right = refs[n_both:]
        gram = load_left(refs[:n_own], refs[n_own:n_both], replica_of(), left, stack)

        def step(i, _):
            both = lax.dot_general(stack[...], fixed[tile_at(i), :], NT, preferred_element_type=F32)
            right[:, tile_at(i)] = both[:RANK] + both[RANK:]
            return 0

        lax.fori_loop(0, rows // TILE, step, 0)
        packed = jnp.concatenate([gram[:HALF], gram[HALF:]], axis=1)
        halve(right, core_of(), keep.at[:, :rows], [give_1, give_2.at[:, :rest]])
        keep[:, rows:] = packed
        give_2[:, rest:] = packed

    widths = (rows + 2 * RANK, cut, rest + 2 * RANK)
    return run(
        kernel,
        [(x, VMEM) for x in (*owns, *others, fixed)],
        [((HALF, n), F32, VMEM) for n in widths] + [((RANK, cols), F32, VMEM)],
        [pltpu.VMEM((2 * RANK, cols), BF16), pltpu.VMEM((RANK, rows), F32)],
        mib=4,
        after=after,
    )


def inverses(grams):
    row_at = lax.broadcasted_iota(jnp.int32, (RANK, RANK), 0)
    col_at = lax.broadcasted_iota(jnp.int32, (RANK, RANK), 1)
    lane = lax.broadcasted_iota(jnp.int32, (1, RANK), 1)

    def scaled(a):
        diagonal = jnp.where(row_at == col_at, a, 0.0)
        down = lax.rsqrt(jnp.sum(diagonal, axis=1, keepdims=True))
        across = lax.rsqrt(jnp.sum(diagonal, axis=0, keepdims=True))
        return a * down * across, down, across

    def sweep(a, k):
        one, two = (row_at == k, row_at == k + 1)
        here = one | two | (col_at == k) | (col_at == k + 1)
        col_1 = jnp.broadcast_to(a[:, k : k + 1], (RANK, RANK))
        col_2 = jnp.broadcast_to(a[:, k + 1 : k + 2], (RANK, RANK))
        p, q, r = col_1[k : k + 1], col_2[k : k + 1], col_2[k + 1 : k + 2]
        row_1 = jnp.where(lane == k, 1.0, jnp.where(lane == k + 1, 0.0, a[k : k + 1]))
        row_2 = jnp.where(lane == k + 1, 1.0, jnp.where(lane == k, 0.0, a[k + 1 : k + 2]))
        inv = 1.0 / (p * r - q * q)
        new_1 = (r * row_1 - q * row_2) * inv
        new_2 = (p * row_2 - q * row_1) * inv
        col_1 = jnp.where(one, -1.0, jnp.where(two, 0.0, col_1))
        col_2 = jnp.where(two, -1.0, jnp.where(one, 0.0, col_2))
        return jnp.where(here, 0.0, a) - col_1 * new_1 - col_2 * new_2

    systems = [scaled(a) for a in grams]
    values = [a for a, _, _ in systems]
    for k in range(0, RANK, 2):
        values = [sweep(a, k) for a in values]
    return [a * down * across for a, (_, down, across) in zip(values, systems)]


def stacked(refs, order, stack):
    at = 0
    for ref in refs:
        parts = parts_of(ref[...])
        n = ref.shape[0]
        for k, which in enumerate(order):
            stack[k * RANK + at : k * RANK + at + n, :] = parts[which]
        at += n


ROW_ORDER, COL_ORDER = (0, 1, 0, 1), (0, 0, 1, 1)


def turn(stack, turned):
    for i in range(0, stack.shape[1], TILE):
        turned[i : i + TILE, :] = stack[:, i : i + TILE].T


def gram_sums(run, packed, whole, after=()):
    n = len(packed)

    def kernel(*refs):
        a = sum((ref[...] for ref in refs[1:n]), refs[0][...])
        refs[-2][...] = jnp.concatenate([a[:, :RANK], a[:, RANK:]], axis=0)
        refs[-1][...] = sum((ref[...] for ref in refs[n + 1 : -2]), refs[n][...])

    outs = [((RANK, RANK), F32, VMEM)] * 2
    return run(kernel, [(x, VMEM) for x in (*packed, *whole)], outs, mib=2, after=after)


def solve(run, gram_down, left_down, gram_gate, left_gate, after=()):
    cols, rows = left_down.shape[1], left_gate.shape[1]

    def kernel(gram_down, left_down, gram_gate, left_gate, col_stack, row_turned, col, row, row_stack):
        grams = [gram_down[...], gram_gate[...]]
        for place, a, left, out in zip(
            (core_of(), replica_of()), inverses(grams), (left_down, left_gate), (col, row)
        ):
            other = jnp.concatenate([a[HALF:], a[:HALF]], axis=0)
            a = jnp.where(place == 0, a, other) * (1.0 / REPLICAS)
            out[...] = jnp.dot(
                a, left[...], preferred_element_type=F32, precision=lax.Precision.HIGHEST
            )
        stacked([col], COL_ORDER, col_stack)
        stacked([row], ROW_ORDER, row_stack)
        turn(row_stack, row_turned)

    return run(
        kernel,
        [(x, VMEM) for x in (gram_down, left_down, gram_gate, left_gate)],
        [((4 * RANK, cols), BF16, VMEM), ((rows, 4 * RANK), BF16, VMEM)],
        [
            pltpu.VMEM((RANK, cols), F32),
            pltpu.VMEM((RANK, rows), F32),
            pltpu.VMEM((4 * RANK, rows), BF16),
        ],
        mib=6,
        after=after,
    )


def rebuild(run, row_turned, col_stack, owns, others, fixed, height, after=()):
    halves = [
        (x, half, sum(widths_of(xs[:i])))
        for half, xs in ((0, owns), (HALF, others))
        for i, x in enumerate(xs)
    ]
    rows, cols = fixed.shape
    tiles = rows // REPLICAS // height
    rows_late = row_turned is None
    scratch = [pltpu.VMEM((4 * RANK, rows if rows_late else cols), BF16)]
    if rows_late:
        scratch.append(pltpu.VMEM((rows, 4 * RANK), BF16))
    n_half = len(halves)

    def kernel(ready, *refs):
        fixed, new_error, update, done, late, *turned = refs[n_half:]
        done[...] = jnp.zeros_like(done)
        order = ROW_ORDER if rows_late else COL_ORDER
        for (_, at, left), ref in zip(halves, refs):
            parts = parts_of(ref[...])
            n, width = ref.shape
            for k, which in enumerate(order):
                late[k * RANK + at : k * RANK + at + n, left : left + width] = parts[which]
        row, col = ready, late
        if rows_late:
            row, col = turned[0], ready
            turn(late, row)
        replica = replica_of()
        mine, theirs = replica * tiles, (1 - replica) * tiles

        def tile_of(i):
            return jnp.where(i < tiles, mine + i, theirs + i - tiles)

        def step(e, u):
            i = pl.program_id(0)
            at = pl.ds(pl.multiple_of(tile_of(i) * height, height), height)

            def tile(with_update):
                row_here = row[at, :]
                for j in range(0, cols, TILE):
                    here = slice(j, j + TILE)
                    value = jnp.dot(row_here, col[:, here], preferred_element_type=F32)
                    e[:, here] = (fixed[at, here].astype(F32) - value).astype(BF16)
                    if with_update:
                        u[:, here] = value.astype(BF16)

            pl.when(i < tiles)(lambda: tile(True))
            pl.when(i >= tiles)(lambda: tile(False))

        block = (height, cols)
        pltpu.emit_pipeline(
            step,
            grid=(REPLICAS * tiles,),
            out_specs=[
                pl.BlockSpec(block, lambda i: (tile_of(i), 0)),
                pl.BlockSpec(block, lambda i: (jnp.minimum(i, tiles - 1), 0)),
            ],
        )(new_error, update)

    pieces = [x for x, _, _ in halves]
    return run(
        kernel,
        [(x, VMEM) for x in (col_stack if rows_late else row_turned, *pieces, fixed)],
        [((rows, cols), BF16, HBM), ((rows // REPLICAS, cols), BF16, HBM), ((8, 128), F32, VMEM)],
        scratch,
        mib=18,
        after=after,
    )


def local(grad_gate, grad_down, error_gate, error_down, start_gate, start_down):
    slab, width = grad_gate.shape
    n_dp, n_t = lax.axis_size("dp"), lax.axis_size("tensor")
    run = Calls()
    hops, steps = row_steps(), col_steps()
    tiles = slab // TILE

    _, fixed_down, keep, give = down_left(run, grad_down, error_down, start_down, 0, tiles)
    got = exchange(give, other_replica)
    gate_args = (run, grad_gate, error_gate, start_gate)
    first = gate_left(*gate_args, 0, tiles // 2, after=(keep,))
    (down,) = add(run, [keep], [got], after=(first[0],))
    got = exchange(down, steps[0])
    _, fixed_gate, keep_gate, *gives = gate_left(
        *gate_args, tiles // 2, tiles - tiles // 2, first, after=(down,)
    )
    (gate,) = add(run, [keep_gate], to_other_core(gives))
    got_gate = exchange(gate, hops[0])
    for i in range(len(steps)):
        (down,) = add(run, [down], [got], after=(gate,))
        if i + 1 < len(steps):
            got = exchange(down, steps[i + 1])
    other_down = exchange(down, other_replica)
    for hop in hops[1:]:
        (gate,) = add(run, [gate], [got_gate], after=(down,))
        got_gate = exchange(gate, hop)

    keep, *gives, left_down = down_right(run, [down], [other_down], fixed_down, after=(gate,))
    gots = to_other_core(gives)
    gates = add(run, [gate], [got_gate], in_two(slab), after=(keep,))
    others_gate = to_other_core(gates)
    down, gram_down = add(run, [keep], gots, [slab, 2 * RANK], after=(gates[0],))
    grams_down = [gram_down] + [
        exchange(gram_down, lambda d, t, b=b: (d, t ^ b)) for b in range(2, n_t, 2)
    ]
    got = exchange(down, hops[0])
    keep_gate, give_gate, gram_gate, left_gate = gate_right(
        run, gates, others_gate, fixed_gate, after=(down,)
    )
    got_gate = exchange(give_gate, other_replica)
    grams_gate = [gram_gate] + [
        exchange(gram_gate, lambda d, t, b=b: (d ^ b, t)) for b in range(REPLICAS, n_dp, REPLICAS)
    ]
    gram_down, gram_gate = gram_sums(run, grams_down, grams_gate)
    for hop in hops[1:]:
        (down,) = add(run, [down], [got], after=(gram_gate,))
        got = exchange(down, hop)
    (gate,) = add(run, [keep_gate], [got_gate], after=(down,))
    got_gate = exchange(gate, steps[0])
    col_stack, row_turned = solve(run, gram_down, left_down, gram_gate, left_gate, after=(gate,))
    downs = add(run, [down], [got], in_two(slab), after=(col_stack,))
    others_down = to_other_core(downs)
    for i in range(len(steps)):
        (gate,) = add(run, [gate], [got_gate], after=(downs[0],))
        if i + 1 < len(steps):
            got_gate = exchange(gate, steps[i + 1])
    other_gate = exchange(gate, other_replica)
    new_error_down, update_down, done = rebuild(
        run, None, col_stack, downs, others_down, fixed_down, slab // 8, after=(gate,)
    )
    new_error_gate, update_gate, _ = rebuild(
        run, row_turned, None, [gate], [other_gate], fixed_gate, slab // 4, after=(done,)
    )
    return (update_gate, update_down, new_error_gate, new_error_down)


def solution(mesh):
    split = P(("mix", "dp"), "tensor")
    in_specs = (split, split, split, split, P(None, "tensor"), P())
    out_specs = (split, split, split, split)

    def run(grad_gate, *rest):
        groups = mesh.shape["mix"] * mesh.shape["dp"]
        slab = grad_gate.shape[0] // groups
        width = grad_gate.shape[1] // mesh.shape["tensor"]
        fits = slab % (REPLICAS * TILE) == 0 and width % TILE == 0
        body = local if fits else local_plain
        return jax.shard_map(
            body, mesh=mesh, in_specs=in_specs, out_specs=out_specs, check_vma=False
        )(grad_gate, *rest)

    return run
```

```python
import functools

import jax
import jax.numpy as jnp
from jax import lax
from jax.experimental import pallas as pl
from jax.experimental.pallas import tpu as pltpu
from jax.sharding import PartitionSpec as P

REPLICAS = 2
RANK = 64
TILE = 256
FLOPS = 1.15e9
WEIGHTS = (8.0, 4.0, 1.0, 4.0, 0.1, 5.0, 1.0, 5.0, 1.0, 1.0, 4.0, 0.1, 0.1, 1.0, 5.0, 1.0, 1.0, 8.0, 8.0)
MIB = 1 << 20
BF16 = jnp.bfloat16
F32 = jnp.float32

NN = (((1,), (0,)), ((), ()))
NT = (((1,), (1,)), ((), ()))
TN = (((0,), (0,)), ((), ()))


def from_partner(shard, axis, stride):
    return lax.ppermute(shard, axis, [(i, i ^ 1 << stride) for i in range(lax.axis_size(axis))])


def corrected(grad, error):
    return (grad.astype(F32) + error.astype(F32)).astype(BF16)


def transposed(matrix, ortho):
    return lax.dot_general(matrix, ortho.astype(BF16), TN, preferred_element_type=F32)


def gram_of(left):
    return jnp.dot(left.T, left, precision=lax.Precision.HIGHEST)


def factored(left, inner):
    lower = jnp.linalg.cholesky(inner)
    return lax.linalg.triangular_solve(lower, left, left_side=False, lower=True, transpose_a=True)


def local_plain(grad_gate, grad_down, error_gate, error_down, start_gate, start_down):
    high = lax.Precision.HIGHEST
    dp_place = lax.axis_index("dp")
    block = dp_place // REPLICAS
    replica = dp_place % REPLICAS
    fixed_gate = corrected(grad_gate, error_gate)
    fixed_down = corrected(grad_down, error_down)
    slab = fixed_gate.shape[0]
    cols_down = lax.dynamic_slice_in_dim(start_down, block * slab, slab, 1)
    left_gate = lax.dot_general(fixed_gate, start_gate, NT, preferred_element_type=F32)
    left_down = lax.dot_general(
        fixed_down, cols_down, (((0,), (1,)), ((), ())), preferred_element_type=F32
    )
    left_gate = lax.psum(left_gate, "tensor")
    left_gate = left_gate + from_partner(left_gate, "dp", 0)
    left_down = lax.psum(left_down, "dp")
    keep_gate = (replica == 0).astype(F32)
    inner_gate = lax.psum(gram_of(left_gate) * keep_gate, "dp")
    inner_down = lax.psum(gram_of(left_down), "tensor")
    ortho_gate = factored(left_gate, inner_gate)
    ortho_down = factored(left_down, inner_down)
    right_gate = transposed(fixed_gate, ortho_gate)
    right_gate = lax.psum(right_gate, "dp") / REPLICAS
    right_down = jnp.dot(fixed_down, ortho_down.astype(BF16), preferred_element_type=F32)
    right_down = lax.psum(right_down, "tensor")
    right_down = right_down + from_partner(right_down, "dp", 0)
    right_down = right_down / REPLICAS
    rebuilt_gate = jnp.dot(ortho_gate, right_gate.T, precision=high)
    rebuilt_down = jnp.dot(right_down, ortho_down.T, precision=high)
    share = slab // REPLICAS
    update_gate = lax.dynamic_slice_in_dim(rebuilt_gate, replica * share, share, 0).astype(BF16)
    update_down = lax.dynamic_slice_in_dim(rebuilt_down, replica * share, share, 0).astype(BF16)
    new_error_gate = (fixed_gate.astype(F32) - rebuilt_gate).astype(BF16)
    new_error_down = (fixed_down.astype(F32) - rebuilt_down).astype(BF16)
    return (update_gate, update_down, new_error_gate, new_error_down)


def core_of():
    return lax.rem(lax.axis_index("tensor"), 2)


def replica_of():
    return lax.rem(lax.axis_index("dp"), REPLICAS)


def exchange(x, partner):
    n_dp, n_t = lax.axis_size("dp"), lax.axis_size("tensor")
    pairs = []
    for d in range(n_dp):
        for t in range(n_t):
            to_d, to_t = partner(d, t)
            pairs.append((d * n_t + t, to_d * n_t + to_t))
    return lax.ppermute(x, ("dp", "tensor"), pairs)


def bits(n, low):
    out, b = [], low
    while b < n:
        out.append(b)
        b *= 2
    return out


def row_steps():
    steps = [(0, b) for b in bits(lax.axis_size("tensor"), 2)] + [(1, 0)]

    def partner(i, d, t):
        r, b = steps[i] if t % 2 == 0 else steps[-1 - i]
        return d ^ r, t ^ b

    return [functools.partial(partner, i) for i in range(len(steps))]


def col_steps():
    return [lambda d, t, b=b: (d ^ b, t) for b in bits(lax.axis_size("dp"), REPLICAS)]


def other_core(d, t):
    return d, t ^ 1


def other_replica(d, t):
    return d ^ 1, t


def to_other_core(pieces):
    return [exchange(x, other_core) for x in pieces]


VMEM = pl.BlockSpec(memory_space=pltpu.VMEM)
HBM = pl.BlockSpec(memory_space=pltpu.HBM)
ANY = pl.BlockSpec(memory_space=pl.ANY)
HALF = RANK // 2


class Calls:
    def __init__(self):
        self.count = 0

    def __call__(self, kernel, args, outs, scratch=(), mib=8, aliases=None, after=()):
        n_in, n_after = len(args), len(after)
        operands = [
            pltpu.with_memory_space_constraint(x, pltpu.VMEM if spec is VMEM else pltpu.HBM)
            for x, spec in args
        ]

        def body(*refs):
            kernel(*refs[:n_in], *refs[n_in + n_after :])

        out = pl.pallas_call(
            body,
            out_shape=tuple(
                (pltpu.VMEM if spec is VMEM else pltpu.HBM)(shape, kind) for shape, kind, spec in outs
            ),
            in_specs=[spec for _, spec in args] + [ANY] * n_after,
            out_specs=tuple(spec for *_, spec in outs),
            scratch_shapes=list(scratch),
            input_output_aliases=aliases or {},
            compiler_params=pltpu.CompilerParams(vmem_limit_bytes=mib * MIB),
            cost_estimate=pl.CostEstimate(
                flops=int(WEIGHTS[self.count] * FLOPS), bytes_accessed=1 << 10, transcendentals=0
            ),
        )(*operands, *after)
        self.count += 1
        return out


def parts_of(x):
    hi = x.astype(BF16)
    lo = (x - hi.astype(F32)).astype(BF16)
    return hi, lo


def spans(*widths):
    edges = sorted({sum(w[:i]) for w in widths for i in range(len(w) + 1)})
    for low, high in zip(edges, edges[1:]):
        places = []
        for w in widths:
            k = max(i for i in range(len(w)) if sum(w[:i]) <= low)
            places.append((k, low - sum(w[:k]), high - sum(w[:k])))
        yield places


def widths_of(refs):
    return [ref.shape[1] for ref in refs]


def add(run, xs, ys, widths=None, after=()):
    widths = widths or widths_of(xs)
    n_x, n_y = len(xs), len(ys)

    def kernel(*refs):
        x, y, out = refs[:n_x], refs[n_x : n_x + n_y], refs[n_x + n_y :]
        for (i, i0, i1), (j, j0, j1), (k, k0, k1) in spans(widths_of(x), widths_of(y), widths):
            out[k][:, k0:k1] = x[i][:, i0:i1] + y[j][:, j0:j1]

    outs = [((HALF, n), F32, VMEM) for n in widths]
    return list(run(kernel, [(x, VMEM) for x in (*xs, *ys)], outs, mib=2, after=after))


def in_two(width):
    cut = width // 256 * 128
    return [cut, width - cut]


def halve(whole, place, keep, gives):
    keep[...] = whole[pl.ds(pl.multiple_of(place * HALF, HALF), HALF), :]
    at = 0
    for give in gives:
        n = give.shape[1]
        give[...] = whole[pl.ds(pl.multiple_of((1 - place) * HALF, HALF), HALF), at : at + n]
        at += n


def tile_at(i):
    return pl.ds(pl.multiple_of(i * TILE, TILE), TILE)


def gate_left(run, grad, error, start, first, count, before=None, after=()):
    rows, cols = grad.shape
    last = (first + count) * TILE == rows

    def kernel(grad, error, start, *refs):
        if before is not None:
            refs = refs[2:]
        left, fixed = refs[:2]

        def step(g, e):
            at = tile_at(first + pl.program_id(0))
            term = jnp.zeros((RANK, TILE), F32)
            for j in range(0, cols, TILE):
                here = slice(j, j + TILE)
                c = g[:, here] + e[:, here]
                fixed[at, here] = c
                term += lax.dot_general(start[:, here], c, NT, preferred_element_type=F32)
            left[:, at] = term

        spec = pl.BlockSpec((TILE, cols), lambda i: (first + i, 0), pipeline_mode=pl.Buffered(3))
        pltpu.emit_pipeline(step, grid=(count,), in_specs=[spec, spec])(grad, error)
        if last:
            halve(left, core_of(), refs[2], refs[3:])

    args = [(grad, HBM), (error, HBM), (start, VMEM)]
    outs = [((RANK, rows), F32, VMEM), ((rows, cols), BF16, VMEM)]
    if last:
        outs += [((HALF, n), F32, VMEM) for n in (rows, *in_two(rows))]
    aliases = None
    if before is not None:
        args += [(x, VMEM) for x in before]
        aliases = {3: 0, 4: 1}
    return run(kernel, args, outs, mib=8, aliases=aliases, after=after)


def down_left(run, grad, error, start, first, count, before=None, after=()):
    rows, cols = grad.shape
    last = (first + count) * TILE == rows

    def kernel(grad, error, start, *refs):
        if before is not None:
            refs = refs[2:]
        left, fixed = refs[:2]
        block = lax.div(lax.axis_index("dp"), REPLICAS) * (rows // TILE) + first
        if before is None:
            left[...] = jnp.zeros_like(left)

        def step(g, e, s):
            at = tile_at(first + pl.program_id(0))
            for j in range(0, cols, TILE):
                here = slice(j, j + TILE)
                c = g[:, here] + e[:, here]
                fixed[at, here] = c
                left[:, here] += jnp.dot(s[...], c, preferred_element_type=F32)

        spec = pl.BlockSpec((TILE, cols), lambda i: (first + i, 0), pipeline_mode=pl.Buffered(3))
        part = pl.BlockSpec((RANK, TILE), lambda i: (0, block + i))
        pltpu.emit_pipeline(step, grid=(count,), in_specs=[spec, spec, part])(grad, error, start)
        if last:
            halve(left, replica_of(), refs[2], refs[3:])

    args = [(grad, HBM), (error, HBM), (start, HBM)]
    outs = [((RANK, cols), F32, VMEM), ((rows, cols), BF16, VMEM)]
    if last:
        outs += [((HALF, cols), F32, VMEM)] * 2
    aliases = None
    if before is not None:
        args += [(x, VMEM) for x in before]
        aliases = {3: 0, 4: 1}
    return run(kernel, args, outs, mib=8, aliases=aliases, after=after)


def load_left(owns, others, place, left, stack):
    for refs, half in ((owns, place), (others, 1 - place)):
        at = 0
        for ref in refs:
            n = ref.shape[1]
            left[pl.ds(pl.multiple_of(half * HALF, HALF), HALF), at : at + n] = ref[...]
            at += n
    hi, lo = parts_of(left[...])
    stack[:RANK, :] = hi
    stack[RANK : 2 * RANK, :] = lo
    stack[2 * RANK :, :] = hi
    return lax.dot_general(
        left[...], left[...], NT, preferred_element_type=F32, precision=lax.Precision.HIGHEST
    )


def gate_right(run, owns, others, fixed, after=()):
    rows, cols = fixed.shape
    n_own, n_both = len(owns), len(owns) + len(others)

    def kernel(*refs):
        fixed, keep, give, gram, stack, left, right = refs[n_both:]
        gram[...] = load_left(refs[:n_own], refs[n_own:n_both], core_of(), left, stack)

        def step(i, _):
            both = jnp.dot(stack[: 2 * RANK], fixed[:, tile_at(i)], preferred_element_type=F32)
            right[:, tile_at(i)] = both[:RANK] + both[RANK:]
            return 0

        lax.fori_loop(0, cols // TILE, step, 0)
        halve(right, replica_of(), keep, [give])

    return run(
        kernel,
        [(x, VMEM) for x in (*owns, *others, fixed)],
        [((HALF, cols), F32, VMEM)] * 2 + [((RANK, RANK), F32, VMEM), ((3 * RANK, rows), BF16, VMEM)],
        [pltpu.VMEM((RANK, rows), F32), pltpu.VMEM((RANK, cols), F32)],
        mib=4,
        after=after,
    )


def down_right(run, owns, others, fixed, after=()):
    rows, cols = fixed.shape
    n_own, n_both = len(owns), len(owns) + len(others)
    cut, rest = in_two(rows)

    def kernel(*refs):
        fixed, keep, give_1, give_2, stack, left, right = refs[n_both:]
        gram = load_left(refs[:n_own], refs[n_own:n_both], replica_of(), left, stack)

        def step(i, _):
            both = lax.dot_general(stack[: 2 * RANK], fixed[tile_at(i), :], NT, preferred_element_type=F32)
            right[:, tile_at(i)] = both[:RANK] + both[RANK:]
            return 0

        lax.fori_loop(0, rows // TILE, step, 0)
        packed = jnp.concatenate([gram[:HALF], gram[HALF:]], axis=1)
        halve(right, core_of(), keep.at[:, :rows], [give_1, give_2.at[:, :rest]])
        keep[:, rows:] = packed
        give_2[:, rest:] = packed

    widths = (rows + 2 * RANK, cut, rest + 2 * RANK)
    return run(
        kernel,
        [(x, VMEM) for x in (*owns, *others, fixed)],
        [((HALF, n), F32, VMEM) for n in widths] + [((3 * RANK, cols), BF16, VMEM)],
        [pltpu.VMEM((RANK, cols), F32), pltpu.VMEM((RANK, rows), F32)],
        mib=4,
        after=after,
    )


def inverses(grams):
    row_at = lax.broadcasted_iota(jnp.int32, (RANK, RANK), 0)
    col_at = lax.broadcasted_iota(jnp.int32, (RANK, RANK), 1)
    lane = lax.broadcasted_iota(jnp.int32, (1, RANK), 1)

    def scaled(a):
        diagonal = jnp.where(row_at == col_at, a, 0.0)
        down = lax.rsqrt(jnp.sum(diagonal, axis=1, keepdims=True))
        across = lax.rsqrt(jnp.sum(diagonal, axis=0, keepdims=True))
        return a * down * across, down, across

    def sweep(a, k):
        one, two = (row_at == k, row_at == k + 1)
        here = one | two | (col_at == k) | (col_at == k + 1)
        col_1 = jnp.broadcast_to(a[:, k : k + 1], (RANK, RANK))
        col_2 = jnp.broadcast_to(a[:, k + 1 : k + 2], (RANK, RANK))
        p, q, r = col_1[k : k + 1], col_2[k : k + 1], col_2[k + 1 : k + 2]
        row_1 = jnp.where(lane == k, 1.0, jnp.where(lane == k + 1, 0.0, a[k : k + 1]))
        row_2 = jnp.where(lane == k + 1, 1.0, jnp.where(lane == k, 0.0, a[k + 1 : k + 2]))
        inv = 1.0 / (p * r - q * q)
        new_1 = (r * row_1 - q * row_2) * inv
        new_2 = (p * row_2 - q * row_1) * inv
        col_1 = jnp.where(one, -1.0, jnp.where(two, 0.0, col_1))
        col_2 = jnp.where(two, -1.0, jnp.where(one, 0.0, col_2))
        return jnp.where(here, 0.0, a) - col_1 * new_1 - col_2 * new_2

    systems = [scaled(a) for a in grams]
    values = [a for a, _, _ in systems]
    for k in range(0, RANK, 2):
        values = [sweep(a, k) for a in values]
    return [a * down * across for a, (_, down, across) in zip(values, systems)]


def stacked(refs, order, stack):
    at = 0
    for ref in refs:
        parts = parts_of(ref[...])
        n = ref.shape[0]
        for k, which in enumerate(order):
            stack[k * RANK + at : k * RANK + at + n, :] = parts[which]
        at += n


ROW_ORDER, COL_ORDER = (0, 1, 0, 1), (0, 0, 1, 1)


def turn(stack, turned):
    for i in range(0, stack.shape[1], TILE):
        turned[i : i + TILE, :] = stack[:, i : i + TILE].T


def gram_sums(run, packed, whole, after=()):
    n = len(packed)

    def kernel(*refs):
        a = sum((ref[...] for ref in refs[1:n]), refs[0][...])
        refs[-2][...] = jnp.concatenate([a[:, :RANK], a[:, RANK:]], axis=0)
        refs[-1][...] = sum((ref[...] for ref in refs[n + 1 : -2]), refs[n][...])

    outs = [((RANK, RANK), F32, VMEM)] * 2
    return run(kernel, [(x, VMEM) for x in (*packed, *whole)], outs, mib=2, after=after)


def solve(run, gram_down, left_down, gram_gate, left_gate, after=()):
    cols, rows = left_down.shape[1], left_gate.shape[1]

    def kernel(gram_down, left_down, gram_gate, left_gate, col_stack, row_turned, col, row, row_stack):
        grams = [gram_down[...], gram_gate[...]]
        for place, a, left, out in zip(
            (core_of(), replica_of()), inverses(grams), (left_down, left_gate), (col, row)
        ):
            other = jnp.concatenate([a[HALF:], a[:HALF]], axis=0)
            a = jnp.where(place == 0, a, other) * (1.0 / REPLICAS)
            hi, lo = parts_of(a)
            both = jnp.concatenate([hi, hi, lo], axis=1)
            out[...] = jnp.dot(both, left[...], preferred_element_type=F32)
        stacked([col], COL_ORDER, col_stack)
        stacked([row], ROW_ORDER, row_stack)
        turn(row_stack, row_turned)

    return run(
        kernel,
        [(x, VMEM) for x in (gram_down, left_down, gram_gate, left_gate)],
        [((4 * RANK, cols), BF16, VMEM), ((rows, 4 * RANK), BF16, VMEM)],
        [
            pltpu.VMEM((RANK, cols), F32),
            pltpu.VMEM((RANK, rows), F32),
            pltpu.VMEM((4 * RANK, rows), BF16),
        ],
        mib=6,
        after=after,
    )


def rebuild(run, row_turned, col_stack, owns, others, fixed, height, after=()):
    halves = [
        (x, half, sum(widths_of(xs[:i])))
        for half, xs in ((0, owns), (HALF, others))
        for i, x in enumerate(xs)
    ]
    rows, cols = fixed.shape
    tiles = rows // REPLICAS // height
    rows_late = row_turned is None
    scratch = [pltpu.VMEM((4 * RANK, rows if rows_late else cols), BF16)]
    if rows_late:
        scratch.append(pltpu.VMEM((rows, 4 * RANK), BF16))
    n_half = len(halves)

    def kernel(ready, *refs):
        fixed, new_error, update, done, late, *turned = refs[n_half:]
        done[...] = jnp.zeros_like(done)
        order = ROW_ORDER if rows_late else COL_ORDER
        for (_, at, left), ref in zip(halves, refs):
            parts = parts_of(ref[...])
            n, width = ref.shape
            for k, which in enumerate(order):
                late[k * RANK + at : k * RANK + at + n, left : left + width] = parts[which]
        row, col = ready, late
        if rows_late:
            row, col = turned[0], ready
            turn(late, row)
        replica = replica_of()
        mine, theirs = replica * tiles, (1 - replica) * tiles

        def tile_of(i):
            return jnp.where(i < tiles, mine + i, theirs + i - tiles)

        def step(e, u):
            i = pl.program_id(0)
            at = pl.ds(pl.multiple_of(tile_of(i) * height, height), height)

            def tile(with_update):
                row_here = row[at, :]
                for j in range(0, cols, TILE):
                    here = slice(j, j + TILE)
                    value = jnp.dot(row_here, col[:, here], preferred_element_type=F32)
                    e[:, here] = (fixed[at, here].astype(F32) - value).astype(BF16)
                    if with_update:
                        u[:, here] = value.astype(BF16)

            pl.when(i < tiles)(lambda: tile(True))
            pl.when(i >= tiles)(lambda: tile(False))

        block = (height, cols)
        pltpu.emit_pipeline(
            step,
            grid=(REPLICAS * tiles,),
            out_specs=[
                pl.BlockSpec(block, lambda i: (tile_of(i), 0)),
                pl.BlockSpec(block, lambda i: (jnp.minimum(i, tiles - 1), 0)),
            ],
        )(new_error, update)

    pieces = [x for x, _, _ in halves]
    return run(
        kernel,
        [(x, VMEM) for x in (col_stack if rows_late else row_turned, *pieces, fixed)],
        [((rows, cols), BF16, HBM), ((rows // REPLICAS, cols), BF16, HBM), ((8, 128), F32, VMEM)],
        scratch,
        mib=18,
        after=after,
    )


def local(grad_gate, grad_down, error_gate, error_down, start_gate, start_down):
    slab, width = grad_gate.shape
    n_dp, n_t = lax.axis_size("dp"), lax.axis_size("tensor")
    run = Calls()
    hops, steps = row_steps(), col_steps()
    tiles = slab // TILE

    _, fixed_down, keep, give = down_left(run, grad_down, error_down, start_down, 0, tiles)
    got = exchange(give, other_replica)
    gate_args = (run, grad_gate, error_gate, start_gate)
    first = gate_left(*gate_args, 0, tiles // 2, after=(keep,))
    (down,) = add(run, [keep], [got], after=(first[0],))
    got = exchange(down, steps[0])
    _, fixed_gate, keep_gate, *gives = gate_left(
        *gate_args, tiles // 2, tiles - tiles // 2, first, after=(down,)
    )
    (gate,) = add(run, [keep_gate], to_other_core(gives))
    got_gate = exchange(gate, hops[0])
    for i in range(len(steps)):
        (down,) = add(run, [down], [got], after=(gate,))
        if i + 1 < len(steps):
            got = exchange(down, steps[i + 1])
    other_down = exchange(down, other_replica)
    for hop in hops[1:]:
        (gate,) = add(run, [gate], [got_gate], after=(down,))
        got_gate = exchange(gate, hop)

    keep, *gives, left_down = down_right(run, [down], [other_down], fixed_down, after=(gate,))
    gots = to_other_core(gives)
    gates = add(run, [gate], [got_gate], in_two(slab), after=(keep,))
    others_gate = to_other_core(gates)
    down, gram_down = add(run, [keep], gots, [slab, 2 * RANK], after=(gates[0],))
    grams_down = [gram_down] + [
        exchange(gram_down, lambda d, t, b=b: (d, t ^ b)) for b in range(2, n_t, 2)
    ]
    got = exchange(down, hops[0])
    keep_gate, give_gate, gram_gate, left_gate = gate_right(
        run, gates, others_gate, fixed_gate, after=(down,)
    )
    got_gate = exchange(give_gate, other_replica)
    grams_gate = [gram_gate] + [
        exchange(gram_gate, lambda d, t, b=b: (d ^ b, t)) for b in range(REPLICAS, n_dp, REPLICAS)
    ]
    for hop in hops[1:]:
        (down,) = add(run, [down], [got], after=(gram_gate,))
        got = exchange(down, hop)
    gram_down, gram_gate = gram_sums(run, grams_down, grams_gate, after=(down,))
    (gate,) = add(run, [keep_gate], [got_gate], after=(gram_gate,))
    got_gate = exchange(gate, steps[0])
    col_stack, row_turned = solve(run, gram_down, left_down, gram_gate, left_gate, after=(gate,))
    downs = add(run, [down], [got], in_two(slab), after=(col_stack,))
    others_down = to_other_core(downs)
    for i in range(len(steps)):
        (gate,) = add(run, [gate], [got_gate], after=(downs[0],))
        if i + 1 < len(steps):
            got_gate = exchange(gate, steps[i + 1])
    other_gate = exchange(gate, other_replica)
    new_error_down, update_down, done = rebuild(
        run, None, col_stack, downs, others_down, fixed_down, slab // 4, after=(gate,)
    )
    new_error_gate, update_gate, _ = rebuild(
        run, row_turned, None, [gate], [other_gate], fixed_gate, slab // 4, after=(done,)
    )
    return (update_gate, update_down, new_error_gate, new_error_down)


def solution(mesh):
    split = P(("mix", "dp"), "tensor")
    in_specs = (split, split, split, split, P(None, "tensor"), P())
    out_specs = (split, split, split, split)

    def run(grad_gate, *rest):
        groups = mesh.shape["mix"] * mesh.shape["dp"]
        slab = grad_gate.shape[0] // groups
        width = grad_gate.shape[1] // mesh.shape["tensor"]
        fits = slab % (REPLICAS * TILE) == 0 and width % TILE == 0
        body = local if fits else local_plain
        return jax.shard_map(
            body, mesh=mesh, in_specs=in_specs, out_specs=out_specs, check_vma=False
        )(grad_gate, *rest)

    return run
```

```python
import functools

import jax
import jax.numpy as jnp
from jax import lax
from jax.experimental import pallas as pl
from jax.experimental.pallas import tpu as pltpu
from jax.sharding import PartitionSpec as P

REPLICAS = 2
RANK = 64
TILE = 256
FLOPS = 1.15e9
WEIGHTS = (8.0, 4.0, 1.0, 4.0, 0.1, 5.0, 1.0, 1.0, 0.1, 5.0, 0.1, 5.0, 0.1, 0.1, 5.0, 1.0, 1.0, 8.0, 8.0)
MIB = 1 << 20
BF16 = jnp.bfloat16
F32 = jnp.float32

NN = (((1,), (0,)), ((), ()))
NT = (((1,), (1,)), ((), ()))
TN = (((0,), (0,)), ((), ()))


def from_partner(shard, axis, stride):
    return lax.ppermute(shard, axis, [(i, i ^ 1 << stride) for i in range(lax.axis_size(axis))])


def corrected(grad, error):
    return (grad.astype(F32) + error.astype(F32)).astype(BF16)


def transposed(matrix, ortho):
    return lax.dot_general(matrix, ortho.astype(BF16), TN, preferred_element_type=F32)


def gram_of(left):
    return jnp.dot(left.T, left, precision=lax.Precision.HIGHEST)


def factored(left, inner):
    lower = jnp.linalg.cholesky(inner)
    return lax.linalg.triangular_solve(lower, left, left_side=False, lower=True, transpose_a=True)


def local_plain(grad_gate, grad_down, error_gate, error_down, start_gate, start_down):
    high = lax.Precision.HIGHEST
    dp_place = lax.axis_index("dp")
    block = dp_place // REPLICAS
    replica = dp_place % REPLICAS
    fixed_gate = corrected(grad_gate, error_gate)
    fixed_down = corrected(grad_down, error_down)
    slab = fixed_gate.shape[0]
    cols_down = lax.dynamic_slice_in_dim(start_down, block * slab, slab, 1)
    left_gate = lax.dot_general(fixed_gate, start_gate, NT, preferred_element_type=F32)
    left_down = lax.dot_general(
        fixed_down, cols_down, (((0,), (1,)), ((), ())), preferred_element_type=F32
    )
    left_gate = lax.psum(left_gate, "tensor")
    left_gate = left_gate + from_partner(left_gate, "dp", 0)
    left_down = lax.psum(left_down, "dp")
    keep_gate = (replica == 0).astype(F32)
    inner_gate = lax.psum(gram_of(left_gate) * keep_gate, "dp")
    inner_down = lax.psum(gram_of(left_down), "tensor")
    ortho_gate = factored(left_gate, inner_gate)
    ortho_down = factored(left_down, inner_down)
    right_gate = transposed(fixed_gate, ortho_gate)
    right_gate = lax.psum(right_gate, "dp") / REPLICAS
    right_down = jnp.dot(fixed_down, ortho_down.astype(BF16), preferred_element_type=F32)
    right_down = lax.psum(right_down, "tensor")
    right_down = right_down + from_partner(right_down, "dp", 0)
    right_down = right_down / REPLICAS
    rebuilt_gate = jnp.dot(ortho_gate, right_gate.T, precision=high)
    rebuilt_down = jnp.dot(right_down, ortho_down.T, precision=high)
    share = slab // REPLICAS
    update_gate = lax.dynamic_slice_in_dim(rebuilt_gate, replica * share, share, 0).astype(BF16)
    update_down = lax.dynamic_slice_in_dim(rebuilt_down, replica * share, share, 0).astype(BF16)
    new_error_gate = (fixed_gate.astype(F32) - rebuilt_gate).astype(BF16)
    new_error_down = (fixed_down.astype(F32) - rebuilt_down).astype(BF16)
    return (update_gate, update_down, new_error_gate, new_error_down)


def core_of():
    return lax.rem(lax.axis_index("tensor"), 2)


def replica_of():
    return lax.rem(lax.axis_index("dp"), REPLICAS)


def exchange(x, partner):
    n_dp, n_t = lax.axis_size("dp"), lax.axis_size("tensor")
    pairs = []
    for d in range(n_dp):
        for t in range(n_t):
            to_d, to_t = partner(d, t)
            pairs.append((d * n_t + t, to_d * n_t + to_t))
    return lax.ppermute(x, ("dp", "tensor"), pairs)


def bits(n, low):
    out, b = [], low
    while b < n:
        out.append(b)
        b *= 2
    return out


def row_steps():
    steps = [(0, b) for b in bits(lax.axis_size("tensor"), 2)] + [(1, 0)]

    def partner(i, d, t):
        r, b = steps[i] if t % 2 == 0 else steps[-1 - i]
        return d ^ r, t ^ b

    return [functools.partial(partner, i) for i in range(len(steps))]


def col_steps():
    return [lambda d, t, b=b: (d ^ b, t) for b in bits(lax.axis_size("dp"), REPLICAS)]


def other_core(d, t):
    return d, t ^ 1


def other_replica(d, t):
    return d ^ 1, t


def each(pieces, partner):
    return [exchange(x, partner) for x in pieces]


VMEM = pl.BlockSpec(memory_space=pltpu.VMEM)
HBM = pl.BlockSpec(memory_space=pltpu.HBM)
ANY = pl.BlockSpec(memory_space=pl.ANY)
HALF = RANK // 2


class Calls:
    def __init__(self):
        self.count = 0

    def __call__(self, kernel, args, outs, scratch=(), mib=8, aliases=None, after=()):
        n_in, n_after = len(args), len(after)
        operands = [
            pltpu.with_memory_space_constraint(x, pltpu.VMEM if spec is VMEM else pltpu.HBM)
            for x, spec in args
        ]

        def body(*refs):
            kernel(*refs[:n_in], *refs[n_in + n_after :])

        out = pl.pallas_call(
            body,
            out_shape=tuple(
                (pltpu.VMEM if spec is VMEM else pltpu.HBM)(shape, kind) for shape, kind, spec in outs
            ),
            in_specs=[spec for _, spec in args] + [ANY] * n_after,
            out_specs=tuple(spec for *_, spec in outs),
            scratch_shapes=list(scratch),
            input_output_aliases=aliases or {},
            compiler_params=pltpu.CompilerParams(vmem_limit_bytes=mib * MIB),
            cost_estimate=pl.CostEstimate(
                flops=int(WEIGHTS[self.count] * FLOPS), bytes_accessed=1 << 10, transcendentals=0
            ),
        )(*operands, *after)
        self.count += 1
        return out


def parts_of(x):
    hi = x.astype(BF16)
    lo = (x - hi.astype(F32)).astype(BF16)
    return hi, lo


def spans(*widths):
    edges = sorted({sum(w[:i]) for w in widths for i in range(len(w) + 1)})
    for low, high in zip(edges, edges[1:]):
        places = []
        for w in widths:
            k = max(i for i in range(len(w)) if sum(w[:i]) <= low)
            places.append((k, low - sum(w[:k]), high - sum(w[:k])))
        yield places


def widths_of(refs):
    return [ref.shape[1] for ref in refs]


def add(run, xs, ys, widths=None, after=()):
    widths = widths or widths_of(xs)
    n_x, n_y = len(xs), len(ys)

    def kernel(*refs):
        x, y, out = refs[:n_x], refs[n_x : n_x + n_y], refs[n_x + n_y :]
        for (i, i0, i1), (j, j0, j1), (k, k0, k1) in spans(widths_of(x), widths_of(y), widths):
            out[k][:, k0:k1] = x[i][:, i0:i1] + y[j][:, j0:j1]

    outs = [((HALF, n), F32, VMEM) for n in widths]
    return list(run(kernel, [(x, VMEM) for x in (*xs, *ys)], outs, mib=2, after=after))


def in_two(width):
    cut = width // 256 * 128
    return [cut, width - cut]


def halve(whole, place, keep, gives):
    keep[...] = whole[pl.ds(pl.multiple_of(place * HALF, HALF), HALF), :]
    at = 0
    for give in gives:
        n = give.shape[1]
        give[...] = whole[pl.ds(pl.multiple_of((1 - place) * HALF, HALF), HALF), at : at + n]
        at += n


def tile_at(i):
    return pl.ds(pl.multiple_of(i * TILE, TILE), TILE)


def gate_left(run, grad, error, start, first, count, before=None, after=()):
    rows, cols = grad.shape
    last = (first + count) * TILE == rows

    def kernel(grad, error, start, *refs):
        if before is not None:
            refs = refs[2:]
        left, fixed = refs[:2]

        def step(g, e):
            at = tile_at(first + pl.program_id(0))
            term = jnp.zeros((RANK, TILE), F32)
            for j in range(0, cols, TILE):
                here = slice(j, j + TILE)
                c = g[:, here] + e[:, here]
                fixed[at, here] = c
                term += lax.dot_general(start[:, here], c, NT, preferred_element_type=F32)
            left[:, at] = term

        spec = pl.BlockSpec((TILE, cols), lambda i: (first + i, 0), pipeline_mode=pl.Buffered(3))
        pltpu.emit_pipeline(step, grid=(count,), in_specs=[spec, spec])(grad, error)
        if last:
            halve(left, core_of(), refs[2], refs[3:])

    args = [(grad, HBM), (error, HBM), (start, VMEM)]
    outs = [((RANK, rows), F32, VMEM), ((rows, cols), BF16, VMEM)]
    if last:
        outs += [((HALF, n), F32, VMEM) for n in (rows, *in_two(rows))]
    aliases = None
    if before is not None:
        args += [(x, VMEM) for x in before]
        aliases = {3: 0, 4: 1}
    return run(kernel, args, outs, mib=8, aliases=aliases, after=after)


def down_left(run, grad, error, start, first, count, before=None, after=()):
    rows, cols = grad.shape
    last = (first + count) * TILE == rows

    def kernel(grad, error, start, *refs):
        if before is not None:
            refs = refs[2:]
        left, fixed = refs[:2]
        block = lax.div(lax.axis_index("dp"), REPLICAS) * (rows // TILE) + first
        if before is None:
            left[...] = jnp.zeros_like(left)

        def step(g, e, s):
            at = tile_at(first + pl.program_id(0))
            for j in range(0, cols, TILE):
                here = slice(j, j + TILE)
                c = g[:, here] + e[:, here]
                fixed[at, here] = c
                left[:, here] += jnp.dot(s[...], c, preferred_element_type=F32)

        spec = pl.BlockSpec((TILE, cols), lambda i: (first + i, 0), pipeline_mode=pl.Buffered(3))
        part = pl.BlockSpec((RANK, TILE), lambda i: (0, block + i))
        pltpu.emit_pipeline(step, grid=(count,), in_specs=[spec, spec, part])(grad, error, start)
        if last:
            halve(left, replica_of(), refs[2], refs[3:])

    args = [(grad, HBM), (error, HBM), (start, HBM)]
    outs = [((RANK, cols), F32, VMEM), ((rows, cols), BF16, VMEM)]
    if last:
        outs += [((HALF, cols), F32, VMEM)] * 2
    aliases = None
    if before is not None:
        args += [(x, VMEM) for x in before]
        aliases = {3: 0, 4: 1}
    return run(kernel, args, outs, mib=8, aliases=aliases, after=after)


def load_left(owns, others, place, left, stack):
    for refs, half in ((owns, place), (others, 1 - place)):
        at = 0
        for ref in refs:
            n = ref.shape[1]
            left[pl.ds(pl.multiple_of(half * HALF, HALF), HALF), at : at + n] = ref[...]
            at += n
    hi, lo = parts_of(left[...])
    stack[:RANK, :] = hi
    stack[RANK : 2 * RANK, :] = lo
    stack[2 * RANK :, :] = hi
    return lax.dot_general(
        left[...], left[...], NT, preferred_element_type=F32, precision=lax.Precision.HIGHEST
    )


def gate_right(run, owns, others, fixed, after=()):
    rows, cols = fixed.shape
    n_own, n_both = len(owns), len(owns) + len(others)

    def kernel(*refs):
        fixed, keep, give, gram, stack, left, right = refs[n_both:]
        gram[...] = load_left(refs[:n_own], refs[n_own:n_both], core_of(), left, stack)

        def step(i, _):
            both = jnp.dot(stack[: 2 * RANK], fixed[:, tile_at(i)], preferred_element_type=F32)
            right[:, tile_at(i)] = both[:RANK] + both[RANK:]
            return 0

        lax.fori_loop(0, cols // TILE, step, 0)
        halve(right, replica_of(), keep, [give])

    return run(
        kernel,
        [(x, VMEM) for x in (*owns, *others, fixed)],
        [((HALF, cols), F32, VMEM)] * 2 + [((RANK, RANK), F32, VMEM), ((3 * RANK, rows), BF16, VMEM)],
        [pltpu.VMEM((RANK, rows), F32), pltpu.VMEM((RANK, cols), F32)],
        mib=4,
        after=after,
    )


def down_right(run, owns, others, fixed, after=()):
    rows, cols = fixed.shape
    n_own, n_both = len(owns), len(owns) + len(others)
    cut, rest = in_two(rows)

    def kernel(*refs):
        fixed, keep, give_1, give_2, stack, left, right = refs[n_both:]
        gram = load_left(refs[:n_own], refs[n_own:n_both], replica_of(), left, stack)

        def step(i, _):
            both = lax.dot_general(stack[: 2 * RANK], fixed[tile_at(i), :], NT, preferred_element_type=F32)
            right[:, tile_at(i)] = both[:RANK] + both[RANK:]
            return 0

        lax.fori_loop(0, rows // TILE, step, 0)
        packed = jnp.concatenate([gram[:HALF], gram[HALF:]], axis=1)
        halve(right, core_of(), keep.at[:, :rows], [give_1, give_2.at[:, :rest]])
        keep[:, rows:] = packed
        give_2[:, rest:] = packed

    widths = (rows + 2 * RANK, cut, rest + 2 * RANK)
    return run(
        kernel,
        [(x, VMEM) for x in (*owns, *others, fixed)],
        [((HALF, n), F32, VMEM) for n in widths] + [((3 * RANK, cols), BF16, VMEM)],
        [pltpu.VMEM((RANK, cols), F32), pltpu.VMEM((RANK, rows), F32)],
        mib=4,
        after=after,
    )


def inverses(grams):
    row_at = lax.broadcasted_iota(jnp.int32, (RANK, RANK), 0)
    col_at = lax.broadcasted_iota(jnp.int32, (RANK, RANK), 1)
    lane = lax.broadcasted_iota(jnp.int32, (1, RANK), 1)

    def scaled(a):
        diagonal = jnp.where(row_at == col_at, a, 0.0)
        down = lax.rsqrt(jnp.sum(diagonal, axis=1, keepdims=True))
        across = lax.rsqrt(jnp.sum(diagonal, axis=0, keepdims=True))
        return a * down * across, down, across

    def sweep(a, k):
        one, two = (row_at == k, row_at == k + 1)
        here = one | two | (col_at == k) | (col_at == k + 1)
        col_1 = jnp.broadcast_to(a[:, k : k + 1], (RANK, RANK))
        col_2 = jnp.broadcast_to(a[:, k + 1 : k + 2], (RANK, RANK))
        p, q, r = col_1[k : k + 1], col_2[k : k + 1], col_2[k + 1 : k + 2]
        row_1 = jnp.where(lane == k, 1.0, jnp.where(lane == k + 1, 0.0, a[k : k + 1]))
        row_2 = jnp.where(lane == k + 1, 1.0, jnp.where(lane == k, 0.0, a[k + 1 : k + 2]))
        inv = 1.0 / (p * r - q * q)
        new_1 = (r * row_1 - q * row_2) * inv
        new_2 = (p * row_2 - q * row_1) * inv
        col_1 = jnp.where(one, -1.0, jnp.where(two, 0.0, col_1))
        col_2 = jnp.where(two, -1.0, jnp.where(one, 0.0, col_2))
        return jnp.where(here, 0.0, a) - col_1 * new_1 - col_2 * new_2

    systems = [scaled(a) for a in grams]
    values = [a for a, _, _ in systems]
    for k in range(0, RANK, 2):
        values = [sweep(a, k) for a in values]
    return [a * down * across for a, (_, down, across) in zip(values, systems)]


def stacked(refs, order, stack):
    at = 0
    for ref in refs:
        parts = parts_of(ref[...])
        n = ref.shape[0]
        for k, which in enumerate(order):
            stack[k * RANK + at : k * RANK + at + n, :] = parts[which]
        at += n


ROW_ORDER, COL_ORDER = (0, 1, 0, 1), (0, 0, 1, 1)


def turn(stack, turned):
    for i in range(0, stack.shape[1], TILE):
        turned[i : i + TILE, :] = stack[:, i : i + TILE].T


def gram_sums(run, packed, whole, after=()):
    n = len(packed)

    def kernel(*refs):
        a = sum((ref[...] for ref in refs[1:n]), refs[0][...])
        refs[-2][...] = jnp.concatenate([a[:, :RANK], a[:, RANK:]], axis=0)
        refs[-1][...] = sum((ref[...] for ref in refs[n + 1 : -2]), refs[n][...])

    outs = [((RANK, RANK), F32, VMEM)] * 2
    return run(kernel, [(x, VMEM) for x in (*packed, *whole)], outs, mib=2, after=after)


def solve(run, gram_down, left_down, gram_gate, left_gate, after=()):
    cols, rows = left_down.shape[1], left_gate.shape[1]

    def kernel(gram_down, left_down, gram_gate, left_gate, col_stack, row_turned, col, row, row_stack):
        grams = [gram_down[...], gram_gate[...]]
        for place, a, left, out in zip(
            (core_of(), replica_of()), inverses(grams), (left_down, left_gate), (col, row)
        ):
            other = jnp.concatenate([a[HALF:], a[:HALF]], axis=0)
            a = jnp.where(place == 0, a, other) * (1.0 / REPLICAS)
            hi, lo = parts_of(a)
            both = jnp.concatenate([hi, hi, lo], axis=1)
            out[...] = jnp.dot(both, left[...], preferred_element_type=F32)
        stacked([col], COL_ORDER, col_stack)
        stacked([row], ROW_ORDER, row_stack)
        turn(row_stack, row_turned)

    return run(
        kernel,
        [(x, VMEM) for x in (gram_down, left_down, gram_gate, left_gate)],
        [((4 * RANK, cols), BF16, VMEM), ((rows, 4 * RANK), BF16, VMEM)],
        [
            pltpu.VMEM((RANK, cols), F32),
            pltpu.VMEM((RANK, rows), F32),
            pltpu.VMEM((4 * RANK, rows), BF16),
        ],
        mib=6,
        after=after,
    )


def rebuild(run, row_turned, col_stack, owns, others, fixed, height, after=()):
    halves = [
        (x, half, sum(widths_of(xs[:i])))
        for half, xs in ((0, owns), (HALF, others))
        for i, x in enumerate(xs)
    ]
    rows, cols = fixed.shape
    tiles = rows // REPLICAS // height
    rows_late = row_turned is None
    scratch = [pltpu.VMEM((4 * RANK, rows if rows_late else cols), BF16)]
    if rows_late:
        scratch.append(pltpu.VMEM((rows, 4 * RANK), BF16))
    n_half = len(halves)

    def kernel(ready, *refs):
        fixed, new_error, update, done, late, *turned = refs[n_half:]
        done[...] = jnp.zeros_like(done)
        order = ROW_ORDER if rows_late else COL_ORDER
        for (_, at, left), ref in zip(halves, refs):
            parts = parts_of(ref[...])
            n, width = ref.shape
            for k, which in enumerate(order):
                late[k * RANK + at : k * RANK + at + n, left : left + width] = parts[which]
        row, col = ready, late
        if rows_late:
            row, col = turned[0], ready
            turn(late, row)
        replica = replica_of()
        mine, theirs = replica * tiles, (1 - replica) * tiles

        def tile_of(i):
            return jnp.where(i < tiles, mine + i, theirs + i - tiles)

        def step(e, u):
            i = pl.program_id(0)
            at = pl.ds(pl.multiple_of(tile_of(i) * height, height), height)

            def tile(with_update):
                row_here = row[at, :]
                for j in range(0, cols, TILE):
                    here = slice(j, j + TILE)
                    value = jnp.dot(row_here, col[:, here], preferred_element_type=F32)
                    e[:, here] = (fixed[at, here].astype(F32) - value).astype(BF16)
                    if with_update:
                        u[:, here] = value.astype(BF16)

            pl.when(i < tiles)(lambda: tile(True))
            pl.when(i >= tiles)(lambda: tile(False))

        block = (height, cols)
        pltpu.emit_pipeline(
            step,
            grid=(REPLICAS * tiles,),
            out_specs=[
                pl.BlockSpec(block, lambda i: (tile_of(i), 0)),
                pl.BlockSpec(block, lambda i: (jnp.minimum(i, tiles - 1), 0)),
            ],
        )(new_error, update)

    pieces = [x for x, _, _ in halves]
    return run(
        kernel,
        [(x, VMEM) for x in (col_stack if rows_late else row_turned, *pieces, fixed)],
        [((rows, cols), BF16, HBM), ((rows // REPLICAS, cols), BF16, HBM), ((8, 128), F32, VMEM)],
        scratch,
        mib=18,
        after=after,
    )


def local(grad_gate, grad_down, error_gate, error_down, start_gate, start_down):
    slab, width = grad_gate.shape
    n_dp, n_t = lax.axis_size("dp"), lax.axis_size("tensor")
    run = Calls()
    hops, steps = row_steps(), col_steps()
    tiles = slab // TILE

    _, fixed_down, keep, give = down_left(run, grad_down, error_down, start_down, 0, tiles)
    got = exchange(give, other_replica)
    gate_args = (run, grad_gate, error_gate, start_gate)
    cut = tiles * 3 // 5
    first = gate_left(*gate_args, 0, cut, after=(keep,))
    (down,) = add(run, [keep], [got], after=(first[0],))
    got = exchange(down, steps[0])
    _, fixed_gate, keep_gate, *gives = gate_left(
        *gate_args, cut, tiles - cut, first, after=(down,)
    )
    gate = add(run, [keep_gate], each(gives, other_core), in_two(slab))
    gots_gate = each(gate, hops[0])
    for i in range(len(steps)):
        (down,) = add(run, [down], [got], after=(gate[0],))
        if i + 1 < len(steps):
            got = exchange(down, steps[i + 1])
    other_down = exchange(down, other_replica)
    for hop in hops[1:]:
        gate = add(run, gate, gots_gate, after=(down,))
        gots_gate = each(gate, hop)
    gate = add(run, gate, gots_gate)
    others_gate = each(gate, other_core)

    keep_gate, give, gram_gate, left_gate = gate_right(run, gate, others_gate, fixed_gate)
    got_gate = exchange(give, other_replica)
    grams_gate = [gram_gate] + [
        exchange(gram_gate, lambda d, t, b=b: (d ^ b, t)) for b in range(REPLICAS, n_dp, REPLICAS)
    ]
    keep, *gives, left_down = down_right(
        run, [down], [other_down], fixed_down, after=(gram_gate,)
    )
    *down, gram_down = add(run, [keep], each(gives, other_core), [*in_two(slab), 2 * RANK])
    grams_down = [gram_down] + [
        exchange(gram_down, lambda d, t, b=b: (d, t ^ b)) for b in range(2, n_t, 2)
    ]
    gots = each(down, hops[0])
    (gate,) = add(run, [keep_gate], [got_gate], after=(gram_down,))
    got_gate = exchange(gate, steps[0])
    for hop in hops[1:]:
        down = add(run, down, gots, after=(gate,))
        gots = each(down, hop)
    gram_down, gram_gate = gram_sums(run, grams_down, grams_gate, after=(down[0],))
    col_stack, row_turned = solve(run, gram_down, left_down, gram_gate, left_gate)
    down = add(run, down, gots, after=(col_stack,))
    others_down = each(down, other_core)
    for i in range(len(steps)):
        (gate,) = add(run, [gate], [got_gate], after=(down[0],))
        if i + 1 < len(steps):
            got_gate = exchange(gate, steps[i + 1])
    other_gate = exchange(gate, other_replica)
    new_error_down, update_down, done = rebuild(
        run, None, col_stack, down, others_down, fixed_down, slab // 4, after=(gate,)
    )
    new_error_gate, update_gate, _ = rebuild(
        run, row_turned, None, [gate], [other_gate], fixed_gate, slab // 4, after=(done,)
    )
    return (update_gate, update_down, new_error_gate, new_error_down)


def solution(mesh):
    split = P(("mix", "dp"), "tensor")
    in_specs = (split, split, split, split, P(None, "tensor"), P())
    out_specs = (split, split, split, split)

    def run(grad_gate, *rest):
        groups = mesh.shape["mix"] * mesh.shape["dp"]
        slab = grad_gate.shape[0] // groups
        width = grad_gate.shape[1] // mesh.shape["tensor"]
        fits = slab % (REPLICAS * TILE) == 0 and width % TILE == 0
        body = local if fits else local_plain
        return jax.shard_map(
            body, mesh=mesh, in_specs=in_specs, out_specs=out_specs, check_vma=False
        )(grad_gate, *rest)

    return run
```

```python
import functools

import jax
import jax.numpy as jnp
from jax import lax
from jax.experimental import pallas as pl
from jax.experimental.pallas import tpu as pltpu
from jax.sharding import PartitionSpec as P

REPLICAS = 2
RANK = 64
TILE = 256
FLOPS = 1.15e9
WEIGHTS = (8.0, 4.0, 1.0, 4.0, 0.1, 5.0, 1.0, 5.0, 1.0, 1.0, 4.0, 0.1, 0.1, 1.0, 5.0, 1.0, 0.1, 1.0, 4.0, 4.0, 4.0)
MIB = 1 << 20
BF16 = jnp.bfloat16
F32 = jnp.float32

NN = (((1,), (0,)), ((), ()))
NT = (((1,), (1,)), ((), ()))
TN = (((0,), (0,)), ((), ()))


def from_partner(shard, axis, stride):
    return lax.ppermute(shard, axis, [(i, i ^ 1 << stride) for i in range(lax.axis_size(axis))])


def corrected(grad, error):
    return (grad.astype(F32) + error.astype(F32)).astype(BF16)


def transposed(matrix, ortho):
    return lax.dot_general(matrix, ortho.astype(BF16), TN, preferred_element_type=F32)


def gram_of(left):
    return jnp.dot(left.T, left, precision=lax.Precision.HIGHEST)


def factored(left, inner):
    lower = jnp.linalg.cholesky(inner)
    return lax.linalg.triangular_solve(lower, left, left_side=False, lower=True, transpose_a=True)


def local_plain(grad_gate, grad_down, error_gate, error_down, start_gate, start_down):
    high = lax.Precision.HIGHEST
    dp_place = lax.axis_index("dp")
    block = dp_place // REPLICAS
    replica = dp_place % REPLICAS
    fixed_gate = corrected(grad_gate, error_gate)
    fixed_down = corrected(grad_down, error_down)
    slab = fixed_gate.shape[0]
    cols_down = lax.dynamic_slice_in_dim(start_down, block * slab, slab, 1)
    left_gate = lax.dot_general(fixed_gate, start_gate, NT, preferred_element_type=F32)
    left_down = lax.dot_general(
        fixed_down, cols_down, (((0,), (1,)), ((), ())), preferred_element_type=F32
    )
    left_gate = lax.psum(left_gate, "tensor")
    left_gate = left_gate + from_partner(left_gate, "dp", 0)
    left_down = lax.psum(left_down, "dp")
    keep_gate = (replica == 0).astype(F32)
    inner_gate = lax.psum(gram_of(left_gate) * keep_gate, "dp")
    inner_down = lax.psum(gram_of(left_down), "tensor")
    ortho_gate = factored(left_gate, inner_gate)
    ortho_down = factored(left_down, inner_down)
    right_gate = transposed(fixed_gate, ortho_gate)
    right_gate = lax.psum(right_gate, "dp") / REPLICAS
    right_down = jnp.dot(fixed_down, ortho_down.astype(BF16), preferred_element_type=F32)
    right_down = lax.psum(right_down, "tensor")
    right_down = right_down + from_partner(right_down, "dp", 0)
    right_down = right_down / REPLICAS
    rebuilt_gate = jnp.dot(ortho_gate, right_gate.T, precision=high)
    rebuilt_down = jnp.dot(right_down, ortho_down.T, precision=high)
    share = slab // REPLICAS
    update_gate = lax.dynamic_slice_in_dim(rebuilt_gate, replica * share, share, 0).astype(BF16)
    update_down = lax.dynamic_slice_in_dim(rebuilt_down, replica * share, share, 0).astype(BF16)
    new_error_gate = (fixed_gate.astype(F32) - rebuilt_gate).astype(BF16)
    new_error_down = (fixed_down.astype(F32) - rebuilt_down).astype(BF16)
    return (update_gate, update_down, new_error_gate, new_error_down)


def core_of():
    return lax.rem(lax.axis_index("tensor"), 2)


def replica_of():
    return lax.rem(lax.axis_index("dp"), REPLICAS)


def exchange(x, partner):
    n_dp, n_t = lax.axis_size("dp"), lax.axis_size("tensor")
    pairs = []
    for d in range(n_dp):
        for t in range(n_t):
            to_d, to_t = partner(d, t)
            pairs.append((d * n_t + t, to_d * n_t + to_t))
    return lax.ppermute(x, ("dp", "tensor"), pairs)


def bits(n, low):
    out, b = [], low
    while b < n:
        out.append(b)
        b *= 2
    return out


def row_steps():
    steps = [(0, b) for b in bits(lax.axis_size("tensor"), 2)] + [(1, 0)]

    def partner(i, d, t):
        r, b = steps[i] if t % 2 == 0 else steps[-1 - i]
        return d ^ r, t ^ b

    return [functools.partial(partner, i) for i in range(len(steps))]


def col_steps():
    return [lambda d, t, b=b: (d ^ b, t) for b in bits(lax.axis_size("dp"), REPLICAS)]


def other_core(d, t):
    return d, t ^ 1


def other_replica(d, t):
    return d ^ 1, t


def to_other_core(pieces):
    return [exchange(x, other_core) for x in pieces]


VMEM = pl.BlockSpec(memory_space=pltpu.VMEM)
HBM = pl.BlockSpec(memory_space=pltpu.HBM)
ANY = pl.BlockSpec(memory_space=pl.ANY)
HALF = RANK // 2


class Calls:
    def __init__(self):
        self.count = 0

    def __call__(self, kernel, args, outs, scratch=(), mib=8, aliases=None, after=()):
        n_in, n_after = len(args), len(after)
        operands = [
            pltpu.with_memory_space_constraint(x, pltpu.VMEM if spec is VMEM else pltpu.HBM)
            for x, spec in args
        ]

        def body(*refs):
            kernel(*refs[:n_in], *refs[n_in + n_after :])

        out = pl.pallas_call(
            body,
            out_shape=tuple(
                (pltpu.VMEM if spec is VMEM else pltpu.HBM)(shape, kind) for shape, kind, spec in outs
            ),
            in_specs=[spec for _, spec in args] + [ANY] * n_after,
            out_specs=tuple(spec for *_, spec in outs),
            scratch_shapes=list(scratch),
            input_output_aliases=aliases or {},
            compiler_params=pltpu.CompilerParams(vmem_limit_bytes=mib * MIB),
            cost_estimate=pl.CostEstimate(
                flops=int(WEIGHTS[self.count] * FLOPS), bytes_accessed=1 << 10, transcendentals=0
            ),
        )(*operands, *after)
        self.count += 1
        return out


def parts_of(x):
    hi = x.astype(BF16)
    lo = (x - hi.astype(F32)).astype(BF16)
    return hi, lo


def spans(*widths):
    edges = sorted({sum(w[:i]) for w in widths for i in range(len(w) + 1)})
    for low, high in zip(edges, edges[1:]):
        places = []
        for w in widths:
            k = max(i for i in range(len(w)) if sum(w[:i]) <= low)
            places.append((k, low - sum(w[:k]), high - sum(w[:k])))
        yield places


def widths_of(refs):
    return [ref.shape[1] for ref in refs]


def add(run, xs, ys, widths=None, after=()):
    widths = widths or widths_of(xs)
    n_x, n_y = len(xs), len(ys)

    def kernel(*refs):
        x, y, out = refs[:n_x], refs[n_x : n_x + n_y], refs[n_x + n_y :]
        for (i, i0, i1), (j, j0, j1), (k, k0, k1) in spans(widths_of(x), widths_of(y), widths):
            out[k][:, k0:k1] = x[i][:, i0:i1] + y[j][:, j0:j1]

    outs = [((HALF, n), F32, VMEM) for n in widths]
    return list(run(kernel, [(x, VMEM) for x in (*xs, *ys)], outs, mib=2, after=after))


def in_two(width):
    cut = width // 256 * 128
    return [cut, width - cut]


def halve(whole, place, keep, gives):
    keep[...] = whole[pl.ds(pl.multiple_of(place * HALF, HALF), HALF), :]
    at = 0
    for give in gives:
        n = give.shape[1]
        give[...] = whole[pl.ds(pl.multiple_of((1 - place) * HALF, HALF), HALF), at : at + n]
        at += n


def tile_at(i):
    return pl.ds(pl.multiple_of(i * TILE, TILE), TILE)


def gate_left(run, grad, error, start, first, count, before=None, after=()):
    rows, cols = grad.shape
    last = (first + count) * TILE == rows

    def kernel(grad, error, start, *refs):
        if before is not None:
            refs = refs[2:]
        left, fixed = refs[:2]

        def step(g, e):
            at = tile_at(first + pl.program_id(0))
            term = jnp.zeros((RANK, TILE), F32)
            for j in range(0, cols, TILE):
                here = slice(j, j + TILE)
                c = g[:, here] + e[:, here]
                fixed[at, here] = c
                term += lax.dot_general(start[:, here], c, NT, preferred_element_type=F32)
            left[:, at] = term

        spec = pl.BlockSpec((TILE, cols), lambda i: (first + i, 0), pipeline_mode=pl.Buffered(3))
        pltpu.emit_pipeline(step, grid=(count,), in_specs=[spec, spec])(grad, error)
        if last:
            halve(left, core_of(), refs[2], refs[3:])

    args = [(grad, HBM), (error, HBM), (start, VMEM)]
    outs = [((RANK, rows), F32, VMEM), ((rows, cols), BF16, VMEM)]
    if last:
        outs += [((HALF, n), F32, VMEM) for n in (rows, *in_two(rows))]
    aliases = None
    if before is not None:
        args += [(x, VMEM) for x in before]
        aliases = {3: 0, 4: 1}
    return run(kernel, args, outs, mib=8, aliases=aliases, after=after)


def down_left(run, grad, error, start, first, count, before=None, after=()):
    rows, cols = grad.shape
    last = (first + count) * TILE == rows

    def kernel(grad, error, start, *refs):
        if before is not None:
            refs = refs[2:]
        left, fixed = refs[:2]
        block = lax.div(lax.axis_index("dp"), REPLICAS) * (rows // TILE) + first
        if before is None:
            left[...] = jnp.zeros_like(left)

        def step(g, e, s):
            at = tile_at(first + pl.program_id(0))
            for j in range(0, cols, TILE):
                here = slice(j, j + TILE)
                c = g[:, here] + e[:, here]
                fixed[at, here] = c
                left[:, here] += jnp.dot(s[...], c, preferred_element_type=F32)

        spec = pl.BlockSpec((TILE, cols), lambda i: (first + i, 0), pipeline_mode=pl.Buffered(3))
        part = pl.BlockSpec((RANK, TILE), lambda i: (0, block + i))
        pltpu.emit_pipeline(step, grid=(count,), in_specs=[spec, spec, part])(grad, error, start)
        if last:
            halve(left, replica_of(), refs[2], refs[3:])

    args = [(grad, HBM), (error, HBM), (start, HBM)]
    outs = [((RANK, cols), F32, VMEM), ((rows, cols), BF16, VMEM)]
    if last:
        outs += [((HALF, cols), F32, VMEM)] * 2
    aliases = None
    if before is not None:
        args += [(x, VMEM) for x in before]
        aliases = {3: 0, 4: 1}
    return run(kernel, args, outs, mib=8, aliases=aliases, after=after)


def load_left(owns, others, place, left, stack):
    for refs, half in ((owns, place), (others, 1 - place)):
        at = 0
        for ref in refs:
            n = ref.shape[1]
            left[pl.ds(pl.multiple_of(half * HALF, HALF), HALF), at : at + n] = ref[...]
            at += n
    hi, lo = parts_of(left[...])
    stack[:RANK, :] = hi
    stack[RANK : 2 * RANK, :] = lo
    stack[2 * RANK :, :] = hi
    return lax.dot_general(
        left[...], left[...], NT, preferred_element_type=F32, precision=lax.Precision.HIGHEST
    )


def gate_right(run, owns, others, fixed, after=()):
    rows, cols = fixed.shape
    n_own, n_both = len(owns), len(owns) + len(others)

    def kernel(*refs):
        fixed, keep, give, gram, stack, left, right = refs[n_both:]
        gram[...] = load_left(refs[:n_own], refs[n_own:n_both], core_of(), left, stack)

        def step(i, _):
            both = jnp.dot(stack[: 2 * RANK], fixed[:, tile_at(i)], preferred_element_type=F32)
            right[:, tile_at(i)] = both[:RANK] + both[RANK:]
            return 0

        lax.fori_loop(0, cols // TILE, step, 0)
        halve(right, replica_of(), keep, [give])

    return run(
        kernel,
        [(x, VMEM) for x in (*owns, *others, fixed)],
        [((HALF, cols), F32, VMEM)] * 2 + [((RANK, RANK), F32, VMEM), ((3 * RANK, rows), BF16, VMEM)],
        [pltpu.VMEM((RANK, rows), F32), pltpu.VMEM((RANK, cols), F32)],
        mib=4,
        after=after,
    )


def down_right(run, owns, others, fixed, after=()):
    rows, cols = fixed.shape
    n_own, n_both = len(owns), len(owns) + len(others)
    cut, rest = in_two(rows)

    def kernel(*refs):
        fixed, keep, give_1, give_2, stack, left, right = refs[n_both:]
        gram = load_left(refs[:n_own], refs[n_own:n_both], replica_of(), left, stack)

        def step(i, _):
            both = lax.dot_general(stack[: 2 * RANK], fixed[tile_at(i), :], NT, preferred_element_type=F32)
            right[:, tile_at(i)] = both[:RANK] + both[RANK:]
            return 0

        lax.fori_loop(0, rows // TILE, step, 0)
        packed = jnp.concatenate([gram[:HALF], gram[HALF:]], axis=1)
        halve(right, core_of(), keep.at[:, :rows], [give_1, give_2.at[:, :rest]])
        keep[:, rows:] = packed
        give_2[:, rest:] = packed

    widths = (rows + 2 * RANK, cut, rest + 2 * RANK)
    return run(
        kernel,
        [(x, VMEM) for x in (*owns, *others, fixed)],
        [((HALF, n), F32, VMEM) for n in widths] + [((3 * RANK, cols), BF16, VMEM)],
        [pltpu.VMEM((RANK, cols), F32), pltpu.VMEM((RANK, rows), F32)],
        mib=4,
        after=after,
    )


def inverses(grams):
    row_at = lax.broadcasted_iota(jnp.int32, (RANK, RANK), 0)
    col_at = lax.broadcasted_iota(jnp.int32, (RANK, RANK), 1)
    lane = lax.broadcasted_iota(jnp.int32, (1, RANK), 1)

    def scaled(a):
        diagonal = jnp.where(row_at == col_at, a, 0.0)
        down = lax.rsqrt(jnp.sum(diagonal, axis=1, keepdims=True))
        across = lax.rsqrt(jnp.sum(diagonal, axis=0, keepdims=True))
        return a * down * across, down, across

    def sweep(a, k):
        one, two = (row_at == k, row_at == k + 1)
        here = one | two | (col_at == k) | (col_at == k + 1)
        col_1 = jnp.broadcast_to(a[:, k : k + 1], (RANK, RANK))
        col_2 = jnp.broadcast_to(a[:, k + 1 : k + 2], (RANK, RANK))
        p, q, r = col_1[k : k + 1], col_2[k : k + 1], col_2[k + 1 : k + 2]
        row_1 = jnp.where(lane == k, 1.0, jnp.where(lane == k + 1, 0.0, a[k : k + 1]))
        row_2 = jnp.where(lane == k + 1, 1.0, jnp.where(lane == k, 0.0, a[k + 1 : k + 2]))
        inv = 1.0 / (p * r - q * q)
        new_1 = (r * row_1 - q * row_2) * inv
        new_2 = (p * row_2 - q * row_1) * inv
        col_1 = jnp.where(one, -1.0, jnp.where(two, 0.0, col_1))
        col_2 = jnp.where(two, -1.0, jnp.where(one, 0.0, col_2))
        return jnp.where(here, 0.0, a) - col_1 * new_1 - col_2 * new_2

    systems = [scaled(a) for a in grams]
    values = [a for a, _, _ in systems]
    for k in range(0, RANK, 2):
        values = [sweep(a, k) for a in values]
    return [a * down * across for a, (_, down, across) in zip(values, systems)]


def stacked(refs, order, stack):
    at = 0
    for ref in refs:
        parts = parts_of(ref[...])
        n = ref.shape[0]
        for k, which in enumerate(order):
            stack[k * RANK + at : k * RANK + at + n, :] = parts[which]
        at += n


ROW_ORDER, COL_ORDER = (0, 1, 0, 1), (0, 0, 1, 1)


def turn(stack, turned):
    for i in range(0, stack.shape[1], TILE):
        turned[i : i + TILE, :] = stack[:, i : i + TILE].T


def gram_sums(run, packed, whole, after=()):
    n = len(packed)

    def kernel(*refs):
        a = sum((ref[...] for ref in refs[1:n]), refs[0][...])
        refs[-2][...] = jnp.concatenate([a[:, :RANK], a[:, RANK:]], axis=0)
        refs[-1][...] = sum((ref[...] for ref in refs[n + 1 : -2]), refs[n][...])

    outs = [((RANK, RANK), F32, VMEM)] * 2
    return run(kernel, [(x, VMEM) for x in (*packed, *whole)], outs, mib=2, after=after)


def solve(run, gram_down, left_down, gram_gate, left_gate, after=()):
    cols, rows = left_down.shape[1], left_gate.shape[1]

    def kernel(gram_down, left_down, gram_gate, left_gate, col_stack, row_turned, col, row, row_stack):
        grams = [gram_down[...], gram_gate[...]]
        for place, a, left, out in zip(
            (core_of(), replica_of()), inverses(grams), (left_down, left_gate), (col, row)
        ):
            other = jnp.concatenate([a[HALF:], a[:HALF]], axis=0)
            a = jnp.where(place == 0, a, other) * (1.0 / REPLICAS)
            hi, lo = parts_of(a)
            both = jnp.concatenate([hi, hi, lo], axis=1)
            out[...] = jnp.dot(both, left[...], preferred_element_type=F32)
        stacked([col], COL_ORDER, col_stack)
        stacked([row], ROW_ORDER, row_stack)
        turn(row_stack, row_turned)

    return run(
        kernel,
        [(x, VMEM) for x in (gram_down, left_down, gram_gate, left_gate)],
        [((4 * RANK, cols), BF16, VMEM), ((rows, 4 * RANK), BF16, VMEM)],
        [
            pltpu.VMEM((RANK, cols), F32),
            pltpu.VMEM((RANK, rows), F32),
            pltpu.VMEM((4 * RANK, rows), BF16),
        ],
        mib=6,
        after=after,
    )


def rebuild(run, ready, owns, others, fixed, shares, first=0, before=None, after=()):
    rows, cols = fixed.shape
    share = rows // REPLICAS
    height = share // 2
    rows_late = ready[0] is None
    late_width = sum(widths_of(owns))
    width = ready[1].shape[1] if rows_late or not owns else late_width
    n_ready = sum(x is not None for x in ready)
    n_own, n_late = len(owns), len(owns) + len(others)
    n_before = 0 if before is None else len(before)
    with_update = 0 in shares
    spots = [(s, t, j) for s in shares for t in range(2) for j in range(0, width, TILE)]

    def kernel(*refs):
        given, late = refs[:n_ready], refs[n_ready : n_ready + n_late]
        fixed = refs[n_ready + n_late]
        refs = refs[n_ready + n_late + 1 + n_before :]
        new_error, update, turned = refs[0], refs[1], refs[2]
        errors, updates, stack, error_sems, update_sems = refs[3:]
        if late:
            order = ROW_ORDER if rows_late else COL_ORDER
            for at, pieces in ((0, late[:n_own]), (HALF, late[n_own:])):
                left = 0
                for ref in pieces:
                    parts = parts_of(ref[...])
                    n, w = ref.shape
                    for k, which in enumerate(order):
                        stack[k * RANK + at : k * RANK + at + n, left : left + w] = parts[which]
                    left += w
        if rows_late:
            turn(stack, turned)
            row, col = turned, given[0]
        else:
            turned[...] = jnp.zeros_like(turned)
            row, col = given[0], given[1] if n_ready == 2 else stack
        replica = replica_of()
        copies = []
        for k, (s, t, j) in enumerate(spots):
            at = pl.multiple_of((replica if s == 0 else 1 - replica) * share, height) + t * height
            at = pl.ds(pl.multiple_of(at, height), height)
            here, there = slice(j, j + TILE), pl.ds(first + j, TILE)
            mine = pl.ds(t * height, height)
            value = jnp.dot(row[at, :], col[:, here], preferred_element_type=F32)
            slot = pl.ds((shares.index(s) * 2 + t) * height, height)
            errors[slot, here] = (fixed[at, there].astype(F32) - value).astype(BF16)
            copies.append(
                pltpu.make_async_copy(errors.at[slot, here], new_error.at[at, there], error_sems.at[k])
            )
            copies[-1].start()
            if s == 0:
                updates[mine, here] = value.astype(BF16)
                copies.append(
                    pltpu.make_async_copy(updates.at[mine, here], update.at[mine, there], update_sems.at[k])
                )
                copies[-1].start()
        for copy in copies:
            copy.wait()

    turned_shape = (rows, 4 * RANK) if rows_late else (16, 128)
    args = [(x, VMEM) for x in (*(x for x in ready if x is not None), *owns, *others, fixed)]
    aliases = None
    if before is not None:
        aliases = {len(args): 0, len(args) + 1: 1}
        args += [(x, HBM) for x in before]
    return run(
        kernel,
        args,
        [((rows, cols), BF16, HBM), ((share, cols), BF16, HBM), (turned_shape, BF16, VMEM)],
        [
            pltpu.VMEM((len(shares) * share, width), BF16),
            pltpu.VMEM((share if with_update else 16, width), BF16),
            pltpu.VMEM((4 * RANK, late_width if n_late else 128), BF16),
            pltpu.SemaphoreType.DMA((len(spots),)),
            pltpu.SemaphoreType.DMA((len(spots),)),
        ],
        mib=18,
        aliases=aliases,
        after=after,
    )


def local(grad_gate, grad_down, error_gate, error_down, start_gate, start_down):
    slab, width = grad_gate.shape
    n_dp, n_t = lax.axis_size("dp"), lax.axis_size("tensor")
    run = Calls()
    hops, steps = row_steps(), col_steps()
    tiles = slab // TILE

    _, fixed_down, keep, give = down_left(run, grad_down, error_down, start_down, 0, tiles)
    got = exchange(give, other_replica)
    gate_args = (run, grad_gate, error_gate, start_gate)
    cut = tiles * 3 // 5
    first = gate_left(*gate_args, 0, cut, after=(keep,))
    (down,) = add(run, [keep], [got], after=(first[0],))
    got = exchange(down, steps[0])
    _, fixed_gate, keep_gate, *gives = gate_left(
        *gate_args, cut, tiles - cut, first, after=(down,)
    )
    (gate,) = add(run, [keep_gate], to_other_core(gives))
    got_gate = exchange(gate, hops[0])
    for i in range(len(steps)):
        (down,) = add(run, [down], [got], after=(gate,))
        if i + 1 < len(steps):
            got = exchange(down, steps[i + 1])
    other_down = exchange(down, other_replica)
    for hop in hops[1:]:
        (gate,) = add(run, [gate], [got_gate], after=(down,))
        got_gate = exchange(gate, hop)

    keep, *gives, left_down = down_right(run, [down], [other_down], fixed_down, after=(gate,))
    gots = to_other_core(gives)
    gates = add(run, [gate], [got_gate], in_two(slab), after=(keep,))
    others_gate = to_other_core(gates)
    down, gram_down = add(run, [keep], gots, [slab, 2 * RANK], after=(gates[0],))
    grams_down = [gram_down] + [
        exchange(gram_down, lambda d, t, b=b: (d, t ^ b)) for b in range(2, n_t, 2)
    ]
    got = exchange(down, hops[0])
    keep_gate, give_gate, gram_gate, left_gate = gate_right(
        run, gates, others_gate, fixed_gate, after=(down,)
    )
    got_gate = exchange(give_gate, other_replica)
    grams_gate = [gram_gate] + [
        exchange(gram_gate, lambda d, t, b=b: (d ^ b, t)) for b in range(REPLICAS, n_dp, REPLICAS)
    ]
    for hop in hops[1:]:
        (down,) = add(run, [down], [got], after=(gram_gate,))
        got = exchange(down, hop)
    gram_down, gram_gate = gram_sums(run, grams_down, grams_gate, after=(down,))
    (gate,) = add(run, [keep_gate], [got_gate], after=(gram_gate,))
    got_gate = exchange(gate, steps[0])
    col_stack, row_turned = solve(run, gram_down, left_down, gram_gate, left_gate, after=(gate,))
    downs = add(run, [down], [got], in_two(slab), after=(col_stack,))
    others_down = to_other_core(downs)
    *outs_down, turned = rebuild(
        run, (None, col_stack), downs, others_down, fixed_down, (0,), after=(downs[0],)
    )
    few = width // TILE * 3 // 7 * TILE
    for i in range(len(steps)):
        last = i + 1 == len(steps)
        gate = add(run, [gate], [got_gate], [few, width - few] if last else None, after=(turned,))
        if not last:
            (gate,) = gate
            got_gate = exchange(gate, steps[i + 1])
    others_gate = [exchange(x, other_replica) for x in gate]
    new_error_down, update_down, done = rebuild(
        run, (turned, col_stack), [], [], fixed_down, (1,), before=outs_down, after=(gate[0],)
    )
    *outs_gate, done = rebuild(
        run, (row_turned, None), gate[:1], others_gate[:1], fixed_gate, (0, 1), after=(done,)
    )
    new_error_gate, update_gate, _ = rebuild(
        run, (row_turned, None), gate[1:], others_gate[1:], fixed_gate, (0, 1), few, outs_gate,
        after=(done,),
    )
    return (update_gate, update_down, new_error_gate, new_error_down)


def solution(mesh):
    split = P(("mix", "dp"), "tensor")
    in_specs = (split, split, split, split, P(None, "tensor"), P())
    out_specs = (split, split, split, split)

    def run(grad_gate, *rest):
        groups = mesh.shape["mix"] * mesh.shape["dp"]
        slab = grad_gate.shape[0] // groups
        width = grad_gate.shape[1] // mesh.shape["tensor"]
        fits = slab % (REPLICAS * TILE) == 0 and width % TILE == 0
        body = local if fits else local_plain
        return jax.shard_map(
            body, mesh=mesh, in_specs=in_specs, out_specs=out_specs, check_vma=False
        )(grad_gate, *rest)

    return run
```

```python
import functools

import jax
import jax.numpy as jnp
from jax import lax
from jax.experimental import pallas as pl
from jax.experimental.pallas import tpu as pltpu
from jax.sharding import PartitionSpec as P

REPLICAS = 2
RANK = 64
TILE = 256
FLOPS = 1.15e9
WEIGHTS = (8.0, 4.0, 1.0, 4.0, 0.1, 5.0, 1.0, 5.0, 1.0, 1.0, 2.0, 2.0, 0.1, 5.0, 5.0, 1.0, 0.1, 0.5, 1.0, 8.0, 8.0)
MIB = 1 << 20
BF16 = jnp.bfloat16
F32 = jnp.float32

NN = (((1,), (0,)), ((), ()))
NT = (((1,), (1,)), ((), ()))
TN = (((0,), (0,)), ((), ()))


def from_partner(shard, axis, stride):
    return lax.ppermute(shard, axis, [(i, i ^ 1 << stride) for i in range(lax.axis_size(axis))])


def corrected(grad, error):
    return (grad.astype(F32) + error.astype(F32)).astype(BF16)


def transposed(matrix, ortho):
    return lax.dot_general(matrix, ortho.astype(BF16), TN, preferred_element_type=F32)


def gram_of(left):
    return jnp.dot(left.T, left, precision=lax.Precision.HIGHEST)


def factored(left, inner):
    lower = jnp.linalg.cholesky(inner)
    return lax.linalg.triangular_solve(lower, left, left_side=False, lower=True, transpose_a=True)


def local_plain(grad_gate, grad_down, error_gate, error_down, start_gate, start_down):
    high = lax.Precision.HIGHEST
    dp_place = lax.axis_index("dp")
    block = dp_place // REPLICAS
    replica = dp_place % REPLICAS
    fixed_gate = corrected(grad_gate, error_gate)
    fixed_down = corrected(grad_down, error_down)
    slab = fixed_gate.shape[0]
    cols_down = lax.dynamic_slice_in_dim(start_down, block * slab, slab, 1)
    left_gate = lax.dot_general(fixed_gate, start_gate, NT, preferred_element_type=F32)
    left_down = lax.dot_general(
        fixed_down, cols_down, (((0,), (1,)), ((), ())), preferred_element_type=F32
    )
    left_gate = lax.psum(left_gate, "tensor")
    left_gate = left_gate + from_partner(left_gate, "dp", 0)
    left_down = lax.psum(left_down, "dp")
    keep_gate = (replica == 0).astype(F32)
    inner_gate = lax.psum(gram_of(left_gate) * keep_gate, "dp")
    inner_down = lax.psum(gram_of(left_down), "tensor")
    ortho_gate = factored(left_gate, inner_gate)
    ortho_down = factored(left_down, inner_down)
    right_gate = transposed(fixed_gate, ortho_gate)
    right_gate = lax.psum(right_gate, "dp") / REPLICAS
    right_down = jnp.dot(fixed_down, ortho_down.astype(BF16), preferred_element_type=F32)
    right_down = lax.psum(right_down, "tensor")
    right_down = right_down + from_partner(right_down, "dp", 0)
    right_down = right_down / REPLICAS
    rebuilt_gate = jnp.dot(ortho_gate, right_gate.T, precision=high)
    rebuilt_down = jnp.dot(right_down, ortho_down.T, precision=high)
    share = slab // REPLICAS
    update_gate = lax.dynamic_slice_in_dim(rebuilt_gate, replica * share, share, 0).astype(BF16)
    update_down = lax.dynamic_slice_in_dim(rebuilt_down, replica * share, share, 0).astype(BF16)
    new_error_gate = (fixed_gate.astype(F32) - rebuilt_gate).astype(BF16)
    new_error_down = (fixed_down.astype(F32) - rebuilt_down).astype(BF16)
    return (update_gate, update_down, new_error_gate, new_error_down)


def core_of():
    return lax.rem(lax.axis_index("tensor"), 2)


def replica_of():
    return lax.rem(lax.axis_index("dp"), REPLICAS)


def exchange(x, partner):
    n_dp, n_t = lax.axis_size("dp"), lax.axis_size("tensor")
    pairs = []
    for d in range(n_dp):
        for t in range(n_t):
            to_d, to_t = partner(d, t)
            pairs.append((d * n_t + t, to_d * n_t + to_t))
    return lax.ppermute(x, ("dp", "tensor"), pairs)


def bits(n, low):
    out, b = [], low
    while b < n:
        out.append(b)
        b *= 2
    return out


def row_steps():
    steps = [(0, b) for b in bits(lax.axis_size("tensor"), 2)] + [(1, 0)]

    def partner(i, d, t):
        r, b = steps[i] if t % 2 == 0 else steps[-1 - i]
        return d ^ r, t ^ b

    return [functools.partial(partner, i) for i in range(len(steps))]


def col_steps():
    return [lambda d, t, b=b: (d ^ b, t) for b in bits(lax.axis_size("dp"), REPLICAS)]


def other_core(d, t):
    return d, t ^ 1


def other_replica(d, t):
    return d ^ 1, t


def to_other_core(pieces):
    return [exchange(x, other_core) for x in pieces]


VMEM = pl.BlockSpec(memory_space=pltpu.VMEM)
HBM = pl.BlockSpec(memory_space=pltpu.HBM)
ANY = pl.BlockSpec(memory_space=pl.ANY)
HALF = RANK // 2


class Calls:
    def __init__(self):
        self.count = 0

    def __call__(self, kernel, args, outs, scratch=(), mib=8, aliases=None, after=()):
        n_in, n_after = len(args), len(after)
        operands = [
            pltpu.with_memory_space_constraint(x, pltpu.VMEM if spec is VMEM else pltpu.HBM)
            for x, spec in args
        ]

        def body(*refs):
            kernel(*refs[:n_in], *refs[n_in + n_after :])

        out = pl.pallas_call(
            body,
            out_shape=tuple(
                (pltpu.VMEM if spec is VMEM else pltpu.HBM)(shape, kind) for shape, kind, spec in outs
            ),
            in_specs=[spec for _, spec in args] + [ANY] * n_after,
            out_specs=tuple(spec for *_, spec in outs),
            scratch_shapes=list(scratch),
            input_output_aliases=aliases or {},
            compiler_params=pltpu.CompilerParams(vmem_limit_bytes=mib * MIB),
            cost_estimate=pl.CostEstimate(
                flops=int(WEIGHTS[self.count] * FLOPS), bytes_accessed=1 << 10, transcendentals=0
            ),
        )(*operands, *after)
        self.count += 1
        return out


def parts_of(x):
    hi = x.astype(BF16)
    lo = (x - hi.astype(F32)).astype(BF16)
    return hi, lo


def spans(*widths):
    edges = sorted({sum(w[:i]) for w in widths for i in range(len(w) + 1)})
    for low, high in zip(edges, edges[1:]):
        places = []
        for w in widths:
            k = max(i for i in range(len(w)) if sum(w[:i]) <= low)
            places.append((k, low - sum(w[:k]), high - sum(w[:k])))
        yield places


def widths_of(refs):
    return [ref.shape[1] for ref in refs]


def add(run, xs, ys, widths=None, beside=None, after=()):
    widths = list(widths or widths_of(xs))
    more = 0 if beside is None else beside.shape[1]
    n_x, n_y = len(xs), len(ys)

    def kernel(*refs):
        x, y, out = refs[:n_x], refs[n_x : n_x + n_y], refs[-len(widths) :]
        for (i, i0, i1), (j, j0, j1), (k, k0, k1) in spans(widths_of(x), widths_of(y), widths):
            out[k][:, k0:k1] = x[i][:, i0:i1] + y[j][:, j0:j1]
        if more:
            out[-1][:, widths[-1] :] = refs[n_x + n_y][...]

    outs = [((HALF, n), F32, VMEM) for n in (*widths[:-1], widths[-1] + more)]
    args = [(x, VMEM) for x in (*xs, *ys)]
    if more:
        args.append((beside, VMEM))
    return list(run(kernel, args, outs, mib=2, after=after))


def in_two(width):
    cut = width // 256 * 128
    return [cut, width - cut]


def halve(whole, place, keep, gives):
    keep[...] = whole[pl.ds(pl.multiple_of(place * HALF, HALF), HALF), :]
    at = 0
    for give in gives:
        n = give.shape[1]
        give[...] = whole[pl.ds(pl.multiple_of((1 - place) * HALF, HALF), HALF), at : at + n]
        at += n


def tile_at(i):
    return pl.ds(pl.multiple_of(i * TILE, TILE), TILE)


def gate_left(run, grad, error, start, first, count, before=None, after=()):
    rows, cols = grad.shape
    last = (first + count) * TILE == rows

    def kernel(grad, error, start, *refs):
        if before is not None:
            refs = refs[2:]
        left, fixed = refs[:2]

        def step(g, e):
            at = tile_at(first + pl.program_id(0))
            term = jnp.zeros((RANK, TILE), F32)
            for j in range(0, cols, TILE):
                here = slice(j, j + TILE)
                c = g[:, here] + e[:, here]
                fixed[at, here] = c
                term += lax.dot_general(start[:, here], c, NT, preferred_element_type=F32)
            left[:, at] = term

        spec = pl.BlockSpec((TILE, cols), lambda i: (first + i, 0), pipeline_mode=pl.Buffered(3))
        pltpu.emit_pipeline(step, grid=(count,), in_specs=[spec, spec])(grad, error)
        if last:
            halve(left, core_of(), refs[2], refs[3:])

    args = [(grad, HBM), (error, HBM), (start, VMEM)]
    outs = [((RANK, rows), F32, VMEM), ((rows, cols), BF16, VMEM)]
    if last:
        outs += [((HALF, n), F32, VMEM) for n in (rows, *in_two(rows))]
    aliases = None
    if before is not None:
        args += [(x, VMEM) for x in before]
        aliases = {3: 0, 4: 1}
    return run(kernel, args, outs, mib=8, aliases=aliases, after=after)


def down_left(run, grad, error, start, first, count, before=None, after=()):
    rows, cols = grad.shape
    last = (first + count) * TILE == rows

    def kernel(grad, error, start, *refs):
        if before is not None:
            refs = refs[2:]
        left, fixed = refs[:2]
        pair = 2 * TILE
        block = lax.div(lax.axis_index("dp"), REPLICAS) * (rows // pair) + first // 2
        if before is None:
            left[...] = jnp.zeros_like(left)

        def step(g, e, s):
            i = pl.program_id(0)
            at = tile_at(first + i)
            for j in range(0, cols, TILE):
                here = slice(j, j + TILE)
                fixed[at, here] = g[:, here] + e[:, here]

            @pl.when(lax.rem(i, 2) == 1)
            def _():
                both = pl.ds(pl.multiple_of((first + i - 1) * TILE, pair), pair)
                for j in range(0, cols, TILE):
                    here = slice(j, j + TILE)
                    left[:, here] += jnp.dot(s[...], fixed[both, here], preferred_element_type=F32)

        spec = pl.BlockSpec((TILE, cols), lambda i: (first + i, 0), pipeline_mode=pl.Buffered(3))
        part = pl.BlockSpec((RANK, pair), lambda i: (0, block + lax.div(i, 2)))
        pltpu.emit_pipeline(step, grid=(count,), in_specs=[spec, spec, part])(grad, error, start)
        if last:
            halve(left, replica_of(), refs[2], refs[3:])

    args = [(grad, HBM), (error, HBM), (start, HBM)]
    outs = [((RANK, cols), F32, VMEM), ((rows, cols), BF16, VMEM)]
    if last:
        outs += [((HALF, cols), F32, VMEM)] * 2
    aliases = None
    if before is not None:
        args += [(x, VMEM) for x in before]
        aliases = {3: 0, 4: 1}
    return run(kernel, args, outs, mib=8, aliases=aliases, after=after)


def load_left(owns, others, place, left, stack):
    for refs, half in ((owns, place), (others, 1 - place)):
        at = 0
        for ref in refs:
            n = ref.shape[1]
            left[pl.ds(pl.multiple_of(half * HALF, HALF), HALF), at : at + n] = ref[...]
            at += n
    hi, lo = parts_of(left[...])
    stack[:RANK, :] = hi
    stack[RANK : 2 * RANK, :] = lo
    stack[2 * RANK :, :] = hi
    return lax.dot_general(
        left[...], left[...], NT, preferred_element_type=F32, precision=lax.Precision.HIGHEST
    )


def packed(gram):
    return jnp.concatenate([gram[:HALF], gram[HALF:]], axis=1)


def gate_right(run, owns, others, fixed, count, after=()):
    rows = fixed.shape[0]
    width = count * TILE
    n_own, n_both = len(owns), len(owns) + len(others)

    def kernel(*refs):
        fixed, keep, give, gram, stack, left, right = refs[n_both:]
        gram[...] = packed(load_left(refs[:n_own], refs[n_own:n_both], core_of(), left, stack))

        def step(i, _):
            both = jnp.dot(stack[: 2 * RANK], fixed[:, tile_at(i)], preferred_element_type=F32)
            right[:, tile_at(i)] = both[:RANK] + both[RANK:]
            return 0

        lax.fori_loop(0, count, step, 0)
        halve(right, replica_of(), keep, [give])

    return run(
        kernel,
        [(x, VMEM) for x in (*owns, *others, fixed)],
        [((HALF, width), F32, VMEM)] * 2
        + [((HALF, 2 * RANK), F32, VMEM), ((3 * RANK, rows), BF16, VMEM)],
        [pltpu.VMEM((RANK, rows), F32), pltpu.VMEM((RANK, width), F32)],
        mib=4,
        after=after,
    )


def gate_right_rest(run, stack, fixed, first, after=()):
    width = fixed.shape[1] - first * TILE

    def kernel(stack, fixed, keep, give, right):
        def step(i, _):
            both = jnp.dot(
                stack[: 2 * RANK], fixed[:, tile_at(first + i)], preferred_element_type=F32
            )
            right[:, tile_at(i)] = both[:RANK] + both[RANK:]
            return 0

        lax.fori_loop(0, width // TILE, step, 0)
        halve(right, replica_of(), keep, [give])

    return run(
        kernel,
        [(stack, VMEM), (fixed, VMEM)],
        [((HALF, width), F32, VMEM)] * 2,
        [pltpu.VMEM((RANK, width), F32)],
        mib=4,
        after=after,
    )


def down_right(run, owns, others, fixed, after=()):
    rows, cols = fixed.shape
    n_own, n_both = len(owns), len(owns) + len(others)
    cut, rest = in_two(rows)

    def kernel(*refs):
        fixed, keep, give_1, give_2, stack, left, right = refs[n_both:]
        gram = load_left(refs[:n_own], refs[n_own:n_both], replica_of(), left, stack)

        def step(i, _):
            both = lax.dot_general(stack[: 2 * RANK], fixed[tile_at(i), :], NT, preferred_element_type=F32)
            right[:, tile_at(i)] = both[:RANK] + both[RANK:]
            return 0

        lax.fori_loop(0, rows // TILE, step, 0)
        halve(right, core_of(), keep.at[:, :rows], [give_1, give_2.at[:, :rest]])
        keep[:, rows:] = packed(gram)
        give_2[:, rest:] = packed(gram)

    widths = (rows + 2 * RANK, cut, rest + 2 * RANK)
    return run(
        kernel,
        [(x, VMEM) for x in (*owns, *others, fixed)],
        [((HALF, n), F32, VMEM) for n in widths] + [((3 * RANK, cols), BF16, VMEM)],
        [pltpu.VMEM((RANK, cols), F32), pltpu.VMEM((RANK, rows), F32)],
        mib=4,
        after=after,
    )


def inverses(grams):
    row_at = lax.broadcasted_iota(jnp.int32, (RANK, RANK), 0)
    col_at = lax.broadcasted_iota(jnp.int32, (RANK, RANK), 1)
    lane = lax.broadcasted_iota(jnp.int32, (1, RANK), 1)

    def scaled(a):
        diagonal = jnp.where(row_at == col_at, a, 0.0)
        down = lax.rsqrt(jnp.sum(diagonal, axis=1, keepdims=True))
        across = lax.rsqrt(jnp.sum(diagonal, axis=0, keepdims=True))
        return a * down * across, down, across

    def sweep(a, k):
        one, two = (row_at == k, row_at == k + 1)
        here = one | two | (col_at == k) | (col_at == k + 1)
        col_1 = jnp.broadcast_to(a[:, k : k + 1], (RANK, RANK))
        col_2 = jnp.broadcast_to(a[:, k + 1 : k + 2], (RANK, RANK))
        p, q, r = col_1[k : k + 1], col_2[k : k + 1], col_2[k + 1 : k + 2]
        row_1 = jnp.where(lane == k, 1.0, jnp.where(lane == k + 1, 0.0, a[k : k + 1]))
        row_2 = jnp.where(lane == k + 1, 1.0, jnp.where(lane == k, 0.0, a[k + 1 : k + 2]))
        inv = 1.0 / (p * r - q * q)
        new_1 = (r * row_1 - q * row_2) * inv
        new_2 = (p * row_2 - q * row_1) * inv
        col_1 = jnp.where(one, -1.0, jnp.where(two, 0.0, col_1))
        col_2 = jnp.where(two, -1.0, jnp.where(one, 0.0, col_2))
        return jnp.where(here, 0.0, a) - col_1 * new_1 - col_2 * new_2

    systems = [scaled(a) for a in grams]
    values = [a for a, _, _ in systems]
    for k in range(0, RANK, 2):
        values = [sweep(a, k) for a in values]
    return [a * down * across for a, (_, down, across) in zip(values, systems)]


def stacked(refs, order, stack):
    at = 0
    for ref in refs:
        parts = parts_of(ref[...])
        n = ref.shape[0]
        for k, which in enumerate(order):
            stack[k * RANK + at : k * RANK + at + n, :] = parts[which]
        at += n


ROW_ORDER, COL_ORDER = (0, 1, 0, 1), (0, 0, 1, 1)


def turn(stack, turned):
    for i in range(0, stack.shape[1], TILE):
        turned[i : i + TILE, :] = stack[:, i : i + TILE].T


def solve(run, grams_down, left_down, gram_gate, left_gate, after=()):
    cols, rows = left_down.shape[1], left_gate.shape[1]

    n = len(grams_down)

    def kernel(*refs):
        gram_gate, left_down, left_gate, col_stack, row_turned, col, row, row_stack = refs[n:]
        gram_down = sum((ref[...] for ref in refs[1:n]), refs[0][...])
        grams = [
            jnp.concatenate([a[:, :RANK], a[:, RANK:]], axis=0) for a in (gram_down, gram_gate[...])
        ]
        for place, a, left, out in zip(
            (core_of(), replica_of()), inverses(grams), (left_down, left_gate), (col, row)
        ):
            other = jnp.concatenate([a[HALF:], a[:HALF]], axis=0)
            a = jnp.where(place == 0, a, other) * (1.0 / REPLICAS)
            hi, lo = parts_of(a)
            both = jnp.concatenate([hi, hi, lo], axis=1)
            out[...] = jnp.dot(both, left[...], preferred_element_type=F32)
        stacked([col], COL_ORDER, col_stack)
        stacked([row], ROW_ORDER, row_stack)
        turn(row_stack, row_turned)

    return run(
        kernel,
        [(x, VMEM) for x in (*grams_down, gram_gate, left_down, left_gate)],
        [((4 * RANK, cols), BF16, VMEM), ((rows, 4 * RANK), BF16, VMEM)],
        [
            pltpu.VMEM((RANK, cols), F32),
            pltpu.VMEM((RANK, rows), F32),
            pltpu.VMEM((4 * RANK, rows), BF16),
        ],
        mib=6,
        after=after,
    )


def rebuild(run, ready, owns, others, fixed, shares, height, first=0, before=None, after=()):
    rows, cols = fixed.shape
    share = rows // REPLICAS
    parts = share // height
    rows_late = ready[0] is None
    late_width = sum(widths_of(owns))
    width = ready[1].shape[1] if rows_late or not owns else late_width
    n_ready = sum(x is not None for x in ready)
    n_own, n_late = len(owns), len(owns) + len(others)
    n_before = 0 if before is None else len(before)
    with_update = 0 in shares
    spots = [(s, t, j) for s in shares for t in range(parts) for j in range(0, width, TILE)]

    def kernel(*refs):
        given, late = refs[:n_ready], refs[n_ready : n_ready + n_late]
        fixed = refs[n_ready + n_late]
        refs = refs[n_ready + n_late + 1 + n_before :]
        new_error, update, turned = refs[0], refs[1], refs[2]
        errors, updates, stack, error_sems, update_sems = refs[3:]
        if late:
            order = ROW_ORDER if rows_late else COL_ORDER
            for at, pieces in ((0, late[:n_own]), (HALF, late[n_own:])):
                left = 0
                for ref in pieces:
                    split = parts_of(ref[...])
                    n, w = ref.shape
                    for k, which in enumerate(order):
                        stack[k * RANK + at : k * RANK + at + n, left : left + w] = split[which]
                    left += w
        if rows_late:
            turn(stack, turned)
            row, col = turned, given[0]
        else:
            turned[...] = jnp.zeros_like(turned)
            row, col = given[0], given[1] if n_ready == 2 else stack
        replica = replica_of()
        copies = []
        for k, (s, t, j) in enumerate(spots):
            at = pl.multiple_of((replica if s == 0 else 1 - replica) * share, height) + t * height
            at = pl.ds(pl.multiple_of(at, height), height)
            here, there = slice(j, j + TILE), pl.ds(first + j, TILE)
            mine = pl.ds(t * height, height)
            value = jnp.dot(row[at, :], col[:, here], preferred_element_type=F32)
            slot = pl.ds((shares.index(s) * parts + t) * height, height)
            errors[slot, here] = (fixed[at, there].astype(F32) - value).astype(BF16)
            copies.append(
                pltpu.make_async_copy(errors.at[slot, here], new_error.at[at, there], error_sems.at[k])
            )
            copies[-1].start()
            if s == 0:
                updates[mine, here] = value.astype(BF16)
                copies.append(
                    pltpu.make_async_copy(updates.at[mine, here], update.at[mine, there], update_sems.at[k])
                )
                copies[-1].start()
        for copy in copies:
            copy.wait()

    turned_shape = (rows, 4 * RANK) if rows_late else (16, 128)
    args = [(x, VMEM) for x in (*(x for x in ready if x is not None), *owns, *others, fixed)]
    aliases = None
    if before is not None:
        aliases = {len(args): 0, len(args) + 1: 1}
        args += [(x, HBM) for x in before]
    return run(
        kernel,
        args,
        [((rows, cols), BF16, HBM), ((share, cols), BF16, HBM), (turned_shape, BF16, VMEM)],
        [
            pltpu.VMEM((len(shares) * share, width), BF16),
            pltpu.VMEM((share if with_update else 16, width), BF16),
            pltpu.VMEM((4 * RANK, late_width if n_late else 128), BF16),
            pltpu.SemaphoreType.DMA((len(spots),)),
            pltpu.SemaphoreType.DMA((len(spots),)),
        ],
        mib=18,
        aliases=aliases,
        after=after,
    )


def local(grad_gate, grad_down, error_gate, error_down, start_gate, start_down):
    slab, width = grad_gate.shape
    n_dp, n_t = lax.axis_size("dp"), lax.axis_size("tensor")
    run = Calls()
    hops, steps = row_steps(), col_steps()
    tiles = slab // TILE

    _, fixed_down, keep, give = down_left(run, grad_down, error_down, start_down, 0, tiles)
    got = exchange(give, other_replica)
    gate_args = (run, grad_gate, error_gate, start_gate)
    cut = tiles * 3 // 5
    first = gate_left(*gate_args, 0, cut, after=(keep,))
    (down,) = add(run, [keep], [got], after=(first[0],))
    got = exchange(down, steps[0])
    _, fixed_gate, keep_gate, *gives = gate_left(
        *gate_args, cut, tiles - cut, first, after=(down,)
    )
    (gate,) = add(run, [keep_gate], to_other_core(gives))
    got_gate = exchange(gate, hops[0])
    for i in range(len(steps)):
        (down,) = add(run, [down], [got], after=(gate,))
        if i + 1 < len(steps):
            got = exchange(down, steps[i + 1])
    other_down = exchange(down, other_replica)
    for hop in hops[1:]:
        (gate,) = add(run, [gate], [got_gate], after=(down,))
        got_gate = exchange(gate, hop)

    keep, *gives, left_down = down_right(run, [down], [other_down], fixed_down, after=(gate,))
    gots = to_other_core(gives)
    gates = add(run, [gate], [got_gate], in_two(slab), after=(keep,))
    others_gate = to_other_core(gates)
    down, gram_down = add(run, [keep], gots, [slab, 2 * RANK], after=(gates[0],))
    grams_down = [gram_down] + [
        exchange(gram_down, lambda d, t, b=b: (d, t ^ b)) for b in range(2, n_t, 2)
    ]
    got = exchange(down, hops[0])
    few = width // TILE * 3 // 7
    keep_a, give_a, gram_gate, left_gate = gate_right(
        run, gates, others_gate, fixed_gate, few, after=(down,)
    )
    got_a = exchange(give_a, other_replica)
    keep_b, give_b = gate_right_rest(run, left_gate, fixed_gate, few)
    got_b = exchange(give_b, other_replica)
    for hop in hops[1:]:
        (down,) = add(run, [down], [got], after=(give_b,))
        got = exchange(down, hop)
    (gate_a,) = add(run, [keep_a], [got_a], beside=gram_gate, after=(down,))
    got_a = exchange(gate_a, steps[0])
    (gate_b,) = add(run, [keep_b], [got_b], after=(gate_a,))
    got_b = exchange(gate_b, steps[0])
    downs = add(run, [down], [got], in_two(slab), after=(gate_b,))
    others_down = to_other_core(downs)
    for step in steps[1:]:
        (gate_a,) = add(run, [gate_a], [got_a])
        got_a = exchange(gate_a, step)
        (gate_b,) = add(run, [gate_b], [got_b])
        got_b = exchange(gate_b, step)
    gate_a, gram_gate = add(run, [gate_a], [got_a], [few * TILE, 2 * RANK], after=(downs[0],))
    other_a = exchange(gate_a, other_replica)
    col_stack, row_turned = solve(run, grams_down, left_down, gram_gate, left_gate)
    (gate_b,) = add(run, [gate_b], [got_b], after=(col_stack,))
    other_b = exchange(gate_b, other_replica)
    new_error_down, update_down, turned = rebuild(
        run, (None, col_stack), downs, others_down, fixed_down, (0, 1), slab // 8, after=(gate_b,)
    )
    new_error_gate, update_gate, _ = rebuild(
        run, (row_turned, None), [gate_a, gate_b], [other_a, other_b], fixed_gate, (0, 1), slab // 2,
        after=(turned,),
    )
    return (update_gate, update_down, new_error_gate, new_error_down)


def solution(mesh):
    split = P(("mix", "dp"), "tensor")
    in_specs = (split, split, split, split, P(None, "tensor"), P())
    out_specs = (split, split, split, split)

    def run(grad_gate, *rest):
        groups = mesh.shape["mix"] * mesh.shape["dp"]
        slab = grad_gate.shape[0] // groups
        width = grad_gate.shape[1] // mesh.shape["tensor"]
        fits = slab % (REPLICAS * TILE) == 0 and width % TILE == 0
        body = local if fits else local_plain
        return jax.shard_map(
            body, mesh=mesh, in_specs=in_specs, out_specs=out_specs, check_vma=False
        )(grad_gate, *rest)

    return run
```

```python
import functools

import jax
import jax.numpy as jnp
from jax import lax
from jax.experimental import pallas as pl
from jax.experimental.pallas import tpu as pltpu
from jax.sharding import PartitionSpec as P

REPLICAS = 2
RANK = 64
TILE = 256
FLOPS = 1.15e9
WEIGHTS = (8.0, 4.0, 1.0, 4.0, 0.1, 5.0, 1.0, 5.0, 1.0, 1.0, 4.0, 0.1, 0.1, 1.0, 5.0, 1.0, 0.1, 1.0, 4.0, 4.0, 4.0)
MIB = 1 << 20
BF16 = jnp.bfloat16
F32 = jnp.float32

NN = (((1,), (0,)), ((), ()))
NT = (((1,), (1,)), ((), ()))
TN = (((0,), (0,)), ((), ()))


def from_partner(shard, axis, stride):
    return lax.ppermute(shard, axis, [(i, i ^ 1 << stride) for i in range(lax.axis_size(axis))])


def corrected(grad, error):
    return (grad.astype(F32) + error.astype(F32)).astype(BF16)


def transposed(matrix, ortho):
    return lax.dot_general(matrix, ortho.astype(BF16), TN, preferred_element_type=F32)


def gram_of(left):
    return jnp.dot(left.T, left, precision=lax.Precision.HIGHEST)


def factored(left, inner):
    lower = jnp.linalg.cholesky(inner)
    return lax.linalg.triangular_solve(lower, left, left_side=False, lower=True, transpose_a=True)


def local_plain(grad_gate, grad_down, error_gate, error_down, start_gate, start_down):
    high = lax.Precision.HIGHEST
    dp_place = lax.axis_index("dp")
    block = dp_place // REPLICAS
    replica = dp_place % REPLICAS
    fixed_gate = corrected(grad_gate, error_gate)
    fixed_down = corrected(grad_down, error_down)
    slab = fixed_gate.shape[0]
    cols_down = lax.dynamic_slice_in_dim(start_down, block * slab, slab, 1)
    left_gate = lax.dot_general(fixed_gate, start_gate, NT, preferred_element_type=F32)
    left_down = lax.dot_general(
        fixed_down, cols_down, (((0,), (1,)), ((), ())), preferred_element_type=F32
    )
    left_gate = lax.psum(left_gate, "tensor")
    left_gate = left_gate + from_partner(left_gate, "dp", 0)
    left_down = lax.psum(left_down, "dp")
    keep_gate = (replica == 0).astype(F32)
    inner_gate = lax.psum(gram_of(left_gate) * keep_gate, "dp")
    inner_down = lax.psum(gram_of(left_down), "tensor")
    ortho_gate = factored(left_gate, inner_gate)
    ortho_down = factored(left_down, inner_down)
    right_gate = transposed(fixed_gate, ortho_gate)
    right_gate = lax.psum(right_gate, "dp") / REPLICAS
    right_down = jnp.dot(fixed_down, ortho_down.astype(BF16), preferred_element_type=F32)
    right_down = lax.psum(right_down, "tensor")
    right_down = right_down + from_partner(right_down, "dp", 0)
    right_down = right_down / REPLICAS
    rebuilt_gate = jnp.dot(ortho_gate, right_gate.T, precision=high)
    rebuilt_down = jnp.dot(right_down, ortho_down.T, precision=high)
    share = slab // REPLICAS
    update_gate = lax.dynamic_slice_in_dim(rebuilt_gate, replica * share, share, 0).astype(BF16)
    update_down = lax.dynamic_slice_in_dim(rebuilt_down, replica * share, share, 0).astype(BF16)
    new_error_gate = (fixed_gate.astype(F32) - rebuilt_gate).astype(BF16)
    new_error_down = (fixed_down.astype(F32) - rebuilt_down).astype(BF16)
    return (update_gate, update_down, new_error_gate, new_error_down)


def core_of():
    return lax.rem(lax.axis_index("tensor"), 2)


def replica_of():
    return lax.rem(lax.axis_index("dp"), REPLICAS)


def exchange(x, partner):
    n_dp, n_t = lax.axis_size("dp"), lax.axis_size("tensor")
    pairs = []
    for d in range(n_dp):
        for t in range(n_t):
            to_d, to_t = partner(d, t)
            pairs.append((d * n_t + t, to_d * n_t + to_t))
    return lax.ppermute(x, ("dp", "tensor"), pairs)


def bits(n, low):
    out, b = [], low
    while b < n:
        out.append(b)
        b *= 2
    return out


def row_steps():
    steps = [(0, b) for b in bits(lax.axis_size("tensor"), 2)] + [(1, 0)]

    def partner(i, d, t):
        r, b = steps[i] if t % 2 == 0 else steps[-1 - i]
        return d ^ r, t ^ b

    return [functools.partial(partner, i) for i in range(len(steps))]


def col_steps():
    return [lambda d, t, b=b: (d ^ b, t) for b in bits(lax.axis_size("dp"), REPLICAS)]


def other_core(d, t):
    return d, t ^ 1


def other_replica(d, t):
    return d ^ 1, t


def to_other_core(pieces):
    return [exchange(x, other_core) for x in pieces]


VMEM = pl.BlockSpec(memory_space=pltpu.VMEM)
HBM = pl.BlockSpec(memory_space=pltpu.HBM)
ANY = pl.BlockSpec(memory_space=pl.ANY)
HALF = RANK // 2


class Calls:
    def __init__(self):
        self.count = 0

    def __call__(self, kernel, args, outs, scratch=(), mib=8, aliases=None, after=()):
        n_in, n_after = len(args), len(after)
        operands = [
            pltpu.with_memory_space_constraint(x, pltpu.VMEM if spec is VMEM else pltpu.HBM)
            for x, spec in args
        ]

        def body(*refs):
            kernel(*refs[:n_in], *refs[n_in + n_after :])

        out = pl.pallas_call(
            body,
            out_shape=tuple(
                (pltpu.VMEM if spec is VMEM else pltpu.HBM)(shape, kind) for shape, kind, spec in outs
            ),
            in_specs=[spec for _, spec in args] + [ANY] * n_after,
            out_specs=tuple(spec for *_, spec in outs),
            scratch_shapes=list(scratch),
            input_output_aliases=aliases or {},
            compiler_params=pltpu.CompilerParams(vmem_limit_bytes=mib * MIB),
            cost_estimate=pl.CostEstimate(
                flops=int(WEIGHTS[self.count] * FLOPS), bytes_accessed=1 << 10, transcendentals=0
            ),
        )(*operands, *after)
        self.count += 1
        return out


def parts_of(x):
    hi = x.astype(BF16)
    lo = (x - hi.astype(F32)).astype(BF16)
    return hi, lo


def spans(*widths):
    edges = sorted({sum(w[:i]) for w in widths for i in range(len(w) + 1)})
    for low, high in zip(edges, edges[1:]):
        places = []
        for w in widths:
            k = max(i for i in range(len(w)) if sum(w[:i]) <= low)
            places.append((k, low - sum(w[:k]), high - sum(w[:k])))
        yield places


def widths_of(refs):
    return [ref.shape[1] for ref in refs]


def add(run, xs, ys, widths=None, after=()):
    widths = widths or widths_of(xs)
    n_x, n_y = len(xs), len(ys)

    def kernel(*refs):
        x, y, out = refs[:n_x], refs[n_x : n_x + n_y], refs[n_x + n_y :]
        for (i, i0, i1), (j, j0, j1), (k, k0, k1) in spans(widths_of(x), widths_of(y), widths):
            out[k][:, k0:k1] = x[i][:, i0:i1] + y[j][:, j0:j1]

    outs = [((HALF, n), F32, VMEM) for n in widths]
    return list(run(kernel, [(x, VMEM) for x in (*xs, *ys)], outs, mib=2, after=after))


def in_two(width):
    cut = width // 256 * 128
    return [cut, width - cut]


def halve(whole, place, keep, gives):
    keep[...] = whole[pl.ds(pl.multiple_of(place * HALF, HALF), HALF), :]
    at = 0
    for give in gives:
        n = give.shape[1]
        give[...] = whole[pl.ds(pl.multiple_of((1 - place) * HALF, HALF), HALF), at : at + n]
        at += n


def tile_at(i):
    return pl.ds(pl.multiple_of(i * TILE, TILE), TILE)


def gate_left(run, grad, error, start, first, count, before=None, after=()):
    rows, cols = grad.shape
    last = (first + count) * TILE == rows

    def kernel(grad, error, start, *refs):
        if before is not None:
            refs = refs[2:]
        left, fixed = refs[:2]

        def step(g, e):
            at = tile_at(first + pl.program_id(0))
            term = jnp.zeros((RANK, TILE), F32)
            for j in range(0, cols, TILE):
                here = slice(j, j + TILE)
                c = g[:, here] + e[:, here]
                fixed[at, here] = c
                term += lax.dot_general(start[:, here], c, NT, preferred_element_type=F32)
            left[:, at] = term

        spec = pl.BlockSpec((TILE, cols), lambda i: (first + i, 0), pipeline_mode=pl.Buffered(3))
        pltpu.emit_pipeline(step, grid=(count,), in_specs=[spec, spec])(grad, error)
        if last:
            halve(left, core_of(), refs[2], refs[3:])

    args = [(grad, HBM), (error, HBM), (start, VMEM)]
    outs = [((RANK, rows), F32, VMEM), ((rows, cols), BF16, VMEM)]
    if last:
        outs += [((HALF, n), F32, VMEM) for n in (rows, *in_two(rows))]
    aliases = None
    if before is not None:
        args += [(x, VMEM) for x in before]
        aliases = {3: 0, 4: 1}
    return run(kernel, args, outs, mib=8, aliases=aliases, after=after)


def down_left(run, grad, error, start, first, count, before=None, after=()):
    rows, cols = grad.shape
    last = (first + count) * TILE == rows

    def kernel(grad, error, start, *refs):
        if before is not None:
            refs = refs[2:]
        left, fixed = refs[:2]
        pair = 2 * TILE
        block = lax.div(lax.axis_index("dp"), REPLICAS) * (rows // pair) + first // 2
        if before is None:
            left[...] = jnp.zeros_like(left)

        def step(g, e, s):
            i = pl.program_id(0)
            at = tile_at(first + i)
            for j in range(0, cols, TILE):
                here = slice(j, j + TILE)
                fixed[at, here] = g[:, here] + e[:, here]

            @pl.when(lax.rem(i, 2) == 1)
            def _():
                both = pl.ds(pl.multiple_of((first + i - 1) * TILE, pair), pair)
                for j in range(0, cols, TILE):
                    here = slice(j, j + TILE)
                    left[:, here] += jnp.dot(s[...], fixed[both, here], preferred_element_type=F32)

        spec = pl.BlockSpec((TILE, cols), lambda i: (first + i, 0), pipeline_mode=pl.Buffered(3))
        part = pl.BlockSpec((RANK, pair), lambda i: (0, block + lax.div(i, 2)))
        pltpu.emit_pipeline(step, grid=(count,), in_specs=[spec, spec, part])(grad, error, start)
        if last:
            halve(left, replica_of(), refs[2], refs[3:])

    args = [(grad, HBM), (error, HBM), (start, HBM)]
    outs = [((RANK, cols), F32, VMEM), ((rows, cols), BF16, VMEM)]
    if last:
        outs += [((HALF, cols), F32, VMEM)] * 2
    aliases = None
    if before is not None:
        args += [(x, VMEM) for x in before]
        aliases = {3: 0, 4: 1}
    return run(kernel, args, outs, mib=8, aliases=aliases, after=after)


def load_left(owns, others, place, left, stack):
    for refs, half in ((owns, place), (others, 1 - place)):
        at = 0
        for ref in refs:
            n = ref.shape[1]
            left[pl.ds(pl.multiple_of(half * HALF, HALF), HALF), at : at + n] = ref[...]
            at += n
    hi, lo = parts_of(left[...])
    stack[:RANK, :] = hi
    stack[RANK : 2 * RANK, :] = lo
    stack[2 * RANK :, :] = hi
    parts = stack[: 2 * RANK]
    gram = lax.dot_general(parts, parts, NT, preferred_element_type=F32)
    mixed = gram[:RANK, RANK:] + gram[RANK:, :RANK]
    return gram[:RANK, :RANK] + (mixed + gram[RANK:, RANK:])


def gate_right(run, owns, others, fixed, after=()):
    rows, cols = fixed.shape
    n_own, n_both = len(owns), len(owns) + len(others)

    def kernel(*refs):
        fixed, keep, give, gram, stack, left, right = refs[n_both:]
        gram[...] = load_left(refs[:n_own], refs[n_own:n_both], core_of(), left, stack)

        def step(i, _):
            both = jnp.dot(stack[: 2 * RANK], fixed[:, tile_at(i)], preferred_element_type=F32)
            right[:, tile_at(i)] = both[:RANK] + both[RANK:]
            return 0

        lax.fori_loop(0, cols // TILE, step, 0)
        halve(right, replica_of(), keep, [give])

    return run(
        kernel,
        [(x, VMEM) for x in (*owns, *others, fixed)],
        [((HALF, cols), F32, VMEM)] * 2 + [((RANK, RANK), F32, VMEM), ((3 * RANK, rows), BF16, VMEM)],
        [pltpu.VMEM((RANK, rows), F32), pltpu.VMEM((RANK, cols), F32)],
        mib=4,
        after=after,
    )


def down_right(run, owns, others, fixed, after=()):
    rows, cols = fixed.shape
    n_own, n_both = len(owns), len(owns) + len(others)
    cut, rest = in_two(rows)

    def kernel(*refs):
        fixed, keep, give_1, give_2, stack, left, right = refs[n_both:]
        gram = load_left(refs[:n_own], refs[n_own:n_both], replica_of(), left, stack)

        def step(i, _):
            both = lax.dot_general(stack[: 2 * RANK], fixed[tile_at(i), :], NT, preferred_element_type=F32)
            right[:, tile_at(i)] = both[:RANK] + both[RANK:]
            return 0

        lax.fori_loop(0, rows // TILE, step, 0)
        packed = jnp.concatenate([gram[:HALF], gram[HALF:]], axis=1)
        halve(right, core_of(), keep.at[:, :rows], [give_1, give_2.at[:, :rest]])
        keep[:, rows:] = packed
        give_2[:, rest:] = packed

    widths = (rows + 2 * RANK, cut, rest + 2 * RANK)
    return run(
        kernel,
        [(x, VMEM) for x in (*owns, *others, fixed)],
        [((HALF, n), F32, VMEM) for n in widths] + [((3 * RANK, cols), BF16, VMEM)],
        [pltpu.VMEM((RANK, cols), F32), pltpu.VMEM((RANK, rows), F32)],
        mib=4,
        after=after,
    )


def inverses(grams):
    row_at = lax.broadcasted_iota(jnp.int32, (RANK, RANK), 0)
    col_at = lax.broadcasted_iota(jnp.int32, (RANK, RANK), 1)
    lane = lax.broadcasted_iota(jnp.int32, (1, RANK), 1)

    def scaled(a):
        diagonal = jnp.where(row_at == col_at, a, 0.0)
        down = lax.rsqrt(jnp.sum(diagonal, axis=1, keepdims=True))
        across = lax.rsqrt(jnp.sum(diagonal, axis=0, keepdims=True))
        return a * down * across, down, across

    def sweep(a, k):
        one, two = (row_at == k, row_at == k + 1)
        here = one | two | (col_at == k) | (col_at == k + 1)
        col_1 = jnp.broadcast_to(a[:, k : k + 1], (RANK, RANK))
        col_2 = jnp.broadcast_to(a[:, k + 1 : k + 2], (RANK, RANK))
        p, q, r = col_1[k : k + 1], col_2[k : k + 1], col_2[k + 1 : k + 2]
        row_1 = jnp.where(lane == k, 1.0, jnp.where(lane == k + 1, 0.0, a[k : k + 1]))
        row_2 = jnp.where(lane == k + 1, 1.0, jnp.where(lane == k, 0.0, a[k + 1 : k + 2]))
        inv = 1.0 / (p * r - q * q)
        new_1 = (r * row_1 - q * row_2) * inv
        new_2 = (p * row_2 - q * row_1) * inv
        col_1 = jnp.where(one, -1.0, jnp.where(two, 0.0, col_1))
        col_2 = jnp.where(two, -1.0, jnp.where(one, 0.0, col_2))
        return jnp.where(here, 0.0, a) - col_1 * new_1 - col_2 * new_2

    systems = [scaled(a) for a in grams]
    values = [a for a, _, _ in systems]
    for k in range(0, RANK, 2):
        values = [sweep(a, k) for a in values]
    return [a * down * across for a, (_, down, across) in zip(values, systems)]


def stacked(refs, order, stack):
    at = 0
    for ref in refs:
        parts = parts_of(ref[...])
        n = ref.shape[0]
        for k, which in enumerate(order):
            stack[k * RANK + at : k * RANK + at + n, :] = parts[which]
        at += n


ROW_ORDER, COL_ORDER = (0, 1, 0, 1), (0, 0, 1, 1)


def turn(stack, turned):
    for i in range(0, stack.shape[1], TILE):
        turned[i : i + TILE, :] = stack[:, i : i + TILE].T


def gram_sums(run, packed, whole, after=()):
    n = len(packed)

    def kernel(*refs):
        a = sum((ref[...] for ref in refs[1:n]), refs[0][...])
        refs[-2][...] = jnp.concatenate([a[:, :RANK], a[:, RANK:]], axis=0)
        refs[-1][...] = sum((ref[...] for ref in refs[n + 1 : -2]), refs[n][...])

    outs = [((RANK, RANK), F32, VMEM)] * 2
    return run(kernel, [(x, VMEM) for x in (*packed, *whole)], outs, mib=2, after=after)


def solve(run, gram_down, left_down, gram_gate, left_gate, after=()):
    cols, rows = left_down.shape[1], left_gate.shape[1]

    def kernel(gram_down, left_down, gram_gate, left_gate, col_stack, row_turned, col, row, row_stack):
        grams = [gram_down[...], gram_gate[...]]
        for place, a, left, out in zip(
            (core_of(), replica_of()), inverses(grams), (left_down, left_gate), (col, row)
        ):
            other = jnp.concatenate([a[HALF:], a[:HALF]], axis=0)
            a = jnp.where(place == 0, a, other) * (1.0 / REPLICAS)
            hi, lo = parts_of(a)
            both = jnp.concatenate([hi, hi, lo], axis=1)
            out[...] = jnp.dot(both, left[...], preferred_element_type=F32)
        stacked([col], COL_ORDER, col_stack)
        stacked([row], ROW_ORDER, row_stack)
        turn(row_stack, row_turned)

    return run(
        kernel,
        [(x, VMEM) for x in (gram_down, left_down, gram_gate, left_gate)],
        [((4 * RANK, cols), BF16, VMEM), ((rows, 4 * RANK), BF16, VMEM)],
        [
            pltpu.VMEM((RANK, cols), F32),
            pltpu.VMEM((RANK, rows), F32),
            pltpu.VMEM((4 * RANK, rows), BF16),
        ],
        mib=6,
        after=after,
    )


def rebuild(run, ready, owns, others, fixed, shares, height, first=0, before=None, after=()):
    rows, cols = fixed.shape
    share = rows // REPLICAS
    parts = share // height
    rows_late = ready[0] is None
    late_width = sum(widths_of(owns))
    width = ready[1].shape[1] if rows_late or not owns else late_width
    n_ready = sum(x is not None for x in ready)
    n_own, n_late = len(owns), len(owns) + len(others)
    n_before = 0 if before is None else len(before)
    with_update = 0 in shares
    spots = [(s, t, j) for s in shares for t in range(parts) for j in range(0, width, TILE)]

    def kernel(*refs):
        given, late = refs[:n_ready], refs[n_ready : n_ready + n_late]
        fixed = refs[n_ready + n_late]
        refs = refs[n_ready + n_late + 1 + n_before :]
        new_error, update, turned = refs[0], refs[1], refs[2]
        errors, updates, stack, error_sems, update_sems = refs[3:]
        if late:
            order = ROW_ORDER if rows_late else COL_ORDER
            for at, pieces in ((0, late[:n_own]), (HALF, late[n_own:])):
                left = 0
                for ref in pieces:
                    split = parts_of(ref[...])
                    n, w = ref.shape
                    for k, which in enumerate(order):
                        stack[k * RANK + at : k * RANK + at + n, left : left + w] = split[which]
                    left += w
        if rows_late:
            turn(stack, turned)
            row, col = turned, given[0]
        else:
            turned[...] = jnp.zeros_like(turned)
            row, col = given[0], given[1] if n_ready == 2 else stack
        replica = replica_of()
        copies = []
        for k, (s, t, j) in enumerate(spots):
            at = pl.multiple_of((replica if s == 0 else 1 - replica) * share, height) + t * height
            at = pl.ds(pl.multiple_of(at, height), height)
            here, there = slice(j, j + TILE), pl.ds(first + j, TILE)
            mine = pl.ds(t * height, height)
            value = jnp.dot(row[at, :], col[:, here], preferred_element_type=F32)
            slot = pl.ds((shares.index(s) * parts + t) * height, height)
            errors[slot, here] = (fixed[at, there].astype(F32) - value).astype(BF16)
            copies.append(
                pltpu.make_async_copy(errors.at[slot, here], new_error.at[at, there], error_sems.at[k])
            )
            copies[-1].start()
            if s == 0:
                updates[mine, here] = value.astype(BF16)
                copies.append(
                    pltpu.make_async_copy(updates.at[mine, here], update.at[mine, there], update_sems.at[k])
                )
                copies[-1].start()
        for copy in copies:
            copy.wait()

    turned_shape = (rows, 4 * RANK) if rows_late else (16, 128)
    args = [(x, VMEM) for x in (*(x for x in ready if x is not None), *owns, *others, fixed)]
    aliases = None
    if before is not None:
        aliases = {len(args): 0, len(args) + 1: 1}
        args += [(x, HBM) for x in before]
    return run(
        kernel,
        args,
        [((rows, cols), BF16, HBM), ((share, cols), BF16, HBM), (turned_shape, BF16, VMEM)],
        [
            pltpu.VMEM((len(shares) * share, width), BF16),
            pltpu.VMEM((share if with_update else 16, width), BF16),
            pltpu.VMEM((4 * RANK, late_width if n_late else 128), BF16),
            pltpu.SemaphoreType.DMA((len(spots),)),
            pltpu.SemaphoreType.DMA((len(spots),)),
        ],
        mib=18,
        aliases=aliases,
        after=after,
    )


def local(grad_gate, grad_down, error_gate, error_down, start_gate, start_down):
    slab, width = grad_gate.shape
    n_dp, n_t = lax.axis_size("dp"), lax.axis_size("tensor")
    run = Calls()
    hops, steps = row_steps(), col_steps()
    tiles = slab // TILE

    _, fixed_down, keep, give = down_left(run, grad_down, error_down, start_down, 0, tiles)
    got = exchange(give, other_replica)
    gate_args = (run, grad_gate, error_gate, start_gate)
    cut = tiles * 3 // 5
    first = gate_left(*gate_args, 0, cut, after=(keep,))
    (down,) = add(run, [keep], [got], after=(first[0],))
    got = exchange(down, steps[0])
    _, fixed_gate, keep_gate, *gives = gate_left(
        *gate_args, cut, tiles - cut, first, after=(down,)
    )
    (gate,) = add(run, [keep_gate], to_other_core(gives))
    got_gate = exchange(gate, hops[0])
    for i in range(len(steps)):
        (down,) = add(run, [down], [got], after=(gate,))
        if i + 1 < len(steps):
            got = exchange(down, steps[i + 1])
    other_down = exchange(down, other_replica)
    for hop in hops[1:]:
        (gate,) = add(run, [gate], [got_gate], after=(down,))
        got_gate = exchange(gate, hop)

    keep, *gives, left_down = down_right(run, [down], [other_down], fixed_down, after=(gate,))
    gots = to_other_core(gives)
    gates = add(run, [gate], [got_gate], after=(keep,))
    others_gate = to_other_core(gates)
    down, gram_down = add(run, [keep], gots, [slab, 2 * RANK], after=(gates[0],))
    grams_down = [gram_down] + [
        exchange(gram_down, lambda d, t, b=b: (d, t ^ b)) for b in range(2, n_t, 2)
    ]
    got = exchange(down, hops[0])
    keep_gate, give_gate, gram_gate, left_gate = gate_right(
        run, gates, others_gate, fixed_gate, after=(down,)
    )
    got_gate = exchange(give_gate, other_replica)
    grams_gate = [gram_gate] + [
        exchange(gram_gate, lambda d, t, b=b: (d ^ b, t)) for b in range(REPLICAS, n_dp, REPLICAS)
    ]
    for hop in hops[1:]:
        (down,) = add(run, [down], [got], after=(gram_gate,))
        got = exchange(down, hop)
    gram_down, gram_gate = gram_sums(run, grams_down, grams_gate, after=(down,))
    (gate,) = add(run, [keep_gate], [got_gate], after=(gram_gate,))
    got_gate = exchange(gate, steps[0])
    col_stack, row_turned = solve(run, gram_down, left_down, gram_gate, left_gate, after=(gate,))
    downs = add(run, [down], [got], in_two(slab), after=(col_stack,))
    others_down = to_other_core(downs)
    *outs_down, turned = rebuild(
        run, (None, col_stack), downs, others_down, fixed_down, (0,), slab // 8, after=(downs[0],)
    )
    few = width // TILE * 3 // 7 * TILE
    for i in range(len(steps)):
        last = i + 1 == len(steps)
        gate = add(run, [gate], [got_gate], [few, width - few] if last else None, after=(turned,))
        if not last:
            (gate,) = gate
            got_gate = exchange(gate, steps[i + 1])
    others_gate = [exchange(x, other_replica) for x in gate]
    new_error_down, update_down, done = rebuild(
        run, (turned, col_stack), [], [], fixed_down, (1,), slab // 8, before=outs_down, after=(gate[0],)
    )
    *outs_gate, done = rebuild(
        run, (row_turned, None), gate[:1], others_gate[:1], fixed_gate, (0, 1), slab // 8, after=(done,)
    )
    new_error_gate, update_gate, _ = rebuild(
        run, (row_turned, None), gate[1:], others_gate[1:], fixed_gate, (0, 1), slab // 8, few, outs_gate,
        after=(done,),
    )
    return (update_gate, update_down, new_error_gate, new_error_down)


def solution(mesh):
    split = P(("mix", "dp"), "tensor")
    in_specs = (split, split, split, split, P(None, "tensor"), P())
    out_specs = (split, split, split, split)

    def run(grad_gate, *rest):
        groups = mesh.shape["mix"] * mesh.shape["dp"]
        slab = grad_gate.shape[0] // groups
        width = grad_gate.shape[1] // mesh.shape["tensor"]
        fits = slab % (REPLICAS * TILE) == 0 and width % TILE == 0
        body = local if fits else local_plain
        return jax.shard_map(
            body, mesh=mesh, in_specs=in_specs, out_specs=out_specs, check_vma=False
        )(grad_gate, *rest)

    return run
```

```python
import functools

import jax
import jax.numpy as jnp
from jax import lax
from jax.experimental import pallas as pl
from jax.experimental.pallas import tpu as pltpu
from jax.sharding import PartitionSpec as P

REPLICAS = 2
RANK = 64
TILE = 256
FLOPS = 1.15e9
WEIGHTS = (8.0, 4.0, 1.0, 4.0, 0.1, 5.0, 1.0, 5.0, 1.0, 4.0, 1.0, 0.1, 1.0, 0.1, 5.0, 1.0, 1.0, 8.0, 8.0)
MIB = 1 << 20
BF16 = jnp.bfloat16
F32 = jnp.float32

NN = (((1,), (0,)), ((), ()))
NT = (((1,), (1,)), ((), ()))
TN = (((0,), (0,)), ((), ()))


def from_partner(shard, axis, stride):
    return lax.ppermute(shard, axis, [(i, i ^ 1 << stride) for i in range(lax.axis_size(axis))])


def corrected(grad, error):
    return (grad.astype(F32) + error.astype(F32)).astype(BF16)


def transposed(matrix, ortho):
    return lax.dot_general(matrix, ortho.astype(BF16), TN, preferred_element_type=F32)


def gram_of(left):
    return jnp.dot(left.T, left, precision=lax.Precision.HIGHEST)


def factored(left, inner):
    lower = jnp.linalg.cholesky(inner)
    return lax.linalg.triangular_solve(lower, left, left_side=False, lower=True, transpose_a=True)


def local_plain(grad_gate, grad_down, error_gate, error_down, start_gate, start_down):
    high = lax.Precision.HIGHEST
    dp_place = lax.axis_index("dp")
    block = dp_place // REPLICAS
    replica = dp_place % REPLICAS
    fixed_gate = corrected(grad_gate, error_gate)
    fixed_down = corrected(grad_down, error_down)
    slab = fixed_gate.shape[0]
    cols_down = lax.dynamic_slice_in_dim(start_down, block * slab, slab, 1)
    left_gate = lax.dot_general(fixed_gate, start_gate, NT, preferred_element_type=F32)
    left_down = lax.dot_general(
        fixed_down, cols_down, (((0,), (1,)), ((), ())), preferred_element_type=F32
    )
    left_gate = lax.psum(left_gate, "tensor")
    left_gate = left_gate + from_partner(left_gate, "dp", 0)
    left_down = lax.psum(left_down, "dp")
    keep_gate = (replica == 0).astype(F32)
    inner_gate = lax.psum(gram_of(left_gate) * keep_gate, "dp")
    inner_down = lax.psum(gram_of(left_down), "tensor")
    ortho_gate = factored(left_gate, inner_gate)
    ortho_down = factored(left_down, inner_down)
    right_gate = transposed(fixed_gate, ortho_gate)
    right_gate = lax.psum(right_gate, "dp") / REPLICAS
    right_down = jnp.dot(fixed_down, ortho_down.astype(BF16), preferred_element_type=F32)
    right_down = lax.psum(right_down, "tensor")
    right_down = right_down + from_partner(right_down, "dp", 0)
    right_down = right_down / REPLICAS
    rebuilt_gate = jnp.dot(ortho_gate, right_gate.T, precision=high)
    rebuilt_down = jnp.dot(right_down, ortho_down.T, precision=high)
    share = slab // REPLICAS
    update_gate = lax.dynamic_slice_in_dim(rebuilt_gate, replica * share, share, 0).astype(BF16)
    update_down = lax.dynamic_slice_in_dim(rebuilt_down, replica * share, share, 0).astype(BF16)
    new_error_gate = (fixed_gate.astype(F32) - rebuilt_gate).astype(BF16)
    new_error_down = (fixed_down.astype(F32) - rebuilt_down).astype(BF16)
    return (update_gate, update_down, new_error_gate, new_error_down)


def core_of():
    return lax.rem(lax.axis_index("tensor"), 2)


def replica_of():
    return lax.rem(lax.axis_index("dp"), REPLICAS)


def exchange(x, partner):
    n_dp, n_t = lax.axis_size("dp"), lax.axis_size("tensor")
    pairs = []
    for d in range(n_dp):
        for t in range(n_t):
            to_d, to_t = partner(d, t)
            pairs.append((d * n_t + t, to_d * n_t + to_t))
    return lax.ppermute(x, ("dp", "tensor"), pairs)


def bits(n, low):
    out, b = [], low
    while b < n:
        out.append(b)
        b *= 2
    return out


def row_steps():
    steps = [(0, b) for b in bits(lax.axis_size("tensor"), 2)] + [(1, 0)]

    def partner(i, d, t):
        r, b = steps[i] if t % 2 == 0 else steps[-1 - i]
        return d ^ r, t ^ b

    return [functools.partial(partner, i) for i in range(len(steps))]


def col_steps():
    return [lambda d, t, b=b: (d ^ b, t) for b in bits(lax.axis_size("dp"), REPLICAS)]


def other_core(d, t):
    return d, t ^ 1


def other_replica(d, t):
    return d ^ 1, t


def to_other_core(pieces):
    return [exchange(x, other_core) for x in pieces]


VMEM = pl.BlockSpec(memory_space=pltpu.VMEM)
HBM = pl.BlockSpec(memory_space=pltpu.HBM)
ANY = pl.BlockSpec(memory_space=pl.ANY)
HALF = RANK // 2


class Calls:
    def __init__(self):
        self.count = 0

    def __call__(self, kernel, args, outs, scratch=(), mib=8, aliases=None, after=()):
        n_in, n_after = len(args), len(after)
        operands = [
            pltpu.with_memory_space_constraint(x, pltpu.VMEM if spec is VMEM else pltpu.HBM)
            for x, spec in args
        ]

        def body(*refs):
            kernel(*refs[:n_in], *refs[n_in + n_after :])

        out = pl.pallas_call(
            body,
            out_shape=tuple(
                (pltpu.VMEM if spec is VMEM else pltpu.HBM)(shape, kind) for shape, kind, spec in outs
            ),
            in_specs=[spec for _, spec in args] + [ANY] * n_after,
            out_specs=tuple(spec for *_, spec in outs),
            scratch_shapes=list(scratch),
            input_output_aliases=aliases or {},
            compiler_params=pltpu.CompilerParams(vmem_limit_bytes=mib * MIB),
            cost_estimate=pl.CostEstimate(
                flops=int(WEIGHTS[self.count] * FLOPS), bytes_accessed=1 << 10, transcendentals=0
            ),
        )(*operands, *after)
        self.count += 1
        return out


def parts_of(x):
    hi = x.astype(BF16)
    lo = (x - hi.astype(F32)).astype(BF16)
    return hi, lo


def spans(*widths):
    edges = sorted({sum(w[:i]) for w in widths for i in range(len(w) + 1)})
    for low, high in zip(edges, edges[1:]):
        places = []
        for w in widths:
            k = max(i for i in range(len(w)) if sum(w[:i]) <= low)
            places.append((k, low - sum(w[:k]), high - sum(w[:k])))
        yield places


def widths_of(refs):
    return [ref.shape[1] for ref in refs]


def add(run, xs, ys, widths=None, after=()):
    widths = widths or widths_of(xs)
    n_x, n_y = len(xs), len(ys)

    def kernel(*refs):
        x, y, out = refs[:n_x], refs[n_x : n_x + n_y], refs[n_x + n_y :]
        for (i, i0, i1), (j, j0, j1), (k, k0, k1) in spans(widths_of(x), widths_of(y), widths):
            out[k][:, k0:k1] = x[i][:, i0:i1] + y[j][:, j0:j1]

    outs = [((HALF, n), F32, VMEM) for n in widths]
    return list(run(kernel, [(x, VMEM) for x in (*xs, *ys)], outs, mib=2, after=after))


def in_two(width):
    cut = width // 256 * 128
    return [cut, width - cut]


def halve(whole, place, keep, gives):
    keep[...] = whole[pl.ds(pl.multiple_of(place * HALF, HALF), HALF), :]
    at = 0
    for give in gives:
        n = give.shape[1]
        give[...] = whole[pl.ds(pl.multiple_of((1 - place) * HALF, HALF), HALF), at : at + n]
        at += n


def tile_at(i):
    return pl.ds(pl.multiple_of(i * TILE, TILE), TILE)


def gate_left(run, grad, error, start, first, count, before=None, after=()):
    rows, cols = grad.shape
    last = (first + count) * TILE == rows

    def kernel(grad, error, start, *refs):
        if before is not None:
            refs = refs[2:]
        left, fixed = refs[:2]

        def step(g, e):
            at = tile_at(first + pl.program_id(0))
            term = jnp.zeros((RANK, TILE), F32)
            for j in range(0, cols, TILE):
                here = slice(j, j + TILE)
                c = g[:, here] + e[:, here]
                fixed[at, here] = c
                term += lax.dot_general(start[:, here], c, NT, preferred_element_type=F32)
            left[:, at] = term

        spec = pl.BlockSpec((TILE, cols), lambda i: (first + i, 0), pipeline_mode=pl.Buffered(3))
        pltpu.emit_pipeline(step, grid=(count,), in_specs=[spec, spec])(grad, error)
        if last:
            halve(left, core_of(), refs[2], refs[3:])

    args = [(grad, HBM), (error, HBM), (start, VMEM)]
    outs = [((RANK, rows), F32, VMEM), ((rows, cols), BF16, VMEM)]
    if last:
        outs += [((HALF, n), F32, VMEM) for n in (rows, *in_two(rows))]
    aliases = None
    if before is not None:
        args += [(x, VMEM) for x in before]
        aliases = {3: 0, 4: 1}
    return run(kernel, args, outs, mib=8, aliases=aliases, after=after)


def down_left(run, grad, error, start, first, count, before=None, after=()):
    rows, cols = grad.shape
    last = (first + count) * TILE == rows

    def kernel(grad, error, start, *refs):
        if before is not None:
            refs = refs[2:]
        left, fixed = refs[:2]
        pair = 2 * TILE
        block = lax.div(lax.axis_index("dp"), REPLICAS) * (rows // pair) + first // 2
        if before is None:
            left[...] = jnp.zeros_like(left)

        def step(g, e, s):
            i = pl.program_id(0)
            at = tile_at(first + i)
            for j in range(0, cols, TILE):
                here = slice(j, j + TILE)
                fixed[at, here] = g[:, here] + e[:, here]

            @pl.when(lax.rem(i, 2) == 1)
            def _():
                both = pl.ds(pl.multiple_of((first + i - 1) * TILE, pair), pair)
                for j in range(0, cols, TILE):
                    here = slice(j, j + TILE)
                    left[:, here] += jnp.dot(s[...], fixed[both, here], preferred_element_type=F32)

        spec = pl.BlockSpec((TILE, cols), lambda i: (first + i, 0), pipeline_mode=pl.Buffered(3))
        part = pl.BlockSpec((RANK, pair), lambda i: (0, block + lax.div(i, 2)))
        pltpu.emit_pipeline(step, grid=(count,), in_specs=[spec, spec, part])(grad, error, start)
        if last:
            halve(left, replica_of(), refs[2], refs[3:])

    args = [(grad, HBM), (error, HBM), (start, HBM)]
    outs = [((RANK, cols), F32, VMEM), ((rows, cols), BF16, VMEM)]
    if last:
        outs += [((HALF, cols), F32, VMEM)] * 2
    aliases = None
    if before is not None:
        args += [(x, VMEM) for x in before]
        aliases = {3: 0, 4: 1}
    return run(kernel, args, outs, mib=8, aliases=aliases, after=after)


def load_left(owns, others, place, left, stack):
    for refs, half in ((owns, place), (others, 1 - place)):
        at = 0
        for ref in refs:
            n = ref.shape[1]
            left[pl.ds(pl.multiple_of(half * HALF, HALF), HALF), at : at + n] = ref[...]
            at += n
    hi, lo = parts_of(left[...])
    stack[:RANK, :] = hi
    stack[RANK : 2 * RANK, :] = lo
    stack[2 * RANK :, :] = hi
    parts = stack[: 2 * RANK]
    gram = lax.dot_general(parts, parts, NT, preferred_element_type=F32)
    mixed = gram[:RANK, RANK:] + gram[RANK:, :RANK]
    return gram[:RANK, :RANK] + (mixed + gram[RANK:, RANK:])


def gate_right(run, owns, others, fixed, after=()):
    rows, cols = fixed.shape
    n_own, n_both = len(owns), len(owns) + len(others)

    def kernel(*refs):
        fixed, keep, give, gram, stack, left, right = refs[n_both:]
        gram[...] = load_left(refs[:n_own], refs[n_own:n_both], core_of(), left, stack)

        def step(i, _):
            both = jnp.dot(stack[: 2 * RANK], fixed[:, tile_at(i)], preferred_element_type=F32)
            right[:, tile_at(i)] = both[:RANK] + both[RANK:]
            return 0

        lax.fori_loop(0, cols // TILE, step, 0)
        halve(right, replica_of(), keep, [give])

    return run(
        kernel,
        [(x, VMEM) for x in (*owns, *others, fixed)],
        [((HALF, cols), F32, VMEM)] * 2 + [((RANK, RANK), F32, VMEM), ((3 * RANK, rows), BF16, VMEM)],
        [pltpu.VMEM((RANK, rows), F32), pltpu.VMEM((RANK, cols), F32)],
        mib=4,
        after=after,
    )


def down_right(run, owns, others, fixed, after=()):
    rows, cols = fixed.shape
    n_own, n_both = len(owns), len(owns) + len(others)
    cut, rest = in_two(rows)

    def kernel(*refs):
        fixed, keep, give_1, give_2, stack, left, right = refs[n_both:]
        gram = load_left(refs[:n_own], refs[n_own:n_both], replica_of(), left, stack)

        def step(i, _):
            both = lax.dot_general(stack[: 2 * RANK], fixed[tile_at(i), :], NT, preferred_element_type=F32)
            right[:, tile_at(i)] = both[:RANK] + both[RANK:]
            return 0

        lax.fori_loop(0, rows // TILE, step, 0)
        packed = jnp.concatenate([gram[:HALF], gram[HALF:]], axis=1)
        halve(right, core_of(), keep.at[:, :rows], [give_1, give_2.at[:, :rest]])
        keep[:, rows:] = packed
        give_2[:, rest:] = packed

    widths = (rows + 2 * RANK, cut, rest + 2 * RANK)
    return run(
        kernel,
        [(x, VMEM) for x in (*owns, *others, fixed)],
        [((HALF, n), F32, VMEM) for n in widths] + [((3 * RANK, cols), BF16, VMEM)],
        [pltpu.VMEM((RANK, cols), F32), pltpu.VMEM((RANK, rows), F32)],
        mib=4,
        after=after,
    )


def inverses(grams):
    row_at = lax.broadcasted_iota(jnp.int32, (RANK, RANK), 0)
    col_at = lax.broadcasted_iota(jnp.int32, (RANK, RANK), 1)
    lane = lax.broadcasted_iota(jnp.int32, (1, RANK), 1)

    def scaled(a):
        diagonal = jnp.where(row_at == col_at, a, 0.0)
        down = lax.rsqrt(jnp.sum(diagonal, axis=1, keepdims=True))
        across = lax.rsqrt(jnp.sum(diagonal, axis=0, keepdims=True))
        return a * down * across, down, across

    def sweep(a, k):
        one, two = (row_at == k, row_at == k + 1)
        here = one | two | (col_at == k) | (col_at == k + 1)
        col_1 = jnp.broadcast_to(a[:, k : k + 1], (RANK, RANK))
        col_2 = jnp.broadcast_to(a[:, k + 1 : k + 2], (RANK, RANK))
        p, q, r = col_1[k : k + 1], col_2[k : k + 1], col_2[k + 1 : k + 2]
        row_1 = jnp.where(lane == k, 1.0, jnp.where(lane == k + 1, 0.0, a[k : k + 1]))
        row_2 = jnp.where(lane == k + 1, 1.0, jnp.where(lane == k, 0.0, a[k + 1 : k + 2]))
        inv = 1.0 / (p * r - q * q)
        new_1 = (r * row_1 - q * row_2) * inv
        new_2 = (p * row_2 - q * row_1) * inv
        col_1 = jnp.where(one, -1.0, jnp.where(two, 0.0, col_1))
        col_2 = jnp.where(two, -1.0, jnp.where(one, 0.0, col_2))
        return jnp.where(here, 0.0, a) - col_1 * new_1 - col_2 * new_2

    systems = [scaled(a) for a in grams]
    values = [a for a, _, _ in systems]
    for k in range(0, RANK, 2):
        values = [sweep(a, k) for a in values]
    return [a * down * across for a, (_, down, across) in zip(values, systems)]


def stacked(refs, order, stack):
    at = 0
    for ref in refs:
        parts = parts_of(ref[...])
        n = ref.shape[0]
        for k, which in enumerate(order):
            stack[k * RANK + at : k * RANK + at + n, :] = parts[which]
        at += n


ROW_ORDER, COL_ORDER = (0, 1, 0, 1), (0, 0, 1, 1)


def turn(stack, turned):
    for i in range(0, stack.shape[1], TILE):
        turned[i : i + TILE, :] = stack[:, i : i + TILE].T


def gram_sums(run, packed, whole, after=()):
    n = len(packed)

    def kernel(*refs):
        a = sum((ref[...] for ref in refs[1:n]), refs[0][...])
        refs[-2][...] = jnp.concatenate([a[:, :RANK], a[:, RANK:]], axis=0)
        refs[-1][...] = sum((ref[...] for ref in refs[n + 1 : -2]), refs[n][...])

    outs = [((RANK, RANK), F32, VMEM)] * 2
    return run(kernel, [(x, VMEM) for x in (*packed, *whole)], outs, mib=2, after=after)


def solve(run, gram_down, left_down, gram_gate, left_gate, after=()):
    cols, rows = left_down.shape[1], left_gate.shape[1]

    def kernel(gram_down, left_down, gram_gate, left_gate, col_stack, row_turned, col, row, row_stack):
        grams = [gram_down[...], gram_gate[...]]
        for place, a, left, out in zip(
            (core_of(), replica_of()), inverses(grams), (left_down, left_gate), (col, row)
        ):
            other = jnp.concatenate([a[HALF:], a[:HALF]], axis=0)
            a = jnp.where(place == 0, a, other) * (1.0 / REPLICAS)
            hi, lo = parts_of(a)
            both = jnp.concatenate([hi, hi, lo], axis=1)
            out[...] = jnp.dot(both, left[...], preferred_element_type=F32)
        stacked([col], COL_ORDER, col_stack)
        stacked([row], ROW_ORDER, row_stack)
        turn(row_stack, row_turned)

    return run(
        kernel,
        [(x, VMEM) for x in (gram_down, left_down, gram_gate, left_gate)],
        [((4 * RANK, cols), BF16, VMEM), ((rows, 4 * RANK), BF16, VMEM)],
        [
            pltpu.VMEM((RANK, cols), F32),
            pltpu.VMEM((RANK, rows), F32),
            pltpu.VMEM((4 * RANK, rows), BF16),
        ],
        mib=6,
        after=after,
    )


def rebuild(run, ready, owns, others, fixed, shares, height, first=0, before=None, after=()):
    rows, cols = fixed.shape
    share = rows // REPLICAS
    parts = share // height
    rows_late = ready[0] is None
    late_width = sum(widths_of(owns))
    width = ready[1].shape[1] if rows_late or not owns else late_width
    n_ready = sum(x is not None for x in ready)
    n_own, n_late = len(owns), len(owns) + len(others)
    n_before = 0 if before is None else len(before)
    with_update = 0 in shares
    spots = [(s, t, j) for s in shares for t in range(parts) for j in range(0, width, TILE)]

    def kernel(*refs):
        given, late = refs[:n_ready], refs[n_ready : n_ready + n_late]
        fixed = refs[n_ready + n_late]
        refs = refs[n_ready + n_late + 1 + n_before :]
        new_error, update, turned = refs[0], refs[1], refs[2]
        errors, updates, stack, error_sems, update_sems = refs[3:]
        if late:
            order = ROW_ORDER if rows_late else COL_ORDER
            for at, pieces in ((0, late[:n_own]), (HALF, late[n_own:])):
                left = 0
                for ref in pieces:
                    split = parts_of(ref[...])
                    n, w = ref.shape
                    for k, which in enumerate(order):
                        stack[k * RANK + at : k * RANK + at + n, left : left + w] = split[which]
                    left += w
        if rows_late:
            turn(stack, turned)
            row, col = turned, given[0]
        else:
            turned[...] = jnp.zeros_like(turned)
            row, col = given[0], given[1] if n_ready == 2 else stack
        replica = replica_of()
        copies = []
        for k, (s, t, j) in enumerate(spots):
            at = pl.multiple_of((replica if s == 0 else 1 - replica) * share, height) + t * height
            at = pl.ds(pl.multiple_of(at, height), height)
            here, there = slice(j, j + TILE), pl.ds(first + j, TILE)
            mine = pl.ds(t * height, height)
            value = jnp.dot(row[at, :], col[:, here], preferred_element_type=F32)
            slot = pl.ds((shares.index(s) * parts + t) * height, height)
            errors[slot, here] = (fixed[at, there].astype(F32) - value).astype(BF16)
            copies.append(
                pltpu.make_async_copy(errors.at[slot, here], new_error.at[at, there], error_sems.at[k])
            )
            copies[-1].start()
            if s == 0:
                updates[mine, here] = value.astype(BF16)
                copies.append(
                    pltpu.make_async_copy(updates.at[mine, here], update.at[mine, there], update_sems.at[k])
                )
                copies[-1].start()
        for copy in copies:
            copy.wait()

    turned_shape = (rows, 4 * RANK) if rows_late else (16, 128)
    args = [(x, VMEM) for x in (*(x for x in ready if x is not None), *owns, *others, fixed)]
    aliases = None
    if before is not None:
        aliases = {len(args): 0, len(args) + 1: 1}
        args += [(x, HBM) for x in before]
    return run(
        kernel,
        args,
        [((rows, cols), BF16, HBM), ((share, cols), BF16, HBM), (turned_shape, BF16, VMEM)],
        [
            pltpu.VMEM((len(shares) * share, width), BF16),
            pltpu.VMEM((share if with_update else 16, width), BF16),
            pltpu.VMEM((4 * RANK, late_width if n_late else 128), BF16),
            pltpu.SemaphoreType.DMA((len(spots),)),
            pltpu.SemaphoreType.DMA((len(spots),)),
        ],
        mib=18,
        aliases=aliases,
        after=after,
    )


def local(grad_gate, grad_down, error_gate, error_down, start_gate, start_down):
    slab, width = grad_gate.shape
    n_dp, n_t = lax.axis_size("dp"), lax.axis_size("tensor")
    run = Calls()
    hops, steps = row_steps(), col_steps()
    tiles = slab // TILE

    _, fixed_down, keep, give = down_left(run, grad_down, error_down, start_down, 0, tiles)
    got = exchange(give, other_replica)
    gate_args = (run, grad_gate, error_gate, start_gate)
    cut = tiles * 3 // 5
    first = gate_left(*gate_args, 0, cut, after=(keep,))
    (down,) = add(run, [keep], [got], after=(first[0],))
    got = exchange(down, steps[0])
    _, fixed_gate, keep_gate, *gives = gate_left(
        *gate_args, cut, tiles - cut, first, after=(down,)
    )
    (gate,) = add(run, [keep_gate], to_other_core(gives))
    got_gate = exchange(gate, hops[0])
    for i in range(len(steps)):
        (down,) = add(run, [down], [got], after=(gate,))
        if i + 1 < len(steps):
            got = exchange(down, steps[i + 1])
    other_down = exchange(down, other_replica)
    for hop in hops[1:]:
        (gate,) = add(run, [gate], [got_gate], after=(down,))
        got_gate = exchange(gate, hop)

    keep, *gives, left_down = down_right(run, [down], [other_down], fixed_down, after=(gate,))
    gots = to_other_core(gives)
    gates = add(run, [gate], [got_gate], after=(keep,))
    others_gate = to_other_core(gates)
    keep_gate, give_gate, gram_gate, left_gate = gate_right(run, gates, others_gate, fixed_gate)
    got_gate = exchange(give_gate, other_replica)
    grams_gate = [gram_gate] + [
        exchange(gram_gate, lambda d, t, b=b: (d ^ b, t)) for b in range(REPLICAS, n_dp, REPLICAS)
    ]
    down, gram_down = add(run, [keep], gots, [slab, 2 * RANK], after=(gram_gate,))
    grams_down = [gram_down] + [
        exchange(gram_down, lambda d, t, b=b: (d, t ^ b)) for b in range(2, n_t, 2)
    ]
    got = exchange(down, hops[0])
    gram_down, gram_gate = gram_sums(run, grams_down, grams_gate)
    (gate,) = add(run, [keep_gate], [got_gate], after=(gram_gate,))
    got_gate = exchange(gate, steps[0])
    for hop in hops[1:]:
        (down,) = add(run, [down], [got], after=(gate,))
        got = exchange(down, hop)
    col_stack, row_turned = solve(
        run, gram_down, left_down, gram_gate, left_gate, after=(down,)
    )
    downs = add(run, [down], [got], in_two(slab), after=(col_stack,))
    others_down = to_other_core(downs)
    for i in range(len(steps)):
        (gate,) = add(run, [gate], [got_gate], after=(downs[0],))
        if i + 1 < len(steps):
            got_gate = exchange(gate, steps[i + 1])
    other_gate = exchange(gate, other_replica)
    new_error_down, update_down, done = rebuild(
        run, (None, col_stack), downs, others_down, fixed_down, (0, 1), slab // 8, after=(gate,)
    )
    new_error_gate, update_gate, _ = rebuild(
        run, (row_turned, None), [gate], [other_gate], fixed_gate, (0, 1), slab // 8, after=(done,)
    )
    return (update_gate, update_down, new_error_gate, new_error_down)


def solution(mesh):
    split = P(("mix", "dp"), "tensor")
    in_specs = (split, split, split, split, P(None, "tensor"), P())
    out_specs = (split, split, split, split)

    def run(grad_gate, *rest):
        groups = mesh.shape["mix"] * mesh.shape["dp"]
        slab = grad_gate.shape[0] // groups
        width = grad_gate.shape[1] // mesh.shape["tensor"]
        fits = slab % (REPLICAS * TILE) == 0 and width % TILE == 0
        body = local if fits else local_plain
        return jax.shard_map(
            body, mesh=mesh, in_specs=in_specs, out_specs=out_specs, check_vma=False
        )(grad_gate, *rest)

    return run
```

```python
import functools

import jax
import jax.numpy as jnp
from jax import lax
from jax.experimental import pallas as pl
from jax.experimental.pallas import tpu as pltpu
from jax.sharding import PartitionSpec as P

REPLICAS = 2
RANK = 64
TILE = 256
FLOPS = 1.15e9
WEIGHTS = (8.0, 4.0, 1.0, 4.0, 0.1, 5.0, 1.0, 5.0, 1.0, 1.0, 4.0, 1.0, 1.0, 1.0, 0.1, 5.0, 0.1, 1.0, 8.0, 8.0)
MIB = 1 << 20
BF16 = jnp.bfloat16
F32 = jnp.float32

NN = (((1,), (0,)), ((), ()))
NT = (((1,), (1,)), ((), ()))
TN = (((0,), (0,)), ((), ()))


def from_partner(shard, axis, stride):
    return lax.ppermute(shard, axis, [(i, i ^ 1 << stride) for i in range(lax.axis_size(axis))])


def corrected(grad, error):
    return (grad.astype(F32) + error.astype(F32)).astype(BF16)


def transposed(matrix, ortho):
    return lax.dot_general(matrix, ortho.astype(BF16), TN, preferred_element_type=F32)


def gram_of(left):
    return jnp.dot(left.T, left, precision=lax.Precision.HIGHEST)


def factored(left, inner):
    lower = jnp.linalg.cholesky(inner)
    return lax.linalg.triangular_solve(lower, left, left_side=False, lower=True, transpose_a=True)


def local_plain(grad_gate, grad_down, error_gate, error_down, start_gate, start_down):
    high = lax.Precision.HIGHEST
    dp_place = lax.axis_index("dp")
    block = dp_place // REPLICAS
    replica = dp_place % REPLICAS
    fixed_gate = corrected(grad_gate, error_gate)
    fixed_down = corrected(grad_down, error_down)
    slab = fixed_gate.shape[0]
    cols_down = lax.dynamic_slice_in_dim(start_down, block * slab, slab, 1)
    left_gate = lax.dot_general(fixed_gate, start_gate, NT, preferred_element_type=F32)
    left_down = lax.dot_general(
        fixed_down, cols_down, (((0,), (1,)), ((), ())), preferred_element_type=F32
    )
    left_gate = lax.psum(left_gate, "tensor")
    left_gate = left_gate + from_partner(left_gate, "dp", 0)
    left_down = lax.psum(left_down, "dp")
    keep_gate = (replica == 0).astype(F32)
    inner_gate = lax.psum(gram_of(left_gate) * keep_gate, "dp")
    inner_down = lax.psum(gram_of(left_down), "tensor")
    ortho_gate = factored(left_gate, inner_gate)
    ortho_down = factored(left_down, inner_down)
    right_gate = transposed(fixed_gate, ortho_gate)
    right_gate = lax.psum(right_gate, "dp") / REPLICAS
    right_down = jnp.dot(fixed_down, ortho_down.astype(BF16), preferred_element_type=F32)
    right_down = lax.psum(right_down, "tensor")
    right_down = right_down + from_partner(right_down, "dp", 0)
    right_down = right_down / REPLICAS
    rebuilt_gate = jnp.dot(ortho_gate, right_gate.T, precision=high)
    rebuilt_down = jnp.dot(right_down, ortho_down.T, precision=high)
    share = slab // REPLICAS
    update_gate = lax.dynamic_slice_in_dim(rebuilt_gate, replica * share, share, 0).astype(BF16)
    update_down = lax.dynamic_slice_in_dim(rebuilt_down, replica * share, share, 0).astype(BF16)
    new_error_gate = (fixed_gate.astype(F32) - rebuilt_gate).astype(BF16)
    new_error_down = (fixed_down.astype(F32) - rebuilt_down).astype(BF16)
    return (update_gate, update_down, new_error_gate, new_error_down)


def core_of():
    return lax.rem(lax.axis_index("tensor"), 2)


def pair_of():
    return lax.rem(lax.div(lax.axis_index("tensor"), 2), 2)


def replica_of():
    return lax.rem(lax.axis_index("dp"), REPLICAS)


def exchange(x, partner):
    n_dp, n_t = lax.axis_size("dp"), lax.axis_size("tensor")
    pairs = []
    for d in range(n_dp):
        for t in range(n_t):
            to_d, to_t = partner(d, t)
            pairs.append((d * n_t + t, to_d * n_t + to_t))
    return lax.ppermute(x, ("dp", "tensor"), pairs)


def bits(n, low):
    out, b = [], low
    while b < n:
        out.append(b)
        b *= 2
    return out


def row_steps():
    steps = [(0, b) for b in bits(lax.axis_size("tensor"), 2)] + [(1, 0)]

    def partner(i, d, t):
        r, b = steps[i] if t % 2 == 0 else steps[-1 - i]
        return d ^ r, t ^ b

    return [functools.partial(partner, i) for i in range(len(steps))]


def col_steps():
    return [lambda d, t, b=b: (d ^ b, t) for b in bits(lax.axis_size("dp"), REPLICAS)]


def other_core(d, t):
    return d, t ^ 1


def other_replica(d, t):
    return d ^ 1, t


def other_pair(d, t):
    return d, t ^ 2


def to_other_core(pieces):
    return [exchange(x, other_core) for x in pieces]


VMEM = pl.BlockSpec(memory_space=pltpu.VMEM)
HBM = pl.BlockSpec(memory_space=pltpu.HBM)
ANY = pl.BlockSpec(memory_space=pl.ANY)
HALF = RANK // 2


class Calls:
    def __init__(self):
        self.count = 0

    def __call__(self, kernel, args, outs, scratch=(), mib=8, aliases=None, after=()):
        n_in, n_after = len(args), len(after)
        operands = [
            pltpu.with_memory_space_constraint(x, pltpu.VMEM if spec is VMEM else pltpu.HBM)
            for x, spec in args
        ]

        def body(*refs):
            kernel(*refs[:n_in], *refs[n_in + n_after :])

        out = pl.pallas_call(
            body,
            out_shape=tuple(
                (pltpu.VMEM if spec is VMEM else pltpu.HBM)(shape, kind) for shape, kind, spec in outs
            ),
            in_specs=[spec for _, spec in args] + [ANY] * n_after,
            out_specs=tuple(spec for *_, spec in outs),
            scratch_shapes=list(scratch),
            input_output_aliases=aliases or {},
            compiler_params=pltpu.CompilerParams(vmem_limit_bytes=mib * MIB),
            cost_estimate=pl.CostEstimate(
                flops=int(WEIGHTS[self.count] * FLOPS), bytes_accessed=1 << 10, transcendentals=0
            ),
        )(*operands, *after)
        self.count += 1
        return out


def parts_of(x):
    hi = x.astype(BF16)
    lo = (x - hi.astype(F32)).astype(BF16)
    return hi, lo


def spans(*widths):
    edges = sorted({sum(w[:i]) for w in widths for i in range(len(w) + 1)})
    for low, high in zip(edges, edges[1:]):
        places = []
        for w in widths:
            k = max(i for i in range(len(w)) if sum(w[:i]) <= low)
            places.append((k, low - sum(w[:k]), high - sum(w[:k])))
        yield places


def widths_of(refs):
    return [ref.shape[1] for ref in refs]


def add(run, xs, ys, widths=None, after=()):
    widths = widths or widths_of(xs)
    n_x, n_y = len(xs), len(ys)

    def kernel(*refs):
        x, y, out = refs[:n_x], refs[n_x : n_x + n_y], refs[n_x + n_y :]
        for (i, i0, i1), (j, j0, j1), (k, k0, k1) in spans(widths_of(x), widths_of(y), widths):
            out[k][:, k0:k1] = x[i][:, i0:i1] + y[j][:, j0:j1]

    outs = [((xs[0].shape[0], n), F32, VMEM) for n in widths]
    return list(run(kernel, [(x, VMEM) for x in (*xs, *ys)], outs, mib=2, after=after))


def add_halved(run, xs, ys, width, place_of, after=()):
    rest = sum(widths_of(xs)) - width
    n_x, n_y = len(xs), len(ys)
    high = xs[0].shape[0] // 2

    def kernel(*refs):
        x, y = refs[:n_x], refs[n_x : n_x + n_y]
        keep, give, left_over, total = refs[n_x + n_y :]
        for (i, i0, i1), (j, j0, j1), (k, k0, k1) in spans(widths_of(x), widths_of(y), [width, rest]):
            (total, left_over)[k][:, k0:k1] = x[i][:, i0:i1] + y[j][:, j0:j1]
        place = place_of()
        keep[...] = total[pl.ds(pl.multiple_of(place * high, high), high), :]
        give[...] = total[pl.ds(pl.multiple_of((1 - place) * high, high), high), :]

    outs = [((high, width), F32, VMEM)] * 2 + [((2 * high, rest), F32, VMEM)]
    scratch = [pltpu.VMEM((2 * high, width), F32)]
    return run(kernel, [(x, VMEM) for x in (*xs, *ys)], outs, scratch, mib=3, after=after)


def pass_on(run, x, after):
    def kernel(x, out):
        out[...] = x[...]

    return run(kernel, [(x, VMEM)], [(x.shape, F32, VMEM)], mib=2, after=after)[0]


def in_two(width):
    cut = width // 256 * 128
    return [cut, width - cut]


def halve(whole, place, keep, gives):
    keep[...] = whole[pl.ds(pl.multiple_of(place * HALF, HALF), HALF), :]
    at = 0
    for give in gives:
        n = give.shape[1]
        give[...] = whole[pl.ds(pl.multiple_of((1 - place) * HALF, HALF), HALF), at : at + n]
        at += n


def tile_at(i):
    return pl.ds(pl.multiple_of(i * TILE, TILE), TILE)


def gate_left(run, grad, error, start, first, count, before=None, after=()):
    rows, cols = grad.shape
    last = (first + count) * TILE == rows

    def kernel(grad, error, start, *refs):
        if before is not None:
            refs = refs[2:]
        left, fixed = refs[:2]

        def step(g, e):
            at = tile_at(first + pl.program_id(0))
            term = jnp.zeros((RANK, TILE), F32)
            for j in range(0, cols, TILE):
                here = slice(j, j + TILE)
                c = g[:, here] + e[:, here]
                fixed[at, here] = c
                term += lax.dot_general(start[:, here], c, NT, preferred_element_type=F32)
            left[:, at] = term

        spec = pl.BlockSpec((TILE, cols), lambda i: (first + i, 0), pipeline_mode=pl.Buffered(3))
        pltpu.emit_pipeline(step, grid=(count,), in_specs=[spec, spec])(grad, error)
        if last:
            halve(left, core_of(), refs[2], refs[3:])

    args = [(grad, HBM), (error, HBM), (start, VMEM)]
    outs = [((RANK, rows), F32, VMEM), ((rows, cols), BF16, VMEM)]
    if last:
        outs += [((HALF, n), F32, VMEM) for n in (rows, *in_two(rows))]
    aliases = None
    if before is not None:
        args += [(x, VMEM) for x in before]
        aliases = {3: 0, 4: 1}
    return run(kernel, args, outs, mib=8, aliases=aliases, after=after)


def down_left(run, grad, error, start, first, count, before=None, after=()):
    rows, cols = grad.shape
    last = (first + count) * TILE == rows

    def kernel(grad, error, start, *refs):
        if before is not None:
            refs = refs[2:]
        left, fixed = refs[:2]
        pair = 2 * TILE
        block = lax.div(lax.axis_index("dp"), REPLICAS) * (rows // pair) + first // 2
        if before is None:
            left[...] = jnp.zeros_like(left)

        def step(g, e, s):
            i = pl.program_id(0)
            at = tile_at(first + i)
            for j in range(0, cols, TILE):
                here = slice(j, j + TILE)
                fixed[at, here] = g[:, here] + e[:, here]

            @pl.when(lax.rem(i, 2) == 1)
            def _():
                both = pl.ds(pl.multiple_of((first + i - 1) * TILE, pair), pair)
                for j in range(0, cols, TILE):
                    here = slice(j, j + TILE)
                    left[:, here] += jnp.dot(s[...], fixed[both, here], preferred_element_type=F32)

        spec = pl.BlockSpec((TILE, cols), lambda i: (first + i, 0), pipeline_mode=pl.Buffered(3))
        part = pl.BlockSpec((RANK, pair), lambda i: (0, block + lax.div(i, 2)))
        pltpu.emit_pipeline(step, grid=(count,), in_specs=[spec, spec, part])(grad, error, start)
        if last:
            halve(left, replica_of(), refs[2], refs[3:])

    args = [(grad, HBM), (error, HBM), (start, HBM)]
    outs = [((RANK, cols), F32, VMEM), ((rows, cols), BF16, VMEM)]
    if last:
        outs += [((HALF, cols), F32, VMEM)] * 2
    aliases = None
    if before is not None:
        args += [(x, VMEM) for x in before]
        aliases = {3: 0, 4: 1}
    return run(kernel, args, outs, mib=8, aliases=aliases, after=after)


def load_left(owns, others, place, left, stack):
    for refs, half in ((owns, place), (others, 1 - place)):
        at = 0
        for ref in refs:
            n = ref.shape[1]
            left[pl.ds(pl.multiple_of(half * HALF, HALF), HALF), at : at + n] = ref[...]
            at += n
    hi, lo = parts_of(left[...])
    stack[:RANK, :] = hi
    stack[RANK : 2 * RANK, :] = lo
    stack[2 * RANK :, :] = hi
    parts = stack[: 2 * RANK]
    gram = lax.dot_general(parts, parts, NT, preferred_element_type=F32)
    mixed = gram[:RANK, RANK:] + gram[RANK:, :RANK]
    return gram[:RANK, :RANK] + (mixed + gram[RANK:, RANK:])


def gate_right(run, owns, others, fixed, after=()):
    rows, cols = fixed.shape
    n_own, n_both = len(owns), len(owns) + len(others)

    def kernel(*refs):
        fixed, keep, give, gram, stack, left, right = refs[n_both:]
        gram[...] = load_left(refs[:n_own], refs[n_own:n_both], core_of(), left, stack)

        def step(i, _):
            both = jnp.dot(stack[: 2 * RANK], fixed[:, tile_at(i)], preferred_element_type=F32)
            right[:, tile_at(i)] = both[:RANK] + both[RANK:]
            return 0

        lax.fori_loop(0, cols // TILE, step, 0)
        halve(right, replica_of(), keep, [give])

    return run(
        kernel,
        [(x, VMEM) for x in (*owns, *others, fixed)],
        [((HALF, cols), F32, VMEM)] * 2 + [((RANK, RANK), F32, VMEM), ((3 * RANK, rows), BF16, VMEM)],
        [pltpu.VMEM((RANK, rows), F32), pltpu.VMEM((RANK, cols), F32)],
        mib=4,
        after=after,
    )


def down_right(run, owns, others, fixed, after=()):
    rows, cols = fixed.shape
    n_own, n_both = len(owns), len(owns) + len(others)
    cut, rest = in_two(rows)

    def kernel(*refs):
        fixed, keep, give_1, give_2, stack, left, right = refs[n_both:]
        gram = load_left(refs[:n_own], refs[n_own:n_both], replica_of(), left, stack)

        def step(i, _):
            both = lax.dot_general(stack[: 2 * RANK], fixed[tile_at(i), :], NT, preferred_element_type=F32)
            right[:, tile_at(i)] = both[:RANK] + both[RANK:]
            return 0

        lax.fori_loop(0, rows // TILE, step, 0)
        packed = jnp.concatenate([gram[:HALF], gram[HALF:]], axis=1)
        halve(right, core_of(), keep.at[:, :rows], [give_1, give_2.at[:, :rest]])
        keep[:, rows:] = packed
        give_2[:, rest:] = packed

    widths = (rows + 2 * RANK, cut, rest + 2 * RANK)
    return run(
        kernel,
        [(x, VMEM) for x in (*owns, *others, fixed)],
        [((HALF, n), F32, VMEM) for n in widths] + [((3 * RANK, cols), BF16, VMEM)],
        [pltpu.VMEM((RANK, cols), F32), pltpu.VMEM((RANK, rows), F32)],
        mib=4,
        after=after,
    )


def inverses(grams):
    row_at = lax.broadcasted_iota(jnp.int32, (RANK, RANK), 0)
    col_at = lax.broadcasted_iota(jnp.int32, (RANK, RANK), 1)
    lane = lax.broadcasted_iota(jnp.int32, (1, RANK), 1)

    def scaled(a):
        diagonal = jnp.where(row_at == col_at, a, 0.0)
        down = lax.rsqrt(jnp.sum(diagonal, axis=1, keepdims=True))
        across = lax.rsqrt(jnp.sum(diagonal, axis=0, keepdims=True))
        return a * down * across, down, across

    def sweep(a, k):
        one, two = (row_at == k, row_at == k + 1)
        here = one | two | (col_at == k) | (col_at == k + 1)
        col_1 = jnp.broadcast_to(a[:, k : k + 1], (RANK, RANK))
        col_2 = jnp.broadcast_to(a[:, k + 1 : k + 2], (RANK, RANK))
        p, q, r = col_1[k : k + 1], col_2[k : k + 1], col_2[k + 1 : k + 2]
        row_1 = jnp.where(lane == k, 1.0, jnp.where(lane == k + 1, 0.0, a[k : k + 1]))
        row_2 = jnp.where(lane == k + 1, 1.0, jnp.where(lane == k, 0.0, a[k + 1 : k + 2]))
        inv = 1.0 / (p * r - q * q)
        new_1 = (r * row_1 - q * row_2) * inv
        new_2 = (p * row_2 - q * row_1) * inv
        col_1 = jnp.where(one, -1.0, jnp.where(two, 0.0, col_1))
        col_2 = jnp.where(two, -1.0, jnp.where(one, 0.0, col_2))
        return jnp.where(here, 0.0, a) - col_1 * new_1 - col_2 * new_2

    systems = [scaled(a) for a in grams]
    values = [a for a, _, _ in systems]
    for k in range(0, RANK, 2):
        values = [sweep(a, k) for a in values]
    return [a * down * across for a, (_, down, across) in zip(values, systems)]


def stacked(refs, order, stack):
    at = 0
    for ref in refs:
        parts = parts_of(ref[...])
        n = ref.shape[0]
        for k, which in enumerate(order):
            stack[k * RANK + at : k * RANK + at + n, :] = parts[which]
        at += n


ROW_ORDER, COL_ORDER = (0, 1, 0, 1), (0, 0, 1, 1)


def turn(stack, turned):
    for i in range(0, stack.shape[1], TILE):
        turned[i : i + TILE, :] = stack[:, i : i + TILE].T


def gram_sums(run, packed, whole, after=()):
    n = len(packed)

    def kernel(*refs):
        a = sum((ref[...] for ref in refs[1:n]), refs[0][...])
        refs[-2][...] = jnp.concatenate([a[:, :RANK], a[:, RANK:]], axis=0)
        refs[-1][...] = sum((ref[...] for ref in refs[n + 1 : -2]), refs[n][...])

    outs = [((RANK, RANK), F32, VMEM)] * 2
    return run(kernel, [(x, VMEM) for x in (*packed, *whole)], outs, mib=2, after=after)


def swapped(a, size, place):
    groups = [a[i : i + size] for i in range(0, RANK, size)]
    other = jnp.concatenate([groups[i ^ 1] for i in range(len(groups))], axis=0)
    return jnp.where(place == 0, a, other)


def solve(run, gram_down, left_down, gram_gate, left_gate, after=()):
    cols, rows = left_down.shape[1], left_gate.shape[1]

    def kernel(gram_down, left_down, gram_gate, left_gate, col_stack, row_turned, col, row, row_stack):
        grams = [gram_down[...], gram_gate[...]]
        for place, a, left, out in zip(
            (core_of(), replica_of()), inverses(grams), (left_down, left_gate), (col, row)
        ):
            a = swapped(a, HALF, place) * (1.0 / REPLICAS)
            if out is col:
                a = swapped(a, HALF // 2, pair_of())
            hi, lo = parts_of(a)
            both = jnp.concatenate([hi, hi, lo], axis=1)
            out[...] = jnp.dot(both, left[...], preferred_element_type=F32)
        stacked([col], COL_ORDER, col_stack)
        stacked([row], ROW_ORDER, row_stack)
        turn(row_stack, row_turned)

    return run(
        kernel,
        [(x, VMEM) for x in (gram_down, left_down, gram_gate, left_gate)],
        [((4 * RANK, cols), BF16, VMEM), ((rows, 4 * RANK), BF16, VMEM)],
        [
            pltpu.VMEM((RANK, cols), F32),
            pltpu.VMEM((RANK, rows), F32),
            pltpu.VMEM((4 * RANK, rows), BF16),
        ],
        mib=6,
        after=after,
    )


def rebuild(run, ready, owns, others, fixed, shares, height, first=0, before=None, after=()):
    rows, cols = fixed.shape
    share = rows // REPLICAS
    parts = share // height
    rows_late = ready[0] is None
    late_width = rows if rows_late else sum(widths_of(owns))
    width = ready[1].shape[1] if rows_late or not owns else late_width
    n_ready = sum(x is not None for x in ready)
    n_late = len(owns) + len(others)
    n_before = 0 if before is None else len(before)
    with_update = 0 in shares
    spots = [(s, t, j) for s in shares for t in range(parts) for j in range(0, width, TILE)]

    def kernel(*refs):
        given, late = refs[:n_ready], refs[n_ready : n_ready + n_late]
        fixed = refs[n_ready + n_late]
        refs = refs[n_ready + n_late + 1 + n_before :]
        new_error, update, turned = refs[0], refs[1], refs[2]
        errors, updates, stack, error_sems, update_sems = refs[3:]
        if late:
            order = ROW_ORDER if rows_late else COL_ORDER
            at = left = 0
            for ref in late:
                split = parts_of(ref[...])
                n, w = ref.shape
                for k, which in enumerate(order):
                    stack[k * RANK + at : k * RANK + at + n, left : left + w] = split[which]
                left += w
                if left == late_width:
                    at, left = at + n, 0
        if rows_late:
            turn(stack, turned)
            row, col = turned, given[0]
        else:
            turned[...] = jnp.zeros_like(turned)
            row, col = given[0], given[1] if n_ready == 2 else stack
        replica = replica_of()
        copies = []
        for k, (s, t, j) in enumerate(spots):
            at = pl.multiple_of((replica if s == 0 else 1 - replica) * share, height) + t * height
            at = pl.ds(pl.multiple_of(at, height), height)
            here, there = slice(j, j + TILE), pl.ds(first + j, TILE)
            mine = pl.ds(t * height, height)
            value = jnp.dot(row[at, :], col[:, here], preferred_element_type=F32)
            slot = pl.ds((shares.index(s) * parts + t) * height, height)
            errors[slot, here] = (fixed[at, there].astype(F32) - value).astype(BF16)
            copies.append(
                pltpu.make_async_copy(errors.at[slot, here], new_error.at[at, there], error_sems.at[k])
            )
            copies[-1].start()
            if s == 0:
                updates[mine, here] = value.astype(BF16)
                copies.append(
                    pltpu.make_async_copy(updates.at[mine, here], update.at[mine, there], update_sems.at[k])
                )
                copies[-1].start()
        for copy in copies:
            copy.wait()

    turned_shape = (rows, 4 * RANK) if rows_late else (16, 128)
    args = [(x, VMEM) for x in (*(x for x in ready if x is not None), *owns, *others, fixed)]
    aliases = None
    if before is not None:
        aliases = {len(args): 0, len(args) + 1: 1}
        args += [(x, HBM) for x in before]
    return run(
        kernel,
        args,
        [((rows, cols), BF16, HBM), ((share, cols), BF16, HBM), (turned_shape, BF16, VMEM)],
        [
            pltpu.VMEM((len(shares) * share, width), BF16),
            pltpu.VMEM((share if with_update else 16, width), BF16),
            pltpu.VMEM((4 * RANK, late_width if n_late else 128), BF16),
            pltpu.SemaphoreType.DMA((len(spots),)),
            pltpu.SemaphoreType.DMA((len(spots),)),
        ],
        mib=18,
        aliases=aliases,
        after=after,
    )


def local(grad_gate, grad_down, error_gate, error_down, start_gate, start_down):
    slab, width = grad_gate.shape
    n_dp, n_t = lax.axis_size("dp"), lax.axis_size("tensor")
    run = Calls()
    hops, steps = row_steps(), col_steps()
    tiles = slab // TILE

    _, fixed_down, keep, give = down_left(run, grad_down, error_down, start_down, 0, tiles)
    got = exchange(give, other_replica)
    gate_args = (run, grad_gate, error_gate, start_gate)
    cut = tiles * 3 // 5
    first = gate_left(*gate_args, 0, cut, after=(keep,))
    (down,) = add(run, [keep], [got], after=(first[0],))
    got = exchange(down, steps[0])
    _, fixed_gate, keep_gate, *gives = gate_left(
        *gate_args, cut, tiles - cut, first, after=(down,)
    )
    (gate,) = add(run, [keep_gate], to_other_core(gives))
    got_gate = exchange(gate, hops[0])
    for i in range(len(steps)):
        (down,) = add(run, [down], [got], after=(gate,))
        if i + 1 < len(steps):
            got = exchange(down, steps[i + 1])
    other_down = exchange(down, other_replica)
    for hop in hops[1:]:
        (gate,) = add(run, [gate], [got_gate], after=(down,))
        got_gate = exchange(gate, hop)

    keep, *gives, left_down = down_right(run, [down], [other_down], fixed_down, after=(gate,))
    gots = to_other_core(gives)
    gates = add(run, [gate], [got_gate], after=(keep,))
    others_gate = to_other_core(gates)
    keep, give, gram_down = add_halved(run, [keep], gots, slab, pair_of, after=(gates[0],))
    got = exchange(give, other_pair)
    grams_down = [gram_down] + [
        exchange(gram_down, lambda d, t, b=b: (d, t ^ b)) for b in range(2, n_t, 2)
    ]
    keep_gate, give_gate, gram_gate, left_gate = gate_right(
        run, gates, others_gate, fixed_gate, after=(keep,)
    )
    got_gate = exchange(give_gate, other_replica)
    grams_gate = [gram_gate] + [
        exchange(gram_gate, lambda d, t, b=b: (d ^ b, t)) for b in range(REPLICAS, n_dp, REPLICAS)
    ]
    (down,) = add(run, [keep], [got], after=(gram_gate,))
    for b in bits(n_t, 4):
        (down,) = add(run, [down], [exchange(down, lambda d, t, b=b: (d, t ^ b))])
    got = exchange(down, other_replica)
    gram_down, gram_gate = gram_sums(run, grams_down, grams_gate, after=(down,))
    (gate,) = add(run, [keep_gate], [got_gate], after=(gram_gate,))
    got_gate = exchange(gate, steps[0])
    (down,) = add(run, [down], [got], after=(gate,))
    down_pair = exchange(down, other_pair)
    col_stack, row_turned = solve(
        run, gram_down, left_down, gram_gate, left_gate, after=(down,)
    )
    downs = [down, pass_on(run, down_pair, after=(col_stack,))]
    others_down = to_other_core(downs)
    for i in range(len(steps)):
        (gate,) = add(run, [gate], [got_gate], after=(col_stack, others_down[1]))
        if i + 1 < len(steps):
            got_gate = exchange(gate, steps[i + 1])
    other_gate = exchange(gate, other_replica)
    new_error_down, update_down, done = rebuild(
        run, (None, col_stack), downs, others_down, fixed_down, (0, 1), slab // 8, after=(gate,)
    )
    new_error_gate, update_gate, _ = rebuild(
        run, (row_turned, None), [gate], [other_gate], fixed_gate, (0, 1), slab // 8, after=(done,)
    )
    return (update_gate, update_down, new_error_gate, new_error_down)


def solution(mesh):
    split = P(("mix", "dp"), "tensor")
    in_specs = (split, split, split, split, P(None, "tensor"), P())
    out_specs = (split, split, split, split)

    def run(grad_gate, *rest):
        groups = mesh.shape["mix"] * mesh.shape["dp"]
        slab = grad_gate.shape[0] // groups
        width = grad_gate.shape[1] // mesh.shape["tensor"]
        fits = slab % (REPLICAS * TILE) == 0 and width % TILE == 0 and mesh.shape["tensor"] % 4 == 0
        body = local if fits else local_plain
        return jax.shard_map(
            body, mesh=mesh, in_specs=in_specs, out_specs=out_specs, check_vma=False
        )(grad_gate, *rest)

    return run
```

```python
import functools

import jax
import jax.numpy as jnp
from jax import lax
from jax.experimental import pallas as pl
from jax.experimental.pallas import tpu as pltpu
from jax.sharding import PartitionSpec as P

REPLICAS = 2
RANK = 64
TILE = 256
FLOPS = 1.15e9
WEIGHTS = (8.0, 4.0, 1.0, 4.0, 0.1, 5.0, 1.0, 5.0, 1.0, 1.0, 2.0, 2.0, 0.1, 1.0, 5.0, 0.1, 0.5, 1.0, 1.0, 8.0, 8.0)
MIB = 1 << 20
BF16 = jnp.bfloat16
F32 = jnp.float32

NN = (((1,), (0,)), ((), ()))
NT = (((1,), (1,)), ((), ()))
TN = (((0,), (0,)), ((), ()))


def from_partner(shard, axis, stride):
    return lax.ppermute(shard, axis, [(i, i ^ 1 << stride) for i in range(lax.axis_size(axis))])


def corrected(grad, error):
    return (grad.astype(F32) + error.astype(F32)).astype(BF16)


def transposed(matrix, ortho):
    return lax.dot_general(matrix, ortho.astype(BF16), TN, preferred_element_type=F32)


def gram_of(left):
    return jnp.dot(left.T, left, precision=lax.Precision.HIGHEST)


def factored(left, inner):
    lower = jnp.linalg.cholesky(inner)
    return lax.linalg.triangular_solve(lower, left, left_side=False, lower=True, transpose_a=True)


def local_plain(grad_gate, grad_down, error_gate, error_down, start_gate, start_down):
    high = lax.Precision.HIGHEST
    dp_place = lax.axis_index("dp")
    block = dp_place // REPLICAS
    replica = dp_place % REPLICAS
    fixed_gate = corrected(grad_gate, error_gate)
    fixed_down = corrected(grad_down, error_down)
    slab = fixed_gate.shape[0]
    cols_down = lax.dynamic_slice_in_dim(start_down, block * slab, slab, 1)
    left_gate = lax.dot_general(fixed_gate, start_gate, NT, preferred_element_type=F32)
    left_down = lax.dot_general(
        fixed_down, cols_down, (((0,), (1,)), ((), ())), preferred_element_type=F32
    )
    left_gate = lax.psum(left_gate, "tensor")
    left_gate = left_gate + from_partner(left_gate, "dp", 0)
    left_down = lax.psum(left_down, "dp")
    keep_gate = (replica == 0).astype(F32)
    inner_gate = lax.psum(gram_of(left_gate) * keep_gate, "dp")
    inner_down = lax.psum(gram_of(left_down), "tensor")
    ortho_gate = factored(left_gate, inner_gate)
    ortho_down = factored(left_down, inner_down)
    right_gate = transposed(fixed_gate, ortho_gate)
    right_gate = lax.psum(right_gate, "dp") / REPLICAS
    right_down = jnp.dot(fixed_down, ortho_down.astype(BF16), preferred_element_type=F32)
    right_down = lax.psum(right_down, "tensor")
    right_down = right_down + from_partner(right_down, "dp", 0)
    right_down = right_down / REPLICAS
    rebuilt_gate = jnp.dot(ortho_gate, right_gate.T, precision=high)
    rebuilt_down = jnp.dot(right_down, ortho_down.T, precision=high)
    share = slab // REPLICAS
    update_gate = lax.dynamic_slice_in_dim(rebuilt_gate, replica * share, share, 0).astype(BF16)
    update_down = lax.dynamic_slice_in_dim(rebuilt_down, replica * share, share, 0).astype(BF16)
    new_error_gate = (fixed_gate.astype(F32) - rebuilt_gate).astype(BF16)
    new_error_down = (fixed_down.astype(F32) - rebuilt_down).astype(BF16)
    return (update_gate, update_down, new_error_gate, new_error_down)


def core_of():
    return lax.rem(lax.axis_index("tensor"), 2)


def replica_of():
    return lax.rem(lax.axis_index("dp"), REPLICAS)


def exchange(x, partner):
    n_dp, n_t = lax.axis_size("dp"), lax.axis_size("tensor")
    pairs = []
    for d in range(n_dp):
        for t in range(n_t):
            to_d, to_t = partner(d, t)
            pairs.append((d * n_t + t, to_d * n_t + to_t))
    return lax.ppermute(x, ("dp", "tensor"), pairs)


def bits(n, low):
    out, b = [], low
    while b < n:
        out.append(b)
        b *= 2
    return out


def row_steps():
    steps = [(0, b) for b in bits(lax.axis_size("tensor"), 2)] + [(1, 0)]

    def partner(i, d, t):
        r, b = steps[i] if t % 2 == 0 else steps[-1 - i]
        return d ^ r, t ^ b

    return [functools.partial(partner, i) for i in range(len(steps))]


def col_steps():
    return [lambda d, t, b=b: (d ^ b, t) for b in bits(lax.axis_size("dp"), REPLICAS)]


def other_core(d, t):
    return d, t ^ 1


def other_replica(d, t):
    return d ^ 1, t


def to_other_core(pieces):
    return [exchange(x, other_core) for x in pieces]


VMEM = pl.BlockSpec(memory_space=pltpu.VMEM)
HBM = pl.BlockSpec(memory_space=pltpu.HBM)
ANY = pl.BlockSpec(memory_space=pl.ANY)
HALF = RANK // 2


class Calls:
    def __init__(self):
        self.count = 0

    def __call__(self, kernel, args, outs, scratch=(), mib=8, aliases=None, after=()):
        n_in, n_after = len(args), len(after)
        operands = [
            pltpu.with_memory_space_constraint(x, pltpu.VMEM if spec is VMEM else pltpu.HBM)
            for x, spec in args
        ]

        def body(*refs):
            kernel(*refs[:n_in], *refs[n_in + n_after :])

        out = pl.pallas_call(
            body,
            out_shape=tuple(
                (pltpu.VMEM if spec is VMEM else pltpu.HBM)(shape, kind) for shape, kind, spec in outs
            ),
            in_specs=[spec for _, spec in args] + [ANY] * n_after,
            out_specs=tuple(spec for *_, spec in outs),
            scratch_shapes=list(scratch),
            input_output_aliases=aliases or {},
            compiler_params=pltpu.CompilerParams(vmem_limit_bytes=mib * MIB),
            cost_estimate=pl.CostEstimate(
                flops=int(WEIGHTS[self.count] * FLOPS), bytes_accessed=1 << 10, transcendentals=0
            ),
        )(*operands, *after)
        self.count += 1
        return out


def parts_of(x):
    hi = x.astype(BF16)
    lo = (x - hi.astype(F32)).astype(BF16)
    return hi, lo


def spans(*widths):
    edges = sorted({sum(w[:i]) for w in widths for i in range(len(w) + 1)})
    for low, high in zip(edges, edges[1:]):
        places = []
        for w in widths:
            k = max(i for i in range(len(w)) if sum(w[:i]) <= low)
            places.append((k, low - sum(w[:k]), high - sum(w[:k])))
        yield places


def widths_of(refs):
    return [ref.shape[1] for ref in refs]


def add(run, xs, ys, widths=None, beside=None, after=()):
    widths = list(widths or widths_of(xs))
    more = 0 if beside is None else beside.shape[1]
    n_x, n_y = len(xs), len(ys)

    def kernel(*refs):
        x, y, out = refs[:n_x], refs[n_x : n_x + n_y], refs[-len(widths) :]
        for (i, i0, i1), (j, j0, j1), (k, k0, k1) in spans(widths_of(x), widths_of(y), widths):
            out[k][:, k0:k1] = x[i][:, i0:i1] + y[j][:, j0:j1]
        if more:
            out[-1][:, widths[-1] :] = refs[n_x + n_y][...]

    outs = [((HALF, n), F32, VMEM) for n in (*widths[:-1], widths[-1] + more)]
    args = [(x, VMEM) for x in (*xs, *ys)]
    if more:
        args.append((beside, VMEM))
    return list(run(kernel, args, outs, mib=2, after=after))


def in_two(width):
    cut = width // 256 * 128
    return [cut, width - cut]


def halve(whole, place, keep, gives):
    keep[...] = whole[pl.ds(pl.multiple_of(place * HALF, HALF), HALF), :]
    at = 0
    for give in gives:
        n = give.shape[1]
        give[...] = whole[pl.ds(pl.multiple_of((1 - place) * HALF, HALF), HALF), at : at + n]
        at += n


def tile_at(i):
    return pl.ds(pl.multiple_of(i * TILE, TILE), TILE)


def gate_left(run, grad, error, start, first, count, before=None, after=()):
    rows, cols = grad.shape
    last = (first + count) * TILE == rows

    def kernel(grad, error, start, *refs):
        if before is not None:
            refs = refs[2:]
        left, fixed = refs[:2]

        def step(g, e):
            at = tile_at(first + pl.program_id(0))
            term = jnp.zeros((RANK, TILE), F32)
            for j in range(0, cols, TILE):
                here = slice(j, j + TILE)
                c = g[:, here] + e[:, here]
                fixed[at, here] = c
                term += lax.dot_general(start[:, here], c, NT, preferred_element_type=F32)
            left[:, at] = term

        spec = pl.BlockSpec((TILE, cols), lambda i: (first + i, 0), pipeline_mode=pl.Buffered(3))
        pltpu.emit_pipeline(step, grid=(count,), in_specs=[spec, spec])(grad, error)
        if last:
            halve(left, core_of(), refs[2], refs[3:])

    args = [(grad, HBM), (error, HBM), (start, VMEM)]
    outs = [((RANK, rows), F32, VMEM), ((rows, cols), BF16, VMEM)]
    if last:
        outs += [((HALF, n), F32, VMEM) for n in (rows, *in_two(rows))]
    aliases = None
    if before is not None:
        args += [(x, VMEM) for x in before]
        aliases = {3: 0, 4: 1}
    return run(kernel, args, outs, mib=8, aliases=aliases, after=after)


def down_left(run, grad, error, start, first, count, before=None, after=()):
    rows, cols = grad.shape
    last = (first + count) * TILE == rows

    def kernel(grad, error, start, *refs):
        if before is not None:
            refs = refs[2:]
        left, fixed = refs[:2]
        pair = 2 * TILE
        block = lax.div(lax.axis_index("dp"), REPLICAS) * (rows // pair) + first // 2
        if before is None:
            left[...] = jnp.zeros_like(left)

        def step(g, e, s):
            i = pl.program_id(0)
            at = tile_at(first + i)
            for j in range(0, cols, TILE):
                here = slice(j, j + TILE)
                fixed[at, here] = g[:, here] + e[:, here]

            @pl.when(lax.rem(i, 2) == 1)
            def _():
                both = pl.ds(pl.multiple_of((first + i - 1) * TILE, pair), pair)
                for j in range(0, cols, TILE):
                    here = slice(j, j + TILE)
                    left[:, here] += jnp.dot(s[...], fixed[both, here], preferred_element_type=F32)

        spec = pl.BlockSpec((TILE, cols), lambda i: (first + i, 0), pipeline_mode=pl.Buffered(3))
        part = pl.BlockSpec((RANK, pair), lambda i: (0, block + lax.div(i, 2)))
        pltpu.emit_pipeline(step, grid=(count,), in_specs=[spec, spec, part])(grad, error, start)
        if last:
            halve(left, replica_of(), refs[2], refs[3:])

    args = [(grad, HBM), (error, HBM), (start, HBM)]
    outs = [((RANK, cols), F32, VMEM), ((rows, cols), BF16, VMEM)]
    if last:
        outs += [((HALF, cols), F32, VMEM)] * 2
    aliases = None
    if before is not None:
        args += [(x, VMEM) for x in before]
        aliases = {3: 0, 4: 1}
    return run(kernel, args, outs, mib=8, aliases=aliases, after=after)


def load_left(owns, others, place, left, stack):
    for refs, half in ((owns, place), (others, 1 - place)):
        at = 0
        for ref in refs:
            n = ref.shape[1]
            left[pl.ds(pl.multiple_of(half * HALF, HALF), HALF), at : at + n] = ref[...]
            at += n
    hi, lo = parts_of(left[...])
    stack[:RANK, :] = hi
    stack[RANK : 2 * RANK, :] = lo
    stack[2 * RANK :, :] = hi
    parts = stack[: 2 * RANK]
    gram = lax.dot_general(parts, parts, NT, preferred_element_type=F32)
    mixed = gram[:RANK, RANK:] + gram[RANK:, :RANK]
    return gram[:RANK, :RANK] + (mixed + gram[RANK:, RANK:])


def packed(gram):
    return jnp.concatenate([gram[:HALF], gram[HALF:]], axis=1)


def gate_right(run, owns, others, fixed, count, after=()):
    rows = fixed.shape[0]
    width = count * TILE
    n_own, n_both = len(owns), len(owns) + len(others)

    def kernel(*refs):
        fixed, keep, give, gram, stack, left, right = refs[n_both:]
        gram[...] = packed(load_left(refs[:n_own], refs[n_own:n_both], core_of(), left, stack))

        def step(i, _):
            both = jnp.dot(stack[: 2 * RANK], fixed[:, tile_at(i)], preferred_element_type=F32)
            right[:, tile_at(i)] = both[:RANK] + both[RANK:]
            return 0

        lax.fori_loop(0, count, step, 0)
        halve(right, replica_of(), keep, [give])

    return run(
        kernel,
        [(x, VMEM) for x in (*owns, *others, fixed)],
        [((HALF, width), F32, VMEM)] * 2
        + [((HALF, 2 * RANK), F32, VMEM), ((3 * RANK, rows), BF16, VMEM)],
        [pltpu.VMEM((RANK, rows), F32), pltpu.VMEM((RANK, width), F32)],
        mib=4,
        after=after,
    )


def gate_right_rest(run, stack, fixed, first, after=()):
    width = fixed.shape[1] - first * TILE

    def kernel(stack, fixed, keep, give, right):
        def step(i, _):
            both = jnp.dot(
                stack[: 2 * RANK], fixed[:, tile_at(first + i)], preferred_element_type=F32
            )
            right[:, tile_at(i)] = both[:RANK] + both[RANK:]
            return 0

        lax.fori_loop(0, width // TILE, step, 0)
        halve(right, replica_of(), keep, [give])

    return run(
        kernel,
        [(stack, VMEM), (fixed, VMEM)],
        [((HALF, width), F32, VMEM)] * 2,
        [pltpu.VMEM((RANK, width), F32)],
        mib=4,
        after=after,
    )


def down_right(run, owns, others, fixed, after=()):
    rows, cols = fixed.shape
    n_own, n_both = len(owns), len(owns) + len(others)
    cut, rest = in_two(rows)

    def kernel(*refs):
        fixed, keep, give_1, give_2, stack, left, right = refs[n_both:]
        gram = load_left(refs[:n_own], refs[n_own:n_both], replica_of(), left, stack)

        def step(i, _):
            both = lax.dot_general(stack[: 2 * RANK], fixed[tile_at(i), :], NT, preferred_element_type=F32)
            right[:, tile_at(i)] = both[:RANK] + both[RANK:]
            return 0

        lax.fori_loop(0, rows // TILE, step, 0)
        halve(right, core_of(), keep.at[:, :rows], [give_1, give_2.at[:, :rest]])
        keep[:, rows:] = packed(gram)
        give_2[:, rest:] = packed(gram)

    widths = (rows + 2 * RANK, cut, rest + 2 * RANK)
    return run(
        kernel,
        [(x, VMEM) for x in (*owns, *others, fixed)],
        [((HALF, n), F32, VMEM) for n in widths] + [((3 * RANK, cols), BF16, VMEM)],
        [pltpu.VMEM((RANK, cols), F32), pltpu.VMEM((RANK, rows), F32)],
        mib=4,
        after=after,
    )


def inverses(grams):
    row_at = lax.broadcasted_iota(jnp.int32, (RANK, RANK), 0)
    col_at = lax.broadcasted_iota(jnp.int32, (RANK, RANK), 1)
    lane = lax.broadcasted_iota(jnp.int32, (1, RANK), 1)

    def scaled(a):
        diagonal = jnp.where(row_at == col_at, a, 0.0)
        down = lax.rsqrt(jnp.sum(diagonal, axis=1, keepdims=True))
        across = lax.rsqrt(jnp.sum(diagonal, axis=0, keepdims=True))
        return a * down * across, down, across

    def sweep(a, k):
        one, two = (row_at == k, row_at == k + 1)
        here = one | two | (col_at == k) | (col_at == k + 1)
        col_1 = jnp.broadcast_to(a[:, k : k + 1], (RANK, RANK))
        col_2 = jnp.broadcast_to(a[:, k + 1 : k + 2], (RANK, RANK))
        p, q, r = col_1[k : k + 1], col_2[k : k + 1], col_2[k + 1 : k + 2]
        row_1 = jnp.where(lane == k, 1.0, jnp.where(lane == k + 1, 0.0, a[k : k + 1]))
        row_2 = jnp.where(lane == k + 1, 1.0, jnp.where(lane == k, 0.0, a[k + 1 : k + 2]))
        inv = 1.0 / (p * r - q * q)
        new_1 = (r * row_1 - q * row_2) * inv
        new_2 = (p * row_2 - q * row_1) * inv
        col_1 = jnp.where(one, -1.0, jnp.where(two, 0.0, col_1))
        col_2 = jnp.where(two, -1.0, jnp.where(one, 0.0, col_2))
        return jnp.where(here, 0.0, a) - col_1 * new_1 - col_2 * new_2

    systems = [scaled(a) for a in grams]
    values = [a for a, _, _ in systems]
    for k in range(0, RANK, 2):
        values = [sweep(a, k) for a in values]
    return [a * down * across for a, (_, down, across) in zip(values, systems)]


def stacked(refs, order, stack):
    at = 0
    for ref in refs:
        parts = parts_of(ref[...])
        n = ref.shape[0]
        for k, which in enumerate(order):
            stack[k * RANK + at : k * RANK + at + n, :] = parts[which]
        at += n


ROW_ORDER, COL_ORDER = (0, 1, 0, 1), (0, 0, 1, 1)


def turn(stack, turned):
    for i in range(0, stack.shape[1], TILE):
        turned[i : i + TILE, :] = stack[:, i : i + TILE].T


def solve(run, grams_down, left_down, gram_gate, left_gate, after=()):
    cols, rows = left_down.shape[1], left_gate.shape[1]

    n = len(grams_down)

    def kernel(*refs):
        gram_gate, left_down, left_gate, col_stack, row_turned, col, row, row_stack = refs[n:]
        gram_down = sum((ref[...] for ref in refs[1:n]), refs[0][...])
        grams = [
            jnp.concatenate([a[:, :RANK], a[:, RANK:]], axis=0) for a in (gram_down, gram_gate[...])
        ]
        for place, a, left, out in zip(
            (core_of(), replica_of()), inverses(grams), (left_down, left_gate), (col, row)
        ):
            other = jnp.concatenate([a[HALF:], a[:HALF]], axis=0)
            a = jnp.where(place == 0, a, other) * (1.0 / REPLICAS)
            hi, lo = parts_of(a)
            both = jnp.concatenate([hi, hi, lo], axis=1)
            out[...] = jnp.dot(both, left[...], preferred_element_type=F32)
        stacked([col], COL_ORDER, col_stack)
        stacked([row], ROW_ORDER, row_stack)
        turn(row_stack, row_turned)

    return run(
        kernel,
        [(x, VMEM) for x in (*grams_down, gram_gate, left_down, left_gate)],
        [((4 * RANK, cols), BF16, VMEM), ((rows, 4 * RANK), BF16, VMEM)],
        [
            pltpu.VMEM((RANK, cols), F32),
            pltpu.VMEM((RANK, rows), F32),
            pltpu.VMEM((4 * RANK, rows), BF16),
        ],
        mib=6,
        after=after,
    )


def rebuild(run, ready, owns, others, fixed, shares, height, first=0, before=None, after=()):
    rows, cols = fixed.shape
    share = rows // REPLICAS
    parts = share // height
    rows_late = ready[0] is None
    late_width = sum(widths_of(owns))
    width = ready[1].shape[1] if rows_late or not owns else late_width
    n_ready = sum(x is not None for x in ready)
    n_own, n_late = len(owns), len(owns) + len(others)
    n_before = 0 if before is None else len(before)
    with_update = 0 in shares
    spots = [(s, t, j) for s in shares for t in range(parts) for j in range(0, width, TILE)]

    def kernel(*refs):
        given, late = refs[:n_ready], refs[n_ready : n_ready + n_late]
        fixed = refs[n_ready + n_late]
        refs = refs[n_ready + n_late + 1 + n_before :]
        new_error, update, turned = refs[0], refs[1], refs[2]
        errors, updates, stack, error_sems, update_sems = refs[3:]
        if late:
            order = ROW_ORDER if rows_late else COL_ORDER
            for at, pieces in ((0, late[:n_own]), (HALF, late[n_own:])):
                left = 0
                for ref in pieces:
                    split = parts_of(ref[...])
                    n, w = ref.shape
                    for k, which in enumerate(order):
                        stack[k * RANK + at : k * RANK + at + n, left : left + w] = split[which]
                    left += w
        if rows_late:
            turn(stack, turned)
            row, col = turned, given[0]
        else:
            turned[...] = jnp.zeros_like(turned)
            row, col = given[0], given[1] if n_ready == 2 else stack
        replica = replica_of()
        copies = []
        for k, (s, t, j) in enumerate(spots):
            at = pl.multiple_of((replica if s == 0 else 1 - replica) * share, height) + t * height
            at = pl.ds(pl.multiple_of(at, height), height)
            here, there = slice(j, j + TILE), pl.ds(first + j, TILE)
            mine = pl.ds(t * height, height)
            value = jnp.dot(row[at, :], col[:, here], preferred_element_type=F32)
            slot = pl.ds((shares.index(s) * parts + t) * height, height)
            errors[slot, here] = (fixed[at, there].astype(F32) - value).astype(BF16)
            copies.append(
                pltpu.make_async_copy(errors.at[slot, here], new_error.at[at, there], error_sems.at[k])
            )
            copies[-1].start()
            if s == 0:
                updates[mine, here] = value.astype(BF16)
                copies.append(
                    pltpu.make_async_copy(updates.at[mine, here], update.at[mine, there], update_sems.at[k])
                )
                copies[-1].start()
        for copy in copies:
            copy.wait()

    turned_shape = (rows, 4 * RANK) if rows_late else (16, 128)
    args = [(x, VMEM) for x in (*(x for x in ready if x is not None), *owns, *others, fixed)]
    aliases = None
    if before is not None:
        aliases = {len(args): 0, len(args) + 1: 1}
        args += [(x, HBM) for x in before]
    return run(
        kernel,
        args,
        [((rows, cols), BF16, HBM), ((share, cols), BF16, HBM), (turned_shape, BF16, VMEM)],
        [
            pltpu.VMEM((len(shares) * share, width), BF16),
            pltpu.VMEM((share if with_update else 16, width), BF16),
            pltpu.VMEM((4 * RANK, late_width if n_late else 128), BF16),
            pltpu.SemaphoreType.DMA((len(spots),)),
            pltpu.SemaphoreType.DMA((len(spots),)),
        ],
        mib=18,
        aliases=aliases,
        after=after,
    )


def local(grad_gate, grad_down, error_gate, error_down, start_gate, start_down):
    slab, width = grad_gate.shape
    n_dp, n_t = lax.axis_size("dp"), lax.axis_size("tensor")
    run = Calls()
    hops, steps = row_steps(), col_steps()
    tiles = slab // TILE

    _, fixed_down, keep, give = down_left(run, grad_down, error_down, start_down, 0, tiles)
    got = exchange(give, other_replica)
    gate_args = (run, grad_gate, error_gate, start_gate)
    cut = tiles * 3 // 5
    first = gate_left(*gate_args, 0, cut, after=(keep,))
    (down,) = add(run, [keep], [got], after=(first[0],))
    got = exchange(down, steps[0])
    _, fixed_gate, keep_gate, *gives = gate_left(
        *gate_args, cut, tiles - cut, first, after=(down,)
    )
    (gate,) = add(run, [keep_gate], to_other_core(gives))
    got_gate = exchange(gate, hops[0])
    for i in range(len(steps)):
        (down,) = add(run, [down], [got], after=(gate,))
        if i + 1 < len(steps):
            got = exchange(down, steps[i + 1])
    other_down = exchange(down, other_replica)
    for hop in hops[1:]:
        (gate,) = add(run, [gate], [got_gate], after=(down,))
        got_gate = exchange(gate, hop)

    keep, *gives, left_down = down_right(run, [down], [other_down], fixed_down, after=(gate,))
    gots = to_other_core(gives)
    gates = add(run, [gate], [got_gate], after=(keep,))
    others_gate = to_other_core(gates)
    down, gram_down = add(run, [keep], gots, [slab, 2 * RANK], after=(gates[0],))
    grams_down = [gram_down] + [
        exchange(gram_down, lambda d, t, b=b: (d, t ^ b)) for b in range(2, n_t, 2)
    ]
    got = exchange(down, hops[0])
    few = width // TILE * 3 // 7
    keep_a, give_a, gram_gate, left_gate = gate_right(
        run, gates, others_gate, fixed_gate, few, after=(down,)
    )
    got_a = exchange(give_a, other_replica)
    keep_b, give_b = gate_right_rest(run, left_gate, fixed_gate, few)
    got_b = exchange(give_b, other_replica)
    for hop in hops[1:]:
        (down,) = add(run, [down], [got], after=(give_b,))
        got = exchange(down, hop)
    (gate_a,) = add(run, [keep_a], [got_a], beside=gram_gate, after=(down,))
    got_a = exchange(gate_a, steps[0])
    (gate_b,) = add(run, [keep_b], [got_b], after=(gate_a,))
    got_b = exchange(gate_b, steps[0])
    for step in steps[1:]:
        (gate_a,) = add(run, [gate_a], [got_a])
        got_a = exchange(gate_a, step)
        (gate_b,) = add(run, [gate_b], [got_b])
        got_b = exchange(gate_b, step)
    gate_a, gram_gate = add(run, [gate_a], [got_a], [few * TILE, 2 * RANK], after=(gate_b,))
    other_a = exchange(gate_a, other_replica)
    col_stack, row_turned = solve(run, grams_down, left_down, gram_gate, left_gate)
    downs = add(run, [down], [got], in_two(slab), after=(col_stack,))
    others_down = to_other_core(downs)
    (gate_b,) = add(run, [gate_b], [got_b], after=(downs[0],))
    other_b = exchange(gate_b, other_replica)
    new_error_down, update_down, turned = rebuild(
        run, (None, col_stack), downs, others_down, fixed_down, (0, 1), slab // 8, after=(gate_b,)
    )
    new_error_gate, update_gate, _ = rebuild(
        run, (row_turned, None), [gate_a, gate_b], [other_a, other_b], fixed_gate, (0, 1), slab // 2,
        after=(turned,),
    )
    return (update_gate, update_down, new_error_gate, new_error_down)


def solution(mesh):
    split = P(("mix", "dp"), "tensor")
    in_specs = (split, split, split, split, P(None, "tensor"), P())
    out_specs = (split, split, split, split)

    def run(grad_gate, *rest):
        groups = mesh.shape["mix"] * mesh.shape["dp"]
        slab = grad_gate.shape[0] // groups
        width = grad_gate.shape[1] // mesh.shape["tensor"]
        fits = slab % (REPLICAS * TILE) == 0 and width % TILE == 0
        body = local if fits else local_plain
        return jax.shard_map(
            body, mesh=mesh, in_specs=in_specs, out_specs=out_specs, check_vma=False
        )(grad_gate, *rest)

    return run
```

```python
import functools

import jax
import jax.numpy as jnp
from jax import lax
from jax.experimental import pallas as pl
from jax.experimental.pallas import tpu as pltpu
from jax.sharding import PartitionSpec as P

REPLICAS = 2
RANK = 64
TILE = 256
FLOPS = 1.15e9
WEIGHTS = (8.0, 4.0, 1.0, 4.0, 0.1, 5.0, 1.0, 5.0, 1.0, 1.0, 2.0, 2.0, 5.0, 5.0, 1.0, 0.1, 5.0, 1.0, 1.0, 8.0, 8.0)
MIB = 1 << 20
BF16 = jnp.bfloat16
F32 = jnp.float32

NN = (((1,), (0,)), ((), ()))
NT = (((1,), (1,)), ((), ()))
TN = (((0,), (0,)), ((), ()))


def from_partner(shard, axis, stride):
    return lax.ppermute(shard, axis, [(i, i ^ 1 << stride) for i in range(lax.axis_size(axis))])


def corrected(grad, error):
    return (grad.astype(F32) + error.astype(F32)).astype(BF16)


def transposed(matrix, ortho):
    return lax.dot_general(matrix, ortho.astype(BF16), TN, preferred_element_type=F32)


def gram_of(left):
    return jnp.dot(left.T, left, precision=lax.Precision.HIGHEST)


def factored(left, inner):
    lower = jnp.linalg.cholesky(inner)
    return lax.linalg.triangular_solve(lower, left, left_side=False, lower=True, transpose_a=True)


def local_plain(grad_gate, grad_down, error_gate, error_down, start_gate, start_down):
    high = lax.Precision.HIGHEST
    dp_place = lax.axis_index("dp")
    block = dp_place // REPLICAS
    replica = dp_place % REPLICAS
    fixed_gate = corrected(grad_gate, error_gate)
    fixed_down = corrected(grad_down, error_down)
    slab = fixed_gate.shape[0]
    cols_down = lax.dynamic_slice_in_dim(start_down, block * slab, slab, 1)
    left_gate = lax.dot_general(fixed_gate, start_gate, NT, preferred_element_type=F32)
    left_down = lax.dot_general(
        fixed_down, cols_down, (((0,), (1,)), ((), ())), preferred_element_type=F32
    )
    left_gate = lax.psum(left_gate, "tensor")
    left_gate = left_gate + from_partner(left_gate, "dp", 0)
    left_down = lax.psum(left_down, "dp")
    keep_gate = (replica == 0).astype(F32)
    inner_gate = lax.psum(gram_of(left_gate) * keep_gate, "dp")
    inner_down = lax.psum(gram_of(left_down), "tensor")
    ortho_gate = factored(left_gate, inner_gate)
    ortho_down = factored(left_down, inner_down)
    right_gate = transposed(fixed_gate, ortho_gate)
    right_gate = lax.psum(right_gate, "dp") / REPLICAS
    right_down = jnp.dot(fixed_down, ortho_down.astype(BF16), preferred_element_type=F32)
    right_down = lax.psum(right_down, "tensor")
    right_down = right_down + from_partner(right_down, "dp", 0)
    right_down = right_down / REPLICAS
    rebuilt_gate = jnp.dot(ortho_gate, right_gate.T, precision=high)
    rebuilt_down = jnp.dot(right_down, ortho_down.T, precision=high)
    share = slab // REPLICAS
    update_gate = lax.dynamic_slice_in_dim(rebuilt_gate, replica * share, share, 0).astype(BF16)
    update_down = lax.dynamic_slice_in_dim(rebuilt_down, replica * share, share, 0).astype(BF16)
    new_error_gate = (fixed_gate.astype(F32) - rebuilt_gate).astype(BF16)
    new_error_down = (fixed_down.astype(F32) - rebuilt_down).astype(BF16)
    return (update_gate, update_down, new_error_gate, new_error_down)


def core_of():
    return lax.rem(lax.axis_index("tensor"), 2)


def replica_of():
    return lax.rem(lax.axis_index("dp"), REPLICAS)


def exchange(x, partner):
    n_dp, n_t = lax.axis_size("dp"), lax.axis_size("tensor")
    pairs = []
    for d in range(n_dp):
        for t in range(n_t):
            to_d, to_t = partner(d, t)
            pairs.append((d * n_t + t, to_d * n_t + to_t))
    return lax.ppermute(x, ("dp", "tensor"), pairs)


def bits(n, low):
    out, b = [], low
    while b < n:
        out.append(b)
        b *= 2
    return out


def row_steps():
    steps = [(0, b) for b in bits(lax.axis_size("tensor"), 2)] + [(1, 0)]

    def partner(i, d, t):
        r, b = steps[i] if t % 2 == 0 else steps[-1 - i]
        return d ^ r, t ^ b

    return [functools.partial(partner, i) for i in range(len(steps))]


def col_steps():
    return [lambda d, t, b=b: (d ^ b, t) for b in bits(lax.axis_size("dp"), REPLICAS)]


def other_core(d, t):
    return d, t ^ 1


def other_replica(d, t):
    return d ^ 1, t


def to_other_core(pieces):
    return [exchange(x, other_core) for x in pieces]


VMEM = pl.BlockSpec(memory_space=pltpu.VMEM)
HBM = pl.BlockSpec(memory_space=pltpu.HBM)
ANY = pl.BlockSpec(memory_space=pl.ANY)
HALF = RANK // 2


class Calls:
    def __init__(self):
        self.count = 0

    def __call__(self, kernel, args, outs, scratch=(), mib=8, aliases=None, after=()):
        n_in, n_after = len(args), len(after)
        operands = [
            pltpu.with_memory_space_constraint(x, pltpu.VMEM if spec is VMEM else pltpu.HBM)
            for x, spec in args
        ]

        def body(*refs):
            kernel(*refs[:n_in], *refs[n_in + n_after :])

        out = pl.pallas_call(
            body,
            out_shape=tuple(
                (pltpu.VMEM if spec is VMEM else pltpu.HBM)(shape, kind) for shape, kind, spec in outs
            ),
            in_specs=[spec for _, spec in args] + [ANY] * n_after,
            out_specs=tuple(spec for *_, spec in outs),
            scratch_shapes=list(scratch),
            input_output_aliases=aliases or {},
            compiler_params=pltpu.CompilerParams(vmem_limit_bytes=mib * MIB),
            cost_estimate=pl.CostEstimate(
                flops=int(WEIGHTS[self.count] * FLOPS), bytes_accessed=1 << 10, transcendentals=0
            ),
        )(*operands, *after)
        self.count += 1
        return out


def parts_of(x):
    hi = x.astype(BF16)
    lo = (x - hi.astype(F32)).astype(BF16)
    return hi, lo


def spans(*widths):
    edges = sorted({sum(w[:i]) for w in widths for i in range(len(w) + 1)})
    for low, high in zip(edges, edges[1:]):
        places = []
        for w in widths:
            k = max(i for i in range(len(w)) if sum(w[:i]) <= low)
            places.append((k, low - sum(w[:k]), high - sum(w[:k])))
        yield places


def widths_of(refs):
    return [ref.shape[1] for ref in refs]


def add(run, xs, ys, widths=None, beside=None, after=()):
    widths = list(widths or widths_of(xs))
    more = 0 if beside is None else beside.shape[1]
    n_x, n_y = len(xs), len(ys)

    def kernel(*refs):
        x, y, out = refs[:n_x], refs[n_x : n_x + n_y], refs[-len(widths) :]
        for (i, i0, i1), (j, j0, j1), (k, k0, k1) in spans(widths_of(x), widths_of(y), widths):
            out[k][:, k0:k1] = x[i][:, i0:i1] + y[j][:, j0:j1]
        if more:
            out[-1][:, widths[-1] :] = refs[n_x + n_y][...]

    outs = [((HALF, n), F32, VMEM) for n in (*widths[:-1], widths[-1] + more)]
    args = [(x, VMEM) for x in (*xs, *ys)]
    if more:
        args.append((beside, VMEM))
    return list(run(kernel, args, outs, mib=2, after=after))


def in_two(width):
    cut = width // 256 * 128
    return [cut, width - cut]


def halve(whole, place, keep, gives):
    keep[...] = whole[pl.ds(pl.multiple_of(place * HALF, HALF), HALF), :]
    at = 0
    for give in gives:
        n = give.shape[1]
        give[...] = whole[pl.ds(pl.multiple_of((1 - place) * HALF, HALF), HALF), at : at + n]
        at += n


def tile_at(i):
    return pl.ds(pl.multiple_of(i * TILE, TILE), TILE)


def gate_left(run, grad, error, start, first, count, before=None, after=()):
    rows, cols = grad.shape
    last = (first + count) * TILE == rows

    def kernel(grad, error, start, *refs):
        if before is not None:
            refs = refs[2:]
        left, fixed = refs[:2]

        def step(g, e):
            at = tile_at(first + pl.program_id(0))
            term = jnp.zeros((RANK, TILE), F32)
            for j in range(0, cols, TILE):
                here = slice(j, j + TILE)
                c = g[:, here] + e[:, here]
                fixed[at, here] = c
                term += lax.dot_general(start[:, here], c, NT, preferred_element_type=F32)
            left[:, at] = term

        spec = pl.BlockSpec((TILE, cols), lambda i: (first + i, 0), pipeline_mode=pl.Buffered(3))
        pltpu.emit_pipeline(step, grid=(count,), in_specs=[spec, spec])(grad, error)
        if last:
            halve(left, core_of(), refs[2], refs[3:])

    args = [(grad, HBM), (error, HBM), (start, VMEM)]
    outs = [((RANK, rows), F32, VMEM), ((rows, cols), BF16, VMEM)]
    if last:
        outs += [((HALF, n), F32, VMEM) for n in (rows, *in_two(rows))]
    aliases = None
    if before is not None:
        args += [(x, VMEM) for x in before]
        aliases = {3: 0, 4: 1}
    return run(kernel, args, outs, mib=8, aliases=aliases, after=after)


def down_left(run, grad, error, start, first, count, before=None, after=()):
    rows, cols = grad.shape
    last = (first + count) * TILE == rows

    def kernel(grad, error, start, *refs):
        if before is not None:
            refs = refs[2:]
        left, fixed = refs[:2]
        pair = 2 * TILE
        block = lax.div(lax.axis_index("dp"), REPLICAS) * (rows // pair) + first // 2
        if before is None:
            left[...] = jnp.zeros_like(left)

        def step(g, e, s):
            i = pl.program_id(0)
            at = tile_at(first + i)
            for j in range(0, cols, TILE):
                here = slice(j, j + TILE)
                fixed[at, here] = g[:, here] + e[:, here]

            @pl.when(lax.rem(i, 2) == 1)
            def _():
                both = pl.ds(pl.multiple_of((first + i - 1) * TILE, pair), pair)
                for j in range(0, cols, TILE):
                    here = slice(j, j + TILE)
                    left[:, here] += jnp.dot(s[...], fixed[both, here], preferred_element_type=F32)

        spec = pl.BlockSpec((TILE, cols), lambda i: (first + i, 0), pipeline_mode=pl.Buffered(3))
        part = pl.BlockSpec((RANK, pair), lambda i: (0, block + lax.div(i, 2)))
        pltpu.emit_pipeline(step, grid=(count,), in_specs=[spec, spec, part])(grad, error, start)
        if last:
            halve(left, replica_of(), refs[2], refs[3:])

    args = [(grad, HBM), (error, HBM), (start, HBM)]
    outs = [((RANK, cols), F32, VMEM), ((rows, cols), BF16, VMEM)]
    if last:
        outs += [((HALF, cols), F32, VMEM)] * 2
    aliases = None
    if before is not None:
        args += [(x, VMEM) for x in before]
        aliases = {3: 0, 4: 1}
    return run(kernel, args, outs, mib=8, aliases=aliases, after=after)


def load_left(owns, others, place, left, stack):
    for refs, half in ((owns, place), (others, 1 - place)):
        at = 0
        for ref in refs:
            n = ref.shape[1]
            left[pl.ds(pl.multiple_of(half * HALF, HALF), HALF), at : at + n] = ref[...]
            at += n
    hi, lo = parts_of(left[...])
    stack[:RANK, :] = hi
    stack[RANK : 2 * RANK, :] = lo
    stack[2 * RANK :, :] = hi
    parts = stack[: 2 * RANK]
    gram = lax.dot_general(parts, parts, NT, preferred_element_type=F32)
    mixed = gram[:RANK, RANK:] + gram[RANK:, :RANK]
    return gram[:RANK, :RANK] + (mixed + gram[RANK:, RANK:])


def packed(gram):
    return jnp.concatenate([gram[:HALF], gram[HALF:]], axis=1)


def gate_right(run, owns, others, fixed, count, after=()):
    rows = fixed.shape[0]
    width = count * TILE
    n_own, n_both = len(owns), len(owns) + len(others)

    def kernel(*refs):
        fixed, keep, give, gram, stack, left, right = refs[n_both:]
        gram[...] = packed(load_left(refs[:n_own], refs[n_own:n_both], core_of(), left, stack))

        def step(i, _):
            both = jnp.dot(stack[: 2 * RANK], fixed[:, tile_at(i)], preferred_element_type=F32)
            right[:, tile_at(i)] = both[:RANK] + both[RANK:]
            return 0

        lax.fori_loop(0, count, step, 0)
        halve(right, replica_of(), keep, [give])

    return run(
        kernel,
        [(x, VMEM) for x in (*owns, *others, fixed)],
        [((HALF, width), F32, VMEM)] * 2
        + [((HALF, 2 * RANK), F32, VMEM), ((3 * RANK, rows), BF16, VMEM)],
        [pltpu.VMEM((RANK, rows), F32), pltpu.VMEM((RANK, width), F32)],
        mib=4,
        after=after,
    )


def gate_right_rest(run, stack, fixed, first, after=()):
    width = fixed.shape[1] - first * TILE

    def kernel(stack, fixed, keep, give, right):
        def step(i, _):
            both = jnp.dot(
                stack[: 2 * RANK], fixed[:, tile_at(first + i)], preferred_element_type=F32
            )
            right[:, tile_at(i)] = both[:RANK] + both[RANK:]
            return 0

        lax.fori_loop(0, width // TILE, step, 0)
        halve(right, replica_of(), keep, [give])

    return run(
        kernel,
        [(stack, VMEM), (fixed, VMEM)],
        [((HALF, width), F32, VMEM)] * 2,
        [pltpu.VMEM((RANK, width), F32)],
        mib=4,
        after=after,
    )


def down_right(run, owns, others, fixed, after=()):
    rows, cols = fixed.shape
    n_own, n_both = len(owns), len(owns) + len(others)
    cut, rest = in_two(rows)

    def kernel(*refs):
        fixed, keep, give_1, give_2, stack, left, right = refs[n_both:]
        gram = load_left(refs[:n_own], refs[n_own:n_both], replica_of(), left, stack)

        def step(i, _):
            both = lax.dot_general(stack[: 2 * RANK], fixed[tile_at(i), :], NT, preferred_element_type=F32)
            right[:, tile_at(i)] = both[:RANK] + both[RANK:]
            return 0

        lax.fori_loop(0, rows // TILE, step, 0)
        halve(right, core_of(), keep.at[:, :rows], [give_1, give_2.at[:, :rest]])
        keep[:, rows:] = packed(gram)
        give_2[:, rest:] = packed(gram)

    widths = (rows + 2 * RANK, cut, rest + 2 * RANK)
    return run(
        kernel,
        [(x, VMEM) for x in (*owns, *others, fixed)],
        [((HALF, n), F32, VMEM) for n in widths] + [((3 * RANK, cols), BF16, VMEM)],
        [pltpu.VMEM((RANK, cols), F32), pltpu.VMEM((RANK, rows), F32)],
        mib=4,
        after=after,
    )


def inverses(grams):
    row_at = lax.broadcasted_iota(jnp.int32, (RANK, RANK), 0)
    col_at = lax.broadcasted_iota(jnp.int32, (RANK, RANK), 1)
    lane = lax.broadcasted_iota(jnp.int32, (1, RANK), 1)

    def scaled(a):
        diagonal = jnp.where(row_at == col_at, a, 0.0)
        down = lax.rsqrt(jnp.sum(diagonal, axis=1, keepdims=True))
        across = lax.rsqrt(jnp.sum(diagonal, axis=0, keepdims=True))
        return a * down * across, down, across

    def sweep(a, k):
        one, two = (row_at == k, row_at == k + 1)
        here = one | two | (col_at == k) | (col_at == k + 1)
        col_1 = jnp.broadcast_to(a[:, k : k + 1], (RANK, RANK))
        col_2 = jnp.broadcast_to(a[:, k + 1 : k + 2], (RANK, RANK))
        p, q, r = col_1[k : k + 1], col_2[k : k + 1], col_2[k + 1 : k + 2]
        row_1 = jnp.where(lane == k, 1.0, jnp.where(lane == k + 1, 0.0, a[k : k + 1]))
        row_2 = jnp.where(lane == k + 1, 1.0, jnp.where(lane == k, 0.0, a[k + 1 : k + 2]))
        inv = 1.0 / (p * r - q * q)
        new_1 = (r * row_1 - q * row_2) * inv
        new_2 = (p * row_2 - q * row_1) * inv
        col_1 = jnp.where(one, -1.0, jnp.where(two, 0.0, col_1))
        col_2 = jnp.where(two, -1.0, jnp.where(one, 0.0, col_2))
        return jnp.where(here, 0.0, a) - col_1 * new_1 - col_2 * new_2

    systems = [scaled(a) for a in grams]
    values = [a for a, _, _ in systems]
    for k in range(0, RANK, 2):
        values = [sweep(a, k) for a in values]
    return [a * down * across for a, (_, down, across) in zip(values, systems)]


def stacked(refs, order, stack):
    at = 0
    for ref in refs:
        parts = parts_of(ref[...])
        n = ref.shape[0]
        for k, which in enumerate(order):
            stack[k * RANK + at : k * RANK + at + n, :] = parts[which]
        at += n


ROW_ORDER, COL_ORDER = (0, 1, 0, 1), (0, 0, 1, 1)


def turn(stack, turned):
    for i in range(0, stack.shape[1], TILE):
        turned[i : i + TILE, :] = stack[:, i : i + TILE].T


def solve(run, grams_down, left_down, gram_gate, left_gate, after=()):
    cols, rows = left_down.shape[1], left_gate.shape[1]

    n = len(grams_down)

    def kernel(*refs):
        gram_gate, left_down, left_gate, col_stack, row_turned, col, row, row_stack = refs[n:]
        gram_down = sum((ref[...] for ref in refs[1:n]), refs[0][...])
        grams = [
            jnp.concatenate([a[:, :RANK], a[:, RANK:]], axis=0) for a in (gram_down, gram_gate[...])
        ]
        for place, a, left, out in zip(
            (core_of(), replica_of()), inverses(grams), (left_down, left_gate), (col, row)
        ):
            other = jnp.concatenate([a[HALF:], a[:HALF]], axis=0)
            a = jnp.where(place == 0, a, other) * (1.0 / REPLICAS)
            hi, lo = parts_of(a)
            both = jnp.concatenate([hi, hi, lo], axis=1)
            out[...] = jnp.dot(both, left[...], preferred_element_type=F32)
        stacked([col], COL_ORDER, col_stack)
        stacked([row], ROW_ORDER, row_stack)
        turn(row_stack, row_turned)

    return run(
        kernel,
        [(x, VMEM) for x in (*grams_down, gram_gate, left_down, left_gate)],
        [((4 * RANK, cols), BF16, VMEM), ((rows, 4 * RANK), BF16, VMEM)],
        [
            pltpu.VMEM((RANK, cols), F32),
            pltpu.VMEM((RANK, rows), F32),
            pltpu.VMEM((4 * RANK, rows), BF16),
        ],
        mib=6,
        after=after,
    )


def rebuild(run, ready, owns, others, fixed, shares, height, first=0, before=None, after=()):
    rows, cols = fixed.shape
    share = rows // REPLICAS
    parts = share // height
    rows_late = ready[0] is None
    late_width = sum(widths_of(owns))
    width = ready[1].shape[1] if rows_late or not owns else late_width
    n_ready = sum(x is not None for x in ready)
    n_own, n_late = len(owns), len(owns) + len(others)
    n_before = 0 if before is None else len(before)
    with_update = 0 in shares
    spots = [(s, t, j) for s in shares for t in range(parts) for j in range(0, width, TILE)]

    def kernel(*refs):
        given, late = refs[:n_ready], refs[n_ready : n_ready + n_late]
        fixed = refs[n_ready + n_late]
        refs = refs[n_ready + n_late + 1 + n_before :]
        new_error, update, turned = refs[0], refs[1], refs[2]
        errors, updates, stack, error_sems, update_sems = refs[3:]
        if late:
            order = ROW_ORDER if rows_late else COL_ORDER
            for at, pieces in ((0, late[:n_own]), (HALF, late[n_own:])):
                left = 0
                for ref in pieces:
                    split = parts_of(ref[...])
                    n, w = ref.shape
                    for k, which in enumerate(order):
                        stack[k * RANK + at : k * RANK + at + n, left : left + w] = split[which]
                    left += w
        if rows_late:
            turn(stack, turned)
            row, col = turned, given[0]
        else:
            turned[...] = jnp.zeros_like(turned)
            row, col = given[0], given[1] if n_ready == 2 else stack
        replica = replica_of()
        copies = []
        for k, (s, t, j) in enumerate(spots):
            at = pl.multiple_of((replica if s == 0 else 1 - replica) * share, height) + t * height
            at = pl.ds(pl.multiple_of(at, height), height)
            here, there = slice(j, j + TILE), pl.ds(first + j, TILE)
            mine = pl.ds(t * height, height)
            value = jnp.dot(row[at, :], col[:, here], preferred_element_type=F32)
            slot = pl.ds((shares.index(s) * parts + t) * height, height)
            errors[slot, here] = (fixed[at, there].astype(F32) - value).astype(BF16)
            copies.append(
                pltpu.make_async_copy(errors.at[slot, here], new_error.at[at, there], error_sems.at[k])
            )
            copies[-1].start()
            if s == 0:
                updates[mine, here] = value.astype(BF16)
                copies.append(
                    pltpu.make_async_copy(updates.at[mine, here], update.at[mine, there], update_sems.at[k])
                )
                copies[-1].start()
        for copy in copies:
            copy.wait()

    turned_shape = (rows, 4 * RANK) if rows_late else (16, 128)
    args = [(x, VMEM) for x in (*(x for x in ready if x is not None), *owns, *others, fixed)]
    aliases = None
    if before is not None:
        aliases = {len(args): 0, len(args) + 1: 1}
        args += [(x, HBM) for x in before]
    return run(
        kernel,
        args,
        [((rows, cols), BF16, HBM), ((share, cols), BF16, HBM), (turned_shape, BF16, VMEM)],
        [
            pltpu.VMEM((len(shares) * share, width), BF16),
            pltpu.VMEM((share if with_update else 16, width), BF16),
            pltpu.VMEM((4 * RANK, late_width if n_late else 128), BF16),
            pltpu.SemaphoreType.DMA((len(spots),)),
            pltpu.SemaphoreType.DMA((len(spots),)),
        ],
        mib=18,
        aliases=aliases,
        after=after,
    )


def local(grad_gate, grad_down, error_gate, error_down, start_gate, start_down):
    slab, width = grad_gate.shape
    n_dp, n_t = lax.axis_size("dp"), lax.axis_size("tensor")
    run = Calls()
    hops, steps = row_steps(), col_steps()
    tiles = slab // TILE

    _, fixed_down, keep, give = down_left(run, grad_down, error_down, start_down, 0, tiles)
    got = exchange(give, other_replica)
    gate_args = (run, grad_gate, error_gate, start_gate)
    cut = tiles * 3 // 5
    first = gate_left(*gate_args, 0, cut, after=(keep,))
    (down,) = add(run, [keep], [got], after=(first[0],))
    got = exchange(down, steps[0])
    _, fixed_gate, keep_gate, *gives = gate_left(
        *gate_args, cut, tiles - cut, first, after=(down,)
    )
    (gate,) = add(run, [keep_gate], to_other_core(gives))
    got_gate = exchange(gate, hops[0])
    for i in range(len(steps)):
        (down,) = add(run, [down], [got], after=(gate,))
        if i + 1 < len(steps):
            got = exchange(down, steps[i + 1])
    other_down = exchange(down, other_replica)
    for hop in hops[1:]:
        (gate,) = add(run, [gate], [got_gate], after=(down,))
        got_gate = exchange(gate, hop)

    keep, *gives, left_down = down_right(run, [down], [other_down], fixed_down, after=(gate,))
    gots = to_other_core(gives)
    gates = add(run, [gate], [got_gate], after=(keep,))
    others_gate = to_other_core(gates)
    down, gram_down = add(run, [keep], gots, [slab, 2 * RANK], after=(gates[0],))
    grams_down = [gram_down] + [
        exchange(gram_down, lambda d, t, b=b: (d, t ^ b)) for b in range(2, n_t, 2)
    ]
    got = exchange(down, hops[0])
    few = width // TILE * 2 // 7
    keep_a, give_a, gram_gate, left_gate = gate_right(
        run, gates, others_gate, fixed_gate, few, after=(down,)
    )
    got_a = exchange(give_a, other_replica)
    keep_b, give_b = gate_right_rest(run, left_gate, fixed_gate, few)
    got_b = exchange(give_b, other_replica)
    (gate_a,) = add(run, [keep_a], [got_a], beside=gram_gate, after=(give_b,))
    got_a = exchange(gate_a, steps[0])
    (gate_b,) = add(run, [keep_b], [got_b], after=(gate_a,))
    got_b = exchange(gate_b, steps[0])
    for hop in hops[1:]:
        (down,) = add(run, [down], [got], after=(gate_b,))
        got = exchange(down, hop)
    for step in steps[1:]:
        (gate_a,) = add(run, [gate_a], [got_a])
        got_a = exchange(gate_a, step)
        (gate_b,) = add(run, [gate_b], [got_b])
        got_b = exchange(gate_b, step)
    gate_a, gram_gate = add(run, [gate_a], [got_a], [few * TILE, 2 * RANK], after=(down,))
    other_a = exchange(gate_a, other_replica)
    col_stack, row_turned = solve(run, grams_down, left_down, gram_gate, left_gate)
    downs = add(run, [down], [got], in_two(slab), after=(col_stack,))
    others_down = to_other_core(downs)
    (gate_b,) = add(run, [gate_b], [got_b], after=(downs[0],))
    other_b = exchange(gate_b, other_replica)
    new_error_down, update_down, turned = rebuild(
        run, (None, col_stack), downs, others_down, fixed_down, (0, 1), slab // 8, after=(gate_b,)
    )
    new_error_gate, update_gate, _ = rebuild(
        run, (row_turned, None), [gate_a, gate_b], [other_a, other_b], fixed_gate, (0, 1), slab // 2,
        after=(turned,),
    )
    return (update_gate, update_down, new_error_gate, new_error_down)


def solution(mesh):
    split = P(("mix", "dp"), "tensor")
    in_specs = (split, split, split, split, P(None, "tensor"), P())
    out_specs = (split, split, split, split)

    def run(grad_gate, *rest):
        groups = mesh.shape["mix"] * mesh.shape["dp"]
        slab = grad_gate.shape[0] // groups
        width = grad_gate.shape[1] // mesh.shape["tensor"]
        fits = slab % (REPLICAS * TILE) == 0 and width % TILE == 0
        body = local if fits else local_plain
        return jax.shard_map(
            body, mesh=mesh, in_specs=in_specs, out_specs=out_specs, check_vma=False
        )(grad_gate, *rest)

    return run
```

```python
import functools

import jax
import jax.numpy as jnp
from jax import lax
from jax.experimental import pallas as pl
from jax.experimental.pallas import tpu as pltpu
from jax.sharding import PartitionSpec as P

REPLICAS = 2
RANK = 64
TILE = 256
FLOPS = 1.15e9
WEIGHTS = (8.0, 4.0, 1.0, 4.0, 0.1, 5.0, 1.0, 5.0, 1.0, 1.0, 2.0, 2.0, 0.1, 1.0, 5.0, 0.1, 0.5, 1.0, 1.0, 8.0, 8.0)
MIB = 1 << 20
BF16 = jnp.bfloat16
F32 = jnp.float32

NN = (((1,), (0,)), ((), ()))
NT = (((1,), (1,)), ((), ()))
TN = (((0,), (0,)), ((), ()))


def from_partner(shard, axis, stride):
    return lax.ppermute(shard, axis, [(i, i ^ 1 << stride) for i in range(lax.axis_size(axis))])


def corrected(grad, error):
    return (grad.astype(F32) + error.astype(F32)).astype(BF16)


def transposed(matrix, ortho):
    return lax.dot_general(matrix, ortho.astype(BF16), TN, preferred_element_type=F32)


def gram_of(left):
    return jnp.dot(left.T, left, precision=lax.Precision.HIGHEST)


def factored(left, inner):
    lower = jnp.linalg.cholesky(inner)
    return lax.linalg.triangular_solve(lower, left, left_side=False, lower=True, transpose_a=True)


def local_plain(grad_gate, grad_down, error_gate, error_down, start_gate, start_down):
    high = lax.Precision.HIGHEST
    dp_place = lax.axis_index("dp")
    block = dp_place // REPLICAS
    replica = dp_place % REPLICAS
    fixed_gate = corrected(grad_gate, error_gate)
    fixed_down = corrected(grad_down, error_down)
    slab = fixed_gate.shape[0]
    cols_down = lax.dynamic_slice_in_dim(start_down, block * slab, slab, 1)
    left_gate = lax.dot_general(fixed_gate, start_gate, NT, preferred_element_type=F32)
    left_down = lax.dot_general(
        fixed_down, cols_down, (((0,), (1,)), ((), ())), preferred_element_type=F32
    )
    left_gate = lax.psum(left_gate, "tensor")
    left_gate = left_gate + from_partner(left_gate, "dp", 0)
    left_down = lax.psum(left_down, "dp")
    keep_gate = (replica == 0).astype(F32)
    inner_gate = lax.psum(gram_of(left_gate) * keep_gate, "dp")
    inner_down = lax.psum(gram_of(left_down), "tensor")
    ortho_gate = factored(left_gate, inner_gate)
    ortho_down = factored(left_down, inner_down)
    right_gate = transposed(fixed_gate, ortho_gate)
    right_gate = lax.psum(right_gate, "dp") / REPLICAS
    right_down = jnp.dot(fixed_down, ortho_down.astype(BF16), preferred_element_type=F32)
    right_down = lax.psum(right_down, "tensor")
    right_down = right_down + from_partner(right_down, "dp", 0)
    right_down = right_down / REPLICAS
    rebuilt_gate = jnp.dot(ortho_gate, right_gate.T, precision=high)
    rebuilt_down = jnp.dot(right_down, ortho_down.T, precision=high)
    share = slab // REPLICAS
    update_gate = lax.dynamic_slice_in_dim(rebuilt_gate, replica * share, share, 0).astype(BF16)
    update_down = lax.dynamic_slice_in_dim(rebuilt_down, replica * share, share, 0).astype(BF16)
    new_error_gate = (fixed_gate.astype(F32) - rebuilt_gate).astype(BF16)
    new_error_down = (fixed_down.astype(F32) - rebuilt_down).astype(BF16)
    return (update_gate, update_down, new_error_gate, new_error_down)


def core_of():
    return lax.rem(lax.axis_index("tensor"), 2)


def replica_of():
    return lax.rem(lax.axis_index("dp"), REPLICAS)


def exchange(x, partner):
    n_dp, n_t = lax.axis_size("dp"), lax.axis_size("tensor")
    pairs = []
    for d in range(n_dp):
        for t in range(n_t):
            to_d, to_t = partner(d, t)
            pairs.append((d * n_t + t, to_d * n_t + to_t))
    return lax.ppermute(x, ("dp", "tensor"), pairs)


def bits(n, low):
    out, b = [], low
    while b < n:
        out.append(b)
        b *= 2
    return out


def row_steps():
    steps = [(0, b) for b in bits(lax.axis_size("tensor"), 2)] + [(1, 0)]

    def partner(i, d, t):
        r, b = steps[i] if t % 2 == 0 else steps[-1 - i]
        return d ^ r, t ^ b

    return [functools.partial(partner, i) for i in range(len(steps))]


def col_steps():
    return [lambda d, t, b=b: (d ^ b, t) for b in bits(lax.axis_size("dp"), REPLICAS)]


def other_core(d, t):
    return d, t ^ 1


def other_replica(d, t):
    return d ^ 1, t


def to_other_core(pieces):
    return [exchange(x, other_core) for x in pieces]


VMEM = pl.BlockSpec(memory_space=pltpu.VMEM)
HBM = pl.BlockSpec(memory_space=pltpu.HBM)
ANY = pl.BlockSpec(memory_space=pl.ANY)
HALF = RANK // 2


class Calls:
    def __init__(self):
        self.count = 0

    def __call__(self, kernel, args, outs, scratch=(), mib=8, aliases=None, after=()):
        n_in, n_after = len(args), len(after)
        operands = [
            pltpu.with_memory_space_constraint(x, pltpu.VMEM if spec is VMEM else pltpu.HBM)
            for x, spec in args
        ]

        def body(*refs):
            kernel(*refs[:n_in], *refs[n_in + n_after :])

        out = pl.pallas_call(
            body,
            out_shape=tuple(
                (pltpu.VMEM if spec is VMEM else pltpu.HBM)(shape, kind) for shape, kind, spec in outs
            ),
            in_specs=[spec for _, spec in args] + [ANY] * n_after,
            out_specs=tuple(spec for *_, spec in outs),
            scratch_shapes=list(scratch),
            input_output_aliases=aliases or {},
            compiler_params=pltpu.CompilerParams(vmem_limit_bytes=mib * MIB),
            cost_estimate=pl.CostEstimate(
                flops=int(WEIGHTS[self.count] * FLOPS), bytes_accessed=1 << 10, transcendentals=0
            ),
        )(*operands, *after)
        self.count += 1
        return out


def parts_of(x):
    hi = x.astype(BF16)
    lo = (x - hi.astype(F32)).astype(BF16)
    return hi, lo


def spans(*widths):
    edges = sorted({sum(w[:i]) for w in widths for i in range(len(w) + 1)})
    for low, high in zip(edges, edges[1:]):
        places = []
        for w in widths:
            k = max(i for i in range(len(w)) if sum(w[:i]) <= low)
            places.append((k, low - sum(w[:k]), high - sum(w[:k])))
        yield places


def widths_of(refs):
    return [ref.shape[1] for ref in refs]


def add(run, xs, ys, widths=None, beside=None, after=()):
    widths = list(widths or widths_of(xs))
    more = 0 if beside is None else beside.shape[1]
    n_x, n_y = len(xs), len(ys)

    def kernel(*refs):
        x, y, out = refs[:n_x], refs[n_x : n_x + n_y], refs[-len(widths) :]
        for (i, i0, i1), (j, j0, j1), (k, k0, k1) in spans(widths_of(x), widths_of(y), widths):
            out[k][:, k0:k1] = x[i][:, i0:i1] + y[j][:, j0:j1]
        if more:
            out[-1][:, widths[-1] :] = refs[n_x + n_y][...]

    outs = [((HALF, n), F32, VMEM) for n in (*widths[:-1], widths[-1] + more)]
    args = [(x, VMEM) for x in (*xs, *ys)]
    if more:
        args.append((beside, VMEM))
    return list(run(kernel, args, outs, mib=2, after=after))


def in_two(width):
    cut = width // 256 * 128
    return [cut, width - cut]


def halve(whole, place, keep, gives):
    keep[...] = whole[pl.ds(pl.multiple_of(place * HALF, HALF), HALF), :]
    at = 0
    for give in gives:
        n = give.shape[1]
        give[...] = whole[pl.ds(pl.multiple_of((1 - place) * HALF, HALF), HALF), at : at + n]
        at += n


def tile_at(i):
    return pl.ds(pl.multiple_of(i * TILE, TILE), TILE)


def gate_left(run, grad, error, start, first, count, before=None, after=()):
    rows, cols = grad.shape
    last = (first + count) * TILE == rows

    def kernel(grad, error, start, *refs):
        if before is not None:
            refs = refs[2:]
        left, fixed = refs[:2]

        def step(g, e):
            at = tile_at(first + pl.program_id(0))
            term = jnp.zeros((RANK, TILE), F32)
            for j in range(0, cols, TILE):
                here = slice(j, j + TILE)
                c = g[:, here] + e[:, here]
                fixed[at, here] = c
                term += lax.dot_general(start[:, here], c, NT, preferred_element_type=F32)
            left[:, at] = term

        spec = pl.BlockSpec((TILE, cols), lambda i: (first + i, 0), pipeline_mode=pl.Buffered(3))
        pltpu.emit_pipeline(step, grid=(count,), in_specs=[spec, spec])(grad, error)
        if last:
            halve(left, core_of(), refs[2], refs[3:])

    args = [(grad, HBM), (error, HBM), (start, VMEM)]
    outs = [((RANK, rows), F32, VMEM), ((rows, cols), BF16, VMEM)]
    if last:
        outs += [((HALF, n), F32, VMEM) for n in (rows, *in_two(rows))]
    aliases = None
    if before is not None:
        args += [(x, VMEM) for x in before]
        aliases = {3: 0, 4: 1}
    return run(kernel, args, outs, mib=8, aliases=aliases, after=after)


def down_left(run, grad, error, start, first, count, before=None, after=()):
    rows, cols = grad.shape
    last = (first + count) * TILE == rows

    def kernel(grad, error, start, *refs):
        if before is not None:
            refs = refs[2:]
        left, fixed = refs[:2]
        pair = 2 * TILE
        block = lax.div(lax.axis_index("dp"), REPLICAS) * (rows // pair) + first // 2
        if before is None:
            left[...] = jnp.zeros_like(left)

        def step(g, e, s):
            i = pl.program_id(0)
            at = tile_at(first + i)
            for j in range(0, cols, TILE):
                here = slice(j, j + TILE)
                fixed[at, here] = g[:, here] + e[:, here]

            @pl.when(lax.rem(i, 2) == 1)
            def _():
                both = pl.ds(pl.multiple_of((first + i - 1) * TILE, pair), pair)
                for j in range(0, cols, TILE):
                    here = slice(j, j + TILE)
                    left[:, here] += jnp.dot(s[...], fixed[both, here], preferred_element_type=F32)

        spec = pl.BlockSpec((TILE, cols), lambda i: (first + i, 0), pipeline_mode=pl.Buffered(3))
        part = pl.BlockSpec((RANK, pair), lambda i: (0, block + lax.div(i, 2)))
        pltpu.emit_pipeline(step, grid=(count,), in_specs=[spec, spec, part])(grad, error, start)
        if last:
            halve(left, replica_of(), refs[2], refs[3:])

    args = [(grad, HBM), (error, HBM), (start, HBM)]
    outs = [((RANK, cols), F32, VMEM), ((rows, cols), BF16, VMEM)]
    if last:
        outs += [((HALF, cols), F32, VMEM)] * 2
    aliases = None
    if before is not None:
        args += [(x, VMEM) for x in before]
        aliases = {3: 0, 4: 1}
    return run(kernel, args, outs, mib=8, aliases=aliases, after=after)


def load_left(owns, others, place, left, stack):
    for refs, half in ((owns, place), (others, 1 - place)):
        at = 0
        for ref in refs:
            n = ref.shape[1]
            left[pl.ds(pl.multiple_of(half * HALF, HALF), HALF), at : at + n] = ref[...]
            at += n
    hi, lo = parts_of(left[...])
    stack[:RANK, :] = hi
    stack[RANK : 2 * RANK, :] = lo
    stack[2 * RANK :, :] = hi
    parts = stack[: 2 * RANK]
    gram = lax.dot_general(parts, parts, NT, preferred_element_type=F32)
    mixed = gram[:RANK, RANK:] + gram[RANK:, :RANK]
    return gram[:RANK, :RANK] + (mixed + gram[RANK:, RANK:])


def packed(gram):
    return jnp.concatenate([gram[:HALF], gram[HALF:]], axis=1)


def gate_right(run, owns, others, fixed, count, after=()):
    rows = fixed.shape[0]
    width = count * TILE
    n_own, n_both = len(owns), len(owns) + len(others)

    def kernel(*refs):
        fixed, keep, give, gram, stack, left, right = refs[n_both:]
        gram[...] = packed(load_left(refs[:n_own], refs[n_own:n_both], core_of(), left, stack))

        def step(i, _):
            both = jnp.dot(stack[: 2 * RANK], fixed[:, tile_at(i)], preferred_element_type=F32)
            right[:, tile_at(i)] = both[:RANK] + both[RANK:]
            return 0

        lax.fori_loop(0, count, step, 0)
        halve(right, replica_of(), keep, [give])

    return run(
        kernel,
        [(x, VMEM) for x in (*owns, *others, fixed)],
        [((HALF, width), F32, VMEM)] * 2
        + [((HALF, 2 * RANK), F32, VMEM), ((3 * RANK, rows), BF16, VMEM)],
        [pltpu.VMEM((RANK, rows), F32), pltpu.VMEM((RANK, width), F32)],
        mib=4,
        after=after,
    )


def gate_right_rest(run, stack, fixed, first, after=()):
    width = fixed.shape[1] - first * TILE

    def kernel(stack, fixed, keep, give, right):
        def step(i, _):
            both = jnp.dot(
                stack[: 2 * RANK], fixed[:, tile_at(first + i)], preferred_element_type=F32
            )
            right[:, tile_at(i)] = both[:RANK] + both[RANK:]
            return 0

        lax.fori_loop(0, width // TILE, step, 0)
        halve(right, replica_of(), keep, [give])

    return run(
        kernel,
        [(stack, VMEM), (fixed, VMEM)],
        [((HALF, width), F32, VMEM)] * 2,
        [pltpu.VMEM((RANK, width), F32)],
        mib=4,
        after=after,
    )


def down_right(run, owns, others, fixed, after=()):
    rows, cols = fixed.shape
    n_own, n_both = len(owns), len(owns) + len(others)
    cut, rest = in_two(rows)

    def kernel(*refs):
        fixed, keep, give_1, give_2, stack, left, right = refs[n_both:]
        gram = load_left(refs[:n_own], refs[n_own:n_both], replica_of(), left, stack)

        def step(i, _):
            both = lax.dot_general(stack[: 2 * RANK], fixed[tile_at(i), :], NT, preferred_element_type=F32)
            right[:, tile_at(i)] = both[:RANK] + both[RANK:]
            return 0

        lax.fori_loop(0, rows // TILE, step, 0)
        halve(right, core_of(), keep.at[:, :rows], [give_1, give_2.at[:, :rest]])
        keep[:, rows:] = packed(gram)
        give_2[:, rest:] = packed(gram)

    widths = (rows + 2 * RANK, cut, rest + 2 * RANK)
    return run(
        kernel,
        [(x, VMEM) for x in (*owns, *others, fixed)],
        [((HALF, n), F32, VMEM) for n in widths] + [((3 * RANK, cols), BF16, VMEM)],
        [pltpu.VMEM((RANK, cols), F32), pltpu.VMEM((RANK, rows), F32)],
        mib=4,
        after=after,
    )


def inverses(grams):
    row_at = lax.broadcasted_iota(jnp.int32, (RANK, RANK), 0)
    col_at = lax.broadcasted_iota(jnp.int32, (RANK, RANK), 1)
    lane = lax.broadcasted_iota(jnp.int32, (1, RANK), 1)

    def scaled(a):
        diagonal = jnp.where(row_at == col_at, a, 0.0)
        down = lax.rsqrt(jnp.sum(diagonal, axis=1, keepdims=True))
        across = lax.rsqrt(jnp.sum(diagonal, axis=0, keepdims=True))
        return a * down * across, down, across

    def sweep(a, k):
        one, two = (row_at == k, row_at == k + 1)
        here = one | two | (col_at == k) | (col_at == k + 1)
        col_1 = jnp.broadcast_to(a[:, k : k + 1], (RANK, RANK))
        col_2 = jnp.broadcast_to(a[:, k + 1 : k + 2], (RANK, RANK))
        p, q, r = col_1[k : k + 1], col_2[k : k + 1], col_2[k + 1 : k + 2]
        row_1 = jnp.where(lane == k, 1.0, jnp.where(lane == k + 1, 0.0, a[k : k + 1]))
        row_2 = jnp.where(lane == k + 1, 1.0, jnp.where(lane == k, 0.0, a[k + 1 : k + 2]))
        inv = 1.0 / (p * r - q * q)
        new_1 = (r * row_1 - q * row_2) * inv
        new_2 = (p * row_2 - q * row_1) * inv
        col_1 = jnp.where(one, -1.0, jnp.where(two, 0.0, col_1))
        col_2 = jnp.where(two, -1.0, jnp.where(one, 0.0, col_2))
        return jnp.where(here, 0.0, a) - col_1 * new_1 - col_2 * new_2

    systems = [scaled(a) for a in grams]
    values = [a for a, _, _ in systems]
    for k in range(0, RANK, 2):
        values = [sweep(a, k) for a in values]
    return [a * down * across for a, (_, down, across) in zip(values, systems)]


def stacked(refs, order, stack):
    at = 0
    for ref in refs:
        parts = parts_of(ref[...])
        n = ref.shape[0]
        for k, which in enumerate(order):
            stack[k * RANK + at : k * RANK + at + n, :] = parts[which]
        at += n


ROW_ORDER, COL_ORDER = (0, 1, 0, 1), (0, 0, 1, 1)


def turn(stack, turned):
    for i in range(0, stack.shape[1], TILE):
        turned[i : i + TILE, :] = stack[:, i : i + TILE].T


def solve(run, grams_down, left_down, gram_gate, left_gate, after=()):
    cols, rows = left_down.shape[1], left_gate.shape[1]

    n = len(grams_down)

    def kernel(*refs):
        gram_gate, left_down, left_gate, col_stack, row_turned, col, row, row_stack = refs[n:]
        gram_down = sum((ref[...] for ref in refs[1:n]), refs[0][...])
        grams = [
            jnp.concatenate([a[:, :RANK], a[:, RANK:]], axis=0) for a in (gram_down, gram_gate[...])
        ]
        for place, a, left, out in zip(
            (core_of(), replica_of()), inverses(grams), (left_down, left_gate), (col, row)
        ):
            other = jnp.concatenate([a[HALF:], a[:HALF]], axis=0)
            a = jnp.where(place == 0, a, other) * (1.0 / REPLICAS)
            hi, lo = parts_of(a)
            both = jnp.concatenate([hi, hi, lo], axis=1)
            out[...] = jnp.dot(both, left[...], preferred_element_type=F32)
        stacked([col], COL_ORDER, col_stack)
        stacked([row], ROW_ORDER, row_stack)
        turn(row_stack, row_turned)

    return run(
        kernel,
        [(x, VMEM) for x in (*grams_down, gram_gate, left_down, left_gate)],
        [((4 * RANK, cols), BF16, VMEM), ((rows, 4 * RANK), BF16, VMEM)],
        [
            pltpu.VMEM((RANK, cols), F32),
            pltpu.VMEM((RANK, rows), F32),
            pltpu.VMEM((4 * RANK, rows), BF16),
        ],
        mib=6,
        after=after,
    )


def rebuild(run, ready, owns, others, fixed, shares, height, first=0, before=None, after=()):
    rows, cols = fixed.shape
    share = rows // REPLICAS
    parts = share // height
    rows_late = ready[0] is None
    late_width = sum(widths_of(owns))
    width = ready[1].shape[1] if rows_late or not owns else late_width
    n_ready = sum(x is not None for x in ready)
    n_own, n_late = len(owns), len(owns) + len(others)
    n_before = 0 if before is None else len(before)
    with_update = 0 in shares
    spots = [(s, t, j) for s in shares for t in range(parts) for j in range(0, width, TILE)]

    def kernel(*refs):
        given, late = refs[:n_ready], refs[n_ready : n_ready + n_late]
        fixed = refs[n_ready + n_late]
        refs = refs[n_ready + n_late + 1 + n_before :]
        new_error, update, turned = refs[0], refs[1], refs[2]
        errors, updates, stack, error_sems, update_sems = refs[3:]
        if late:
            order = ROW_ORDER if rows_late else COL_ORDER
            for at, pieces in ((0, late[:n_own]), (HALF, late[n_own:])):
                left = 0
                for ref in pieces:
                    split = parts_of(ref[...])
                    n, w = ref.shape
                    for k, which in enumerate(order):
                        stack[k * RANK + at : k * RANK + at + n, left : left + w] = split[which]
                    left += w
        if rows_late:
            turn(stack, turned)
            row, col = turned, given[0]
        else:
            turned[...] = jnp.zeros_like(turned)
            row, col = given[0], given[1] if n_ready == 2 else stack
        replica = replica_of()
        copies = []
        for k, (s, t, j) in enumerate(spots):
            at = pl.multiple_of((replica if s == 0 else 1 - replica) * share, height) + t * height
            at = pl.ds(pl.multiple_of(at, height), height)
            here, there = slice(j, j + TILE), pl.ds(first + j, TILE)
            mine = pl.ds(t * height, height)
            value = jnp.dot(row[at, :], col[:, here], preferred_element_type=F32)
            slot = pl.ds((shares.index(s) * parts + t) * height, height)
            errors[slot, here] = (fixed[at, there].astype(F32) - value).astype(BF16)
            copies.append(
                pltpu.make_async_copy(errors.at[slot, here], new_error.at[at, there], error_sems.at[k])
            )
            copies[-1].start()
            if s == 0:
                updates[mine, here] = value.astype(BF16)
                copies.append(
                    pltpu.make_async_copy(updates.at[mine, here], update.at[mine, there], update_sems.at[k])
                )
                copies[-1].start()
        for copy in copies:
            copy.wait()

    turned_shape = (rows, 4 * RANK) if rows_late else (16, 128)
    args = [(x, VMEM) for x in (*(x for x in ready if x is not None), *owns, *others, fixed)]
    aliases = None
    if before is not None:
        aliases = {len(args): 0, len(args) + 1: 1}
        args += [(x, HBM) for x in before]
    return run(
        kernel,
        args,
        [((rows, cols), BF16, HBM), ((share, cols), BF16, HBM), (turned_shape, BF16, VMEM)],
        [
            pltpu.VMEM((len(shares) * share, width), BF16),
            pltpu.VMEM((share if with_update else 16, width), BF16),
            pltpu.VMEM((4 * RANK, late_width if n_late else 128), BF16),
            pltpu.SemaphoreType.DMA((len(spots),)),
            pltpu.SemaphoreType.DMA((len(spots),)),
        ],
        mib=18,
        aliases=aliases,
        after=after,
    )


def local(grad_gate, grad_down, error_gate, error_down, start_gate, start_down):
    slab, width = grad_gate.shape
    n_dp, n_t = lax.axis_size("dp"), lax.axis_size("tensor")
    run = Calls()
    hops, steps = row_steps(), col_steps()
    tiles = slab // TILE

    _, fixed_down, keep, give = down_left(run, grad_down, error_down, start_down, 0, tiles)
    got = exchange(give, other_replica)
    gate_args = (run, grad_gate, error_gate, start_gate)
    cut = tiles * 3 // 5
    first = gate_left(*gate_args, 0, cut, after=(keep,))
    (down,) = add(run, [keep], [got], after=(first[0],))
    got = exchange(down, steps[0])
    _, fixed_gate, keep_gate, *gives = gate_left(
        *gate_args, cut, tiles - cut, first, after=(down,)
    )
    (gate,) = add(run, [keep_gate], to_other_core(gives))
    got_gate = exchange(gate, hops[0])
    for i in range(len(steps)):
        (down,) = add(run, [down], [got], after=(gate,))
        if i + 1 < len(steps):
            got = exchange(down, steps[i + 1])
    other_down = exchange(down, other_replica)
    for hop in hops[1:]:
        (gate,) = add(run, [gate], [got_gate], after=(down,))
        got_gate = exchange(gate, hop)

    keep, *gives, left_down = down_right(run, [down], [other_down], fixed_down, after=(gate,))
    gots = to_other_core(gives)
    gates = add(run, [gate], [got_gate], after=(keep,))
    others_gate = to_other_core(gates)
    down, gram_down = add(run, [keep], gots, [slab, 2 * RANK], after=(gates[0],))
    grams_down = [gram_down] + [
        exchange(gram_down, lambda d, t, b=b: (d, t ^ b)) for b in range(2, n_t, 2)
    ]
    got = exchange(down, hops[0])
    few = width // TILE * 2 // 7
    keep_a, give_a, gram_gate, left_gate = gate_right(
        run, gates, others_gate, fixed_gate, few, after=(down,)
    )
    got_a = exchange(give_a, other_replica)
    keep_b, give_b = gate_right_rest(run, left_gate, fixed_gate, few)
    got_b = exchange(give_b, other_replica)
    for hop in hops[1:]:
        (down,) = add(run, [down], [got], after=(give_b,))
        got = exchange(down, hop)
    (gate_a,) = add(run, [keep_a], [got_a], beside=gram_gate, after=(down,))
    got_a = exchange(gate_a, steps[0])
    (gate_b,) = add(run, [keep_b], [got_b], after=(gate_a,))
    got_b = exchange(gate_b, steps[0])
    for step in steps[1:]:
        (gate_a,) = add(run, [gate_a], [got_a])
        got_a = exchange(gate_a, step)
        (gate_b,) = add(run, [gate_b], [got_b])
        got_b = exchange(gate_b, step)
    gate_a, gram_gate = add(run, [gate_a], [got_a], [few * TILE, 2 * RANK], after=(gate_b,))
    other_a = exchange(gate_a, other_replica)
    col_stack, row_turned = solve(run, grams_down, left_down, gram_gate, left_gate)
    downs = add(run, [down], [got], in_two(slab), after=(col_stack,))
    others_down = to_other_core(downs)
    (gate_b,) = add(run, [gate_b], [got_b], after=(downs[0],))
    other_b = exchange(gate_b, other_replica)
    new_error_down, update_down, turned = rebuild(
        run, (None, col_stack), downs, others_down, fixed_down, (0, 1), slab // 8, after=(gate_b,)
    )
    new_error_gate, update_gate, _ = rebuild(
        run, (row_turned, None), [gate_a, gate_b], [other_a, other_b], fixed_gate, (0, 1), slab // 2,
        after=(turned,),
    )
    return (update_gate, update_down, new_error_gate, new_error_down)


def solution(mesh):
    split = P(("mix", "dp"), "tensor")
    in_specs = (split, split, split, split, P(None, "tensor"), P())
    out_specs = (split, split, split, split)

    def run(grad_gate, *rest):
        groups = mesh.shape["mix"] * mesh.shape["dp"]
        slab = grad_gate.shape[0] // groups
        width = grad_gate.shape[1] // mesh.shape["tensor"]
        fits = slab % (REPLICAS * TILE) == 0 and width % TILE == 0
        body = local if fits else local_plain
        return jax.shard_map(
            body, mesh=mesh, in_specs=in_specs, out_specs=out_specs, check_vma=False
        )(grad_gate, *rest)

    return run
```

```python
import functools

import jax
import jax.numpy as jnp
from jax import lax
from jax.experimental import pallas as pl
from jax.experimental.pallas import tpu as pltpu
from jax.sharding import PartitionSpec as P

REPLICAS = 2
RANK = 64
TILE = 256
FLOPS = 1.15e9
WEIGHTS = (8.0, 4.0, 1.0, 4.0, 0.1, 5.0, 1.0, 5.0, 1.0, 1.0, 2.0, 2.0, 0.1, 1.0, 5.0, 0.1, 0.5, 1.0, 1.0, 8.0, 8.0)
MIB = 1 << 20
BF16 = jnp.bfloat16
F32 = jnp.float32

NN = (((1,), (0,)), ((), ()))
NT = (((1,), (1,)), ((), ()))
TN = (((0,), (0,)), ((), ()))


def from_partner(shard, axis, stride):
    return lax.ppermute(shard, axis, [(i, i ^ 1 << stride) for i in range(lax.axis_size(axis))])


def corrected(grad, error):
    return (grad.astype(F32) + error.astype(F32)).astype(BF16)


def transposed(matrix, ortho):
    return lax.dot_general(matrix, ortho.astype(BF16), TN, preferred_element_type=F32)


def gram_of(left):
    return jnp.dot(left.T, left, precision=lax.Precision.HIGHEST)


def factored(left, inner):
    lower = jnp.linalg.cholesky(inner)
    return lax.linalg.triangular_solve(lower, left, left_side=False, lower=True, transpose_a=True)


def local_plain(grad_gate, grad_down, error_gate, error_down, start_gate, start_down):
    high = lax.Precision.HIGHEST
    dp_place = lax.axis_index("dp")
    block = dp_place // REPLICAS
    replica = dp_place % REPLICAS
    fixed_gate = corrected(grad_gate, error_gate)
    fixed_down = corrected(grad_down, error_down)
    slab = fixed_gate.shape[0]
    cols_down = lax.dynamic_slice_in_dim(start_down, block * slab, slab, 1)
    left_gate = lax.dot_general(fixed_gate, start_gate, NT, preferred_element_type=F32)
    left_down = lax.dot_general(
        fixed_down, cols_down, (((0,), (1,)), ((), ())), preferred_element_type=F32
    )
    left_gate = lax.psum(left_gate, "tensor")
    left_gate = left_gate + from_partner(left_gate, "dp", 0)
    left_down = lax.psum(left_down, "dp")
    keep_gate = (replica == 0).astype(F32)
    inner_gate = lax.psum(gram_of(left_gate) * keep_gate, "dp")
    inner_down = lax.psum(gram_of(left_down), "tensor")
    ortho_gate = factored(left_gate, inner_gate)
    ortho_down = factored(left_down, inner_down)
    right_gate = transposed(fixed_gate, ortho_gate)
    right_gate = lax.psum(right_gate, "dp") / REPLICAS
    right_down = jnp.dot(fixed_down, ortho_down.astype(BF16), preferred_element_type=F32)
    right_down = lax.psum(right_down, "tensor")
    right_down = right_down + from_partner(right_down, "dp", 0)
    right_down = right_down / REPLICAS
    rebuilt_gate = jnp.dot(ortho_gate, right_gate.T, precision=high)
    rebuilt_down = jnp.dot(right_down, ortho_down.T, precision=high)
    share = slab // REPLICAS
    update_gate = lax.dynamic_slice_in_dim(rebuilt_gate, replica * share, share, 0).astype(BF16)
    update_down = lax.dynamic_slice_in_dim(rebuilt_down, replica * share, share, 0).astype(BF16)
    new_error_gate = (fixed_gate.astype(F32) - rebuilt_gate).astype(BF16)
    new_error_down = (fixed_down.astype(F32) - rebuilt_down).astype(BF16)
    return (update_gate, update_down, new_error_gate, new_error_down)


def core_of():
    return lax.rem(lax.axis_index("tensor"), 2)


def replica_of():
    return lax.rem(lax.axis_index("dp"), REPLICAS)


def exchange(x, partner):
    n_dp, n_t = lax.axis_size("dp"), lax.axis_size("tensor")
    pairs = []
    for d in range(n_dp):
        for t in range(n_t):
            to_d, to_t = partner(d, t)
            pairs.append((d * n_t + t, to_d * n_t + to_t))
    return lax.ppermute(x, ("dp", "tensor"), pairs)


def bits(n, low):
    out, b = [], low
    while b < n:
        out.append(b)
        b *= 2
    return out


def row_steps():
    steps = [(0, b) for b in bits(lax.axis_size("tensor"), 2)] + [(1, 0)]

    def partner(i, d, t):
        r, b = steps[i] if t % 2 == 0 else steps[-1 - i]
        return d ^ r, t ^ b

    return [functools.partial(partner, i) for i in range(len(steps))]


def col_steps():
    return [lambda d, t, b=b: (d ^ b, t) for b in bits(lax.axis_size("dp"), REPLICAS)]


def other_core(d, t):
    return d, t ^ 1


def other_replica(d, t):
    return d ^ 1, t


def to_other_core(pieces):
    return [exchange(x, other_core) for x in pieces]


VMEM = pl.BlockSpec(memory_space=pltpu.VMEM)
HBM = pl.BlockSpec(memory_space=pltpu.HBM)
ANY = pl.BlockSpec(memory_space=pl.ANY)
HALF = RANK // 2


class Calls:
    def __init__(self):
        self.count = 0

    def __call__(self, kernel, args, outs, scratch=(), mib=8, aliases=None, after=()):
        n_in, n_after = len(args), len(after)
        operands = [
            pltpu.with_memory_space_constraint(x, pltpu.VMEM if spec is VMEM else pltpu.HBM)
            for x, spec in args
        ]

        def body(*refs):
            kernel(*refs[:n_in], *refs[n_in + n_after :])

        out = pl.pallas_call(
            body,
            out_shape=tuple(
                (pltpu.VMEM if spec is VMEM else pltpu.HBM)(shape, kind) for shape, kind, spec in outs
            ),
            in_specs=[spec for _, spec in args] + [ANY] * n_after,
            out_specs=tuple(spec for *_, spec in outs),
            scratch_shapes=list(scratch),
            input_output_aliases=aliases or {},
            compiler_params=pltpu.CompilerParams(vmem_limit_bytes=mib * MIB),
            cost_estimate=pl.CostEstimate(
                flops=int(WEIGHTS[self.count] * FLOPS), bytes_accessed=1 << 10, transcendentals=0
            ),
        )(*operands, *after)
        self.count += 1
        return out


def parts_of(x):
    hi = x.astype(BF16)
    lo = (x - hi.astype(F32)).astype(BF16)
    return hi, lo


def spans(*widths):
    edges = sorted({sum(w[:i]) for w in widths for i in range(len(w) + 1)})
    for low, high in zip(edges, edges[1:]):
        places = []
        for w in widths:
            k = max(i for i in range(len(w)) if sum(w[:i]) <= low)
            places.append((k, low - sum(w[:k]), high - sum(w[:k])))
        yield places


def widths_of(refs):
    return [ref.shape[1] for ref in refs]


def add(run, xs, ys, widths=None, beside=None, after=()):
    widths = list(widths or widths_of(xs))
    more = 0 if beside is None else beside.shape[1]
    n_x, n_y = len(xs), len(ys)

    def kernel(*refs):
        x, y, out = refs[:n_x], refs[n_x : n_x + n_y], refs[-len(widths) :]
        for (i, i0, i1), (j, j0, j1), (k, k0, k1) in spans(widths_of(x), widths_of(y), widths):
            out[k][:, k0:k1] = x[i][:, i0:i1] + y[j][:, j0:j1]
        if more:
            out[-1][:, widths[-1] :] = refs[n_x + n_y][...]

    outs = [((HALF, n), F32, VMEM) for n in (*widths[:-1], widths[-1] + more)]
    args = [(x, VMEM) for x in (*xs, *ys)]
    if more:
        args.append((beside, VMEM))
    return list(run(kernel, args, outs, mib=2, after=after))


def in_two(width):
    cut = width // 256 * 128
    return [cut, width - cut]


def halve(whole, place, keep, gives):
    keep[...] = whole[pl.ds(pl.multiple_of(place * HALF, HALF), HALF), :]
    at = 0
    for give in gives:
        n = give.shape[1]
        give[...] = whole[pl.ds(pl.multiple_of((1 - place) * HALF, HALF), HALF), at : at + n]
        at += n


def tile_at(i):
    return pl.ds(pl.multiple_of(i * TILE, TILE), TILE)


def gate_left(run, grad, error, start, first, count, before=None, after=()):
    rows, cols = grad.shape
    last = (first + count) * TILE == rows

    def kernel(grad, error, start, *refs):
        if before is not None:
            refs = refs[2:]
        left, fixed = refs[:2]

        def step(g, e):
            at = tile_at(first + pl.program_id(0))
            term = jnp.zeros((RANK, TILE), F32)
            for j in range(0, cols, TILE):
                here = slice(j, j + TILE)
                c = g[:, here] + e[:, here]
                fixed[at, here] = c
                term += lax.dot_general(start[:, here], c, NT, preferred_element_type=F32)
            left[:, at] = term

        spec = pl.BlockSpec((TILE, cols), lambda i: (first + i, 0), pipeline_mode=pl.Buffered(3))
        pltpu.emit_pipeline(step, grid=(count,), in_specs=[spec, spec])(grad, error)
        if last:
            halve(left, core_of(), refs[2], refs[3:])

    args = [(grad, HBM), (error, HBM), (start, VMEM)]
    outs = [((RANK, rows), F32, VMEM), ((rows, cols), BF16, VMEM)]
    if last:
        outs += [((HALF, n), F32, VMEM) for n in (rows, *in_two(rows))]
    aliases = None
    if before is not None:
        args += [(x, VMEM) for x in before]
        aliases = {3: 0, 4: 1}
    return run(kernel, args, outs, mib=8, aliases=aliases, after=after)


def down_left(run, grad, error, start, first, count, before=None, after=()):
    rows, cols = grad.shape
    last = (first + count) * TILE == rows

    def kernel(grad, error, start, *refs):
        if before is not None:
            refs = refs[2:]
        left, fixed = refs[:2]
        pair = 2 * TILE
        block = lax.div(lax.axis_index("dp"), REPLICAS) * (rows // pair) + first // 2
        if before is None:
            left[...] = jnp.zeros_like(left)

        def step(g, e, s):
            i = pl.program_id(0)
            at = tile_at(first + i)
            for j in range(0, cols, TILE):
                here = slice(j, j + TILE)
                fixed[at, here] = g[:, here] + e[:, here]

            @pl.when(lax.rem(i, 2) == 1)
            def _():
                both = pl.ds(pl.multiple_of((first + i - 1) * TILE, pair), pair)
                for j in range(0, cols, TILE):
                    here = slice(j, j + TILE)
                    left[:, here] += jnp.dot(s[...], fixed[both, here], preferred_element_type=F32)

        spec = pl.BlockSpec((TILE, cols), lambda i: (first + i, 0), pipeline_mode=pl.Buffered(3))
        part = pl.BlockSpec((RANK, pair), lambda i: (0, block + lax.div(i, 2)))
        pltpu.emit_pipeline(step, grid=(count,), in_specs=[spec, spec, part])(grad, error, start)
        if last:
            halve(left, replica_of(), refs[2], refs[3:])

    args = [(grad, HBM), (error, HBM), (start, HBM)]
    outs = [((RANK, cols), F32, VMEM), ((rows, cols), BF16, VMEM)]
    if last:
        outs += [((HALF, cols), F32, VMEM)] * 2
    aliases = None
    if before is not None:
        args += [(x, VMEM) for x in before]
        aliases = {3: 0, 4: 1}
    return run(kernel, args, outs, mib=8, aliases=aliases, after=after)


def load_left(owns, others, place, left, stack):
    for refs, half in ((owns, place), (others, 1 - place)):
        at = 0
        for ref in refs:
            n = ref.shape[1]
            left[pl.ds(pl.multiple_of(half * HALF, HALF), HALF), at : at + n] = ref[...]
            at += n
    hi, lo = parts_of(left[...])
    stack[:RANK, :] = hi
    stack[RANK : 2 * RANK, :] = lo
    stack[2 * RANK :, :] = hi
    parts = stack[: 2 * RANK]
    gram = lax.dot_general(parts, parts, NT, preferred_element_type=F32)
    mixed = gram[:RANK, RANK:] + gram[RANK:, :RANK]
    return gram[:RANK, :RANK] + (mixed + gram[RANK:, RANK:])


def packed(gram):
    return jnp.concatenate([gram[:HALF], gram[HALF:]], axis=1)


def gate_right(run, owns, others, fixed, count, after=()):
    rows = fixed.shape[0]
    width = count * TILE
    n_own, n_both = len(owns), len(owns) + len(others)

    def kernel(*refs):
        fixed, keep, give, gram, stack, left, right = refs[n_both:]
        gram[...] = packed(load_left(refs[:n_own], refs[n_own:n_both], core_of(), left, stack))

        def step(i, _):
            both = jnp.dot(stack[: 2 * RANK], fixed[:, tile_at(i)], preferred_element_type=F32)
            right[:, tile_at(i)] = both[:RANK] + both[RANK:]
            return 0

        lax.fori_loop(0, count, step, 0)
        halve(right, replica_of(), keep, [give])

    return run(
        kernel,
        [(x, VMEM) for x in (*owns, *others, fixed)],
        [((HALF, width), F32, VMEM)] * 2
        + [((HALF, 2 * RANK), F32, VMEM), ((3 * RANK, rows), BF16, VMEM)],
        [pltpu.VMEM((RANK, rows), F32), pltpu.VMEM((RANK, width), F32)],
        mib=4,
        after=after,
    )


def gate_right_rest(run, stack, fixed, first, after=()):
    width = fixed.shape[1] - first * TILE

    def kernel(stack, fixed, keep, give, right):
        def step(i, _):
            both = jnp.dot(
                stack[: 2 * RANK], fixed[:, tile_at(first + i)], preferred_element_type=F32
            )
            right[:, tile_at(i)] = both[:RANK] + both[RANK:]
            return 0

        lax.fori_loop(0, width // TILE, step, 0)
        halve(right, replica_of(), keep, [give])

    return run(
        kernel,
        [(stack, VMEM), (fixed, VMEM)],
        [((HALF, width), F32, VMEM)] * 2,
        [pltpu.VMEM((RANK, width), F32)],
        mib=4,
        after=after,
    )


def down_right(run, owns, others, fixed, after=()):
    rows, cols = fixed.shape
    n_own, n_both = len(owns), len(owns) + len(others)
    cut, rest = in_two(rows)

    def kernel(*refs):
        fixed, keep, give_1, give_2, stack, left, right = refs[n_both:]
        gram = load_left(refs[:n_own], refs[n_own:n_both], replica_of(), left, stack)

        def step(i, _):
            both = lax.dot_general(stack[: 2 * RANK], fixed[tile_at(i), :], NT, preferred_element_type=F32)
            right[:, tile_at(i)] = both[:RANK] + both[RANK:]
            return 0

        lax.fori_loop(0, rows // TILE, step, 0)
        halve(right, core_of(), keep.at[:, :rows], [give_1, give_2.at[:, :rest]])
        keep[:, rows:] = packed(gram)
        give_2[:, rest:] = packed(gram)

    widths = (rows + 2 * RANK, cut, rest + 2 * RANK)
    return run(
        kernel,
        [(x, VMEM) for x in (*owns, *others, fixed)],
        [((HALF, n), F32, VMEM) for n in widths] + [((3 * RANK, cols), BF16, VMEM)],
        [pltpu.VMEM((RANK, cols), F32), pltpu.VMEM((RANK, rows), F32)],
        mib=4,
        after=after,
    )


def inverses(grams):
    row_at = lax.broadcasted_iota(jnp.int32, (RANK, RANK), 0)
    col_at = lax.broadcasted_iota(jnp.int32, (RANK, RANK), 1)
    lane = lax.broadcasted_iota(jnp.int32, (1, RANK), 1)

    def scaled(a):
        diagonal = jnp.where(row_at == col_at, a, 0.0)
        down = lax.rsqrt(jnp.sum(diagonal, axis=1, keepdims=True))
        across = lax.rsqrt(jnp.sum(diagonal, axis=0, keepdims=True))
        return a * down * across, down, across

    def sweep(a, k):
        one, two = (row_at == k, row_at == k + 1)
        here = one | two | (col_at == k) | (col_at == k + 1)
        col_1 = jnp.broadcast_to(a[:, k : k + 1], (RANK, RANK))
        col_2 = jnp.broadcast_to(a[:, k + 1 : k + 2], (RANK, RANK))
        p, q, r = col_1[k : k + 1], col_2[k : k + 1], col_2[k + 1 : k + 2]
        row_1 = jnp.where(lane == k, 1.0, jnp.where(lane == k + 1, 0.0, a[k : k + 1]))
        row_2 = jnp.where(lane == k + 1, 1.0, jnp.where(lane == k, 0.0, a[k + 1 : k + 2]))
        inv = 1.0 / (p * r - q * q)
        new_1 = (r * row_1 - q * row_2) * inv
        new_2 = (p * row_2 - q * row_1) * inv
        col_1 = jnp.where(one, -1.0, jnp.where(two, 0.0, col_1))
        col_2 = jnp.where(two, -1.0, jnp.where(one, 0.0, col_2))
        return jnp.where(here, 0.0, a) - col_1 * new_1 - col_2 * new_2

    systems = [scaled(a) for a in grams]
    values = [a for a, _, _ in systems]
    for k in range(0, RANK, 2):
        values = [sweep(a, k) for a in values]
    return [a * down * across for a, (_, down, across) in zip(values, systems)]


def stacked(refs, order, stack):
    at = 0
    for ref in refs:
        parts = parts_of(ref[...])
        n = ref.shape[0]
        for k, which in enumerate(order):
            stack[k * RANK + at : k * RANK + at + n, :] = parts[which]
        at += n


ROW_ORDER, COL_ORDER = (0, 1, 0, 1), (0, 0, 1, 1)


def turn(stack, turned):
    for i in range(0, stack.shape[1], TILE):
        turned[i : i + TILE, :] = stack[:, i : i + TILE].T


def solve(run, grams_down, left_down, gram_gate, left_gate, after=()):
    cols, rows = left_down.shape[1], left_gate.shape[1]

    n = len(grams_down)

    def kernel(*refs):
        gram_gate, left_down, left_gate, col_stack, row_turned, col, row, row_stack = refs[n:]
        gram_down = sum((ref[...] for ref in refs[1:n]), refs[0][...])
        grams = [
            jnp.concatenate([a[:, :RANK], a[:, RANK:]], axis=0) for a in (gram_down, gram_gate[...])
        ]
        for place, a, left, out in zip(
            (core_of(), replica_of()), inverses(grams), (left_down, left_gate), (col, row)
        ):
            other = jnp.concatenate([a[HALF:], a[:HALF]], axis=0)
            a = jnp.where(place == 0, a, other) * (1.0 / REPLICAS)
            hi, lo = parts_of(a)
            both = jnp.concatenate([hi, hi, lo], axis=1)
            out[...] = jnp.dot(both, left[...], preferred_element_type=F32)
        stacked([col], COL_ORDER, col_stack)
        stacked([row], ROW_ORDER, row_stack)
        turn(row_stack, row_turned)

    return run(
        kernel,
        [(x, VMEM) for x in (*grams_down, gram_gate, left_down, left_gate)],
        [((4 * RANK, cols), BF16, VMEM), ((rows, 4 * RANK), BF16, VMEM)],
        [
            pltpu.VMEM((RANK, cols), F32),
            pltpu.VMEM((RANK, rows), F32),
            pltpu.VMEM((4 * RANK, rows), BF16),
        ],
        mib=6,
        after=after,
    )


def rebuild(run, ready, owns, others, fixed, shares, height, first=0, before=None, after=()):
    rows, cols = fixed.shape
    share = rows // REPLICAS
    parts = share // height
    rows_late = ready[0] is None
    late_width = sum(widths_of(owns))
    width = ready[1].shape[1] if rows_late or not owns else late_width
    n_ready = sum(x is not None for x in ready)
    n_own, n_late = len(owns), len(owns) + len(others)
    n_before = 0 if before is None else len(before)
    with_update = 0 in shares
    spots = [(s, t, j) for s in shares for t in range(parts) for j in range(0, width, TILE)]

    def kernel(*refs):
        given, late = refs[:n_ready], refs[n_ready : n_ready + n_late]
        fixed = refs[n_ready + n_late]
        refs = refs[n_ready + n_late + 1 + n_before :]
        new_error, update, turned = refs[0], refs[1], refs[2]
        errors, updates, stack, error_sems, update_sems = refs[3:]
        if late:
            order = ROW_ORDER if rows_late else COL_ORDER
            for at, pieces in ((0, late[:n_own]), (HALF, late[n_own:])):
                left = 0
                for ref in pieces:
                    split = parts_of(ref[...])
                    n, w = ref.shape
                    for k, which in enumerate(order):
                        stack[k * RANK + at : k * RANK + at + n, left : left + w] = split[which]
                    left += w
        if rows_late:
            turn(stack, turned)
            row, col = turned, given[0]
        else:
            turned[...] = jnp.zeros_like(turned)
            row, col = given[0], given[1] if n_ready == 2 else stack
        replica = replica_of()
        copies = []
        for k, (s, t, j) in enumerate(spots):
            at = pl.multiple_of((replica if s == 0 else 1 - replica) * share, height) + t * height
            at = pl.ds(pl.multiple_of(at, height), height)
            here, there = slice(j, j + TILE), pl.ds(first + j, TILE)
            mine = pl.ds(t * height, height)
            value = jnp.dot(row[at, :], col[:, here], preferred_element_type=F32)
            slot = pl.ds((shares.index(s) * parts + t) * height, height)
            errors[slot, here] = (fixed[at, there].astype(F32) - value).astype(BF16)
            copies.append(
                pltpu.make_async_copy(errors.at[slot, here], new_error.at[at, there], error_sems.at[k])
            )
            copies[-1].start()
            if s == 0:
                updates[mine, here] = value.astype(BF16)
                copies.append(
                    pltpu.make_async_copy(updates.at[mine, here], update.at[mine, there], update_sems.at[k])
                )
                copies[-1].start()
        for copy in copies:
            copy.wait()

    turned_shape = (rows, 4 * RANK) if rows_late else (16, 128)
    args = [(x, VMEM) for x in (*(x for x in ready if x is not None), *owns, *others, fixed)]
    aliases = None
    if before is not None:
        aliases = {len(args): 0, len(args) + 1: 1}
        args += [(x, HBM) for x in before]
    return run(
        kernel,
        args,
        [((rows, cols), BF16, HBM), ((share, cols), BF16, HBM), (turned_shape, BF16, VMEM)],
        [
            pltpu.VMEM((len(shares) * share, width), BF16),
            pltpu.VMEM((share if with_update else 16, width), BF16),
            pltpu.VMEM((4 * RANK, late_width if n_late else 128), BF16),
            pltpu.SemaphoreType.DMA((len(spots),)),
            pltpu.SemaphoreType.DMA((len(spots),)),
        ],
        mib=18,
        aliases=aliases,
        after=after,
    )


def local(grad_gate, grad_down, error_gate, error_down, start_gate, start_down):
    slab, width = grad_gate.shape
    n_dp, n_t = lax.axis_size("dp"), lax.axis_size("tensor")
    run = Calls()
    hops, steps = row_steps(), col_steps()
    tiles = slab // TILE

    _, fixed_down, keep, give = down_left(run, grad_down, error_down, start_down, 0, tiles)
    got = exchange(give, other_replica)
    gate_args = (run, grad_gate, error_gate, start_gate)
    cut = tiles * 3 // 5
    first = gate_left(*gate_args, 0, cut, after=(keep,))
    (down,) = add(run, [keep], [got], after=(first[0],))
    got = exchange(down, steps[0])
    _, fixed_gate, keep_gate, *gives = gate_left(
        *gate_args, cut, tiles - cut, first, after=(down,)
    )
    (gate,) = add(run, [keep_gate], to_other_core(gives))
    got_gate = exchange(gate, hops[0])
    for i in range(len(steps)):
        (down,) = add(run, [down], [got], after=(gate,))
        if i + 1 < len(steps):
            got = exchange(down, steps[i + 1])
    other_down = exchange(down, other_replica)
    for hop in hops[1:]:
        (gate,) = add(run, [gate], [got_gate], after=(down,))
        got_gate = exchange(gate, hop)

    keep, *gives, left_down = down_right(run, [down], [other_down], fixed_down, after=(gate,))
    gots = to_other_core(gives)
    gates = add(run, [gate], [got_gate], after=(keep,))
    others_gate = to_other_core(gates)
    down, gram_down = add(run, [keep], gots, [slab, 2 * RANK], after=(gates[0],))
    grams_down = [gram_down] + [
        exchange(gram_down, lambda d, t, b=b: (d, t ^ b)) for b in range(2, n_t, 2)
    ]
    got = exchange(down, hops[0])
    few = width // TILE * 3 // 7
    keep_a, give_a, gram_gate, left_gate = gate_right(
        run, gates, others_gate, fixed_gate, few, after=(down,)
    )
    got_a = exchange(give_a, other_replica)
    keep_b, give_b = gate_right_rest(run, left_gate, fixed_gate, few)
    got_b = exchange(give_b, other_replica)
    for hop in hops[1:]:
        (down,) = add(run, [down], [got], after=(give_b,))
        got = exchange(down, hop)
    (gate_a,) = add(run, [keep_a], [got_a], beside=gram_gate, after=(down,))
    got_a = exchange(gate_a, steps[0])
    (gate_b,) = add(run, [keep_b], [got_b], after=(gate_a,))
    got_b = exchange(gate_b, steps[0])
    for step in steps[1:]:
        (gate_a,) = add(run, [gate_a], [got_a])
        got_a = exchange(gate_a, step)
        (gate_b,) = add(run, [gate_b], [got_b])
        got_b = exchange(gate_b, step)
    gate_a, gram_gate = add(run, [gate_a], [got_a], [few * TILE, 2 * RANK], after=(gate_b,))
    other_a = exchange(gate_a, other_replica)
    col_stack, row_turned = solve(run, grams_down, left_down, gram_gate, left_gate)
    downs = add(run, [down], [got], in_two(slab), after=(col_stack,))
    others_down = to_other_core(downs)
    (gate_b,) = add(run, [gate_b], [got_b], after=(downs[0],))
    other_b = exchange(gate_b, other_replica)
    new_error_down, update_down, turned = rebuild(
        run, (None, col_stack), downs, others_down, fixed_down, (0, 1), slab // 2, after=(gate_b,)
    )
    new_error_gate, update_gate, _ = rebuild(
        run, (row_turned, None), [gate_a, gate_b], [other_a, other_b], fixed_gate, (0, 1), slab // 2,
        after=(turned,),
    )
    return (update_gate, update_down, new_error_gate, new_error_down)


def solution(mesh):
    split = P(("mix", "dp"), "tensor")
    in_specs = (split, split, split, split, P(None, "tensor"), P())
    out_specs = (split, split, split, split)

    def run(grad_gate, *rest):
        groups = mesh.shape["mix"] * mesh.shape["dp"]
        slab = grad_gate.shape[0] // groups
        width = grad_gate.shape[1] // mesh.shape["tensor"]
        fits = slab % (REPLICAS * TILE) == 0 and width % TILE == 0
        body = local if fits else local_plain
        return jax.shard_map(
            body, mesh=mesh, in_specs=in_specs, out_specs=out_specs, check_vma=False
        )(grad_gate, *rest)

    return run
```
